32 devices in a mesh: dp: 16 (over z, y, core), mp: 2 (over x).
Axes of the slice: x: 2, y: 2, z: 4, core: 2. Of those that a mesh axis runs over, the one named last changes fastest.
Arguments:
- pixels: bfloat16 [192, 48, 2304], P('dp', 'mp'), may hold values from -6 to 6
- labels: int32 [192], P('dp'), may hold values from 0 to 999
- valid_flags: int32 [192], P('dp'), may hold values 0 or 1
- keep_mask: int32 [3, 192], P(None, 'dp'), may hold values 0 or 1
- step_count: int32 [], replicated, may hold values from 2 to 20
- pointwise_weight: float32 [3, 2, 384, 1536], P(None, None, None, 'mp'), may hold values from -0.3125 to 0.3125
- pointwise_first: float32 [2304, 1536], P('dp', 'mp'), may hold values from -1.5258789e-05 to 1.5258789e-05
- pointwise_second: float32 [2304, 1536], P('dp', 'mp'), may hold values from 9.161251e-14 to 3.6645003e-13
- flat_weight: float32 [813696], replicated, may hold values from -2 to 2
- flat_first: float32 [813696], replicated, may hold values from -1.5258789e-05 to 1.5258789e-05
- flat_second: float32 [813696], replicated, may hold values from 9.161251e-14 to 3.6645003e-13
- vector_weight: float32 [13576], replicated, may hold values from -1 to 1.5
- vector_first: float32 [13576], replicated, may hold values from -6.1035156e-05 to 6.1035156e-05
- vector_second: float32 [13576], replicated, may hold values from 1.4658001e-12 to 5.8632006e-12
Outputs:
- loss_sum: float32 [], replicated
- valid_count: float32 [], replicated
- gradient_norm: float32 [], replicated
- pointwise_new: float32 [2304, 1536], P('dp', 'mp')
- pointwise_first_new: float32 [2304, 1536], P('dp', 'mp')
- pointwise_second_new: float32 [2304, 1536], P('dp', 'mp')
- pointwise_copy: bfloat16 [2304, 1536], P('dp', 'mp')
- flat_new: float32 [813696], replicated
- flat_first_new: float32 [813696], replicated
- flat_second_new: float32 [813696], replicated
- flat_copy: bfloat16 [813696], replicated
- vector_new: float32 [13576], replicated
- vector_first_new: float32 [13576], replicated
- vector_second_new: float32 [13576], replicated
- vector_copy: bfloat16 [13576], replicated
The draws below stay inside these ranges and needn't reach their ends.
All inputs are finite; a program needn't handle non-finite values. No bound on the sum of `valid_flags` or of `keep_mask` on one device may be relied on, other than what follows from the above.
Results may differ from the reference program's by a relative error of at most 0.011.
Values may be sent and summed in bfloat16 or wider, within the bound.
A program may use at most 512 MiB of HBM per device.

```python
import math
import jax
import jax.numpy as jnp
from jax import lax

C1 = 96
C2 = 192
C3 = 384
HID = 1536
CLASSES = 1000
PATCH = 48
KERNEL = 7
LAYERS = 3
SIDE = 12
B_DEV = 12
IMAGES = 192
FLAT = 813696
VEC = 13576
PARAMS = 4366216
N_DP = 16


def draw_flat_weight(key, part):
    lengths = [PATCH * C1, 4 * C1 * C2, 4 * C2 * C3, LAYERS * KERNEL * KERNEL * C3, C3 * CLASSES]
    factors = [PATCH ** (-0.5), (4 * C1) ** (-0.5), (4 * C2) ** (-0.5), 1.0 / KERNEL, 2.0 * C3 ** (-0.5)]
    pieces = []
    for number in range(5):
        subkey = jax.random.fold_in(key, number + 11)
        values = jax.random.truncated_normal(subkey, -3.0, 3.0, (lengths[number],), jnp.float32)
        pieces.append(values * factors[number])
    return jnp.concatenate(pieces)


def draw_vector_weight(key, part):
    gain_count = 2 * C1 + C2 + 2 * LAYERS * C3 + C3
    shift_count = VEC - gain_count
    gain_key = jax.random.fold_in(key, 21)
    shift_key = jax.random.fold_in(key, 22)
    gain_values = 1.0 + 0.15 * jax.random.truncated_normal(gain_key, -2.5, 2.5, (gain_count,), jnp.float32)
    shift_values = 0.2 * jax.random.truncated_normal(shift_key, -3.0, 3.0, (shift_count,), jnp.float32)
    return jnp.concatenate([gain_values, shift_values])


def plant(entries, key, least, largest):
    longest = entries.shape.index(max(entries.shape))
    spots = []
    for shift in (0, 1):
        where = [jax.random.randint(jax.random.fold_in(key, axis), (), 0, length) for axis, length in enumerate(entries.shape)]
        where[longest] = (where[longest] + shift) % entries.shape[longest]
        spots.append(tuple(where))
    return entries.at[spots[0]].set(least).at[spots[1]].set(largest)


def level_of(key, shape, split, least, top_value):
    def one(position, blocks):
        draws = jax.random.uniform(jax.random.fold_in(jax.random.fold_in(key, 6), position), (blocks,), jnp.float32, least / len(split), top_value / len(split))
        return jnp.repeat(jnp.exp(draws), shape[position] // blocks).reshape((-1,) + (1,) * (len(shape) - position - 1))

    gain = one(*split[0])
    for cut in split[1:]:
        gain = gain * one(*cut)
    return gain


def gaussian(key, dims, deviation, reach, split=(), kind=jnp.bfloat16):
    array = deviation * jax.random.normal(key, dims, jnp.float32)
    if split:
        array = array * level_of(key, dims, split, -0.22, 0.18)
    return jnp.clip(array, -reach, reach).astype(kind)


def setup_inputs(seed: int = 0) -> dict:
    streams_of = jax.random.split(jax.random.key(seed), 15)
    return {
        "pixels": gaussian(streams_of[0], (IMAGES, 4 * SIDE, 4 * SIDE * PATCH), 1.0, 6.0, ((0, 16), (1, 2))),
        "labels": plant(jax.random.randint(streams_of[1], (IMAGES,), 0, CLASSES), jax.random.fold_in(streams_of[1], 1), 0, CLASSES - 1).astype(jnp.int32),
        "valid_flags": plant((jax.random.randint(streams_of[2], (IMAGES,), 0, 8) < 7).astype(jnp.int32), jax.random.fold_in(streams_of[2], 1), 0, 1),
        "keep_mask": plant((jax.random.randint(streams_of[3], (LAYERS, IMAGES), 0, 5) < 4).astype(jnp.int32), jax.random.fold_in(streams_of[3], 1), 0, 1),
        "step_count": jax.random.randint(streams_of[4], (), 2, 21).astype(jnp.int32),
        "pointwise_weight": gaussian(streams_of[5], (LAYERS, 2, C3, HID), C3 ** -0.5, 0.3125, ((3, 2),), jnp.float32),
        "pointwise_first": gaussian(streams_of[6], (2 * LAYERS * C3, HID), (0.0022 * PARAMS ** -0.5), 1.52587890625e-05, ((0, 16), (1, 2)), jnp.float32),
        "pointwise_second": jnp.clip(jnp.exp(math.log(3.664500343794619e-13) - 1.3862944 * jax.random.uniform(streams_of[7], (2 * LAYERS * C3, HID), jnp.float32) ** level_of(streams_of[7], (2 * LAYERS * C3, HID), ((0, 16), (1, 2)), -0.2, 0.2)), 9.161250859486547e-14, 3.664500343794619e-13),
        "flat_weight": draw_flat_weight(jax.random.fold_in(streams_of[14], 71), 0),
        "flat_first": gaussian(streams_of[9], (FLAT,), (0.0022 * PARAMS ** -0.5), 1.52587890625e-05, (), jnp.float32),
        "flat_second": jnp.clip(jnp.exp(jax.random.uniform(streams_of[10], (FLAT,), jnp.float32, math.log(9.161250859486547e-14), math.log(3.664500343794619e-13))), 9.161250859486547e-14, 3.664500343794619e-13),
        "vector_weight": draw_vector_weight(jax.random.fold_in(streams_of[14], 71), 0),
        "vector_first": gaussian(streams_of[12], (VEC,), (0.0088 * PARAMS ** -0.5), 6.103515625e-05, (), jnp.float32),
        "vector_second": jnp.clip(jnp.exp(jax.random.uniform(streams_of[13], (VEC,), jnp.float32, math.log(1.4658001375178475e-12), math.log(5.86320055007139e-12))), 1.4658001375178475e-12, 5.86320055007139e-12),
    }


NORM_EPSILON = 1e-06
SMOOTH = 0.1
CLIP_LIMIT = 0.02
LEARN_RATE = 0.05
VECTOR_RATE = 0.15
WEIGHT_DECAY = 0.05
BETA_ONE = 0.9
BETA_TWO = 0.999
ADAM_EPSILON = 1e-08
PRECISE = lax.Precision.HIGHEST

@jax.custom_vjp
def low(v):
    return lax.optimization_barrier(v.astype(jnp.bfloat16)).astype(jnp.float32)

@jax.custom_vjp
def low_back(v):
    return v

def low_keep(v):
    return (low(v), None)

def low_pass(kept, grad):
    return (grad,)

def back_keep(v):
    return (v, None)

def back_low(kept, grad):
    return (low(grad),)
low.defvjp(low_keep, low_pass)
low_back.defvjp(back_keep, back_low)

def layer_norm(values, scales, shifts):
    average = lax.optimization_barrier(jnp.mean(values, axis=-1, keepdims=True))
    centred = values - average
    spread = lax.optimization_barrier(jnp.mean(centred * centred, axis=-1, keepdims=True))
    return centred * lax.rsqrt(spread + NORM_EPSILON) * scales + shifts

def patches(values):
    images, height, across, channels = values.shape
    blocks = values.reshape(images, height // 2, 2, across // 2, 2, channels)
    blocks = jnp.transpose(blocks, (0, 1, 3, 2, 4, 5))
    return blocks.reshape(images, height // 2, across // 2, 4 * channels)

def depthwise(values, kernel, offset):
    height, across = (values.shape[1], values.shape[2])
    margin = KERNEL // 2
    padded = jnp.pad(values, ((0, 0), (margin, margin), (margin, margin), (0, 0)))
    summed = jnp.broadcast_to(offset, values.shape)
    for row_tap in range(KERNEL):
        for column_tap in range(KERNEL):
            window = padded[:, row_tap:row_tap + height, column_tap:column_tap + across, :]
            summed = summed + window * kernel[row_tap * KERNEL + column_tap]
    return summed

def vector_lengths():
    return [C1, C1, C2, LAYERS * C3, LAYERS * C3, C3, C1, C1, C1, C2, C2, C3, LAYERS * C3, LAYERS * C3, LAYERS * HID, LAYERS * C3, C3, CLASSES]

def flat_lengths():
    return [PATCH * C1, 4 * C1 * C2, 4 * C2 * C3, LAYERS * KERNEL * KERNEL * C3, C3 * CLASSES]

def split_sizes(vector, lengths):
    pieces = []
    offset_now = 0
    for length in lengths:
        pieces.append(vector[offset_now:offset_now + length])
        offset_now = offset_now + length
    return pieces

def unpack(flat, vector):
    stem_weight, down_one, down_two, kernels, head_weight = split_sizes(flat, flat_lengths())
    matrices = (stem_weight.reshape(PATCH, C1), down_one.reshape(4 * C1, C2), down_two.reshape(4 * C2, C3), kernels.reshape(LAYERS, KERNEL * KERNEL, C3), head_weight.reshape(C3, CLASSES))
    return (matrices, split_sizes(vector, vector_lengths()))

def forward(params, pixel_group, label_group, valid_group, keep_group, valid_total):
    pointwise, flat, vector = params
    matrices, pieces = unpack(flat, vector)
    stem_weight, down_one, down_two, kernels, head_weight = matrices
    gain_stem, gain_one, gain_two, gain_block, layer_scale, gain_final, bias_stem, shift_stem, shift_one, bias_one, shift_two, bias_two, bias_depth, shift_block, bias_inner, bias_outer, shift_final, bias_head = pieces
    images = pixel_group.shape[0]
    patch_input = pixel_group.reshape(images, 4 * SIDE, 4 * SIDE, PATCH)
    stem_output = low_back(jnp.einsum('bhwp,pc->bhwc', patch_input, low(stem_weight), precision=PRECISE) + bias_stem)
    normed = low(layer_norm(layer_norm(stem_output, gain_stem, shift_stem), gain_one, shift_one))
    section = low_back(jnp.einsum('bhwk,kc->bhwc', patches(normed), low(down_one), precision=PRECISE) + bias_one)
    normed = low(layer_norm(section, gain_two, shift_two))
    residual = low_back(jnp.einsum('bhwk,kc->bhwc', patches(normed), low(down_two), precision=PRECISE) + bias_two)
    pointwise_low = low(pointwise)
    for layer_index in range(LAYERS):
        sent_rows = low(residual)
        depth = depthwise(sent_rows, kernels[layer_index], bias_depth.reshape(LAYERS, C3)[layer_index])
        normed = low(layer_norm(depth, gain_block.reshape(LAYERS, C3)[layer_index], shift_block.reshape(LAYERS, C3)[layer_index]))
        hidden = low_back(jnp.einsum('bhwc,cf->bhwf', normed, pointwise_low[layer_index, 0], precision=PRECISE) + bias_inner.reshape(LAYERS, HID)[layer_index])
        active = low(jax.nn.gelu(hidden, approximate=False))
        output = low_back(jnp.einsum('bhwf,cf->bhwc', active, pointwise_low[layer_index, 1], precision=PRECISE) + bias_outer.reshape(LAYERS, C3)[layer_index])
        residual = residual + layer_scale.reshape(LAYERS, C3)[layer_index] * output * keep_group[layer_index][:, None, None, None]
    pooled = lax.optimization_barrier(jnp.mean(residual, axis=(1, 2)))
    final_norm = low(layer_norm(pooled, gain_final, shift_final))
    logits = low_back(jnp.dot(final_norm, low(head_weight), precision=PRECISE) + bias_head)
    log_chance = jax.nn.log_softmax(logits, axis=-1)
    onehot = (label_group[:, None] == jnp.arange(CLASSES)[None, :]).astype(jnp.float32)
    picked = lax.optimization_barrier(jnp.sum(log_chance * onehot, axis=-1))
    per_image = -(1.0 - SMOOTH) * picked - SMOOTH * lax.optimization_barrier(jnp.mean(log_chance, axis=-1))
    return jnp.sum(per_image * valid_group) / valid_total

def add_pair(first_term, second_term):
    return first_term + second_term

def adam_update(weight, moment_one, moment_two, gradient, step_float, rate):
    first_new = BETA_ONE * moment_one + (1.0 - BETA_ONE) * gradient
    second_new = BETA_TWO * moment_two + (1.0 - BETA_TWO) * gradient * gradient
    first_hat = first_new / (1.0 - BETA_ONE ** step_float)
    second_hat = second_new / (1.0 - BETA_TWO ** step_float)
    weight_new = weight - rate * (first_hat / (jnp.sqrt(second_hat) + ADAM_EPSILON) + WEIGHT_DECAY * weight)
    return (weight_new, first_new, second_new, weight_new.astype(jnp.bfloat16))

def reference(pixels, labels, valid_flags, keep_mask, step_count, pointwise_weight, pointwise_first, pointwise_second, flat_weight, flat_first, flat_second, vector_weight, vector_first, vector_second):
    valid_all = valid_flags.astype(jnp.float32)
    valid_total = jnp.maximum(jnp.sum(valid_all), 1.0)
    params = (pointwise_weight, flat_weight, vector_weight)
    pixel_groups = pixels.astype(jnp.float32).reshape(N_DP, B_DEV, 4 * SIDE, 4 * SIDE * PATCH)
    label_groups = labels.reshape(N_DP, B_DEV)
    valid_groups = valid_all.reshape(N_DP, B_DEV)
    keep_groups = jnp.transpose(keep_mask.astype(jnp.float32).reshape(LAYERS, N_DP, B_DEV), (1, 0, 2))

    def one_group(running, inputs):
        pixel_group, label_group, valid_group, keep_group = inputs

        def loss_of(params_in):
            return forward(params_in, pixel_group, label_group, valid_group, keep_group, valid_total)
        loss_value, pullback = jax.vjp(loss_of, params)
        gradients = pullback(jnp.ones((), loss_value.dtype))[0]
        return (jax.tree.map(add_pair, running, (loss_value, gradients)), None)
    start_state = (jnp.zeros((), jnp.float32), jax.tree.map(jnp.zeros_like, params))
    finished = lax.scan(one_group, start_state, (pixel_groups, label_groups, valid_groups, keep_groups))[0]
    loss_total, gradients = finished
    pointwise_grad, flat_grad, vector_grad = gradients
    pointwise_grad = pointwise_grad.reshape(2 * LAYERS * C3, HID)
    squares = jnp.sum(pointwise_grad * pointwise_grad) + jnp.sum(flat_grad * flat_grad) + jnp.sum(vector_grad * vector_grad)
    gradient_norm = jnp.sqrt(squares)
    factor = CLIP_LIMIT / jnp.maximum(gradient_norm, CLIP_LIMIT)
    step_float = step_count.astype(jnp.float32)
    pointwise_out = adam_update(pointwise_weight.reshape(2 * LAYERS * C3, HID), pointwise_first, pointwise_second, factor * pointwise_grad, step_float, LEARN_RATE)
    flat_out = adam_update(flat_weight, flat_first, flat_second, factor * flat_grad, step_float, LEARN_RATE)
    vector_out = adam_update(vector_weight, vector_first, vector_second, factor * vector_grad, step_float, VECTOR_RATE)
    return (loss_total * valid_total, valid_total, gradient_norm, pointwise_out[0], pointwise_out[1], pointwise_out[2], pointwise_out[3], flat_out[0], flat_out[1], flat_out[2], flat_out[3], vector_out[0], vector_out[1], vector_out[2], vector_out[3])
```

```python
import jax
import numpy as np
from jax.sharding import PartitionSpec as P
import jax.numpy as jnp
from jax import lax
from jax.experimental import pallas as pl
from jax.experimental.pallas import tpu as pltpu

C1 = 96
C2 = 192
C3 = 384
HID = 1536
CLASSES = 1000
PATCH = 48
KERNEL = 7
LAYERS = 3
SIDE = 12
NORM_EPSILON = 1e-06
SMOOTH = 0.1
IMG = 6
COL = SIDE * IMG
ROWS = SIDE * COL
PAIR = 2 * COL
BF = jnp.bfloat16
F32 = jnp.float32
VMEM_LIMIT = 60 * 1024 * 1024
SHIFTED = COL + 40
TAPS = KERNEL * KERNEL


def dot(a, b, da=1, db=0):
    return lax.dot_general(a, b, (((da,), (db,)), ((), ())), preferred_element_type=F32)


def fold8(values):
    rows, lanes = values.shape
    return jnp.sum(values.reshape(rows // 8, 8, lanes), axis=0)


def stats(values, count, mask):
    average = jnp.sum(values, axis=-1, keepdims=True) * (1.0 / count)
    centred = values - average
    if mask is not None:
        centred = centred * mask
    spread = jnp.sum(centred * centred, axis=-1, keepdims=True) * (1.0 / count)
    scale = lax.rsqrt(spread + NORM_EPSILON)
    return centred * scale, scale


def norm_back(delta, xhat, scale, gain, count, mask):
    scaled = delta * gain
    first = jnp.sum(scaled, axis=-1, keepdims=True) * (1.0 / count)
    second = jnp.sum(scaled * xhat, axis=-1, keepdims=True) * (1.0 / count)
    out = (scaled - first - xhat * second) * scale
    if mask is not None:
        out = out * mask
    return out


def front_kernel(x_ref, perm_ref, wbig_ref, d1_ref, d2_ref, vs_ref, v2_ref, v3_ref,
                 xp_ref, n1_ref, s2_ref, n2_ref, res_ref, st_ref, n2s_ref):
    mask1 = (lax.broadcasted_iota(jnp.int32, (1, 128), 1) < C1).astype(F32)
    mask2 = (lax.broadcasted_iota(jnp.int32, (1, 256), 1) < C2).astype(F32)
    bias_stem, gain_stem, shift_stem = vs_ref[0:1, :], vs_ref[1:2, :], vs_ref[2:3, :]
    gain_one, shift_one = vs_ref[3:4, :], vs_ref[4:5, :]
    bias_one, gain_two, shift_two = v2_ref[0:1, :], v2_ref[1:2, :], v2_ref[2:3, :]
    chunk = 96

    def pair(g, _):
        x2 = dot(perm_ref[...], x_ref[:, pl.ds(pl.multiple_of(g * 384, 128), 384)]).astype(BF)
        xp_ref[g] = x2
        for q in range(4):
            o = dot(x2, wbig_ref[:, q * 256:(q + 1) * 256])
            st_ref[2 * q] = o[:, :128]
            st_ref[2 * q + 1] = o[:, 128:]

        def slab(j, _):
            for r in range(288 // chunk):
                v = st_ref[j, r * chunk:(r + 1) * chunk, :] + bias_stem
                xhat, _s = stats(v, C1, mask1)
                y = xhat * gain_stem + shift_stem
                xhat, _s = stats(y, C1, mask1)
                n1_ref[g, r * chunk:(r + 1) * chunk, pl.ds(pl.multiple_of(j * 128, 128), 128)] = (
                    xhat * gain_one + shift_one).astype(BF)
            return 0
        lax.fori_loop(0, 8, slab, 0)
        for q in range(4):
            c2, oc2 = q // 2, q % 2
            lanes = slice(q * 256, (q + 1) * 256)
            s2 = dot(n1_ref[g, 0:144, lanes], d1_ref[0]) + dot(n1_ref[g, 144:288, lanes], d1_ref[1]) + bias_one
            s2_ref[g, q] = s2
            xhat, _s = stats(s2, C2, mask2)
            n2 = xhat * gain_two + shift_two
            for or2 in range(2):
                n2s_ref[or2, c2 * 72:(c2 + 1) * 72, oc2 * 256:(oc2 + 1) * 256] = n2[or2 * 72:(or2 + 1) * 72]
        low0, low1 = n2s_ref[0].astype(BF), n2s_ref[1].astype(BF)
        rows = pl.ds(pl.multiple_of(g * 144, 16), 144)
        n2_ref[0, rows, :] = low0
        n2_ref[1, rows, :] = low1
        res_ref[rows, :] = dot(low0, d2_ref[0]) + dot(low1, d2_ref[1]) + v3_ref[0:1, :]
        return 0
    lax.fori_loop(0, 6, pair, 0)


def call(kernel, outs, scratch, flops=0, nbytes=0, trans=0):
    return pl.pallas_call(
        kernel,
        out_shape=outs,
        scratch_shapes=scratch,
        cost_estimate=pl.CostEstimate(flops=flops, bytes_accessed=nbytes, transcendentals=trans),
        compiler_params=pltpu.CompilerParams(vmem_limit_bytes=VMEM_LIMIT),
    )


def sds(shape, dt=F32):
    return jax.ShapeDtypeStruct(shape, dt)


def front(x, perm, wbig, d1, d2, vs, v2, v3):
    return call(
        front_kernel,
        (sds((6, 288, 384), BF), sds((6, 288, 1024), BF), sds((6, 4, 144, 256)), sds((2, ROWS, 512), BF), sds((ROWS, C3))),
        [pltpu.VMEM((8, 288, 128), F32), pltpu.VMEM((2, 144, 512), F32)],
        flops=4_000_000_000,
    )(x, perm, wbig, d1, d2, vs, v2, v3)


def spread_shifted(cp_ref, lt, c, val):
    for ki in range(4):
        cp_ref[ki, lt, c, 18 - 2 * ki:90 - 2 * ki, :] = val


def zero_edges(cp_ref):
    head, tail = jnp.zeros((24, 128), F32), jnp.zeros((32, 128), F32)
    for ki in range(4):
        for lt in range(3):
            def body(c, _):
                cp_ref[ki, lt, c, 0:24, :] = head
                cp_ref[ki, lt, c, 80:112, :] = tail
                return 0
            lax.fori_loop(0, 12, body, 0)


def gate(h):
    phi_wide = 0.5 * (1.0 + lax.erf(h * 0.7071067811865476))
    dens = jnp.exp(h * h * -0.5) * 0.3989422804014327
    return h * phi_wide, phi_wide + h * dens


def block_kernel(res_ref, kern_ref, vec_ref, bin_ref, keep_ref, own_ref, other_ref,
                 new_ref, depth_ref, normed_ref, act_ref, dg_ref, out_ref, cp_ref, wb_ref):
    zero_edges(cp_ref)

    def prep(c, _):
        rows = pl.ds(pl.multiple_of(c * COL, 8), COL)
        for lt in range(3):
            val = res_ref[rows, lt * 128:(lt + 1) * 128].astype(BF).astype(F32)
            spread_shifted(cp_ref, lt, c, val)
        return 0
    lax.fori_loop(0, SIDE, prep, 0)
    for lt in range(3):
        for t in range(TAPS):
            wb_ref[lt, t] = jnp.broadcast_to(kern_ref[t:t + 1, lt * 128:(lt + 1) * 128], (8, 128))
    for lt in range(3):
        lanes = slice(lt * 128, (lt + 1) * 128)
        bias = jnp.broadcast_to(vec_ref[0:1, lanes], (8, 128))

        def conv(v, _, lt=lt, lanes=lanes, bias=bias):
            acc = [bias] * SIDE
            for i in range(KERNEL):
                k = (6 * i) % 8
                row = pl.ds(pl.multiple_of(6 * i - k + v * 8, 8), 8)
                xs = [cp_ref[k // 2, lt, c, row, :] for c in range(SIDE)]
                for j in range(KERNEL):
                    w = wb_ref[lt, i * KERNEL + j]
                    for c in range(SIDE):
                        cc = c + j - 3
                        if 0 <= cc < SIDE:
                            acc[c] = acc[c] + w * xs[cc]
            for c in range(SIDE):
                depth_ref[pl.ds(pl.multiple_of(c * COL + v * 8, 8), 8), lanes] = acc[c]
            return 0
        lax.fori_loop(0, COL // 8, conv, 0)
    gain, shift = vec_ref[1:2, :], vec_ref[2:3, :]

    def norm(r, _):
        rows = pl.ds(pl.multiple_of(r * 48, 16), 48)
        xhat, _s = stats(depth_ref[rows, :], C3, None)
        normed_ref[rows, :] = (xhat * gain + shift).astype(BF)
        return 0
    lax.fori_loop(0, ROWS // 48, norm, 0)
    bias_out, scale = vec_ref[3:4, :], vec_ref[4:5, :]
    keep_scale = keep_ref[...] * scale

    def mm(m, _):
        rows = pl.ds(pl.multiple_of(m * PAIR, 16), PAIR)
        low = normed_ref[rows, :]
        for n in range(HID // 256):
            lanes = slice(n * 256, (n + 1) * 256)
            half = own_ref if n < 3 else other_ref
            h = dot(low, half[0, :, (n % 3) * 256:(n % 3 + 1) * 256]) + bin_ref[:, lanes]
            act, dg = gate(h)
            act_ref[rows, lanes] = act.astype(BF)
            dg_ref[rows, lanes] = dg.astype(BF)
        o = (dot(act_ref[rows, :HID // 2], own_ref[1], 1, 1) + dot(act_ref[rows, HID // 2:], other_ref[1], 1, 1)
             + bias_out)
        out_ref[rows, :] = o
        new_ref[rows, :] = res_ref[rows, :] + jnp.concatenate([keep_scale, keep_scale], axis=0) * o
        return 0
    lax.fori_loop(0, ROWS // PAIR, mm, 0)


def block(res, kern, vec, bin_, keep, own, other):
    return call(
        block_kernel,
        (sds((ROWS, C3)), sds((ROWS, C3)), sds((ROWS, C3), BF), sds((ROWS, HID), BF), sds((ROWS, HID), BF), sds((ROWS, C3))),
        [pltpu.VMEM((4, 3, SIDE, SHIFTED, 128), F32), pltpu.VMEM((3, TAPS, 8, 128), F32)],
        flops=4_000_000_000,
    )(res, kern, vec, bin_, keep, own, other)


def head_kernel(res_ref, vec_ref, head_ref, bias_ref, label_ref, valid_ref,
                dr_ref, dhead_ref, dbias_ref, dvec_ref, loss_ref, sum_ref):
    def add(c, total):
        return total + res_ref[pl.ds(pl.multiple_of(c * COL, 8), COL), :]
    total = lax.fori_loop(1, SIDE, add, res_ref[0:COL, :])
    sum_ref[...] = total
    pooled = sum_ref[0:IMG, :]
    for r in range(1, SIDE):
        pooled = pooled + sum_ref[r * IMG:(r + 1) * IMG, :]
    pooled = jnp.concatenate([pooled * (1.0 / (SIDE * SIDE)), jnp.zeros((2, C3), F32)], axis=0)
    gain, shift = vec_ref[0:1, :], vec_ref[1:2, :]
    xhat, scale = stats(pooled, C3, None)
    final = (xhat * gain + shift).astype(BF)
    logits = dot(final, head_ref[...]) + bias_ref[...]
    top = jnp.max(logits, axis=-1, keepdims=True)
    shifted = logits - top
    expd = jnp.exp(shifted)
    total = jnp.sum(expd, axis=-1, keepdims=True)
    log_chance = shifted - jnp.log(total)
    onehot = (label_ref[...] == lax.broadcasted_iota(jnp.int32, (8, CLASSES), 1)).astype(F32)
    valid = valid_ref[...]
    per_image = (-(1.0 - SMOOTH) * jnp.sum(log_chance * onehot, axis=-1, keepdims=True)
                 - SMOOTH * jnp.mean(log_chance, axis=-1, keepdims=True))
    loss_ref[...] = jnp.broadcast_to(jnp.sum(per_image * valid, axis=0, keepdims=True), (1, 128))
    delta = (jnp.exp(log_chance) - (1.0 - SMOOTH) * onehot - SMOOTH / CLASSES) * valid
    dbias_ref[...] = jnp.sum(delta, axis=0, keepdims=True)
    high = delta.astype(BF)
    rest = (delta - high.astype(F32)).astype(BF)
    dhead_ref[...] = dot(final, high, 0, 0) + dot(final, rest, 0, 0)
    dfinal = dot(high, head_ref[...], 1, 1) + dot(rest, head_ref[...], 1, 1)
    dvec_ref[0:1, :] = jnp.sum(dfinal * xhat, axis=0, keepdims=True)
    dvec_ref[1:2, :] = jnp.sum(dfinal, axis=0, keepdims=True)
    dpooled = norm_back(dfinal, xhat, scale, gain, C3, None) * (1.0 / (SIDE * SIDE))
    for r in range(SIDE):
        sum_ref[r * IMG:(r + 1) * IMG, :] = dpooled[0:IMG, :]

    def put(c, _):
        dr_ref[pl.ds(pl.multiple_of(c * COL, 8), COL), :] = sum_ref[...]
        return 0
    lax.fori_loop(0, SIDE, put, 0)


def head(res, vec, head_low, bias, labels, valid):
    return call(
        head_kernel,
        (sds((ROWS, C3)), sds((C3, CLASSES)), sds((1, CLASSES)), sds((2, C3)), sds((1, 128))),
        [pltpu.VMEM((COL, C3), F32)],
        flops=20_000_000,
    )(res, vec, head_low, bias, labels, valid)


def block_back_kernel(dr_ref, keep_ref, vec_ref, act_ref, dg_ref, out_ref, normed_ref, depth_ref, res_ref, kern_ref,
                      own_ref, other_ref,
                      new_ref, down_ref, dother_ref, dkern_ref, dvec_ref, dbin_ref,
                      cp_ref, wb_ref, dout_ref, dhid_ref, sent_ref, kacc_ref):
    zero_edges(cp_ref)
    for lt in range(3):
        for t in range(TAPS):
            wb_ref[lt, t] = jnp.broadcast_to(kern_ref[t:t + 1, lt * 128:(lt + 1) * 128], (8, 128))
    kacc_ref[...] = jnp.zeros_like(kacc_ref)
    gain, scale = vec_ref[1:2, :], vec_ref[4:5, :]

    def pre(m, carry):
        a_scale, a_bias = carry
        rows = pl.ds(pl.multiple_of(m * PAIR, 16), PAIR)
        keep = jnp.concatenate([keep_ref[...], keep_ref[...]], axis=0)
        dk = dr_ref[rows, :] * keep
        low = (dk * scale).astype(BF)
        dout_ref[rows, :] = low
        sent_ref[rows, :] = res_ref[rows, :].astype(BF).astype(F32)
        return a_scale + fold8(dk * out_ref[rows, :]), a_bias + fold8(low.astype(F32))
    zero = jnp.zeros((8, C3), F32)
    a_scale, a_bias = lax.fori_loop(0, ROWS // PAIR, pre, (zero, zero))
    dvec_ref[4:5, :] = jnp.sum(a_scale, axis=0, keepdims=True)
    dvec_ref[3:4, :] = jnp.sum(a_bias, axis=0, keepdims=True)
    dbin_ref[...] = jnp.zeros_like(dbin_ref)

    def mm(m, carry):
        a_gain, a_shift, a_depth = carry
        rows = pl.ds(pl.multiple_of(m * PAIR, 16), PAIR)
        low = dout_ref[rows, :]
        for n in range(HID // 256):
            lanes = slice(n * 256, (n + 1) * 256)
            half = own_ref if n < 3 else other_ref
            d = dot(low, half[1, :, (n % 3) * 256:(n % 3 + 1) * 256]) * dg_ref[rows, lanes].astype(F32)
            dlow = d.astype(BF)
            dhid_ref[rows, lanes] = dlow
            dbin_ref[:, lanes] += fold8(dlow.astype(F32))
        dn = dot(dhid_ref[rows, :HID // 2], own_ref[0], 1, 1) + dot(dhid_ref[rows, HID // 2:], other_ref[0], 1, 1)
        for c2 in range(2):
            sub = pl.ds(pl.multiple_of(m * PAIR + c2 * COL, 8), COL)
            xhat, rs = stats(depth_ref[sub, :], C3, None)
            d = dn[c2 * COL:(c2 + 1) * COL]
            a_gain = a_gain + fold8(d * xhat)
            a_shift = a_shift + fold8(d)
            dd = norm_back(d, xhat, rs, gain, C3, None)
            a_depth = a_depth + fold8(dd)
            for lt in range(3):
                spread_shifted(cp_ref, lt, 2 * m + c2, dd[:, lt * 128:(lt + 1) * 128])
        return a_gain, a_shift, a_depth
    a_gain, a_shift, a_depth = lax.fori_loop(0, ROWS // PAIR, mm, (zero, zero, zero))
    dvec_ref[0:1, :] = jnp.sum(a_depth, axis=0, keepdims=True)
    dvec_ref[1:2, :] = jnp.sum(a_gain, axis=0, keepdims=True)
    dvec_ref[2:3, :] = jnp.sum(a_shift, axis=0, keepdims=True)
    dvec_ref[5:8, :] = jnp.zeros((3, C3), F32)
    for n in range(HID // 256):
        lanes = slice(n * 256, (n + 1) * 256)
        half = down_ref if n < 3 else dother_ref
        part = slice((n % 3) * 256, (n % 3 + 1) * 256)
        half[1, :, part] = dot(dout_ref[...], act_ref[:, lanes], 0, 0).astype(BF)
        half[0, :, part] = dot(normed_ref[...], dhid_ref[:, lanes], 0, 0).astype(BF)
    for lt in range(3):
        lanes = slice(lt * 128, (lt + 1) * 128)

        def conv(v, _, lt=lt, lanes=lanes):
            spots = [pl.ds(pl.multiple_of(c * COL + v * 8, 8), 8) for c in range(SIDE)]
            acc = [dr_ref[s, lanes] for s in spots]
            sent = [sent_ref[s, lanes] for s in spots]
            for i in range(KERNEL):
                flip = 6 - i
                k = (6 * flip) % 8
                row = pl.ds(pl.multiple_of(6 * flip - k + v * 8, 8), 8)
                xs = [cp_ref[k // 2, lt, c, row, :] for c in range(SIDE)]
                for j in range(KERNEL):
                    t = i * KERNEL + j
                    w = wb_ref[lt, t]
                    tap = None
                    for c in range(SIDE):
                        cc = c - (j - 3)
                        if 0 <= cc < SIDE:
                            acc[c] = acc[c] + w * xs[cc]
                            term = sent[c] * xs[cc]
                            tap = term if tap is None else tap + term
                    kacc_ref[lt, t] += tap
            for c in range(SIDE):
                new_ref[spots[c], lanes] = acc[c]
            return 0
        lax.fori_loop(0, COL // 8, conv, 0)
    for lt in range(3):
        lanes = slice(lt * 128, (lt + 1) * 128)
        for t in range(TAPS):
            dkern_ref[t:t + 1, lanes] = jnp.sum(kacc_ref[lt, t], axis=0, keepdims=True)


def block_back(dr, keep, vec, act, dg, out, normed, depth, res, kern, own, other):
    return call(
        block_back_kernel,
        (sds((ROWS, C3)), sds((2, C3, HID // 2), BF), sds((2, C3, HID // 2), BF), sds((TAPS, C3)), sds((8, C3)), sds((8, HID))),
        [pltpu.VMEM((4, 3, SIDE, SHIFTED, 128), F32), pltpu.VMEM((3, TAPS, 8, 128), F32),
         pltpu.VMEM((ROWS, C3), BF), pltpu.VMEM((ROWS, HID), BF), pltpu.VMEM((ROWS, C3), F32),
         pltpu.VMEM((3, TAPS, 8, 128), F32)],
        flops=8_000_000_000,
    )(dr, keep, vec, act, dg, out, normed, depth, res, kern, own, other)


def back_kernel(dr_ref, xp_ref, n1_ref, s2_ref, n2_ref, wbig_ref, d1_ref, d2_ref, vs_ref, v2_ref,
                dw_ref, dd1_ref, dd2_ref, dvs_ref, dv2_ref, dv3_ref,
                st_ref, dn1_ref, dlow_ref, base_ref, mid_ref, aw_ref):
    mask1 = (lax.broadcasted_iota(jnp.int32, (1, 128), 1) < C1).astype(F32)
    mask2 = (lax.broadcasted_iota(jnp.int32, (1, 256), 1) < C2).astype(F32)
    bias_stem, gain_stem, shift_stem = vs_ref[0:1, :], vs_ref[1:2, :], vs_ref[2:3, :]
    gain_one = vs_ref[3:4, :]
    gain_two = v2_ref[1:2, :]
    chunk = 96
    z1, z2, z3 = jnp.zeros((8, 128), F32), jnp.zeros((8, 256), F32), jnp.zeros((8, C3), F32)
    dd1_ref[...] = jnp.zeros_like(dd1_ref)
    aw_ref[...] = jnp.zeros_like(aw_ref)

    def pair(g, carry):
        rows = pl.ds(pl.multiple_of(g * 144, 16), 144)
        base = dr_ref[rows, :].astype(BF)
        base_ref[rows, :] = base
        a3 = carry[0] + fold8(base.astype(F32))
        a_bias2, a_gain2, a_shift2 = carry[1:4]
        dn2 = [dot(base, d2_ref[or2], 1, 1) for or2 in range(2)]
        for q in range(4):
            c2, oc2 = q // 2, q % 2
            lanes = slice(q * 256, (q + 1) * 256)
            d = jnp.concatenate(
                [dn2[or2][c2 * 72:(c2 + 1) * 72, oc2 * 256:(oc2 + 1) * 256] for or2 in range(2)], axis=0)
            xhat, rs = stats(s2_ref[g, q], C2, mask2)
            a_gain2 = a_gain2 + fold8(d * xhat)
            a_shift2 = a_shift2 + fold8(d)
            mid = norm_back(d, xhat, rs, gain_two, C2, mask2).astype(BF)
            a_bias2 = a_bias2 + fold8(mid.astype(F32))
            for or1 in range(2):
                part = slice(or1 * 144, (or1 + 1) * 144)
                dd1_ref[or1] += dot(n1_ref[g, part, lanes], mid, 0, 0)
                o = dot(mid, d1_ref[or1], 1, 1)
                dn1_ref[2 * q, part, :] = o[:, :128]
                dn1_ref[2 * q + 1, part, :] = o[:, 128:]
        for q in range(4):
            o = dot(xp_ref[g], wbig_ref[:, q * 256:(q + 1) * 256])
            st_ref[2 * q] = o[:, :128]
            st_ref[2 * q + 1] = o[:, 128:]

        def slab(j, sums):
            b0, g0, s0, g1, s1 = sums
            for r in range(288 // chunk):
                part = slice(r * chunk, (r + 1) * chunk)
                v = st_ref[j, part, :] + bias_stem
                xa, ra = stats(v, C1, mask1)
                y = xa * gain_stem + shift_stem
                xb, rb = stats(y, C1, mask1)
                d = dn1_ref[j, part, :]
                g1 = g1 + fold8(d * xb)
                s1 = s1 + fold8(d)
                dy = norm_back(d, xb, rb, gain_one, C1, mask1)
                g0 = g0 + fold8(dy * xa)
                s0 = s0 + fold8(dy)
                dv = norm_back(dy, xa, ra, gain_stem, C1, mask1).astype(BF)
                b0 = b0 + fold8(dv.astype(F32))
                dlow_ref[part, pl.ds(pl.multiple_of(j * 128, 128), 128)] = dv
            return b0, g0, s0, g1, s1
        sums = lax.fori_loop(0, 8, slab, carry[4:])
        aw_ref[...] += dot(xp_ref[g], dlow_ref[...], 0, 0)
        return (a3, a_bias2, a_gain2, a_shift2) + tuple(sums)
    done = lax.fori_loop(0, 6, pair, (z3, z2, z2, z2, z1, z1, z1, z1, z1))
    for or2 in range(2):
        dd2_ref[or2] = dot(n2_ref[or2], base_ref[...], 0, 0)
    total = aw_ref[0:48, 0:128]
    for j in range(1, 8):
        total = total + aw_ref[j * 48:(j + 1) * 48, j * 128:(j + 1) * 128]
    dw_ref[...] = total
    dv3_ref[...] = jnp.sum(done[0], axis=0, keepdims=True)
    for n in range(3):
        dv2_ref[n:n + 1, :] = jnp.sum(done[1 + n], axis=0, keepdims=True)
    for n in range(5):
        dvs_ref[n:n + 1, :] = jnp.sum(done[4 + n], axis=0, keepdims=True)


def back(dr, xp, n1, s2, n2, wbig, d1, d2, vs, v2):
    return call(
        back_kernel,
        (sds((48, 128)), sds((2, 256, 256)), sds((2, 512, C3)), sds((5, 128)), sds((3, 256)), sds((1, C3))),
        [pltpu.VMEM((8, 288, 128), F32), pltpu.VMEM((8, 288, 128), F32), pltpu.VMEM((288, 1024), BF),
         pltpu.VMEM((ROWS, C3), BF), pltpu.VMEM((8, 128), BF), pltpu.VMEM((384, 1024), F32)],
        flops=8_000_000_000,
    )(dr, xp, n1, s2, n2, wbig, d1, d2, vs, v2)


CLIP_LIMIT = 0.02
LEARN_RATE = 0.05
VECTOR_RATE = 0.15
WEIGHT_DECAY = 0.05
BETA_ONE = 0.9
BETA_TWO = 0.999
ADAM_EPSILON = 1e-08


def vector_lengths():
    return [C1, C1, C2, LAYERS * C3, LAYERS * C3, C3, C1, C1, C1, C2, C2, C3, LAYERS * C3, LAYERS * C3,
            LAYERS * HID, LAYERS * C3, C3, CLASSES]


def flat_lengths():
    return [PATCH * C1, 4 * C1 * C2, 4 * C2 * C3, LAYERS * TAPS * C3, C3 * CLASSES]


def split_sizes(vector, lengths):
    pieces = []
    offset_now = 0
    for length in lengths:
        pieces.append(vector[offset_now:offset_now + length])
        offset_now = offset_now + length
    return pieces


def adam_update(weight, moment_one, moment_two, gradient, step_float, rate):
    first_new = BETA_ONE * moment_one + (1.0 - BETA_ONE) * gradient
    second_new = BETA_TWO * moment_two + (1.0 - BETA_TWO) * gradient * gradient
    first_hat = first_new / (1.0 - BETA_ONE**step_float)
    second_hat = second_new / (1.0 - BETA_TWO**step_float)
    weight_new = weight - rate * (first_hat / (jnp.sqrt(second_hat) + ADAM_EPSILON) + WEIGHT_DECAY * weight)
    return (weight_new, first_new, second_new, weight_new.astype(BF))


def row_source():
    target = np.arange(4 * COL)
    img = target % IMG
    r = target // IMG % SIDE
    or2 = target // COL % 2
    or1 = target // (2 * COL)
    row = 4 * r + 2 * or2 + or1
    return (row // (2 * SIDE)) * (2 * COL) + img * (2 * SIDE) + row % (2 * SIDE)


def widen(vector, width):
    return jnp.pad(vector, (0, width - vector.shape[0]))


def per_device(pixels, labels, valid_flags, keep_mask, step_count, pointwise_weight, pointwise_first, pointwise_second,
               flat_weight, flat_first, flat_second, vector_weight, vector_first, vector_second):
    m = lax.axis_index("mp")
    swap = [(0, 1), (1, 0)]
    half_images = pixels.shape[0] // 2
    mine = lambda a, axis, which: lax.dynamic_slice_in_dim(a, which * half_images, half_images, axis)
    received = lax.ppermute(mine(pixels, 0, 1 - m), "mp", swap)
    x = jnp.concatenate([mine(pixels, 0, m), received], axis=0).reshape(4 * COL, 4 * SIDE * PATCH)
    low = pointwise_weight.astype(BF)
    other = [lax.ppermute(low[l], "mp", swap) for l in range(LAYERS)]
    source = (jnp.asarray(row_source(), jnp.int32) + m * (2 * COL)) % (4 * COL)
    perm = (source[:, None] == lax.broadcasted_iota(jnp.int32, (1, 4 * COL), 1)).astype(BF)
    stem_weight, down_one, down_two, kernels, head_weight = split_sizes(flat_weight, flat_lengths())
    (gain_stem, gain_one, gain_two, gain_block, layer_scale, gain_final, bias_stem, shift_stem, shift_one, bias_one,
     shift_two, bias_two, bias_depth, shift_block, bias_inner, bias_outer, shift_final,
     bias_head) = split_sizes(vector_weight, vector_lengths())
    kernels = kernels.reshape(LAYERS, TAPS, C3)
    stem_pad = jnp.pad(stem_weight.reshape(PATCH, C1).astype(BF), ((0, 0), (0, 32)))
    wbig = (jnp.eye(8, dtype=BF)[:, None, :, None] * stem_pad[None, :, None, :]).reshape(384, 1024)
    d1 = jnp.pad(down_one.astype(BF).reshape(2, 2, C1, C2), ((0, 0), (0, 0), (0, 32), (0, 64))).reshape(2, 256, 256)
    d2 = jnp.pad(down_two.astype(BF).reshape(2, 2, C2, C3), ((0, 0), (0, 0), (0, 64), (0, 0))).reshape(2, 512, C3)
    head_low = head_weight.astype(BF).reshape(C3, CLASSES)
    vs = jnp.stack([widen(v, 128) for v in (bias_stem, gain_stem, shift_stem, gain_one, shift_one)])
    v2 = jnp.stack([widen(v, 256) for v in (bias_one, gain_two, shift_two)])
    v3 = bias_two[None]
    layered = lambda v: v.reshape(LAYERS, -1)
    vec = jnp.stack([layered(v) for v in (bias_depth, gain_block, shift_block, bias_outer, layer_scale)], axis=1)
    bins = bias_inner.reshape(LAYERS, 2, HID // 2)
    bins = jnp.where(m == 0, bins, bins[:, ::-1]).reshape(LAYERS, 1, HID)
    keep = jnp.tile(mine(keep_mask, 1, m).astype(F32), (1, SIDE))
    keep = jnp.broadcast_to(keep[:, :, None], (LAYERS, COL, C3))
    label8 = jnp.pad(mine(labels, 0, m), (0, 2))[:, None]
    valid_own = mine(valid_flags, 0, m).astype(F32)
    valid8 = jnp.pad(valid_own, (0, 2))[:, None]
    xp, n1, s2, n2, res = front(x, perm, wbig, d1, d2, vs, v2, v3)
    kept = []
    for l in range(LAYERS):
        new, depth, normed, act, dg, out = block(res, kernels[l], vec[l], bins[l], keep[l], low[l], other[l])
        kept.append((act, dg, out, normed, depth, res))
        res = new
    dr, dhead, dbias_head, dvec_final, loss = head(res, jnp.stack([gain_final, shift_final]), head_low, bias_head[None],
                                                   label8, valid8)
    grads = [None] * LAYERS
    for l in range(LAYERS - 1, -1, -1):
        dr, gown, gother, dkern, dvec, dbin = block_back(dr, keep[l], vec[l], *kept[l], kernels[l], low[l], other[l])
        grads[l] = (gown, gother, dkern, dvec, jnp.sum(dbin, axis=0))
    dw, dd1, dd2, dvs, dv2, dv3 = back(dr, xp, n1, s2, n2, wbig, d1, d2, vs, v2)
    summed = []
    for l in range(LAYERS):
        summed.append((grads[l][0].astype(F32) + lax.ppermute(grads[l][1], "mp", swap).astype(F32)).astype(BF))
    pointwise_grad = jnp.concatenate(summed).reshape(2 * LAYERS * C3, HID // 2)
    pointwise_own = lax.psum_scatter(pointwise_grad, "dp", scatter_dimension=0, tiled=True).astype(F32)
    dbins = jnp.stack([g[4] for g in grads]).reshape(LAYERS, 2, HID // 2)
    dbins = jnp.where(m == 0, dbins, dbins[:, ::-1])
    flat_grad = jnp.concatenate([
        dw[:, :C1].reshape(-1),
        dd1.reshape(2, 2, 128, 256)[:, :, :C1, :C2].reshape(-1),
        dd2.reshape(2, 2, 256, C3)[:, :, :C2].reshape(-1),
        jnp.stack([g[2] for g in grads]).reshape(-1),
        dhead.reshape(-1),
    ]).astype(BF)
    dvecs = jnp.stack([g[3] for g in grads])
    vector_grad = jnp.concatenate([
        dvs[1, :C1], dvs[3, :C1], dv2[1, :C2], dvecs[:, 1].reshape(-1), dvecs[:, 4].reshape(-1), dvec_final[0],
        dvs[0, :C1], dvs[2, :C1], dvs[4, :C1], dv2[0, :C2], dv2[2, :C2], dv3[0], dvecs[:, 0].reshape(-1),
        dvecs[:, 2].reshape(-1), dbins.reshape(-1), dvecs[:, 3].reshape(-1), dvec_final[1], dbias_head[0],
        loss[0, :1], jnp.sum(valid_own)[None],
    ])
    both = ("dp", "mp")
    flat_sum = lax.psum(flat_grad, both).astype(F32)
    vector_sum = lax.psum(vector_grad, both)
    pointwise_total = lax.psum(jnp.sum(pointwise_own * pointwise_own), both)
    loss_total = vector_sum[-2]
    valid_total = jnp.maximum(vector_sum[-1], 1.0)
    vector_sum = vector_sum[:-2]
    gradient_norm = jnp.sqrt(pointwise_total + jnp.sum(flat_sum * flat_sum) + jnp.sum(vector_sum * vector_sum)) / valid_total
    factor = CLIP_LIMIT / jnp.maximum(gradient_norm, CLIP_LIMIT) / valid_total
    step_float = step_count.astype(F32)
    rows_owned = pointwise_first.shape[0]
    master_rows = pointwise_weight.reshape(2 * LAYERS * C3, HID // 2)
    master_own = lax.dynamic_slice_in_dim(master_rows, lax.axis_index("dp") * rows_owned, rows_owned, 0)
    pointwise_out = adam_update(master_own, pointwise_first, pointwise_second, factor * pointwise_own, step_float, LEARN_RATE)
    flat_out = adam_update(flat_weight, flat_first, flat_second, factor * flat_sum, step_float, LEARN_RATE)
    vector_out = adam_update(vector_weight, vector_first, vector_second, factor * vector_sum, step_float, VECTOR_RATE)
    return (loss_total, valid_total, gradient_norm, *pointwise_out, *flat_out, *vector_out)


def solution(mesh):
    placed = (P("dp", "mp", None), P("dp"), P("dp"), P(None, "dp"), P(), P(None, None, None, "mp"), P("dp", "mp"),
              P("dp", "mp"), P(), P(), P(), P(), P(), P())
    return jax.shard_map(
        per_device,
        mesh=mesh,
        in_specs=placed,
        out_specs=(P(), P(), P()) + (P("dp", "mp"),) * 4 + (P(),) * 8,
        check_vma=False,
    )
```

```python
import functools
import jax
import numpy as np
from jax.sharding import PartitionSpec as P
import jax.numpy as jnp
from jax import lax
from jax.experimental import pallas as pl
from jax.experimental.pallas import tpu as pltpu

C1 = 96
C2 = 192
C3 = 384
HID = 1536
CLASSES = 1000
PATCH = 48
KERNEL = 7
LAYERS = 3
SIDE = 12
NORM_EPSILON = 1e-06
SMOOTH = 0.1
CLIP_LIMIT = 0.02
IMG = 6
COL = SIDE * IMG
ROWS = SIDE * COL
PAIR = 2 * COL
BF = jnp.bfloat16
F32 = jnp.float32
VMEM_LIMIT = 60 * 1024 * 1024
SHIFTED = COL + 40
TAPS = KERNEL * KERNEL
WIDE = 1024
STEM_LINES = PATCH * C1 // 128
ONE_LINES = 4 * C1 * C2 // 128
TWO_LINES = 4 * C2 * C3 // 128
KERN_LINES = LAYERS * TAPS * C3 // 128
HEAD_LINES = C3 * CLASSES // 128
FLAT_LINES = STEM_LINES + ONE_LINES + TWO_LINES + KERN_LINES + HEAD_LINES


def dot(a, b, da=1, db=0):
    return lax.dot_general(a, b, (((da,), (db,)), ((), ())), preferred_element_type=F32)


def fold8(values):
    rows, lanes = values.shape
    return jnp.sum(values.reshape(rows // 8, 8, lanes), axis=0)


def stats(values, count, mask):
    average = jnp.sum(values, axis=-1, keepdims=True) * (1.0 / count)
    centred = values - average
    if mask is not None:
        centred = centred * mask
    spread = jnp.sum(centred * centred, axis=-1, keepdims=True) * (1.0 / count)
    scale = lax.rsqrt(spread + NORM_EPSILON)
    return centred * scale, scale


def norm_back(delta, xhat, scale, gain, count, mask):
    scaled = delta * gain
    first = jnp.sum(scaled, axis=-1, keepdims=True) * (1.0 / count)
    second = jnp.sum(scaled * xhat, axis=-1, keepdims=True) * (1.0 / count)
    out = (scaled - first - xhat * second) * scale
    if mask is not None:
        out = out * mask
    return out


def front_kernel(x_ref, perm_ref, wbig_ref, d1_ref, d2_ref, vs_ref, v2_ref, v3_ref,
                 xp_ref, n1_ref, s2_ref, n2_ref, res_ref, st_ref, n2s_ref):
    mask1 = (lax.broadcasted_iota(jnp.int32, (1, 128), 1) < C1).astype(F32)
    mask2 = (lax.broadcasted_iota(jnp.int32, (1, 256), 1) < C2).astype(F32)
    bias_stem, gain_stem, shift_stem = vs_ref[0:1, :], vs_ref[1:2, :], vs_ref[2:3, :]
    gain_one, shift_one = vs_ref[3:4, :], vs_ref[4:5, :]
    bias_one, gain_two, shift_two = v2_ref[0:1, :], v2_ref[1:2, :], v2_ref[2:3, :]
    chunk = 96

    def pair(g, _):
        x2 = dot(perm_ref[...], x_ref[:, pl.ds(pl.multiple_of(g * 384, 128), 384)]).astype(BF)
        xp_ref[g] = x2
        for q in range(4):
            o = dot(x2, wbig_ref[:, q * 256:(q + 1) * 256])
            st_ref[2 * q] = o[:, :128]
            st_ref[2 * q + 1] = o[:, 128:]

        def slab(j, _):
            for r in range(288 // chunk):
                v = st_ref[j, r * chunk:(r + 1) * chunk, :] + bias_stem
                xhat, _s = stats(v, C1, mask1)
                y = xhat * gain_stem + shift_stem
                xhat, _s = stats(y, C1, mask1)
                n1_ref[g, r * chunk:(r + 1) * chunk, pl.ds(pl.multiple_of(j * 128, 128), 128)] = (
                    xhat * gain_one + shift_one).astype(BF)
            return 0
        lax.fori_loop(0, 8, slab, 0)
        for q in range(4):
            c2, oc2 = q // 2, q % 2
            lanes = slice(q * 256, (q + 1) * 256)
            s2 = dot(n1_ref[g, 0:144, lanes], d1_ref[0]) + dot(n1_ref[g, 144:288, lanes], d1_ref[1]) + bias_one
            s2_ref[g, q] = s2
            xhat, _s = stats(s2, C2, mask2)
            n2 = xhat * gain_two + shift_two
            for or2 in range(2):
                n2s_ref[or2, c2 * 72:(c2 + 1) * 72, oc2 * 256:(oc2 + 1) * 256] = n2[or2 * 72:(or2 + 1) * 72]
        low0, low1 = n2s_ref[0].astype(BF), n2s_ref[1].astype(BF)
        rows = pl.ds(pl.multiple_of(g * 144, 16), 144)
        n2_ref[0, rows, :] = low0
        n2_ref[1, rows, :] = low1
        res_ref[rows, :] = dot(low0, d2_ref[0]) + dot(low1, d2_ref[1]) + v3_ref[0:1, :]
        return 0
    lax.fori_loop(0, 6, pair, 0)


def call(kernel, outs, scratch, flops=0, collective=None):
    params = pltpu.CompilerParams(vmem_limit_bytes=VMEM_LIMIT)
    if collective is not None:
        params = pltpu.CompilerParams(vmem_limit_bytes=VMEM_LIMIT, collective_id=collective, has_side_effects=True)
    return pl.pallas_call(
        kernel,
        out_shape=outs,
        scratch_shapes=scratch,
        cost_estimate=pl.CostEstimate(flops=flops, bytes_accessed=0, transcendentals=0),
        compiler_params=params,
    )


def sds(shape, dt=F32):
    return jax.ShapeDtypeStruct(shape, dt)


def front(x, perm, wbig, d1, d2, vs, v2, v3):
    return call(
        front_kernel,
        (sds((6, 288, 384), BF), sds((6, 288, 1024), BF), sds((6, 4, 144, 256)), sds((2, ROWS, 512), BF), sds((ROWS, C3))),
        [pltpu.VMEM((8, 288, 128), F32), pltpu.VMEM((2, 144, 512), F32)],
        flops=4_000_000_000,
    )(x, perm, wbig, d1, d2, vs, v2, v3)


def spread_shifted(cp_ref, lt, c, val):
    for ki in range(4):
        cp_ref[ki, lt, c, 18 - 2 * ki:90 - 2 * ki, :] = val


def zero_edges(cp_ref):
    head, tail = jnp.zeros((24, 128), F32), jnp.zeros((32, 128), F32)
    for ki in range(4):
        for lt in range(3):
            def body(c, _):
                cp_ref[ki, lt, c, 0:24, :] = head
                cp_ref[ki, lt, c, 80:112, :] = tail
                return 0
            lax.fori_loop(0, 12, body, 0)


def gate(h):
    phi_wide = 0.5 * (1.0 + lax.erf(h * 0.7071067811865476))
    dens = jnp.exp(h * h * -0.5) * 0.3989422804014327
    return h * phi_wide, phi_wide + h * dens


def block_kernel(res_ref, kern_ref, vec_ref, bin_ref, keep_ref, own_ref, other_ref,
                 new_ref, depth_ref, normed_ref, act_ref, dg_ref, out_ref, cp_ref, wb_ref):
    zero_edges(cp_ref)

    def prep(c, _):
        rows = pl.ds(pl.multiple_of(c * COL, 8), COL)
        for lt in range(3):
            val = res_ref[rows, lt * 128:(lt + 1) * 128].astype(BF).astype(F32)
            spread_shifted(cp_ref, lt, c, val)
        return 0
    lax.fori_loop(0, SIDE, prep, 0)
    for lt in range(3):
        for t in range(TAPS):
            wb_ref[lt, t] = jnp.broadcast_to(kern_ref[3 * t + lt:3 * t + lt + 1, :], (8, 128))
    for lt in range(3):
        lanes = slice(lt * 128, (lt + 1) * 128)
        bias = jnp.broadcast_to(vec_ref[0:1, lanes], (8, 128))

        def conv(v, _, lt=lt, lanes=lanes, bias=bias):
            acc = [bias] * SIDE
            for i in range(KERNEL):
                k = (6 * i) % 8
                row = pl.ds(pl.multiple_of(6 * i - k + v * 8, 8), 8)
                xs = [cp_ref[k // 2, lt, c, row, :] for c in range(SIDE)]
                for j in range(KERNEL):
                    w = wb_ref[lt, i * KERNEL + j]
                    for c in range(SIDE):
                        cc = c + j - 3
                        if 0 <= cc < SIDE:
                            acc[c] = acc[c] + w * xs[cc]
            for c in range(SIDE):
                depth_ref[pl.ds(pl.multiple_of(c * COL + v * 8, 8), 8), lanes] = acc[c]
            return 0
        lax.fori_loop(0, COL // 8, conv, 0)
    gain, shift = vec_ref[1:2, :], vec_ref[2:3, :]

    def norm(r, _):
        rows = pl.ds(pl.multiple_of(r * 48, 16), 48)
        xhat, _s = stats(depth_ref[rows, :], C3, None)
        normed_ref[rows, :] = (xhat * gain + shift).astype(BF)
        return 0
    lax.fori_loop(0, ROWS // 48, norm, 0)
    bias_out, scale = vec_ref[3:4, :], vec_ref[4:5, :]
    keep_scale = keep_ref[...] * scale

    def mm(m, _):
        rows = pl.ds(pl.multiple_of(m * PAIR, 16), PAIR)
        low = normed_ref[rows, :]
        for n in range(HID // 256):
            lanes = slice(n * 256, (n + 1) * 256)
            half = own_ref if n < 3 else other_ref
            h = dot(low, half[0, :, (n % 3) * 256:(n % 3 + 1) * 256]) + bin_ref[:, lanes]
            act, dg = gate(h)
            act_ref[rows, lanes] = act.astype(BF)
            dg_ref[rows, lanes] = dg.astype(BF)
        o = (dot(act_ref[rows, :HID // 2], own_ref[1], 1, 1) + dot(act_ref[rows, HID // 2:], other_ref[1], 1, 1)
             + bias_out)
        out_ref[rows, :] = o
        new_ref[rows, :] = res_ref[rows, :] + jnp.concatenate([keep_scale, keep_scale], axis=0) * o
        return 0
    lax.fori_loop(0, ROWS // PAIR, mm, 0)


def block(res, kern, vec, bin_, keep, own, other):
    return call(
        block_kernel,
        (sds((ROWS, C3)), sds((ROWS, C3)), sds((ROWS, C3), BF), sds((ROWS, HID), BF), sds((ROWS, HID), BF), sds((ROWS, C3))),
        [pltpu.VMEM((4, 3, SIDE, SHIFTED, 128), F32), pltpu.VMEM((3, TAPS, 8, 128), F32)],
        flops=4_000_000_000,
    )(res, kern, vec, bin_, keep, own, other)


def head_flatten(wide_ref, line_ref):
    lane = lax.broadcasted_iota(jnp.int32, (C3 // 16, 128), 1)

    def tile(k, t, shift):
        value = wide_ref[t, pl.ds(k, C3 // 16, stride=16), :]
        return pltpu.roll(value, shift % 128, 1) if shift % 128 else value

    for f in range(CLASSES // 8):
        k, col = f * 128 // CLASSES, f * 128 % CLASSES
        t, s = col // 128, col % 128
        take = min(128, CLASSES - col)
        value = tile(k, t, 128 - s)
        if s and t < 7:
            value = jnp.where(lane < 128 - s, value, tile(k, t + 1, 128 - s))
        if take < 128:
            value = jnp.where(lane < take, value, tile(k + 1, 0, take))
        line_ref[pl.ds(f, C3 // 16, stride=CLASSES // 8), :] = value


def head_kernel(res_ref, vec_ref, head_ref, bias_ref, label_ref, valid_ref,
                dr_ref, dhead_ref, dbias_ref, dvec_ref, loss_ref, sum_ref, wide_ref, line_ref):
    def add(c, total):
        return total + res_ref[pl.ds(pl.multiple_of(c * COL, 8), COL), :]
    total = lax.fori_loop(1, SIDE, add, res_ref[0:COL, :])
    sum_ref[...] = total
    pooled = sum_ref[0:IMG, :]
    for r in range(1, SIDE):
        pooled = pooled + sum_ref[r * IMG:(r + 1) * IMG, :]
    pooled = jnp.concatenate([pooled * (1.0 / (SIDE * SIDE)), jnp.zeros((2, C3), F32)], axis=0)
    gain, shift = vec_ref[0:1, :], vec_ref[1:2, :]
    xhat, scale = stats(pooled, C3, None)
    final = (xhat * gain + shift).astype(BF)
    real = lax.broadcasted_iota(jnp.int32, (8, WIDE), 1) < CLASSES
    logits = jnp.where(real, dot(final, head_ref[...]) + bias_ref[...], -1e30)
    top = jnp.max(logits, axis=-1, keepdims=True)
    shifted = logits - top
    expd = jnp.exp(shifted)
    total = jnp.sum(expd, axis=-1, keepdims=True)
    log_chance = jnp.where(real, shifted - jnp.log(total), 0.0)
    onehot = (label_ref[...] == lax.broadcasted_iota(jnp.int32, (8, WIDE), 1)).astype(F32)
    valid = valid_ref[...]
    per_image = (-(1.0 - SMOOTH) * jnp.sum(log_chance * onehot, axis=-1, keepdims=True)
                 - (SMOOTH / CLASSES) * jnp.sum(log_chance, axis=-1, keepdims=True))
    loss_ref[...] = jnp.broadcast_to(jnp.sum(per_image * valid, axis=0, keepdims=True), (1, 128))
    delta = jnp.where(real, (jnp.exp(log_chance) - (1.0 - SMOOTH) * onehot - SMOOTH / CLASSES) * valid, 0.0)
    dbias_ref[...] = jnp.sum(delta, axis=0, keepdims=True)
    high = delta.astype(BF)
    rest = (delta - high.astype(F32)).astype(BF)
    for t in range(8):
        lanes = slice(t * 128, (t + 1) * 128)
        wide_ref[t] = dot(final, high[:, lanes], 0, 0) + dot(final, rest[:, lanes], 0, 0)
    head_flatten(wide_ref, line_ref)
    dhead_ref[...] = line_ref[...].astype(BF)
    dfinal = dot(high, head_ref[...], 1, 1) + dot(rest, head_ref[...], 1, 1)
    dvec_ref[0:1, :] = jnp.sum(dfinal * xhat, axis=0, keepdims=True)
    dvec_ref[1:2, :] = jnp.sum(dfinal, axis=0, keepdims=True)
    dpooled = norm_back(dfinal, xhat, scale, gain, C3, None) * (1.0 / (SIDE * SIDE))
    for r in range(SIDE):
        sum_ref[r * IMG:(r + 1) * IMG, :] = dpooled[0:IMG, :]

    def put(c, _):
        dr_ref[pl.ds(pl.multiple_of(c * COL, 8), COL), :] = sum_ref[...]
        return 0
    lax.fori_loop(0, SIDE, put, 0)


def head(res, vec, head_low, bias, labels, valid, lines):
    return call(
        head_kernel,
        (sds((ROWS, C3)), sds((lines, 128), BF), sds((1, WIDE)), sds((2, C3)), sds((1, 128))),
        [pltpu.VMEM((COL, C3), F32), pltpu.VMEM((8, C3, 128), F32), pltpu.VMEM((lines, 128), F32)],
        flops=20_000_000,
    )(res, vec, head_low, bias, labels, valid)


def ceil_to(value, step):
    return -(-value // step) * step


class Net:
    def __init__(self, planes):
        self.planes = planes
        self.d = lax.axis_index("dp")
        self.m = lax.axis_index("mp")
        self.c = self.d % 2
        self.y = self.d // 2 % 2
        self.z = self.d // 4
        self.core = (self.d + 1 - 2 * self.c, self.m)
        flip = self.d + 2 - 4 * self.y
        self.plane = [(self.d, 1 - self.m), (flip, self.m), (flip, 1 - self.m)]
        self.column = [(4 * ((self.z + o) % planes) + 2 * self.y + self.c, self.m) for o in range(1, planes)]

    def signal(self, peer):
        pl.semaphore_signal(pltpu.get_barrier_semaphore(), inc=1, device_id=peer, device_id_type=pl.DeviceIdType.MESH)

    def greet(self):
        peers = [self.core] + self.plane + self.column
        for peer in peers:
            self.signal(peer)
        pl.semaphore_wait(pltpu.get_barrier_semaphore(), len(peers))


def remote(src, dst, sems, number, peer):
    return pltpu.make_async_remote_copy(
        src_ref=src, dst_ref=dst, send_sem=sems.at[0, number], recv_sem=sems.at[1, number],
        device_id=peer, device_id_type=pl.DeviceIdType.MESH)


def begin(copies):
    for copy in copies:
        copy.start()


def end(copies):
    for copy in copies:
        copy.wait()


def layer_scratch(planes, rows, width):
    return [
        pltpu.VMEM((2, planes, 2, rows, width), BF),
        pltpu.VMEM((2, 2, planes, rows, width), BF),
        pltpu.VMEM((3, planes, rows, width), BF),
        pltpu.VMEM((planes, rows, width), BF),
        pltpu.VMEM((planes - 1, rows, width), BF),
        pltpu.SemaphoreType.DMA((2, 4 + planes)),
    ]


def layer_steps(net, own, other, out, r1, s1, r2, s2, r3, sems):
    c, y, z = net.c, net.y, net.z
    first = [remote(own.at[:, :, 1 - c], r1.at[0], sems, 0, net.core),
             remote(other.at[:, :, 1 - c], r1.at[1], sems, 1, net.core)]
    second = [remote(s1.at[1, y], r2.at[0], sems, 2, net.plane[0]),
              remote(s1.at[0, 1 - y], r2.at[1], sems, 3, net.plane[1]),
              remote(s1.at[1, 1 - y], r2.at[2], sems, 4, net.plane[2])]
    third = [remote(s2.at[(z + o) % net.planes], r3.at[o - 1], sems, 4 + o, net.column[o - 1])
             for o in range(1, net.planes)]

    def step1():
        end(first)

        def add(k, _):
            for yy in range(2):
                s1[0, yy, k] = (own[k, yy, c].astype(F32) + r1[0, k, yy].astype(F32)).astype(BF)
                s1[1, yy, k] = (other[k, yy, c].astype(F32) + r1[1, k, yy].astype(F32)).astype(BF)
            return 0
        lax.fori_loop(0, net.planes, add, 0)
        begin(second)

    def step2():
        end(second)

        def add(k, _):
            total = s1[0, y, k].astype(F32)
            for n in range(3):
                total = total + r2[n, k].astype(F32)
            s2[k] = total.astype(BF)
            return 0
        lax.fori_loop(0, net.planes, add, 0)
        begin(third)

    def step3():
        end(third)

        def add(k, total):
            return total + r3[k].astype(F32)
        out[...] = lax.fori_loop(0, net.planes - 1, add, s2[z].astype(F32)).astype(BF)

    return [lambda: begin(first), step1, step2, step3]


def flat_scratch(planes, rows, dtype):
    return [
        pltpu.VMEM((2, 2, planes, rows, 128), dtype),
        pltpu.VMEM((2, 2, planes, rows, 128), dtype),
        pltpu.VMEM((3, planes, rows, 128), dtype),
        pltpu.VMEM((planes, rows, 128), dtype),
        pltpu.VMEM((planes - 1, rows, 128), dtype),
        pltpu.SemaphoreType.DMA((2, 6 + 2 * planes)),
    ]


def flat_steps(net, grad, out, r1, s1, r2, s2, r3, sems):
    c, y, z, m = net.c, net.y, net.z, net.m
    planes = net.planes
    dtype = out.dtype
    first = [remote(grad.at[:, :, 1 - c], r1, sems, 0, net.core)]
    second = [remote(s1.at[1 - m, y], r2.at[0], sems, 1, net.plane[0]),
              remote(s1.at[m, 1 - y], r2.at[1], sems, 2, net.plane[1]),
              remote(s1.at[1 - m, 1 - y], r2.at[2], sems, 3, net.plane[2])]
    third = [remote(s2.at[(z + o) % planes], r3.at[o - 1], sems, 3 + o, net.column[o - 1]) for o in range(1, planes)]
    fourth = [remote(out.at[m, y, c, z], out.at[m, y, c, z], sems, 2 + planes + o, net.column[o - 1])
              for o in range(1, planes)]
    fifth = [remote(out.at[m, y, c], out.at[m, y, c], sems, 2 + 2 * planes + k, net.plane[k]) for k in range(3)]
    sixth = [remote(out.at[:, :, c], out.at[:, :, c], sems, 5 + 2 * planes, net.core)]

    def step1():
        end(first)
        for mm in range(2):
            for yy in range(2):
                s1[mm, yy] = (grad[mm, yy, c].astype(F32) + r1[mm, yy].astype(F32)).astype(dtype)
        begin(second)

    def step2():
        end(second)
        total = s1[m, y].astype(F32)
        for n in range(3):
            total = total + r2[n].astype(F32)
        s2[...] = total.astype(dtype)
        begin(third)

    def step3():
        end(third)

        def add(k, total):
            return total + r3[k].astype(F32)
        out[m, y, c, z] = lax.fori_loop(0, planes - 1, add, s2[z].astype(F32)).astype(dtype)
        begin(fourth)

    def step4():
        end(fourth)
        begin(fifth)

    def step5():
        end(fifth)
        begin(sixth)

    return [lambda: begin(first), step1, step2, step3, step4, step5, lambda: end(sixth)]


def block_back_body(hooks, dr_ref, keep_ref, vec_ref, act_ref, dg_ref, out_ref, normed_ref, depth_ref, res_ref, kern_ref,
                      own_ref, other_ref,
                      new_ref, down_ref, dother_ref, dkern_ref, dvec_ref, dbin_ref,
                      cp_ref, wb_ref, dout_ref, dhid_ref, sent_ref, kacc_ref):
    hooks = iter(hooks)
    next(hooks)()
    zero_edges(cp_ref)
    for lt in range(3):
        for t in range(TAPS):
            wb_ref[lt, t] = jnp.broadcast_to(kern_ref[3 * t + lt:3 * t + lt + 1, :], (8, 128))
    kacc_ref[...] = jnp.zeros_like(kacc_ref)
    gain, scale = vec_ref[1:2, :], vec_ref[4:5, :]

    def pre(m, carry):
        a_scale, a_bias = carry
        rows = pl.ds(pl.multiple_of(m * PAIR, 16), PAIR)
        keep = jnp.concatenate([keep_ref[...], keep_ref[...]], axis=0)
        dk = dr_ref[rows, :] * keep
        low = (dk * scale).astype(BF)
        dout_ref[rows, :] = low
        sent_ref[rows, :] = res_ref[rows, :].astype(BF).astype(F32)
        return a_scale + fold8(dk * out_ref[rows, :]), a_bias + fold8(low.astype(F32))
    zero = jnp.zeros((8, C3), F32)
    a_scale, a_bias = lax.fori_loop(0, ROWS // PAIR, pre, (zero, zero))
    dvec_ref[4:5, :] = jnp.sum(a_scale, axis=0, keepdims=True)
    dvec_ref[3:4, :] = jnp.sum(a_bias, axis=0, keepdims=True)
    dbin_ref[...] = jnp.zeros_like(dbin_ref)

    def mm(m, carry):
        a_gain, a_shift, a_depth = carry
        rows = pl.ds(pl.multiple_of(m * PAIR, 16), PAIR)
        low = dout_ref[rows, :]
        for n in range(HID // 256):
            lanes = slice(n * 256, (n + 1) * 256)
            half = own_ref if n < 3 else other_ref
            d = dot(low, half[1, :, (n % 3) * 256:(n % 3 + 1) * 256]) * dg_ref[rows, lanes].astype(F32)
            dlow = d.astype(BF)
            dhid_ref[rows, lanes] = dlow
            dbin_ref[:, lanes] += fold8(dlow.astype(F32))
        dn = dot(dhid_ref[rows, :HID // 2], own_ref[0], 1, 1) + dot(dhid_ref[rows, HID // 2:], other_ref[0], 1, 1)
        for c2 in range(2):
            sub = pl.ds(pl.multiple_of(m * PAIR + c2 * COL, 8), COL)
            xhat, rs = stats(depth_ref[sub, :], C3, None)
            d = dn[c2 * COL:(c2 + 1) * COL]
            a_gain = a_gain + fold8(d * xhat)
            a_shift = a_shift + fold8(d)
            dd = norm_back(d, xhat, rs, gain, C3, None)
            a_depth = a_depth + fold8(dd)
            for lt in range(3):
                spread_shifted(cp_ref, lt, 2 * m + c2, dd[:, lt * 128:(lt + 1) * 128])
        return a_gain, a_shift, a_depth
    sums = lax.fori_loop(0, 3, mm, (zero, zero, zero))
    next(hooks)()
    a_gain, a_shift, a_depth = lax.fori_loop(3, ROWS // PAIR, mm, sums)
    next(hooks)()
    dvec_ref[0:1, :] = jnp.sum(a_depth, axis=0, keepdims=True)
    dvec_ref[1:2, :] = jnp.sum(a_gain, axis=0, keepdims=True)
    dvec_ref[2:3, :] = jnp.sum(a_shift, axis=0, keepdims=True)
    dvec_ref[5:8, :] = jnp.zeros((3, C3), F32)
    for n in range(HID // 256):
        lanes = slice(n * 256, (n + 1) * 256)
        half = down_ref if n < 3 else dother_ref
        part = slice((n % 3) * 256, (n % 3 + 1) * 256)
        half[1, :, part] = dot(dout_ref[...], act_ref[:, lanes], 0, 0).astype(BF)
        half[0, :, part] = dot(normed_ref[...], dhid_ref[:, lanes], 0, 0).astype(BF)
    next(hooks)()
    for lt in range(3):
        lanes = slice(lt * 128, (lt + 1) * 128)

        def conv(v, _, lt=lt, lanes=lanes):
            spots = [pl.ds(pl.multiple_of(c * COL + v * 8, 8), 8) for c in range(SIDE)]
            acc = [dr_ref[s, lanes] for s in spots]
            sent = [sent_ref[s, lanes] for s in spots]
            for i in range(KERNEL):
                flip = 6 - i
                k = (6 * flip) % 8
                row = pl.ds(pl.multiple_of(6 * flip - k + v * 8, 8), 8)
                xs = [cp_ref[k // 2, lt, c, row, :] for c in range(SIDE)]
                for j in range(KERNEL):
                    t = i * KERNEL + j
                    w = wb_ref[lt, t]
                    tap = None
                    for c in range(SIDE):
                        cc = c - (j - 3)
                        if 0 <= cc < SIDE:
                            acc[c] = acc[c] + w * xs[cc]
                            term = sent[c] * xs[cc]
                            tap = term if tap is None else tap + term
                    kacc_ref[lt, t] += tap
            for c in range(SIDE):
                new_ref[spots[c], lanes] = acc[c]
            return 0
        lax.fori_loop(0, COL // 8, conv, 0)
        next(hooks)()
    for lt in range(3):
        for t in range(TAPS):
            dkern_ref[3 * t + lt:3 * t + lt + 1, :] = jnp.sum(kacc_ref[lt, t], axis=0, keepdims=True)


def block_back_flat_kernel(planes, *refs):
    grad_ref, out_ref = refs[12], refs[19]
    steps = flat_steps(Net(planes), grad_ref, out_ref, *refs[26:])

    def begin_all():
        Net(planes).greet()
        steps[0]()
    hooks = [begin_all] + steps[1:]
    block_back_body(hooks, *refs[:12], *refs[13:19], *refs[20:26])


def block_back_layer_kernel(planes, *refs):
    own_ref, other_ref, out_ref = refs[12], refs[13], refs[20]
    steps = layer_steps(Net(planes), own_ref, other_ref, out_ref, *refs[27:])

    def begin_all():
        Net(planes).greet()
        steps[0]()
    skip = lambda: None
    hooks = [begin_all, steps[1], skip, steps[2], skip, steps[3], skip]
    block_back_body(hooks, *refs[:12], *refs[14:20], *refs[21:27])


BACK_SHAPES = ((ROWS, C3), F32), ((2, C3, HID // 2), BF), ((2, C3, HID // 2), BF), ((3 * TAPS, 128), F32), ((8, C3), F32), ((8, HID), F32)


def back_scratch():
    return [pltpu.VMEM((4, 3, SIDE, SHIFTED, 128), F32), pltpu.VMEM((3, TAPS, 8, 128), F32),
            pltpu.VMEM((ROWS, C3), BF), pltpu.VMEM((ROWS, HID), BF), pltpu.VMEM((ROWS, C3), F32),
            pltpu.VMEM((3, TAPS, 8, 128), F32)]


def block_back_flat(planes, args, grad):
    outs = tuple(sds(*s) for s in BACK_SHAPES) + (sds(grad.shape, BF),)
    scratch = back_scratch() + flat_scratch(planes, grad.shape[4], BF)
    return call(functools.partial(block_back_flat_kernel, planes), outs, scratch, 8_000_000_000, 1)(*args, grad)


def block_back_layer(planes, args, own, other):
    rows, width = own.shape[3:]
    outs = tuple(sds(*s) for s in BACK_SHAPES) + (sds((rows, width), BF),)
    scratch = back_scratch() + layer_scratch(planes, rows, width)
    return call(functools.partial(block_back_layer_kernel, planes), outs, scratch, 8_000_000_000, 2)(*args, own, other)


def back_kernel(planes, dr_ref, xp_ref, n1_ref, s2_ref, n2_ref, wbig_ref, d1_ref, d2_ref, vs_ref, v2_ref, dkern_ref,
                own_ref, other_ref,
                tail_ref, dvs_ref, dv2_ref, dv3_ref, two_ref, piece_ref,
                st_ref, dn1_ref, dlow_ref, base_ref, aw_ref, dd1_ref, line_ref, grad_ref, *scratch):
    net = Net(planes)
    net.greet()
    layer = layer_steps(net, own_ref, other_ref, piece_ref, *scratch[:6])
    layer[0]()
    mask1 = (lax.broadcasted_iota(jnp.int32, (1, 128), 1) < C1).astype(F32)
    mask2 = (lax.broadcasted_iota(jnp.int32, (1, 256), 1) < C2).astype(F32)
    bias_stem, gain_stem, shift_stem = vs_ref[0:1, :], vs_ref[1:2, :], vs_ref[2:3, :]
    gain_one = vs_ref[3:4, :]
    gain_two = v2_ref[1:2, :]
    chunk = 96
    z1, z2, z3 = jnp.zeros((8, 128), F32), jnp.zeros((8, 256), F32), jnp.zeros((8, C3), F32)
    dd1_ref[...] = jnp.zeros_like(dd1_ref)
    aw_ref[...] = jnp.zeros_like(aw_ref)

    base_ref[...] = dr_ref[...].astype(BF)
    shard = grad_ref.shape[4]
    for or2 in range(2):
        total = dot(n2_ref[or2], base_ref[...], 0, 0)
        for oc2 in range(2):
            for lt in range(3):
                line_ref[pl.ds(3 * (or2 * 384 + oc2 * 192) + lt, 192, stride=3), :] = (
                    total[oc2 * 256:oc2 * 256 + 192, lt * 128:(lt + 1) * 128])
    for l in range(LAYERS):
        line_ref[TWO_LINES + l * 3 * TAPS:TWO_LINES + (l + 1) * 3 * TAPS, :] = dkern_ref[l]
    line_ref[TWO_LINES + KERN_LINES:, :] = jnp.zeros((8 * planes * shard - TWO_LINES - KERN_LINES, 128), F32)
    for mm in range(2):
        for yy in range(2):
            for cc in range(2):
                for k in range(planes):
                    at = (((mm * 2 + yy) * 2 + cc) * planes + k) * shard
                    grad_ref[mm, yy, cc, k] = line_ref[at:at + shard, :].astype(BF)
    flat = flat_steps(net, grad_ref, two_ref, *scratch[6:])
    flat[0]()

    def pair(g, carry):
        rows = pl.ds(pl.multiple_of(g * 144, 16), 144)
        base = base_ref[rows, :]
        a3 = carry[0] + fold8(base.astype(F32))
        a_bias2, a_gain2, a_shift2 = carry[1:4]
        dn2 = [dot(base, d2_ref[or2], 1, 1) for or2 in range(2)]
        for q in range(4):
            c2, oc2 = q // 2, q % 2
            lanes = slice(q * 256, (q + 1) * 256)
            d = jnp.concatenate(
                [dn2[or2][c2 * 72:(c2 + 1) * 72, oc2 * 256:(oc2 + 1) * 256] for or2 in range(2)], axis=0)
            xhat, rs = stats(s2_ref[g, q], C2, mask2)
            a_gain2 = a_gain2 + fold8(d * xhat)
            a_shift2 = a_shift2 + fold8(d)
            mid = norm_back(d, xhat, rs, gain_two, C2, mask2).astype(BF)
            a_bias2 = a_bias2 + fold8(mid.astype(F32))
            for or1 in range(2):
                part = slice(or1 * 144, (or1 + 1) * 144)
                dd1_ref[or1] += dot(n1_ref[g, part, lanes], mid, 0, 0)
                o = dot(mid, d1_ref[or1], 1, 1)
                dn1_ref[2 * q, part, :] = o[:, :128]
                dn1_ref[2 * q + 1, part, :] = o[:, 128:]
        for q in range(4):
            o = dot(xp_ref[g], wbig_ref[:, q * 256:(q + 1) * 256])
            st_ref[2 * q] = o[:, :128]
            st_ref[2 * q + 1] = o[:, 128:]

        def slab(j, sums):
            b0, g0, s0, g1, s1 = sums
            for r in range(288 // chunk):
                part = slice(r * chunk, (r + 1) * chunk)
                v = st_ref[j, part, :] + bias_stem
                xa, ra = stats(v, C1, mask1)
                y = xa * gain_stem + shift_stem
                xb, rb = stats(y, C1, mask1)
                d = dn1_ref[j, part, :]
                g1 = g1 + fold8(d * xb)
                s1 = s1 + fold8(d)
                dy = norm_back(d, xb, rb, gain_one, C1, mask1)
                g0 = g0 + fold8(dy * xa)
                s0 = s0 + fold8(dy)
                dv = norm_back(dy, xa, ra, gain_stem, C1, mask1).astype(BF)
                b0 = b0 + fold8(dv.astype(F32))
                dlow_ref[part, pl.ds(pl.multiple_of(j * 128, 128), 128)] = dv
            return b0, g0, s0, g1, s1
        sums = lax.fori_loop(0, 8, slab, carry[4:])
        aw_ref[...] += dot(xp_ref[g], dlow_ref[...], 0, 0)
        return (a3, a_bias2, a_gain2, a_shift2) + tuple(sums)

    pair_loop = lambda g, sums: lax.fori_loop(g, g + 1, pair, sums)
    sums = (z3, z2, z2, z2, z1, z1, z1, z1, z1)
    hooks = [[layer[1], flat[1]], [layer[2], flat[2]], [layer[3], flat[3]], [flat[4]], [flat[5]], [flat[6]]]
    for g in range(6):
        sums = pair_loop(g, sums)
        for hook in hooks[g]:
            hook()
    done = sums
    total = aw_ref[0:48, 0:128]
    for j in range(1, 8):
        total = total + aw_ref[j * 48:(j + 1) * 48, j * 128:(j + 1) * 128]
    dv3_ref[...] = jnp.sum(done[0], axis=0, keepdims=True)
    for n in range(3):
        dv2_ref[n:n + 1, :] = jnp.sum(done[1 + n], axis=0, keepdims=True)
    for n in range(5):
        dvs_ref[n:n + 1, :] = jnp.sum(done[4 + n], axis=0, keepdims=True)
    base = st_ref.at[0]
    base[0:48, :] = total
    lane = lax.broadcasted_iota(jnp.int32, (12, 128), 1)
    a0, a1, a2, a3 = [base[pl.ds(n, 12, stride=4), :] for n in range(4)]
    tail_ref[pl.ds(0, 12, stride=3), :] = jnp.where(lane < 96, a0, pltpu.roll(a1, 96, 1))
    tail_ref[pl.ds(1, 12, stride=3), :] = jnp.where(lane < 64, pltpu.roll(a1, 96, 1), pltpu.roll(a2, 64, 1))
    tail_ref[pl.ds(2, 12, stride=3), :] = jnp.where(lane < 32, pltpu.roll(a2, 64, 1), pltpu.roll(a3, 32, 1))
    lane = lax.broadcasted_iota(jnp.int32, (48, 128), 1)
    for or1 in range(2):
        for oc1 in range(2):
            left, right = st_ref.at[1], st_ref.at[2]
            left[0:96, :] = dd1_ref[or1, oc1 * 128:oc1 * 128 + 96, 0:128]
            right[0:96, :] = dd1_ref[or1, oc1 * 128:oc1 * 128 + 96, 128:256]
            e0, o0 = left[pl.ds(0, 48, stride=2), :], left[pl.ds(1, 48, stride=2), :]
            e1, o1 = right[pl.ds(0, 48, stride=2), :], right[pl.ds(1, 48, stride=2), :]
            at = STEM_LINES + (or1 * 192 + oc1 * 96) * 3 // 2
            tail_ref[pl.ds(at, 48, stride=3), :] = e0
            tail_ref[pl.ds(at + 1, 48, stride=3), :] = jnp.where(lane < 64, e1, pltpu.roll(o0, 64, 1))
            tail_ref[pl.ds(at + 2, 48, stride=3), :] = jnp.where(lane < 64, pltpu.roll(o0, 64, 1), pltpu.roll(o1, 64, 1))


def back(planes, dr, xp, n1, s2, n2, wbig, d1, d2, vs, v2, dkern, own, other):
    shard = ceil_to(TWO_LINES + KERN_LINES, 8 * planes * 16) // (8 * planes)
    rows, width = own.shape[3:]
    shape = (2, 2, 2, planes, shard, 128)
    return call(
        functools.partial(back_kernel, planes),
        (sds((STEM_LINES + ONE_LINES, 128)), sds((5, 128)), sds((3, 256)), sds((1, C3)), sds(shape, BF), sds((rows, width), BF)),
        [pltpu.VMEM((8, 288, 128), F32), pltpu.VMEM((8, 288, 128), F32), pltpu.VMEM((288, 1024), BF),
         pltpu.VMEM((ROWS, C3), BF), pltpu.VMEM((384, 1024), F32), pltpu.VMEM((2, 256, 256), F32),
         pltpu.VMEM((8 * planes * shard, 128), F32), pltpu.VMEM(shape, BF)]
        + layer_scratch(planes, rows, width) + flat_scratch(planes, shard, BF),
        8_000_000_000, 3,
    )(dr, xp, n1, s2, n2, wbig, d1, d2, vs, v2, dkern, own, other)


VECTOR_WIDTHS = (C1, C1, C2, LAYERS * C3, LAYERS * C3, C3, C1, C1, C1, C2, C2, C3, LAYERS * C3, LAYERS * C3, LAYERS * HID,
                 LAYERS * C3, C3, CLASSES)
VECTOR_NAMES = ("gain_stem", "gain_one", "gain_two", "gain_block", "layer_scale", "gain_final", "bias_stem", "shift_stem",
                "shift_one", "bias_one", "shift_two", "bias_two", "bias_depth", "shift_block", "bias_inner", "bias_outer",
                "shift_final", "bias_head")
VECTOR = sum(VECTOR_WIDTHS)
VECTOR_LINES = ceil_to(VECTOR, 1024) // 128


def vector_plan():
    plan, offset, row = {}, 0, 0
    for name, width in zip(VECTOR_NAMES, VECTOR_WIDTHS):
        plan[name] = (offset, width, row)
        offset, row = offset + width, row + ceil_to(width, 128) // 128
    return plan, row


VECTOR_PLAN, PADDED_LINES = vector_plan()
TAIL_LINES = STEM_LINES + ONE_LINES + PADDED_LINES + 1


def prep_kernel(flat_ref, vector_ref, wbig_ref, d1_ref, d2_ref, kern_ref, head_ref, vs_ref, v2_ref, v3_ref, vec_ref,
                bin_ref, hv_ref, hb_ref, wide_ref, pad_ref):
    m = lax.axis_index("mp")
    for name in VECTOR_NAMES:
        offset, width, row = VECTOR_PLAN[name]
        lines = ceil_to(width, 128) // 128
        at, s = offset // 128, offset % 128
        lane = lax.broadcasted_iota(jnp.int32, (lines, 128), 1)
        value = vector_ref[at:at + lines, :]
        if s:
            value = jnp.where(lane < 128 - s, pltpu.roll(value, 128 - s, 1),
                              pltpu.roll(vector_ref[at + 1:at + 1 + lines, :], 128 - s, 1))
        if width % 128:
            spot = lax.broadcasted_iota(jnp.int32, (lines, 128), 0) * 128 + lane
            value = jnp.where(spot < width, value, 0.0)
        pad_ref[row:row + lines, :] = value

    def place(ref, at, name, start, lines):
        row = VECTOR_PLAN[name][2] + start
        for n in range(lines):
            ref[at + (slice(n * 128, (n + 1) * 128),)] = pad_ref[row + n:row + n + 1, :]
    one = lambda n: (slice(n, n + 1),)
    for n, name in enumerate(("bias_stem", "gain_stem", "shift_stem", "gain_one", "shift_one")):
        place(vs_ref, one(n), name, 0, 1)
    for n, name in enumerate(("bias_one", "gain_two", "shift_two")):
        place(v2_ref, one(n), name, 0, 2)
    place(v3_ref, one(0), "bias_two", 0, 3)
    for l in range(LAYERS):
        for n, name in enumerate(("bias_depth", "gain_block", "shift_block", "bias_outer", "layer_scale")):
            place(vec_ref.at[l], one(n), name, 3 * l, 3)
        for n in range(12):
            part = (n // 6 + m) % 2
            row = VECTOR_PLAN["bias_inner"][2] + 12 * l + part * 6 + n % 6
            bin_ref[l, :, n * 128:(n + 1) * 128] = pad_ref[pl.ds(row, 1), :]
    place(hv_ref, one(0), "gain_final", 0, 3)
    place(hv_ref, one(1), "shift_final", 0, 3)
    place(hb_ref, one(0), "bias_head", 0, 8)
    lane = lax.broadcasted_iota(jnp.int32, (12, 128), 1)
    f0, f1, f2 = [flat_ref[pl.ds(n, 12, stride=3), :] for n in range(3)]
    parts = (f0, jnp.where(lane < 32, pltpu.roll(f0, 32, 1), pltpu.roll(f1, 32, 1)),
             jnp.where(lane < 64, pltpu.roll(f1, 64, 1), pltpu.roll(f2, 64, 1)), pltpu.roll(f2, 96, 1))
    for n in range(4):
        wide_ref[0, pl.ds(n, 12, stride=4), :] = jnp.where(lane < C1, parts[n], 0.0)
    stem = wide_ref[0, 0:48, :].astype(BF)
    wbig_ref[...] = jnp.zeros_like(wbig_ref)
    for j in range(8):
        wbig_ref[j * 48:(j + 1) * 48, j * 128:(j + 1) * 128] = stem
    lane = lax.broadcasted_iota(jnp.int32, (192, 128), 1)
    f0, f1, f2 = [flat_ref[pl.ds(STEM_LINES + n, 192, stride=3), :] for n in range(3)]
    f1 = pltpu.roll(f1, 64, 1)
    f2 = pltpu.roll(f2, 64, 1)
    wide_ref[0, pl.ds(0, 192, stride=2), :] = f0
    wide_ref[1, pl.ds(0, 192, stride=2), :] = jnp.where(lane < 64, pltpu.roll(f1, 64, 1), 0.0)
    wide_ref[0, pl.ds(1, 192, stride=2), :] = jnp.where(lane < 64, f1, f2)
    wide_ref[1, pl.ds(1, 192, stride=2), :] = jnp.where(lane < 64, f2, 0.0)
    d1_ref[...] = jnp.zeros_like(d1_ref)
    d2_ref[...] = jnp.zeros_like(d2_ref)
    for or1 in range(2):
        for oc1 in range(2):
            at = or1 * 192 + oc1 * 96
            for t in range(2):
                d1_ref[or1, oc1 * 128:oc1 * 128 + 96, t * 128:(t + 1) * 128] = wide_ref[t, at:at + 96, :].astype(BF)
    base = STEM_LINES + ONE_LINES
    for lt in range(3):
        for or2 in range(2):
            for oc2 in range(2):
                at = base + (or2 * 384 + oc2 * 192) * 3 + lt
                d2_ref[or2, oc2 * 256:oc2 * 256 + 192, lt * 128:(lt + 1) * 128] = flat_ref[pl.ds(at, 192, stride=3), :].astype(BF)
    base = base + TWO_LINES
    for l in range(LAYERS):
        kern_ref[l] = flat_ref[base + l * 3 * TAPS:base + (l + 1) * 3 * TAPS, :]
    base = base + KERN_LINES
    count = C3 // 16
    lane = lax.broadcasted_iota(jnp.int32, (count, 128), 1)
    for k in range(16):
        for t in range(8):
            start = k * CLASSES + t * 128
            f, s = start // 128, start % 128
            need = min(128, CLASSES - t * 128)
            value = flat_ref[pl.ds(base + f, count, stride=CLASSES // 8), :]
            if s:
                value = pltpu.roll(value, 128 - s, 1)
                if need > 128 - s:
                    after = flat_ref[pl.ds(base + f + 1, count, stride=CLASSES // 8), :]
                    value = jnp.where(lane < 128 - s, value, pltpu.roll(after, 128 - s, 1))
            if need < 128:
                value = jnp.where(lane < need, value, 0.0)
            wide_ref[t, pl.ds(k, count, stride=16), :] = value
    for t in range(8):
        head_ref[:, t * 128:(t + 1) * 128] = wide_ref[t].astype(BF)


def prep(flat, vector):
    return call(
        prep_kernel,
        (sds((384, 1024), BF), sds((2, 256, 256), BF), sds((2, 512, C3), BF), sds((LAYERS, 3 * TAPS, 128)),
         sds((C3, WIDE), BF), sds((8, 128)), sds((8, 256)), sds((8, C3)), sds((LAYERS, 8, C3)), sds((LAYERS, 1, HID)),
         sds((2, C3)), sds((1, WIDE))),
        [pltpu.VMEM((8, C3, 128), F32), pltpu.VMEM((ceil_to(PADDED_LINES, 8), 128), F32)],
    )(flat, vector)


def block_of(number, dp):
    return number // 3, number % 3


def finish_kernel(planes, pieces_ref, tail_ref, dvs_ref, dv2_ref, dv3_ref, dvec_ref, dbin_ref, dfinal_ref, dbias_ref,
                  loss_ref, valid_ref, head_ref, two_ref,
                  own_ref, flat_ref, vector_ref, info_ref,
                  grad_ref, full_ref, line_ref, arrived_ref, move_sem, local_sem, *scratch):
    net = Net(planes)
    m, d = net.m, net.d
    dp = 4 * planes
    shard = grad_ref.shape[4]
    targets = [((l * dp + d) // 3, (l * dp + d) % 3) for l in range(LAYERS)]
    sources = [(3 * d + s) % dp for s in range(LAYERS)]
    for s in range(LAYERS):
        @pl.when(sources[s] != d)
        def _(s=s):
            net.signal((sources[s], m))
    peers = [net.core] + net.plane + net.column
    for peer in peers:
        net.signal(peer)
    awaited = len(peers)
    for l in range(LAYERS):
        awaited = awaited + jnp.where(targets[l][0] != d, 1, 0)
    pl.semaphore_wait(pltpu.get_barrier_semaphore(), awaited)

    def move(l):
        owner, slot = targets[l]
        return pltpu.make_async_remote_copy(
            src_ref=pieces_ref.at[l], dst_ref=arrived_ref.at[slot], send_sem=move_sem.at[0, l],
            recv_sem=move_sem.at[1, slot], device_id=(owner, m), device_id_type=pl.DeviceIdType.MESH)

    def keep(l):
        return pltpu.make_async_copy(pieces_ref.at[l], arrived_ref.at[targets[l][1]], local_sem.at[l])

    for l in range(LAYERS):
        @pl.when(targets[l][0] != d)
        def _(l=l):
            move(l).start()

        @pl.when(targets[l][0] == d)
        def _(l=l):
            keep(l).start()
    squares = jnp.zeros((8, 128), F32)
    for l in range(LAYERS):
        piece = pieces_ref[l].astype(F32)
        line = jnp.sum(piece * piece, axis=0, keepdims=True)
        for n in range(6):
            squares = squares + jnp.concatenate([line[:, n * 128:(n + 1) * 128], jnp.zeros((7, 128), F32)], axis=0)
    square = jnp.sum(squares, axis=(0, 1), keepdims=True)
    lead = STEM_LINES + ONE_LINES
    line_ref[0:lead, :] = tail_ref[...]
    line_ref[lead:, :] = jnp.zeros((8 * planes * shard - lead, 128), F32)

    def place(name, start, value):
        row = lead + VECTOR_PLAN[name][2] + start
        for n in range(value.shape[1] // 128):
            line_ref[row + n:row + n + 1, :] = value[:, n * 128:(n + 1) * 128]
    for n, name in enumerate(("bias_stem", "gain_stem", "shift_stem", "gain_one", "shift_one")):
        place(name, 0, dvs_ref[n:n + 1, :])
    for n, name in enumerate(("bias_one", "gain_two", "shift_two")):
        place(name, 0, dv2_ref[n:n + 1, :])
    place("bias_two", 0, dv3_ref[...])
    for l in range(LAYERS):
        for n, name in enumerate(("bias_depth", "gain_block", "shift_block", "bias_outer", "layer_scale")):
            place(name, 3 * l, dvec_ref[l, n:n + 1, :])
        sums = jnp.sum(dbin_ref[l], axis=0, keepdims=True)
        for n in range(12):
            part = (n // 6 + m) % 2
            row = lead + VECTOR_PLAN["bias_inner"][2] + 12 * l + part * 6 + n % 6
            line_ref[pl.ds(row, 1), :] = sums[:, n * 128:(n + 1) * 128]
    place("gain_final", 0, dfinal_ref[0:1, :])
    place("shift_final", 0, dfinal_ref[1:2, :])
    place("bias_head", 0, dbias_ref[...])
    lane = lax.broadcasted_iota(jnp.int32, (1, 128), 1)
    count = jnp.sum(valid_ref[...], axis=0, keepdims=True)
    info = jnp.where(lane == 0, loss_ref[...], jnp.where(lane == 1, count, jnp.where(lane == 2, square, 0.0)))
    line_ref[lead + PADDED_LINES:lead + PADDED_LINES + 1, :] = info

    def each_shard(move_one):
        for mm in range(2):
            for yy in range(2):
                for cc in range(2):
                    for k in range(planes):
                        move_one((mm, yy, cc, k), ((((mm * 2 + yy) * 2 + cc) * planes) + k))

    def pack(where, n):
        grad_ref[where] = line_ref[n * shard:(n + 1) * shard, :]
    each_shard(pack)
    steps = flat_steps(net, grad_ref, full_ref, *scratch)
    for step in steps[:2]:
        step()
    big = head_ref.shape[4]
    total = jnp.zeros((8, 128), F32)
    side = two_ref.shape[4]

    def unpack_big(ref, size, base, lines):
        def inner(where, n):
            at = n * size
            if at < lines:
                rows = min(size, lines - at)
                value = ref[where].astype(F32)
                flat_ref[base + at:base + at + rows, :] = value[0:rows]
        each_shard(inner)
    unpack_big(two_ref, side, lead, TWO_LINES + KERN_LINES)
    steps[2]()
    unpack_big(head_ref, big, lead + TWO_LINES + KERN_LINES, HEAD_LINES)
    steps[3]()

    def square_rows(k, total):
        value = flat_ref[pl.ds(lead + k * 45, 45), :]
        return total + jnp.sum(value * value, axis=0, keepdims=True)
    known = (TWO_LINES + KERN_LINES + HEAD_LINES) // 45
    total = lax.fori_loop(0, known, square_rows, jnp.zeros((1, 128), F32))
    rest = lead + known * 45
    if rest < FLAT_LINES:
        value = flat_ref[rest:FLAT_LINES, :]
        total = total + jnp.sum(value * value, axis=0, keepdims=True)
    for step in steps[4:]:
        step()

    def unpack(where, n):
        line_ref[n * shard:(n + 1) * shard, :] = full_ref[where]
    each_shard(unpack)
    value = line_ref[0:lead, :]
    flat_ref[0:lead, :] = value
    total = total + jnp.sum(value * value, axis=0, keepdims=True)
    value = line_ref[lead:lead + PADDED_LINES, :]
    total = total + jnp.sum(value * value, axis=0, keepdims=True)
    info = line_ref[lead + PADDED_LINES:lead + PADDED_LINES + 1, :]
    pick = lambda n: jnp.sum(jnp.where(lane == n, info, 0.0), axis=1, keepdims=True)
    count = jnp.maximum(pick(1), 1.0)
    norm = jnp.sqrt(jnp.sum(total, axis=1, keepdims=True) + pick(2)) / count
    factor = CLIP_LIMIT / jnp.maximum(norm, CLIP_LIMIT) / count
    info_ref[...] = jnp.where(lane == 0, pick(0), jnp.where(lane == 1, count, jnp.where(lane == 2, norm, factor)))
    vector_ref[...] = jnp.zeros_like(vector_ref)
    for name in VECTOR_NAMES:
        offset, width, row = VECTOR_PLAN[name]
        lines = ceil_to(width, 128) // 128
        at, s = offset // 128, offset % 128
        lane8 = lax.broadcasted_iota(jnp.int32, (lines, 128), 1)
        value = line_ref[lead + row:lead + row + lines, :]
        if s:
            value = pltpu.roll(value, s, 1)
            vector_ref[at:at + lines, :] += jnp.where(lane8 < s, 0.0, value)
            vector_ref[at + 1:at + 1 + lines, :] += jnp.where(lane8 < s, value, 0.0)
        else:
            vector_ref[at:at + lines, :] += value
    for l in range(LAYERS):
        @pl.when(targets[l][0] != d)
        def _(l=l):
            move(l).wait_send()

        @pl.when(targets[l][0] == d)
        def _(l=l):
            keep(l).wait()
    for s in range(LAYERS):
        @pl.when(sources[s] != d)
        def _(s=s):
            pltpu.make_async_remote_copy(
                src_ref=pieces_ref.at[s], dst_ref=arrived_ref.at[s], send_sem=move_sem.at[0, s],
                recv_sem=move_sem.at[1, s], device_id=(sources[s], m), device_id_type=pl.DeviceIdType.MESH).wait_recv()
    own_ref[...] = arrived_ref[...]


def finish(planes, pieces, tail, dvs, dv2, dv3, dvec, dbin, dfinal, dbias, loss, valid, head_sum, two_sum):
    shard = ceil_to(TAIL_LINES, 8 * planes * 8) // (8 * planes)
    shape = (2, 2, 2, planes, shard, 128)
    return call(
        functools.partial(finish_kernel, planes),
        (sds(pieces.shape, BF), sds((FLAT_LINES, 128)), sds((VECTOR_LINES, 128)), sds((1, 128))),
        [pltpu.VMEM(shape, F32), pltpu.VMEM(shape, F32), pltpu.VMEM((8 * planes * shard, 128), F32),
         pltpu.VMEM(pieces.shape, BF), pltpu.SemaphoreType.DMA((2, LAYERS)), pltpu.SemaphoreType.DMA((LAYERS,))]
        + flat_scratch(planes, shard, F32),
        0, 4,
    )(pieces, tail, dvs, dv2, dv3, dvec, dbin, dfinal, dbias, loss, valid, head_sum, two_sum)


LEARN_RATE = 0.05
VECTOR_RATE = 0.15
WEIGHT_DECAY = 0.05
BETA_ONE = 0.9
BETA_TWO = 0.999
ADAM_EPSILON = 1e-08


def vector_lengths():
    return list(VECTOR_WIDTHS)


def flat_lengths():
    return [PATCH * C1, 4 * C1 * C2, 4 * C2 * C3, LAYERS * TAPS * C3, C3 * CLASSES]


def adam_update(weight, moment_one, moment_two, gradient, step_float, rate):
    first_new = BETA_ONE * moment_one + (1.0 - BETA_ONE) * gradient
    second_new = BETA_TWO * moment_two + (1.0 - BETA_TWO) * gradient * gradient
    first_hat = first_new / (1.0 - BETA_ONE**step_float)
    second_hat = second_new / (1.0 - BETA_TWO**step_float)
    weight_new = weight - rate * (first_hat / (jnp.sqrt(second_hat) + ADAM_EPSILON) + WEIGHT_DECAY * weight)
    return (weight_new, first_new, second_new, weight_new.astype(BF))


def row_source():
    target = np.arange(4 * COL)
    img = target % IMG
    r = target // IMG % SIDE
    or2 = target // COL % 2
    or1 = target // (2 * COL)
    row = 4 * r + 2 * or2 + or1
    return (row // (2 * SIDE)) * (2 * COL) + img * (2 * SIDE) + row % (2 * SIDE)


def per_device(pixels, labels, valid_flags, keep_mask, step_count, pointwise_weight, pointwise_first, pointwise_second,
               flat_weight, flat_first, flat_second, vector_weight, vector_first, vector_second):
    m = lax.axis_index("mp")
    swap = [(0, 1), (1, 0)]
    half_images = pixels.shape[0] // 2
    mine = lambda a, axis, which: lax.dynamic_slice_in_dim(a, which * half_images, half_images, axis)
    received = lax.ppermute(mine(pixels, 0, 1 - m), "mp", swap)
    x = jnp.concatenate([mine(pixels, 0, m), received], axis=0).reshape(4 * COL, 4 * SIDE * PATCH)
    low = pointwise_weight.astype(BF)
    other = [lax.ppermute(low[l], "mp", swap) for l in range(LAYERS)]
    source = (jnp.asarray(row_source(), jnp.int32) + m * (2 * COL)) % (4 * COL)
    perm = (source[:, None] == lax.broadcasted_iota(jnp.int32, (1, 4 * COL), 1)).astype(BF)
    flat_lines = lambda a: a.reshape(FLAT_LINES, 128)
    vector_lines = lambda a: jnp.pad(a, (0, VECTOR_LINES * 128 - VECTOR)).reshape(VECTOR_LINES, 128)
    wbig, d1, d2, kern, head_low, vs, v2, v3, vec, bins, hv, hb = prep(flat_lines(flat_weight), vector_lines(vector_weight))
    keep = jnp.tile(mine(keep_mask, 1, m).astype(F32), (1, SIDE))
    keep = jnp.broadcast_to(keep[:, :, None], (LAYERS, COL, C3))
    label8 = jnp.pad(mine(labels, 0, m), (0, 2))[:, None]
    valid_own = mine(valid_flags, 0, m).astype(F32)
    valid8 = jnp.pad(valid_own, (0, 2))[:, None]
    xp, n1, s2, n2, res = front(x, perm, wbig, d1, d2, vs, v2, v3)
    dp = lax.axis_size("dp")
    planes = dp // 4
    kept = []
    for l in range(LAYERS):
        new, depth, normed, act, dg, out = block(res, kern[l], vec[l], bins[l], keep[l], low[l], other[l])
        kept.append((keep[l], vec[l], act, dg, out, normed, depth, res, kern[l], low[l], other[l]))
        res = new
    shard = ceil_to(HEAD_LINES, 8 * planes * 16) // (8 * planes)
    dr, dhead, dbias, dfinal, loss = head(res, hv, head_low, hb, label8, valid8, 8 * planes * shard)
    blocked = lambda a: a.reshape(planes, 2, 2, 2 * C3 // dp, HID // 2)
    top = LAYERS - 1
    dr, own, other_half, dk, dv, db, head_sum = block_back_flat(
        planes, (dr,) + kept[top], dhead.reshape(2, 2, 2, planes, shard, 128))
    pieces, dkern, dvec, dbin = [None] * LAYERS, [None] * LAYERS, [None] * LAYERS, [None] * LAYERS
    dkern[top], dvec[top], dbin[top] = dk, dv, db
    for l in range(top - 1, -1, -1):
        dr, own_new, other_new, dkern[l], dvec[l], dbin[l], pieces[l + 1] = block_back_layer(
            planes, (dr,) + kept[l], blocked(own), blocked(other_half))
        own, other_half = own_new, other_new
    tail, dvs, dv2, dv3, two_sum, pieces[0] = back(
        planes, dr, xp, n1, s2, n2, wbig, d1, d2, vs, v2, jnp.stack(dkern), blocked(own), blocked(other_half))
    pointwise_own, flat_sum, vector_sum, info = finish(
        planes, jnp.stack(pieces), tail, dvs, dv2, dv3, jnp.stack(dvec), jnp.stack(dbin), dfinal, dbias, loss, valid8,
        head_sum, two_sum)
    loss_total, valid_total, gradient_norm, factor = info[0, 0], info[0, 1], info[0, 2], info[0, 3]
    pointwise_own = pointwise_own.reshape(pointwise_first.shape).astype(F32)
    flat_sum = flat_sum.reshape(-1)
    vector_sum = vector_sum.reshape(-1)[:VECTOR]
    step_float = step_count.astype(F32)
    rows_owned = pointwise_first.shape[0]
    master_rows = pointwise_weight.reshape(2 * LAYERS * C3, HID // 2)
    master_own = lax.dynamic_slice_in_dim(master_rows, lax.axis_index("dp") * rows_owned, rows_owned, 0)
    pointwise_out = adam_update(master_own, pointwise_first, pointwise_second, factor * pointwise_own, step_float, LEARN_RATE)
    flat_out = adam_update(flat_weight, flat_first, flat_second, factor * flat_sum, step_float, LEARN_RATE)
    vector_out = adam_update(vector_weight, vector_first, vector_second, factor * vector_sum, step_float, VECTOR_RATE)
    return (loss_total, valid_total, gradient_norm, *pointwise_out, *flat_out, *vector_out)


def solution(mesh):
    placed = (P("dp", "mp", None), P("dp"), P("dp"), P(None, "dp"), P(), P(None, None, None, "mp"), P("dp", "mp"),
              P("dp", "mp"), P(), P(), P(), P(), P(), P())
    return jax.shard_map(
        per_device,
        mesh=mesh,
        in_specs=placed,
        out_specs=(P(), P(), P()) + (P("dp", "mp"),) * 4 + (P(),) * 8,
        check_vma=False,
    )
```

```python
import functools
import jax
import numpy as np
from jax.sharding import PartitionSpec as P
import jax.numpy as jnp
from jax import lax
from jax.experimental import pallas as pl
from jax.experimental.pallas import tpu as pltpu

C1 = 96
C2 = 192
C3 = 384
HID = 1536
CLASSES = 1000
PATCH = 48
KERNEL = 7
LAYERS = 3
SIDE = 12
NORM_EPSILON = 1e-06
SMOOTH = 0.1
CLIP_LIMIT = 0.02
IMG = 6
COL = SIDE * IMG
ROWS = SIDE * COL
PAIR = 2 * COL
FORE = 432
REAR = 288
WF = 256
WB = 256
BF = jnp.bfloat16
F32 = jnp.float32
VMEM_LIMIT = 60 * 1024 * 1024
SHIFTED = COL + 40
TAPS = KERNEL * KERNEL
WIDE = 1024
STEM_LINES = PATCH * C1 // 128
ONE_LINES = 4 * C1 * C2 // 128
TWO_LINES = 4 * C2 * C3 // 128
KERN_LINES = LAYERS * TAPS * C3 // 128
HEAD_LINES = C3 * CLASSES // 128
FLAT_LINES = STEM_LINES + ONE_LINES + TWO_LINES + KERN_LINES + HEAD_LINES


def dot(a, b, da=1, db=0):
    return lax.dot_general(a, b, (((da,), (db,)), ((), ())), preferred_element_type=F32)


def fold8(values):
    rows, lanes = values.shape
    return jnp.sum(values.reshape(rows // 8, 8, lanes), axis=0)


def stats(values, count, mask):
    average = jnp.sum(values, axis=-1, keepdims=True) * (1.0 / count)
    centred = values - average
    if mask is not None:
        centred = centred * mask
    spread = jnp.sum(centred * centred, axis=-1, keepdims=True) * (1.0 / count)
    scale = lax.rsqrt(spread + NORM_EPSILON)
    return centred * scale, scale


def norm_back(delta, xhat, scale, gain, count, mask):
    scaled = delta * gain
    first = jnp.sum(scaled, axis=-1, keepdims=True) * (1.0 / count)
    second = jnp.sum(scaled * xhat, axis=-1, keepdims=True) * (1.0 / count)
    out = (scaled - first - xhat * second) * scale
    if mask is not None:
        out = out * mask
    return out


def sds(shape, dt=F32):
    return jax.ShapeDtypeStruct(shape, dt)


VM, AN, SM = pltpu.VMEM, pl.ANY, pltpu.SMEM


def call(kernel, ins, outs, scratch, flops=0, collective=None):
    params = pltpu.CompilerParams(vmem_limit_bytes=VMEM_LIMIT)
    if collective is not None:
        params = pltpu.CompilerParams(vmem_limit_bytes=VMEM_LIMIT, collective_id=collective, has_side_effects=True)
    return pl.pallas_call(
        kernel,
        in_specs=[pl.BlockSpec(memory_space=space) for _, space in ins],
        out_specs=[pl.BlockSpec(memory_space=space) for _, space in outs],
        out_shape=[shape for shape, _ in outs],
        scratch_shapes=scratch,
        cost_estimate=pl.CostEstimate(flops=flops, bytes_accessed=0, transcendentals=0),
        compiler_params=params,
    )(*[array for array, _ in ins])


def listed(space, *arrays):
    return [(array, space) for array in arrays]


def spread_shifted(cp_ref, lt, c, val):
    for ki in range(4):
        cp_ref[ki, lt, c, 18 - 2 * ki:90 - 2 * ki, :] = val


def zero_edges(cp_ref):
    head, tail = jnp.zeros((24, 128), F32), jnp.zeros((32, 128), F32)
    for ki in range(4):
        for lt in range(3):
            def body(c, _):
                cp_ref[ki, lt, c, 0:24, :] = head
                cp_ref[ki, lt, c, 80:112, :] = tail
                return 0
            lax.fori_loop(0, 12, body, 0)


def gate(h):
    phi_wide = 0.5 * (1.0 + lax.erf(h * 0.7071067811865476))
    dens = jnp.exp(h * h * -0.5) * 0.3989422804014327
    return h * phi_wide, phi_wide + h * dens


WEIGHT_PARTS = 3


def weight_steps(net, low, far, sems):
    c, y = net.c, net.y
    size = C3 // 2 // WEIGHT_PARTS
    first, second, third = [], [], []
    for k in range(WEIGHT_PARTS):
        mine = pl.ds(pl.multiple_of(y * (C3 // 2) + k * size, 16), size)
        theirs = pl.ds(pl.multiple_of((1 - y) * (C3 // 2) + k * size, 16), size)
        first.append([remote(low.at[c, mine, :], far.at[c, mine, :], sems, 4 * k, net.plane[0])])
        second.append([remote(far.at[c, mine, :], far.at[c, mine, :], sems, 4 * k + 1, net.plane[1])])
        third.append([remote(far.at[c, mine, :], far.at[c, mine, :], sems, 4 * k + 2, net.core),
                      remote(far.at[c, theirs, :], far.at[c, theirs, :], sems, 4 * k + 3, net.core)])

    def step0():
        for k in range(WEIGHT_PARTS):
            begin(first[k])

    def step1(k):
        end(first[k])
        begin(second[k])
        third[k][0].start()

    def step2(k):
        end(second[k])
        third[k][1].start()

    def step3():
        for k in range(WEIGHT_PARTS):
            end(third[k])

    return step0, step1, step2, step3


def block_kernel(planes, *refs):
    res_ref, kern_ref, vec_ref, bin_ref, keep_ref, own_any, other_any = refs[:7]
    refs = refs[7:]
    if planes:
        low_ref, refs = refs[0], refs[1:]
    new_ref, depth_out, normed_out, act_out, dg_out, out_out = refs[:6]
    refs = refs[6:]
    if planes:
        far_out, refs = refs[0], refs[1:]
    cp_ref, wb_ref, own_ref, other_ref, depth_ref, normed_ref, act_ref, dg_ref, out_ref, in_sem, out_sem = refs[:11]
    loads = [pltpu.make_async_copy(own_any, own_ref, in_sem.at[0]), pltpu.make_async_copy(other_any, other_ref, in_sem.at[1])]
    begin(loads)
    if planes:
        net = Net(planes)
        peers = [net.core] + net.plane[:2]
        for peer in peers:
            net.signal(peer)
        pl.semaphore_wait(pltpu.get_barrier_semaphore(), len(peers))
        weights0, weights1, weights2, weights3 = weight_steps(net, low_ref, far_out, refs[11])
        weights0()
    zero_edges(cp_ref)

    def prep_rows(c, _):
        rows = pl.ds(pl.multiple_of(c * COL, 8), COL)
        for lt in range(3):
            val = res_ref[rows, lt * 128:(lt + 1) * 128].astype(BF).astype(F32)
            spread_shifted(cp_ref, lt, c, val)
        return 0
    lax.fori_loop(0, SIDE, prep_rows, 0)
    for lt in range(3):
        for t in range(TAPS):
            wb_ref[lt, t] = jnp.broadcast_to(kern_ref[3 * t + lt:3 * t + lt + 1, :], (8, 128))
    for lt in range(3):
        lanes = slice(lt * 128, (lt + 1) * 128)
        bias = jnp.broadcast_to(vec_ref[0:1, lanes], (8, 128))

        def conv(v, _, lt=lt, lanes=lanes, bias=bias):
            acc = [bias] * SIDE
            for i in range(KERNEL):
                k = (6 * i) % 8
                row = pl.ds(pl.multiple_of(6 * i - k + v * 8, 8), 8)
                xs = [cp_ref[k // 2, lt, c, row, :] for c in range(SIDE)]
                for j in range(KERNEL):
                    w = wb_ref[lt, i * KERNEL + j]
                    for c in range(SIDE):
                        cc = c + j - 3
                        if 0 <= cc < SIDE:
                            acc[c] = acc[c] + w * xs[cc]
            for c in range(SIDE):
                depth_ref[pl.ds(pl.multiple_of(c * COL + v * 8, 8), 8), lanes] = acc[c]
            return 0
        lax.fori_loop(0, COL // 8, conv, 0)
        if planes and lt:
            weights1(lt - 1)
    writes = [pltpu.make_async_copy(depth_ref, depth_out, out_sem.at[0])]
    writes[0].start()
    gain, shift = vec_ref[1:2, :], vec_ref[2:3, :]
    for r in range(ROWS // FORE):
        rows = slice(r * FORE, (r + 1) * FORE)
        xhat, _s = stats(depth_ref[rows, :], C3, None)
        normed_ref[rows, :] = (xhat * gain + shift).astype(BF)
    writes.append(pltpu.make_async_copy(normed_ref, normed_out, out_sem.at[1]))
    writes[1].start()
    bias_out, scale = vec_ref[3:4, :], vec_ref[4:5, :]
    keep_scale = keep_ref[...] * scale
    end(loads)
    for m in range(ROWS // FORE):
        rows, at_rows = slice(m * FORE, (m + 1) * FORE), pl.ds(m * FORE, FORE)
        low = normed_ref[rows, :]
        for n in range(HID // WF):
            lanes = slice(n * WF, (n + 1) * WF)
            half = own_ref if n * WF < HID // 2 else other_ref
            at = n * WF % (HID // 2)
            h = dot(low, half[0, :, at:at + WF]) + bin_ref[:, lanes]
            act, dg = gate(h)
            act_ref[rows, lanes] = act.astype(BF)
            dg_ref[rows, lanes] = dg.astype(BF)
            if n == HID // WF // 2 - 1 or n == HID // WF - 1:
                side = pl.ds(0 if n < HID // WF - 1 else HID // 2, HID // 2)
                for ref, out in ((act_ref, act_out), (dg_ref, dg_out)):
                    writes.append(pltpu.make_async_copy(ref.at[at_rows, side], out.at[at_rows, side], out_sem.at[len(writes)]))
                    writes[-1].start()
        if planes:
            if m == 0:
                weights1(2)
                weights2(0)
            else:
                weights2(1)
        o = (dot(act_ref[rows, :HID // 2], own_ref[1], 1, 1) + dot(act_ref[rows, HID // 2:], other_ref[1], 1, 1)
             + bias_out)
        out_ref[rows, :] = o
        writes.append(pltpu.make_async_copy(out_ref.at[at_rows, :], out_out.at[at_rows, :], out_sem.at[len(writes)]))
        writes[-1].start()
        new_ref[rows, :] = res_ref[rows, :] + jnp.concatenate([keep_scale] * (FORE // COL), axis=0) * o
    if planes:
        weights2(2)
    end(writes)
    if planes:
        weights3()


def block(planes, res, kern, vec, bin_, keep, own, other, low=None):
    comm = low is not None
    kept = [sds((ROWS, C3)), sds((ROWS, C3), BF), sds((ROWS, HID), BF), sds((ROWS, HID), BF), sds((ROWS, C3))]
    outs = listed(VM, sds((ROWS, C3))) + listed(AN, *kept)
    ins = listed(VM, res, kern, vec, bin_, keep) + listed(AN, own, other)
    scratch = [pltpu.VMEM((4, 3, SIDE, SHIFTED, 128), F32), pltpu.VMEM((3, TAPS, 8, 128), F32),
               pltpu.VMEM((2, C3, HID // 2), BF), pltpu.VMEM((2, C3, HID // 2), BF)]
    scratch += [pltpu.VMEM(k.shape, k.dtype) for k in kept]
    scratch += [pltpu.SemaphoreType.DMA((2,)), pltpu.SemaphoreType.DMA((2 + 5 * ROWS // FORE,))]
    if comm:
        ins = ins + listed(AN, low)
        outs = outs + listed(AN, sds((2, C3, HID // 2), BF))
        scratch.append(pltpu.SemaphoreType.DMA((2, 4 * WEIGHT_PARTS)))
    return call(functools.partial(block_kernel, planes if comm else 0), ins, outs, scratch, 4_000_000_000, 7 if comm else None)


def head_flatten(wide_ref, line_ref):
    lane = lax.broadcasted_iota(jnp.int32, (C3 // 16, 128), 1)

    def tile(k, t, shift):
        value = wide_ref[t, pl.ds(k, C3 // 16, stride=16), :]
        return pltpu.roll(value, shift % 128, 1) if shift % 128 else value

    for f in range(CLASSES // 8):
        k, col = f * 128 // CLASSES, f * 128 % CLASSES
        t, s = col // 128, col % 128
        take = min(128, CLASSES - col)
        value = tile(k, t, 128 - s)
        if s and t < 7:
            value = jnp.where(lane < 128 - s, value, tile(k, t + 1, 128 - s))
        if take < 128:
            value = jnp.where(lane < take, value, tile(k + 1, 0, take))
        line_ref[pl.ds(f, C3 // 16, stride=CLASSES // 8), :] = value


def head_kernel(res_ref, vec_ref, head_ref, bias_ref, label_ref, valid_ref,
                dr_ref, dhead_ref, dbias_ref, dvec_ref, loss_ref, sum_ref, wide_ref, line_ref):
    def add(c, total):
        return total + res_ref[pl.ds(pl.multiple_of(c * COL, 8), COL), :]
    total = lax.fori_loop(1, SIDE, add, res_ref[0:COL, :])
    sum_ref[...] = total
    pooled = sum_ref[0:IMG, :]
    for r in range(1, SIDE):
        pooled = pooled + sum_ref[r * IMG:(r + 1) * IMG, :]
    pooled = jnp.concatenate([pooled * (1.0 / (SIDE * SIDE)), jnp.zeros((2, C3), F32)], axis=0)
    gain, shift = vec_ref[0:1, :], vec_ref[1:2, :]
    xhat, scale = stats(pooled, C3, None)
    final = (xhat * gain + shift).astype(BF)
    real = lax.broadcasted_iota(jnp.int32, (8, WIDE), 1) < CLASSES
    logits = jnp.where(real, dot(final, head_ref[...]) + bias_ref[...], -1e30)
    top = jnp.max(logits, axis=-1, keepdims=True)
    shifted = logits - top
    expd = jnp.exp(shifted)
    total = jnp.sum(expd, axis=-1, keepdims=True)
    log_chance = jnp.where(real, shifted - jnp.log(total), 0.0)
    spot = lax.broadcasted_iota(jnp.int32, (8, 1), 0)
    first_image = lax.axis_index("mp") * IMG
    label, valid = jnp.zeros((8, 1), jnp.int32), jnp.zeros((8, 1), jnp.int32)
    for n in range(IMG):
        label = jnp.where(spot == n, label_ref[first_image + n], label)
        valid = jnp.where(spot == n, valid_ref[first_image + n], valid)
    valid = valid.astype(F32)
    onehot = (label == lax.broadcasted_iota(jnp.int32, (8, WIDE), 1)).astype(F32)
    per_image = (-(1.0 - SMOOTH) * jnp.sum(log_chance * onehot, axis=-1, keepdims=True)
                 - (SMOOTH / CLASSES) * jnp.sum(log_chance, axis=-1, keepdims=True))
    lane = lax.broadcasted_iota(jnp.int32, (1, 128), 1)
    loss_ref[...] = jnp.where(lane == 0, jnp.sum(per_image * valid, axis=0, keepdims=True),
                              jnp.where(lane == 1, jnp.sum(valid, axis=0, keepdims=True), 0.0))
    delta = jnp.where(real, (jnp.exp(log_chance) - (1.0 - SMOOTH) * onehot - SMOOTH / CLASSES) * valid, 0.0)
    dbias_ref[...] = jnp.sum(delta, axis=0, keepdims=True)
    high = delta.astype(BF)
    rest = (delta - high.astype(F32)).astype(BF)
    for t in range(8):
        lanes = slice(t * 128, (t + 1) * 128)
        wide_ref[t] = dot(final, high[:, lanes], 0, 0) + dot(final, rest[:, lanes], 0, 0)
    head_flatten(wide_ref, line_ref)
    dhead_ref[...] = line_ref[...].astype(BF)
    dfinal = dot(high, head_ref[...], 1, 1) + dot(rest, head_ref[...], 1, 1)
    dvec_ref[0:1, :] = jnp.sum(dfinal * xhat, axis=0, keepdims=True)
    dvec_ref[1:2, :] = jnp.sum(dfinal, axis=0, keepdims=True)
    dpooled = norm_back(dfinal, xhat, scale, gain, C3, None) * (1.0 / (SIDE * SIDE))
    for r in range(SIDE):
        sum_ref[r * IMG:(r + 1) * IMG, :] = dpooled[0:IMG, :]

    def put(c, _):
        dr_ref[pl.ds(pl.multiple_of(c * COL, 8), COL), :] = sum_ref[...]
        return 0
    lax.fori_loop(0, SIDE, put, 0)


def head(res, vec, head_low, bias, labels, valid, lines):
    return call(
        head_kernel,
        listed(VM, res, vec, head_low, bias) + listed(SM, labels, valid),
        listed(VM, sds((ROWS, C3)), sds((lines, 128), BF), sds((1, WIDE)), sds((2, C3)), sds((1, 128))),
        [pltpu.VMEM((COL, C3), F32), pltpu.VMEM((8, C3, 128), F32), pltpu.VMEM((lines, 128), F32)],
        20_000_000,
    )


def ceil_to(value, step):
    return -(-value // step) * step


class Net:
    def __init__(self, planes):
        self.planes = planes
        self.d = lax.axis_index("dp")
        self.m = lax.axis_index("mp")
        self.c = self.d % 2
        self.y = self.d // 2 % 2
        self.z = self.d // 4
        self.core = (self.d + 1 - 2 * self.c, self.m)
        flip = self.d + 2 - 4 * self.y
        self.plane = [(self.d, 1 - self.m), (flip, self.m), (flip, 1 - self.m)]
        self.column = [(4 * ((self.z + o) % planes) + 2 * self.y + self.c, self.m) for o in range(1, planes)]

    def signal(self, peer):
        pl.semaphore_signal(pltpu.get_barrier_semaphore(), inc=1, device_id=peer, device_id_type=pl.DeviceIdType.MESH)

    def greet(self):
        peers = [self.core] + self.plane + self.column
        for peer in peers:
            self.signal(peer)
        pl.semaphore_wait(pltpu.get_barrier_semaphore(), len(peers))


def remote(src, dst, sems, number, peer):
    return pltpu.make_async_remote_copy(
        src_ref=src, dst_ref=dst, send_sem=sems.at[0, number], recv_sem=sems.at[1, number],
        device_id=peer, device_id_type=pl.DeviceIdType.MESH)


def begin(copies):
    for copy in copies:
        copy.start()


def end(copies):
    for copy in copies:
        copy.wait()


CHUNKS = 2


def layer_scratch(planes, rows, width):
    part = width // CHUNKS
    return [
        pltpu.VMEM((CHUNKS, 2, planes, 2, rows, part), BF),
        pltpu.VMEM((CHUNKS, 2, 2, planes, rows, part), BF),
        pltpu.VMEM((CHUNKS, 3, planes, rows, part), BF),
        pltpu.VMEM((2, planes, 2, rows, width), BF),
        pltpu.SemaphoreType.DMA((2, 5 * CHUNKS)),
        pltpu.SemaphoreType.DMA((2,)),
    ]


def layer_steps(net, own, other, out, r1, s1, r2, held, sems, held_sem):
    c, y = net.c, net.y
    part = own.shape[4] // CHUNKS
    first, second = [], []
    for k in range(CHUNKS):
        lanes = pl.ds(k * part, part)
        first.append([remote(own.at[:, :, 1 - c, :, lanes], r1.at[k, 0], sems, 5 * k, net.core),
                      remote(other.at[:, :, 1 - c, :, lanes], r1.at[k, 1], sems, 5 * k + 1, net.core)])
        second.append([remote(s1.at[k, 1, y], r2.at[k, 0], sems, 5 * k + 2, net.plane[0]),
                       remote(s1.at[k, 0, 1 - y], r2.at[k, 1], sems, 5 * k + 3, net.plane[1]),
                       remote(s1.at[k, 1, 1 - y], r2.at[k, 2], sems, 5 * k + 4, net.plane[2])])

    loads = [pltpu.make_async_copy(own.at[:, :, c], held.at[0], held_sem.at[0]),
             pltpu.make_async_copy(other.at[:, :, c], held.at[1], held_sem.at[1])]

    def step0():
        for k in range(CHUNKS):
            begin(first[k])
        begin(loads)

    def step1(k):
        end(first[k])
        if k == 0:
            end(loads)
        lanes = slice(k * part, (k + 1) * part)

        def add(n, _):
            for yy in range(2):
                s1[k, 0, yy, n] = (held[0, n, yy, :, lanes].astype(F32) + r1[k, 0, n, yy].astype(F32)).astype(BF)
                s1[k, 1, yy, n] = (held[1, n, yy, :, lanes].astype(F32) + r1[k, 1, n, yy].astype(F32)).astype(BF)
            return 0
        lax.fori_loop(0, net.planes, add, 0)
        begin(second[k])

    def step2(k):
        end(second[k])
        lanes = slice(k * part, (k + 1) * part)

        def add(n, _):
            total = s1[k, 0, y, n].astype(F32)
            for j in range(3):
                total = total + r2[k, j, n].astype(F32)
            out[n, :, lanes] = total.astype(BF)
            return 0
        lax.fori_loop(0, net.planes, add, 0)

    return step0, step1, step2


def column_scratch(planes, rows, width):
    return [pltpu.VMEM((planes - 1, rows, width), BF), pltpu.SemaphoreType.DMA((2, planes))]


def column_steps(net, held, out, r3, sems):
    copies = [remote(held.at[(net.z + o) % net.planes], r3.at[o - 1], sems, o - 1, net.column[o - 1])
              for o in range(1, net.planes)]

    def step1():
        end(copies)

        def add(k, total):
            return total + r3[k].astype(F32)
        out[...] = lax.fori_loop(0, net.planes - 1, add, held[net.z].astype(F32)).astype(BF)

    return (lambda: begin(copies)), step1


def flat_scratch(planes, rows, dtype):
    return [
        pltpu.VMEM((2, 2, planes, rows, 128), dtype),
        pltpu.VMEM((2, 2, planes, rows, 128), dtype),
        pltpu.VMEM((3, planes, rows, 128), dtype),
        pltpu.VMEM((planes, rows, 128), dtype),
        pltpu.VMEM((planes - 1, rows, 128), dtype),
        pltpu.SemaphoreType.DMA((2, 3 + planes)),
    ]


def spread_scratch(planes):
    return [pltpu.SemaphoreType.DMA((2, 3 + planes))]


def flat_sum_steps(net, grad, shard, r1, s1, r2, s2, r3, sems):
    c, y, z, m = net.c, net.y, net.z, net.m
    planes = net.planes
    dtype = shard.dtype
    first = [remote(grad.at[:, :, 1 - c], r1, sems, 0, net.core)]
    second = [remote(s1.at[1 - m, y], r2.at[0], sems, 1, net.plane[0]),
              remote(s1.at[m, 1 - y], r2.at[1], sems, 2, net.plane[1]),
              remote(s1.at[1 - m, 1 - y], r2.at[2], sems, 3, net.plane[2])]
    third = [remote(s2.at[(z + o) % planes], r3.at[o - 1], sems, 3 + o, net.column[o - 1]) for o in range(1, planes)]

    def step1():
        end(first)
        for mm in range(2):
            for yy in range(2):
                s1[mm, yy] = (grad[mm, yy, c].astype(F32) + r1[mm, yy].astype(F32)).astype(dtype)
        begin(second)

    def step2():
        end(second)
        total = s1[m, y].astype(F32)
        for n in range(3):
            total = total + r2[n].astype(F32)
        s2[...] = total.astype(dtype)
        begin(third)

    def step3():
        end(third)

        def add(k, total):
            return total + r3[k].astype(F32)
        shard[...] = lax.fori_loop(0, planes - 1, add, s2[z].astype(F32)).astype(dtype)

    return [lambda: begin(first), step1, step2, step3]


def spread_steps(net, shard, out, sems):
    c, y, z, m = net.c, net.y, net.z, net.m
    planes = net.planes
    first = [remote(out.at[m, y, c, z], out.at[m, y, c, z], sems, o - 1, net.column[o - 1]) for o in range(1, planes)]
    second = [remote(out.at[m, y, c], out.at[m, y, c], sems, planes - 1 + k, net.plane[k]) for k in range(3)]
    third = [remote(out.at[:, :, c], out.at[:, :, c], sems, planes + 2, net.core)]

    def step0():
        out[m, y, c, z] = shard[...]
        begin(first)

    def step1():
        end(first)
        begin(second)

    def step2():
        end(second)
        begin(third)

    return [step0, step1, step2, lambda: end(third)]


def block_back_body(hooks, dr_ref, keep_ref, vec_ref, kern_ref, act_any, dg_any, out_any, normed_any, depth_any, res_any,
                    own_any, other_any,
                    new_ref, down_any, dother_any, dkern_ref, dvec_ref, dbin_ref,
                    cp_ref, wb_ref, dout_ref, dhid_ref, kacc_ref, act_ref, dg_ref, out_ref, normed_ref, depth_ref, res_ref,
                    own_ref, other_ref, down_ref, dother_ref, in_sem):
    pairs = ((out_any, out_ref), (own_any, own_ref), (other_any, other_ref), (dg_any, dg_ref), (depth_any, depth_ref),
             (act_any, act_ref), (normed_any, normed_ref), (res_any, res_ref))
    load = [pltpu.make_async_copy(a, b, in_sem.at[n]) for n, (a, b) in enumerate(pairs)]
    begin(load)
    hooks = iter(hooks)

    def tick():
        for hook in next(hooks):
            hook()
    tick()
    zero_edges(cp_ref)
    for lt in range(3):
        for t in range(TAPS):
            wb_ref[lt, t] = jnp.broadcast_to(kern_ref[3 * t + lt:3 * t + lt + 1, :], (8, 128))
    kacc_ref[...] = jnp.zeros_like(kacc_ref)
    gain, scale = vec_ref[1:2, :], vec_ref[4:5, :]
    load[0].wait()

    def pre(m, carry):
        a_scale, a_bias = carry
        rows = pl.ds(pl.multiple_of(m * PAIR, 16), PAIR)
        keep = jnp.concatenate([keep_ref[...], keep_ref[...]], axis=0)
        dk = dr_ref[rows, :] * keep
        low = (dk * scale).astype(BF)
        dout_ref[rows, :] = low
        return a_scale + fold8(dk * out_ref[rows, :]), a_bias + fold8(low.astype(F32))
    zero = jnp.zeros((8, C3), F32)
    a_scale, a_bias = lax.fori_loop(0, ROWS // PAIR, pre, (zero, zero))
    dvec_ref[4:5, :] = jnp.sum(a_scale, axis=0, keepdims=True)
    dvec_ref[3:4, :] = jnp.sum(a_bias, axis=0, keepdims=True)
    dbin_ref[...] = jnp.zeros_like(dbin_ref)
    end(load[1:5])

    def mm(m, carry):
        a_gain, a_shift, a_depth = carry
        rows = slice(m * REAR, (m + 1) * REAR)
        low = dout_ref[rows, :]
        for n in range(HID // WB):
            lanes = slice(n * WB, (n + 1) * WB)
            half = own_ref if n * WB < HID // 2 else other_ref
            at = n * WB % (HID // 2)
            d = dot(low, half[1, :, at:at + WB]) * dg_ref[rows, lanes].astype(F32)
            dlow = d.astype(BF)
            dhid_ref[rows, lanes] = dlow
            dbin_ref[:, lanes] += fold8(dlow.astype(F32))
        d = dot(dhid_ref[rows, :HID // 2], own_ref[0], 1, 1) + dot(dhid_ref[rows, HID // 2:], other_ref[0], 1, 1)
        xhat, rs = stats(depth_ref[rows, :], C3, None)
        a_gain = a_gain + fold8(d * xhat)
        a_shift = a_shift + fold8(d)
        dd = norm_back(d, xhat, rs, gain, C3, None)
        a_depth = a_depth + fold8(dd)
        for n in range(REAR // COL):
            for lt in range(3):
                spread_shifted(cp_ref, lt, m * (REAR // COL) + n, dd[n * COL:(n + 1) * COL, lt * 128:(lt + 1) * 128])
        return a_gain, a_shift, a_depth
    sums = (zero, zero, zero)
    for n in range(ROWS // REAR):
        sums = mm(n, sums)
        tick()
    end(load[5:])
    a_gain, a_shift, a_depth = sums
    dvec_ref[0:1, :] = jnp.sum(a_depth, axis=0, keepdims=True)
    dvec_ref[1:2, :] = jnp.sum(a_gain, axis=0, keepdims=True)
    dvec_ref[2:3, :] = jnp.sum(a_shift, axis=0, keepdims=True)
    dvec_ref[5:8, :] = jnp.zeros((3, C3), F32)
    writes = []
    for n in range(HID // 256):
        lanes = slice(n * 256, (n + 1) * 256)
        half = down_ref if n < 3 else dother_ref
        part = slice((n % 3) * 256, (n % 3 + 1) * 256)
        half[1, :, part] = dot(dout_ref[...], act_ref[:, lanes], 0, 0).astype(BF)
        half[0, :, part] = dot(normed_ref[...], dhid_ref[:, lanes], 0, 0).astype(BF)
        if n % 3 == 2:
            out = down_any if n == 2 else dother_any
            writes.append(pltpu.make_async_copy(half, out, in_sem.at[8 + n // 3]))
            writes[-1].start()
            tick()
    for lt in range(3):
        lanes = slice(lt * 128, (lt + 1) * 128)

        def conv(v, _, lt=lt, lanes=lanes):
            spots = [pl.ds(pl.multiple_of(c * COL + v * 8, 8), 8) for c in range(SIDE)]
            acc = [dr_ref[s, lanes] for s in spots]
            sent = [res_ref[s, lanes].astype(BF).astype(F32) for s in spots]
            for i in range(KERNEL):
                flip = 6 - i
                k = (6 * flip) % 8
                row = pl.ds(pl.multiple_of(6 * flip - k + v * 8, 8), 8)
                xs = [cp_ref[k // 2, lt, c, row, :] for c in range(SIDE)]
                for j in range(KERNEL):
                    t = i * KERNEL + j
                    w = wb_ref[lt, t]
                    tap = None
                    for c in range(SIDE):
                        cc = c - (j - 3)
                        if 0 <= cc < SIDE:
                            acc[c] = acc[c] + w * xs[cc]
                            term = sent[c] * xs[cc]
                            tap = term if tap is None else tap + term
                    kacc_ref[lt, t] += tap
            for c in range(SIDE):
                new_ref[spots[c], lanes] = acc[c]
            return 0
        lax.fori_loop(0, COL // 8, conv, 0)
        tick()
    for lt in range(3):
        for t in range(TAPS):
            dkern_ref[3 * t + lt:3 * t + lt + 1, :] = jnp.sum(kacc_ref[lt, t], axis=0, keepdims=True)
    end(writes)


HOOKS = 9
BODY_INS, BODY_OUTS, BODY_SCRATCH = 12, 6, 16


def back_parts():
    outs = (listed(VM, sds((ROWS, C3))) + listed(AN, sds((2, C3, HID // 2), BF), sds((2, C3, HID // 2), BF))
            + listed(VM, sds((3 * TAPS, 128)), sds((8, C3)), sds((8, HID))))
    wide, half = (ROWS, HID), (2, C3, HID // 2)
    scratch = [pltpu.VMEM((4, 3, SIDE, SHIFTED, 128), F32), pltpu.VMEM((3, TAPS, 8, 128), F32),
               pltpu.VMEM((ROWS, C3), BF), pltpu.VMEM(wide, BF), pltpu.VMEM((3, TAPS, 8, 128), F32),
               pltpu.VMEM(wide, BF), pltpu.VMEM(wide, BF), pltpu.VMEM((ROWS, C3), F32), pltpu.VMEM((ROWS, C3), BF),
               pltpu.VMEM((ROWS, C3), F32), pltpu.VMEM((ROWS, C3), F32), pltpu.VMEM(half, BF), pltpu.VMEM(half, BF),
               pltpu.VMEM(half, BF), pltpu.VMEM(half, BF), pltpu.SemaphoreType.DMA((10,))]
    return outs, scratch


def take(refs, count):
    return refs[:count], refs[count:]


def block_back_kernel(planes, kind, *refs):
    net = Net(planes)
    args, refs = take(refs, BODY_INS)
    more_in, refs = take(refs, (1, 3, 3)[kind])
    outs, refs = take(refs, BODY_OUTS)
    more_out, refs = take(refs, (1, 2, 2)[kind])
    scratch, refs = take(refs, BODY_SCRATCH)
    hooks = [[] for _ in range(HOOKS)]
    if kind == 0:
        steps = flat_sum_steps(net, more_in[0], more_out[0], *refs)
        hooks[0], hooks[2], hooks[4], hooks[6] = [net.greet, steps[0]], [steps[1]], [steps[2]], [steps[3]]
    else:
        step0, step1, step2 = layer_steps(net, more_in[0], more_in[1], more_out[0], *refs[:6])
        hooks[0] = [net.greet, step0]
        hooks[1] = [lambda: step1(0)]
        hooks[2] = [lambda: step1(1)]
        hooks[5] = [lambda: step2(0)]
        hooks[7] = [lambda: step2(1)]
        if kind == 1:
            steps = spread_steps(net, more_in[2], more_out[1], *refs[6:])
            hooks[0] = [net.greet, steps[0], step0]
            hooks[1] = [steps[1], lambda: step1(0)]
            hooks[5] = [steps[2]]
            hooks[6] = [lambda: step2(0)]
            hooks[7] = []
            hooks[8] = [lambda: step2(1), steps[3]]
        else:
            col0, col1 = column_steps(net, more_in[2], more_out[1], *refs[6:])
            hooks[0].append(col0)
            hooks[4].append(col1)
    block_back_body(hooks, *args, *outs, *scratch)


def block_back(planes, kind, args, *more):
    outs, scratch = back_parts()
    ins = listed(VM, *args[:4]) + listed(AN, *args[4:])
    if kind == 0:
        grad, = more
        rows = grad.shape[4]
        ins += listed(VM, grad)
        outs += listed(VM, sds((rows, 128), BF))
        scratch += flat_scratch(planes, rows, BF)
    else:
        own, other, held = more
        rows, width = own.shape[3:]
        ins += listed(AN, own, other) + listed(VM, held)
        outs += listed(VM, sds((planes, rows, width), BF))
        scratch += layer_scratch(planes, rows, width)
        if kind == 1:
            outs += listed(VM, sds((2, 2, 2, planes) + held.shape, BF))
            scratch += spread_scratch(planes)
        else:
            outs += listed(VM, sds((rows, width), BF))
            scratch += column_scratch(planes, rows, width)
    return call(functools.partial(block_back_kernel, planes, kind), ins, outs, scratch, 8_000_000_000, (1, 2, 5)[kind])


def back_kernel(planes, dr_ref, xp_any, n1_any, s2_any, n2_any, wbig_ref, d1_ref, d2_ref, vs_ref, v2_ref, dk0_ref, dk1_ref,
                dk2_ref, own_ref, other_ref, held_ref,
                tail_ref, dvs_ref, dv2_ref, dv3_ref, two_ref, piece0_ref, piece1_ref,
                xp_ref, n1_ref, s2_ref, n2_ref, in_sem,
                sum_ref, shard_ref, st_ref, dn1_ref, dlow_ref, base_ref, aw_ref, dd1_ref, line_ref, grad_ref, *scratch):
    load_n2 = pltpu.make_async_copy(n2_any, n2_ref, in_sem.at[18])
    load_n2.start()
    loads = [[pltpu.make_async_copy(a.at[g], b.at[g], in_sem.at[3 * g + n])
              for n, (a, b) in enumerate(((xp_any, xp_ref), (n1_any, n1_ref), (s2_any, s2_ref)))] for g in range(6)]
    for g in range(6):
        begin(loads[g])
    net = Net(planes)
    net.greet()
    layer0, layer1, layer2 = layer_steps(net, own_ref, other_ref, sum_ref, *scratch[:6])
    high0, high1 = column_steps(net, held_ref, piece1_ref, *scratch[6:8])
    low0, low1 = column_steps(net, sum_ref, piece0_ref, *scratch[8:10])
    high0()
    layer0()
    mask1 = (lax.broadcasted_iota(jnp.int32, (1, 128), 1) < C1).astype(F32)
    mask2 = (lax.broadcasted_iota(jnp.int32, (1, 256), 1) < C2).astype(F32)
    bias_stem, gain_stem, shift_stem = vs_ref[0:1, :], vs_ref[1:2, :], vs_ref[2:3, :]
    gain_one = vs_ref[3:4, :]
    gain_two = v2_ref[1:2, :]
    z1, z2, z3 = jnp.zeros((8, 128), F32), jnp.zeros((8, 256), F32), jnp.zeros((8, C3), F32)
    dd1_ref[...] = jnp.zeros_like(dd1_ref)
    aw_ref[...] = jnp.zeros_like(aw_ref)

    base_ref[...] = dr_ref[...].astype(BF)
    shard = grad_ref.shape[4]
    load_n2.wait()
    for or2 in range(2):
        total = dot(n2_ref[or2], base_ref[...], 0, 0)
        for oc2 in range(2):
            for lt in range(3):
                line_ref[pl.ds(3 * (or2 * 384 + oc2 * 192) + lt, 192, stride=3), :] = (
                    total[oc2 * 256:oc2 * 256 + 192, lt * 128:(lt + 1) * 128])
    for l in range(LAYERS):
        line_ref[TWO_LINES + l * 3 * TAPS:TWO_LINES + (l + 1) * 3 * TAPS, :] = (dk0_ref, dk1_ref, dk2_ref)[l][...]
    line_ref[TWO_LINES + KERN_LINES:, :] = jnp.zeros((8 * planes * shard - TWO_LINES - KERN_LINES, 128), F32)
    for mm in range(2):
        for yy in range(2):
            for cc in range(2):
                for k in range(planes):
                    at = (((mm * 2 + yy) * 2 + cc) * planes + k) * shard
                    grad_ref[mm, yy, cc, k] = line_ref[at:at + shard, :].astype(BF)
    flat = flat_sum_steps(net, grad_ref, shard_ref, *scratch[10:16])
    flat += spread_steps(net, shard_ref, two_ref, *scratch[16:])
    layer1(0)
    flat[0]()

    def pair(g, carry, hooks):
        rows = pl.ds(g * 144, 144)
        base = base_ref[rows, :]
        a3 = carry[0] + fold8(base.astype(F32))
        a_bias2, a_gain2, a_shift2 = carry[1:4]
        dn2 = [dot(base, d2_ref[or2], 1, 1) for or2 in range(2)]
        end(loads[g])
        d = jnp.concatenate(
            [dn2[or2][q // 2 * 72:(q // 2 + 1) * 72, q % 2 * 256:(q % 2 + 1) * 256] for q in range(4) for or2 in range(2)], axis=0)
        xhat, rs = stats(s2_ref[g].reshape(4 * 144, 256), C2, mask2)
        a_gain2 = a_gain2 + fold8(d * xhat)
        a_shift2 = a_shift2 + fold8(d)
        mids = norm_back(d, xhat, rs, gain_two, C2, mask2).astype(BF)
        a_bias2 = a_bias2 + fold8(mids.astype(F32))
        for q in range(4):
            lanes = slice(q * 256, (q + 1) * 256)
            mid = mids[q * 144:(q + 1) * 144]
            for or1 in range(2):
                part = slice(or1 * 144, (or1 + 1) * 144)
                dd1_ref[or1] += dot(n1_ref[g, part, lanes], mid, 0, 0)
                o = dot(mid, d1_ref[or1], 1, 1)
                dn1_ref[2 * q, part, :] = o[:, :128]
                dn1_ref[2 * q + 1, part, :] = o[:, 128:]
        for q in range(4):
            o = dot(xp_ref[g], wbig_ref[:, q * 256:(q + 1) * 256])
            st_ref[2 * q] = o[:, :128]
            st_ref[2 * q + 1] = o[:, 128:]

        for hook in hooks:
            hook()
        b0, g0, s0, g1, s1 = carry[4:]
        v = st_ref[...].reshape(8 * 288, 128) + bias_stem
        xa, ra = stats(v, C1, mask1)
        y = xa * gain_stem + shift_stem
        xb, rb = stats(y, C1, mask1)
        d = dn1_ref[...].reshape(8 * 288, 128)
        g1 = g1 + fold8(d * xb)
        s1 = s1 + fold8(d)
        dy = norm_back(d, xb, rb, gain_one, C1, mask1)
        g0 = g0 + fold8(dy * xa)
        s0 = s0 + fold8(dy)
        dv = norm_back(dy, xa, ra, gain_stem, C1, mask1).astype(BF)
        b0 = b0 + fold8(dv.astype(F32))
        for j in range(8):
            dlow_ref[:, j * 128:(j + 1) * 128] = dv[j * 288:(j + 1) * 288]
        sums = (b0, g0, s0, g1, s1)
        aw_ref[...] += dot(xp_ref[g], dlow_ref[...], 0, 0)
        return (a3, a_bias2, a_gain2, a_shift2) + tuple(sums)

    sums = (z3, z2, z2, z2, z1, z1, z1, z1, z1)
    inner = [[lambda: layer1(1)], [high1], [lambda: layer2(0), flat[2]], [flat[3], flat[4]], [flat[5]], [flat[6]]]
    outer = [[flat[1]], [], [lambda: layer2(1), low0], [low1], [], [flat[7]]]
    for g in range(6):
        sums = pair(g, sums, inner[g])
        for hook in outer[g]:
            hook()
    done = sums
    total = aw_ref[0:48, 0:128]
    for j in range(1, 8):
        total = total + aw_ref[j * 48:(j + 1) * 48, j * 128:(j + 1) * 128]
    dv3_ref[...] = jnp.sum(done[0], axis=0, keepdims=True)
    for n in range(3):
        dv2_ref[n:n + 1, :] = jnp.sum(done[1 + n], axis=0, keepdims=True)
    for n in range(5):
        dvs_ref[n:n + 1, :] = jnp.sum(done[4 + n], axis=0, keepdims=True)
    base = st_ref.at[0]
    base[0:48, :] = total
    lane = lax.broadcasted_iota(jnp.int32, (12, 128), 1)
    a0, a1, a2, a3 = [base[pl.ds(n, 12, stride=4), :] for n in range(4)]
    tail_ref[pl.ds(0, 12, stride=3), :] = jnp.where(lane < 96, a0, pltpu.roll(a1, 96, 1))
    tail_ref[pl.ds(1, 12, stride=3), :] = jnp.where(lane < 64, pltpu.roll(a1, 96, 1), pltpu.roll(a2, 64, 1))
    tail_ref[pl.ds(2, 12, stride=3), :] = jnp.where(lane < 32, pltpu.roll(a2, 64, 1), pltpu.roll(a3, 32, 1))
    lane = lax.broadcasted_iota(jnp.int32, (48, 128), 1)
    for or1 in range(2):
        for oc1 in range(2):
            left, right = st_ref.at[1], st_ref.at[2]
            left[0:96, :] = dd1_ref[or1, oc1 * 128:oc1 * 128 + 96, 0:128]
            right[0:96, :] = dd1_ref[or1, oc1 * 128:oc1 * 128 + 96, 128:256]
            e0, o0 = left[pl.ds(0, 48, stride=2), :], left[pl.ds(1, 48, stride=2), :]
            e1, o1 = right[pl.ds(0, 48, stride=2), :], right[pl.ds(1, 48, stride=2), :]
            at = STEM_LINES + (or1 * 192 + oc1 * 96) * 3 // 2
            tail_ref[pl.ds(at, 48, stride=3), :] = e0
            tail_ref[pl.ds(at + 1, 48, stride=3), :] = jnp.where(lane < 64, e1, pltpu.roll(o0, 64, 1))
            tail_ref[pl.ds(at + 2, 48, stride=3), :] = jnp.where(lane < 64, pltpu.roll(o0, 64, 1), pltpu.roll(o1, 64, 1))


def back(planes, dr, kept, weights, dkern, own, other, held):
    shard = ceil_to(TWO_LINES + KERN_LINES, 8 * planes * 16) // (8 * planes)
    rows, width = own.shape[3:]
    shape = (2, 2, 2, planes, shard, 128)
    return call(
        functools.partial(back_kernel, planes),
        listed(VM, dr) + listed(AN, *kept) + listed(VM, *weights, *dkern) + listed(AN, own, other) + listed(VM, held),
        listed(VM, sds((STEM_LINES + ONE_LINES, 128)), sds((5, 128)), sds((3, 256)), sds((1, C3)), sds(shape, BF),
               sds((rows, width), BF), sds((rows, width), BF)),
        [pltpu.VMEM(k.shape, k.dtype) for k in kept] + [pltpu.SemaphoreType.DMA((19,))]
        + [pltpu.VMEM((planes, rows, width), BF), pltpu.VMEM((shard, 128), BF),
           pltpu.VMEM((8, 288, 128), F32), pltpu.VMEM((8, 288, 128), F32), pltpu.VMEM((288, 1024), BF),
           pltpu.VMEM((ROWS, C3), BF), pltpu.VMEM((384, 1024), F32), pltpu.VMEM((2, 256, 256), F32),
           pltpu.VMEM((8 * planes * shard, 128), F32), pltpu.VMEM(shape, BF)]
        + layer_scratch(planes, rows, width) + column_scratch(planes, rows, width) + column_scratch(planes, rows, width)
        + flat_scratch(planes, shard, BF) + spread_scratch(planes),
        8_000_000_000, 3,
    )


VECTOR_WIDTHS = (C1, C1, C2, LAYERS * C3, LAYERS * C3, C3, C1, C1, C1, C2, C2, C3, LAYERS * C3, LAYERS * C3, LAYERS * HID,
                 LAYERS * C3, C3, CLASSES)
VECTOR_NAMES = ("gain_stem", "gain_one", "gain_two", "gain_block", "layer_scale", "gain_final", "bias_stem", "shift_stem",
                "shift_one", "bias_one", "shift_two", "bias_two", "bias_depth", "shift_block", "bias_inner", "bias_outer",
                "shift_final", "bias_head")
VECTOR = sum(VECTOR_WIDTHS)
VECTOR_LINES = ceil_to(VECTOR, 1024) // 128


def vector_plan():
    plan, offset, row = {}, 0, 0
    for name, width in zip(VECTOR_NAMES, VECTOR_WIDTHS):
        plan[name] = (offset, width, row)
        offset, row = offset + width, row + ceil_to(width, 128) // 128
    return plan, row


VECTOR_PLAN, PADDED_LINES = vector_plan()
TAIL_LINES = STEM_LINES + ONE_LINES + PADDED_LINES + 1


def open_kernel(planes, flat_ref, vector_ref, master_ref, mask_ref, pix_ref, perm_ref,
                xp_out, n1_out, s2_out, n2_out, far_out, low0_out,
                res_ref, wbig_ref, d1_ref, d2_ref, head_ref, vs_ref, v2_ref, v3_ref, hv_ref, hb_ref, *refs):
    kern_ref, vec_ref, bin_ref, keep_ref = [refs[LAYERS * n:LAYERS * (n + 1)] for n in range(4)]
    low_ref = (None,) + refs[4 * LAYERS:4 * LAYERS + 2]
    (wide_ref, pad_ref, master, master_sem, low0_ref, x_ref, xp_ref, n1_ref, s2_ref, n2_ref, st_ref, n2s_ref, pix_sem,
     out_sem, w_sem) = refs[4 * LAYERS + 2:]
    net = Net(planes)
    m = net.m
    peers = [net.core] + net.plane[:2]
    for peer in peers:
        net.signal(peer)
    loads = [pltpu.make_async_copy(master_ref.at[l], master.at[l], master_sem.at[l]) for l in range(LAYERS)]
    begin(loads)
    near = pl.ds(pl.multiple_of(m * PAIR, 16), PAIR)
    far = pl.ds(pl.multiple_of((1 - m) * PAIR, 16), PAIR)
    kept = pltpu.make_async_copy(pix_ref.at[near, :], x_ref.at[near, :], out_sem.at[24])
    kept.start()
    pl.semaphore_wait(pltpu.get_barrier_semaphore(), len(peers))
    moves = []
    for g in range(6):
        lanes = pl.ds(g * 384, 384)
        moves.append(remote(pix_ref.at[far, lanes], x_ref.at[near, lanes], pix_sem, g, net.plane[0]))
    begin(moves[:2])
    weights0, weights1, weights2, weights3 = weight_steps(net, low0_ref, far_out, w_sem)
    loads[0].wait()
    low0_ref[...] = master[0].astype(BF)
    weights0()
    begin(moves[2:])
    keep_low = pltpu.make_async_copy(low0_ref, low0_out, out_sem.at[25])
    keep_low.start()
    for name in VECTOR_NAMES:
        offset, width, row = VECTOR_PLAN[name]
        lines = ceil_to(width, 128) // 128
        at, s = offset // 128, offset % 128
        lane = lax.broadcasted_iota(jnp.int32, (lines, 128), 1)
        value = vector_ref[at:at + lines, :]
        if s:
            value = jnp.where(lane < 128 - s, pltpu.roll(value, 128 - s, 1),
                              pltpu.roll(vector_ref[at + 1:at + 1 + lines, :], 128 - s, 1))
        if width % 128:
            spot = lax.broadcasted_iota(jnp.int32, (lines, 128), 0) * 128 + lane
            value = jnp.where(spot < width, value, 0.0)
        pad_ref[row:row + lines, :] = value

    def place(ref, at, name, start, lines):
        row = VECTOR_PLAN[name][2] + start
        for n in range(lines):
            ref[at + (slice(n * 128, (n + 1) * 128),)] = pad_ref[row + n:row + n + 1, :]
    one = lambda n: (slice(n, n + 1),)
    for n, name in enumerate(("bias_stem", "gain_stem", "shift_stem", "gain_one", "shift_one")):
        place(vs_ref, one(n), name, 0, 1)
    for n, name in enumerate(("bias_one", "gain_two", "shift_two")):
        place(v2_ref, one(n), name, 0, 2)
    place(v3_ref, one(0), "bias_two", 0, 3)
    for l in range(LAYERS):
        for n, name in enumerate(("bias_depth", "gain_block", "shift_block", "bias_outer", "layer_scale")):
            place(vec_ref[l], one(n), name, 3 * l, 3)
        for n in range(12):
            part = (n // 6 + m) % 2
            row = VECTOR_PLAN["bias_inner"][2] + 12 * l + part * 6 + n % 6
            bin_ref[l][:, n * 128:(n + 1) * 128] = pad_ref[pl.ds(row, 1), :]
    place(hv_ref, one(0), "gain_final", 0, 3)
    place(hv_ref, one(1), "shift_final", 0, 3)
    place(hb_ref, one(0), "bias_head", 0, 8)
    lane = lax.broadcasted_iota(jnp.int32, (12, 128), 1)
    f0, f1, f2 = [flat_ref[pl.ds(n, 12, stride=3), :] for n in range(3)]
    parts = (f0, jnp.where(lane < 32, pltpu.roll(f0, 32, 1), pltpu.roll(f1, 32, 1)),
             jnp.where(lane < 64, pltpu.roll(f1, 64, 1), pltpu.roll(f2, 64, 1)), pltpu.roll(f2, 96, 1))
    for n in range(4):
        wide_ref[0, pl.ds(n, 12, stride=4), :] = jnp.where(lane < C1, parts[n], 0.0)
    stem = wide_ref[0, 0:48, :].astype(BF)
    wbig_ref[...] = jnp.zeros_like(wbig_ref)
    for j in range(8):
        wbig_ref[j * 48:(j + 1) * 48, j * 128:(j + 1) * 128] = stem
    lane = lax.broadcasted_iota(jnp.int32, (192, 128), 1)
    f0, f1, f2 = [flat_ref[pl.ds(STEM_LINES + n, 192, stride=3), :] for n in range(3)]
    f1 = pltpu.roll(f1, 64, 1)
    f2 = pltpu.roll(f2, 64, 1)
    wide_ref[0, pl.ds(0, 192, stride=2), :] = f0
    wide_ref[1, pl.ds(0, 192, stride=2), :] = jnp.where(lane < 64, pltpu.roll(f1, 64, 1), 0.0)
    wide_ref[0, pl.ds(1, 192, stride=2), :] = jnp.where(lane < 64, f1, f2)
    wide_ref[1, pl.ds(1, 192, stride=2), :] = jnp.where(lane < 64, f2, 0.0)
    d1_ref[...] = jnp.zeros_like(d1_ref)
    d2_ref[...] = jnp.zeros_like(d2_ref)
    for or1 in range(2):
        for oc1 in range(2):
            at = or1 * 192 + oc1 * 96
            for t in range(2):
                d1_ref[or1, oc1 * 128:oc1 * 128 + 96, t * 128:(t + 1) * 128] = wide_ref[t, at:at + 96, :].astype(BF)
    base = STEM_LINES + ONE_LINES
    for lt in range(3):
        for or2 in range(2):
            for oc2 in range(2):
                at = base + (or2 * 384 + oc2 * 192) * 3 + lt
                d2_ref[or2, oc2 * 256:oc2 * 256 + 192, lt * 128:(lt + 1) * 128] = flat_ref[pl.ds(at, 192, stride=3), :].astype(BF)
    mask1 = (lax.broadcasted_iota(jnp.int32, (1, 128), 1) < C1).astype(F32)
    mask2 = (lax.broadcasted_iota(jnp.int32, (1, 256), 1) < C2).astype(F32)
    bias_stem, gain_stem, shift_stem = vs_ref[0:1, :], vs_ref[1:2, :], vs_ref[2:3, :]
    gain_one, shift_one = vs_ref[3:4, :], vs_ref[4:5, :]
    bias_one, gain_two, shift_two = v2_ref[0:1, :], v2_ref[1:2, :], v2_ref[2:3, :]
    kern_base = STEM_LINES + ONE_LINES + TWO_LINES

    def more_low():
        for l in range(1, LAYERS):
            loads[l].wait()
            low_ref[l][...] = master[l].astype(BF)

    def more_small():
        spot = lax.broadcasted_iota(jnp.int32, (COL, 128), 0) % IMG
        for l in range(LAYERS):
            value = jnp.zeros((COL, 128), jnp.int32)
            for n in range(IMG):
                value = jnp.where(spot == n, mask_ref[l, m * IMG + n], value)
            value = value.astype(F32)
            for lt in range(3):
                keep_ref[l][:, lt * 128:(lt + 1) * 128] = value
        for l in range(LAYERS):
            kern_ref[l][...] = flat_ref[kern_base + l * 3 * TAPS:kern_base + (l + 1) * 3 * TAPS, :]

    def more_head():
        base = kern_base + KERN_LINES
        count = C3 // 16
        lane = lax.broadcasted_iota(jnp.int32, (count, 128), 1)
        for k in range(16):
            for t in range(8):
                start = k * CLASSES + t * 128
                f, s = start // 128, start % 128
                need = min(128, CLASSES - t * 128)
                value = flat_ref[pl.ds(base + f, count, stride=CLASSES // 8), :]
                if s:
                    value = pltpu.roll(value, 128 - s, 1)
                    if need > 128 - s:
                        after = flat_ref[pl.ds(base + f + 1, count, stride=CLASSES // 8), :]
                        value = jnp.where(lane < 128 - s, value, pltpu.roll(after, 128 - s, 1))
                if need < 128:
                    value = jnp.where(lane < need, value, 0.0)
                wide_ref[t, pl.ds(k, count, stride=16), :] = value
        for t in range(8):
            head_ref[:, t * 128:(t + 1) * 128] = wide_ref[t].astype(BF)

    extras = [[more_head], [more_small, lambda: weights1(0)], [more_low, lambda: weights1(1), lambda: weights2(0)],
              [lambda: weights1(2), lambda: weights2(1)], [lambda: weights2(2)], []]
    kept.wait()
    writes = []
    for g in range(6):
        moves[g].wait()
        x2 = dot(perm_ref[...], x_ref[:, g * 384:(g + 1) * 384]).astype(BF)
        xp_ref[g] = x2
        for q in range(4):
            o = dot(x2, wbig_ref[:, q * 256:(q + 1) * 256])
            st_ref[2 * q] = o[:, :128]
            st_ref[2 * q + 1] = o[:, 128:]
        v = st_ref[...].reshape(8 * 288, 128) + bias_stem
        xhat, _s = stats(v, C1, mask1)
        y = xhat * gain_stem + shift_stem
        xhat, _s = stats(y, C1, mask1)
        low = (xhat * gain_one + shift_one).astype(BF).reshape(8, 288, 128)
        for j in range(8):
            n1_ref[g, :, j * 128:(j + 1) * 128] = low[j]
        for q in range(4):
            lanes = slice(q * 256, (q + 1) * 256)
            s2_ref[g, q] = dot(n1_ref[g, 0:144, lanes], d1_ref[0]) + dot(n1_ref[g, 144:288, lanes], d1_ref[1]) + bias_one
        for ref, out, at in ((xp_ref, xp_out, 0), (n1_ref, n1_out, 6), (s2_ref, s2_out, 12)):
            writes.append(pltpu.make_async_copy(ref.at[g], out.at[g], out_sem.at[at + g]))
            writes[-1].start()
        xhat, _s = stats(s2_ref[g].reshape(4 * 144, 256), C2, mask2)
        n2 = xhat * gain_two + shift_two
        for q in range(4):
            c2, oc2 = q // 2, q % 2
            for or2 in range(2):
                at = q * 144 + or2 * 72
                n2s_ref[or2, c2 * 72:(c2 + 1) * 72, oc2 * 256:(oc2 + 1) * 256] = n2[at:at + 72]
        rows = slice(g * 144, (g + 1) * 144)
        low0, low1 = n2s_ref[0].astype(BF), n2s_ref[1].astype(BF)
        n2_ref[0, rows, :] = low0
        n2_ref[1, rows, :] = low1
        writes.append(pltpu.make_async_copy(n2_ref.at[:, pl.ds(g * 144, 144), :], n2_out.at[:, pl.ds(g * 144, 144), :],
                                            out_sem.at[18 + g]))
        writes[-1].start()
        res_ref[rows, :] = dot(low0, d2_ref[0]) + dot(low1, d2_ref[1]) + v3_ref[0:1, :]
        for extra in extras[g]:
            extra()
    end(writes)
    keep_low.wait()
    weights3()


def opening(planes, flat, vector, master, keep_mask, pix, perm):
    kept = [(6, 288, 384), (6, 288, 1024), (6, 4, 144, 256), (2, ROWS, 512)]
    types = [BF, BF, F32, BF]
    half = sds((2, C3, HID // 2), BF)
    each = lambda shape: [sds(shape)] * LAYERS
    outs = ([sds((ROWS, C3)), sds((384, 1024), BF), sds((2, 256, 256), BF), sds((2, 512, C3), BF), sds((C3, WIDE), BF),
             sds((8, 128)), sds((8, 256)), sds((8, C3)), sds((2, C3)), sds((1, WIDE))]
            + each((3 * TAPS, 128)) + each((8, C3)) + each((1, HID)) + each((COL, C3)) + [half, half])
    return call(
        functools.partial(open_kernel, planes),
        listed(VM, flat, vector) + listed(AN, master) + listed(SM, keep_mask) + listed(AN, pix) + listed(VM, perm),
        listed(AN, *[sds(a, b) for a, b in zip(kept, types)], half, half) + listed(VM, *outs),
        [pltpu.VMEM((8, C3, 128), F32), pltpu.VMEM((ceil_to(PADDED_LINES, 8), 128), F32),
         pltpu.VMEM((LAYERS, 2, C3, HID // 2), F32), pltpu.SemaphoreType.DMA((LAYERS,)), pltpu.VMEM((2, C3, HID // 2), BF),
         pltpu.VMEM((4 * COL, 4 * SIDE * PATCH), BF)]
        + [pltpu.VMEM(a, b) for a, b in zip(kept, types)]
        + [pltpu.VMEM((8, 288, 128), F32), pltpu.VMEM((2, 144, 512), F32), pltpu.SemaphoreType.DMA((2, 6)),
           pltpu.SemaphoreType.DMA((26,)), pltpu.SemaphoreType.DMA((2, 4 * WEIGHT_PARTS))],
        4_000_000_000, 6,
    )


def finish_kernel(planes, p0_ref, p1_ref, p2_ref, tail_ref, dvs_ref, dv2_ref, dv3_ref, dvec0_ref, dvec1_ref, dvec2_ref,
                  dbin0_ref, dbin1_ref, dbin2_ref, dfinal_ref, dbias_ref, loss_ref, head_ref, two_ref,
                  own_ref, flat_ref, vector_ref, info_ref,
                  grad_ref, full_ref, shard_ref, line_ref, arrived_ref, move_sem, local_sem, *scratch):
    net = Net(planes)
    m, d = net.m, net.d
    dp = 4 * planes
    pieces_ref, dvec_ref, dbin_ref = (p0_ref, p1_ref, p2_ref), (dvec0_ref, dvec1_ref, dvec2_ref), (dbin0_ref, dbin1_ref, dbin2_ref)
    shard = grad_ref.shape[4]
    targets = [((l * dp + d) // 3, (l * dp + d) % 3) for l in range(LAYERS)]
    sources = [(3 * d + s) % dp for s in range(LAYERS)]
    for s in range(LAYERS):
        @pl.when(sources[s] != d)
        def _(s=s):
            net.signal((sources[s], m))
    peers = [net.core] + net.plane + net.column
    for peer in peers:
        net.signal(peer)
    awaited = len(peers)
    for l in range(LAYERS):
        awaited = awaited + jnp.where(targets[l][0] != d, 1, 0)
    pl.semaphore_wait(pltpu.get_barrier_semaphore(), awaited)

    def move(l):
        owner, slot = targets[l]
        return pltpu.make_async_remote_copy(
            src_ref=pieces_ref[l], dst_ref=arrived_ref.at[slot], send_sem=move_sem.at[0, l],
            recv_sem=move_sem.at[1, slot], device_id=(owner, m), device_id_type=pl.DeviceIdType.MESH)

    def keep(l):
        return pltpu.make_async_copy(pieces_ref[l], arrived_ref.at[targets[l][1]], local_sem.at[l])

    for l in range(LAYERS):
        @pl.when(targets[l][0] != d)
        def _(l=l):
            move(l).start()

        @pl.when(targets[l][0] == d)
        def _(l=l):
            keep(l).start()
    squares = jnp.zeros((8, 128), F32)
    for l in range(LAYERS):
        piece = pieces_ref[l][...].astype(F32)
        line = jnp.sum(piece * piece, axis=0, keepdims=True)
        for n in range(6):
            squares = squares + jnp.concatenate([line[:, n * 128:(n + 1) * 128], jnp.zeros((7, 128), F32)], axis=0)
    square = jnp.sum(squares, axis=(0, 1), keepdims=True)
    lead = STEM_LINES + ONE_LINES
    line_ref[0:lead, :] = tail_ref[...]
    line_ref[lead:, :] = jnp.zeros((8 * planes * shard - lead, 128), F32)

    def place(name, start, value):
        row = lead + VECTOR_PLAN[name][2] + start
        for n in range(value.shape[1] // 128):
            line_ref[row + n:row + n + 1, :] = value[:, n * 128:(n + 1) * 128]
    for n, name in enumerate(("bias_stem", "gain_stem", "shift_stem", "gain_one", "shift_one")):
        place(name, 0, dvs_ref[n:n + 1, :])
    for n, name in enumerate(("bias_one", "gain_two", "shift_two")):
        place(name, 0, dv2_ref[n:n + 1, :])
    place("bias_two", 0, dv3_ref[...])
    for l in range(LAYERS):
        for n, name in enumerate(("bias_depth", "gain_block", "shift_block", "bias_outer", "layer_scale")):
            place(name, 3 * l, dvec_ref[l][n:n + 1, :])
        sums = jnp.sum(dbin_ref[l][...], axis=0, keepdims=True)
        for n in range(12):
            part = (n // 6 + m) % 2
            row = lead + VECTOR_PLAN["bias_inner"][2] + 12 * l + part * 6 + n % 6
            line_ref[pl.ds(row, 1), :] = sums[:, n * 128:(n + 1) * 128]
    place("gain_final", 0, dfinal_ref[0:1, :])
    place("shift_final", 0, dfinal_ref[1:2, :])
    place("bias_head", 0, dbias_ref[...])
    lane = lax.broadcasted_iota(jnp.int32, (1, 128), 1)
    info = jnp.where(lane == 2, square, loss_ref[...])
    line_ref[lead + PADDED_LINES:lead + PADDED_LINES + 1, :] = info

    def each_shard(move_one):
        for mm in range(2):
            for yy in range(2):
                for cc in range(2):
                    for k in range(planes):
                        move_one((mm, yy, cc, k), ((((mm * 2 + yy) * 2 + cc) * planes) + k))

    def pack(where, n):
        grad_ref[where] = line_ref[n * shard:(n + 1) * shard, :]
    each_shard(pack)
    steps = flat_sum_steps(net, grad_ref, shard_ref, *scratch[:6]) + spread_steps(net, shard_ref, full_ref, *scratch[6:])
    for step in steps[:2]:
        step()
    big = head_ref.shape[4]
    total = jnp.zeros((8, 128), F32)
    side = two_ref.shape[4]

    def unpack_big(ref, size, base, lines):
        def inner(where, n):
            at = n * size
            if at < lines:
                rows = min(size, lines - at)
                value = ref[where].astype(F32)
                flat_ref[base + at:base + at + rows, :] = value[0:rows]
        each_shard(inner)
    unpack_big(two_ref, side, lead, TWO_LINES + KERN_LINES)
    steps[2]()
    unpack_big(head_ref, big, lead + TWO_LINES + KERN_LINES, HEAD_LINES)
    steps[3]()

    def square_rows(k, total):
        value = flat_ref[pl.ds(lead + k * 45, 45), :]
        return total + jnp.sum(value * value, axis=0, keepdims=True)
    known = (TWO_LINES + KERN_LINES + HEAD_LINES) // 45
    total = lax.fori_loop(0, known, square_rows, jnp.zeros((1, 128), F32))
    rest = lead + known * 45
    if rest < FLAT_LINES:
        value = flat_ref[rest:FLAT_LINES, :]
        total = total + jnp.sum(value * value, axis=0, keepdims=True)
    for step in steps[4:]:
        step()

    def unpack(where, n):
        line_ref[n * shard:(n + 1) * shard, :] = full_ref[where]
    each_shard(unpack)
    value = line_ref[0:lead, :]
    flat_ref[0:lead, :] = value
    total = total + jnp.sum(value * value, axis=0, keepdims=True)
    value = line_ref[lead:lead + PADDED_LINES, :]
    total = total + jnp.sum(value * value, axis=0, keepdims=True)
    info = line_ref[lead + PADDED_LINES:lead + PADDED_LINES + 1, :]
    pick = lambda n: jnp.sum(jnp.where(lane == n, info, 0.0), axis=1, keepdims=True)
    count = jnp.maximum(pick(1), 1.0)
    norm = jnp.sqrt(jnp.sum(total, axis=1, keepdims=True) + pick(2)) / count
    factor = CLIP_LIMIT / jnp.maximum(norm, CLIP_LIMIT) / count
    info_ref[...] = jnp.where(lane == 0, pick(0), jnp.where(lane == 1, count, jnp.where(lane == 2, norm, factor)))
    vector_ref[...] = jnp.zeros_like(vector_ref)
    for name in VECTOR_NAMES:
        offset, width, row = VECTOR_PLAN[name]
        lines = ceil_to(width, 128) // 128
        at, s = offset // 128, offset % 128
        lane8 = lax.broadcasted_iota(jnp.int32, (lines, 128), 1)
        value = line_ref[lead + row:lead + row + lines, :]
        if s:
            value = pltpu.roll(value, s, 1)
            vector_ref[at:at + lines, :] += jnp.where(lane8 < s, 0.0, value)
            vector_ref[at + 1:at + 1 + lines, :] += jnp.where(lane8 < s, value, 0.0)
        else:
            vector_ref[at:at + lines, :] += value
    for l in range(LAYERS):
        @pl.when(targets[l][0] != d)
        def _(l=l):
            move(l).wait_send()

        @pl.when(targets[l][0] == d)
        def _(l=l):
            keep(l).wait()
    for s in range(LAYERS):
        @pl.when(sources[s] != d)
        def _(s=s):
            pltpu.make_async_remote_copy(
                src_ref=pieces_ref[s], dst_ref=arrived_ref.at[s], send_sem=move_sem.at[0, s],
                recv_sem=move_sem.at[1, s], device_id=(sources[s], m), device_id_type=pl.DeviceIdType.MESH).wait_recv()
    own_ref[...] = arrived_ref[...]


def finish(planes, pieces, tail, dvs, dv2, dv3, dvec, dbin, dfinal, dbias, loss, head_sum, two_sum):
    shard = ceil_to(TAIL_LINES, 8 * planes * 8) // (8 * planes)
    shape = (2, 2, 2, planes, shard, 128)
    held = (LAYERS,) + pieces[0].shape
    return call(
        functools.partial(finish_kernel, planes),
        listed(VM, *pieces, tail, dvs, dv2, dv3, *dvec, *dbin, dfinal, dbias, loss, head_sum, two_sum),
        listed(VM, sds(held, BF), sds((FLAT_LINES, 128)), sds((VECTOR_LINES, 128)), sds((1, 128))),
        [pltpu.VMEM(shape, F32), pltpu.VMEM(shape, F32), pltpu.VMEM((shard, 128), F32),
         pltpu.VMEM((8 * planes * shard, 128), F32),
         pltpu.VMEM(held, BF), pltpu.SemaphoreType.DMA((2, LAYERS)), pltpu.SemaphoreType.DMA((LAYERS,))]
        + flat_scratch(planes, shard, F32) + spread_scratch(planes),
        0, 4,
    )


LEARN_RATE = 0.05
VECTOR_RATE = 0.15
WEIGHT_DECAY = 0.05
BETA_ONE = 0.9
BETA_TWO = 0.999
ADAM_EPSILON = 1e-08


def vector_lengths():
    return list(VECTOR_WIDTHS)


def flat_lengths():
    return [PATCH * C1, 4 * C1 * C2, 4 * C2 * C3, LAYERS * TAPS * C3, C3 * CLASSES]


def adam_update(weight, moment_one, moment_two, gradient, step_float, rate):
    first_new = BETA_ONE * moment_one + (1.0 - BETA_ONE) * gradient
    second_new = BETA_TWO * moment_two + (1.0 - BETA_TWO) * gradient * gradient
    first_hat = first_new / (1.0 - BETA_ONE**step_float)
    second_hat = second_new / (1.0 - BETA_TWO**step_float)
    weight_new = weight - rate * (first_hat / (jnp.sqrt(second_hat) + ADAM_EPSILON) + WEIGHT_DECAY * weight)
    return (weight_new, first_new, second_new, weight_new.astype(BF))


def row_source():
    target = np.arange(4 * COL)
    img = target % IMG
    r = target // IMG % SIDE
    or2 = target // COL % 2
    or1 = target // (2 * COL)
    row = 4 * r + 2 * or2 + or1
    return (row // (2 * SIDE)) * (2 * COL) + img * (2 * SIDE) + row % (2 * SIDE)


def per_device(pixels, labels, valid_flags, keep_mask, step_count, pointwise_weight, pointwise_first, pointwise_second,
               flat_weight, flat_first, flat_second, vector_weight, vector_first, vector_second):
    dp = lax.axis_size("dp")
    planes = dp // 4
    vectors = jnp.pad(vector_weight, (0, VECTOR_LINES * 128 - VECTOR)).reshape(VECTOR_LINES, 128)
    perm = jnp.asarray(row_source()[:, None] == np.arange(4 * COL)[None], BF)
    pix = pixels.reshape(4 * COL, 4 * SIDE * PATCH)
    ready = opening(planes, flat_weight.reshape(FLAT_LINES, 128), vectors, pointwise_weight, keep_mask, pix, perm)
    xp, n1, s2, n2, far, low0, res, wbig, d1, d2, head_low, vs, v2, v3, hv, hb = ready[:16]
    kern, vec, bins, keep = [ready[16 + LAYERS * n:16 + LAYERS * (n + 1)] for n in range(4)]
    low = [low0] + list(ready[16 + 4 * LAYERS:])
    kept = []
    for l in range(LAYERS):
        following = low[l + 1] if l + 1 < LAYERS else None
        new, depth, normed, act, dg, out, *arrived = block(planes, res, kern[l], vec[l], bins[l], keep[l], low[l], far, following)
        kept.append((keep[l], vec[l], kern[l], act, dg, out, normed, depth, res, low[l], far))
        res = new
        if arrived:
            far = arrived[0]
    shard = ceil_to(HEAD_LINES, 8 * planes * 16) // (8 * planes)
    dr, dhead, dbias, dfinal, loss = head(res, hv, head_low, hb, labels, valid_flags, 8 * planes * shard)
    blocked = lambda a: a.reshape(planes, 2, 2, 2 * C3 // dp, HID // 2)
    dkern, dvec, dbin = [None] * LAYERS, [None] * LAYERS, [None] * LAYERS
    dr, own, other, dkern[2], dvec[2], dbin[2], head_shard = block_back(
        planes, 0, (dr,) + kept[2], dhead.reshape(2, 2, 2, planes, shard, 128))
    dr, own_new, other_new, dkern[1], dvec[1], dbin[1], held, head_sum = block_back(
        planes, 1, (dr,) + kept[1], blocked(own), blocked(other), head_shard)
    dr, own, other, dkern[0], dvec[0], dbin[0], held, piece2 = block_back(
        planes, 2, (dr,) + kept[0], blocked(own_new), blocked(other_new), held)
    tail, dvs, dv2, dv3, two_sum, piece0, piece1 = back(
        planes, dr, (xp, n1, s2, n2), (wbig, d1, d2, vs, v2), dkern, blocked(own), blocked(other), held)
    pointwise_own, flat_sum, vector_sum, info = finish(
        planes, (piece0, piece1, piece2), tail, dvs, dv2, dv3, dvec, dbin, dfinal, dbias, loss, head_sum, two_sum)
    loss_total, valid_total, gradient_norm, factor = info[0, 0], info[0, 1], info[0, 2], info[0, 3]
    pointwise_own = pointwise_own.reshape(pointwise_first.shape).astype(F32)
    flat_sum = flat_sum.reshape(-1)
    vector_sum = vector_sum.reshape(-1)[:VECTOR]
    step_float = step_count.astype(F32)
    rows_owned = pointwise_first.shape[0]
    master_rows = pointwise_weight.reshape(2 * LAYERS * C3, HID // 2)
    master_own = lax.dynamic_slice_in_dim(master_rows, lax.axis_index("dp") * rows_owned, rows_owned, 0)
    pointwise_out = adam_update(master_own, pointwise_first, pointwise_second, factor * pointwise_own, step_float, LEARN_RATE)
    flat_out = adam_update(flat_weight, flat_first, flat_second, factor * flat_sum, step_float, LEARN_RATE)
    vector_out = adam_update(vector_weight, vector_first, vector_second, factor * vector_sum, step_float, VECTOR_RATE)
    return (loss_total, valid_total, gradient_norm, *pointwise_out, *flat_out, *vector_out)


def solution(mesh):
    placed = (P("dp", "mp", None), P("dp"), P("dp"), P(None, "dp"), P(), P(None, None, None, "mp"), P("dp", "mp"),
              P("dp", "mp"), P(), P(), P(), P(), P(), P())
    return jax.shard_map(
        per_device,
        mesh=mesh,
        in_specs=placed,
        out_specs=(P(), P(), P()) + (P("dp", "mp"),) * 4 + (P(),) * 8,
        check_vma=False,
    )
```

```python
import functools
import jax
import numpy as np
from jax.sharding import PartitionSpec as P
import jax.numpy as jnp
from jax import lax
from jax.experimental import pallas as pl
from jax.experimental.pallas import tpu as pltpu

C1 = 96
C2 = 192
C3 = 384
HID = 1536
CLASSES = 1000
PATCH = 48
KERNEL = 7
LAYERS = 3
SIDE = 12
NORM_EPSILON = 1e-06
SMOOTH = 0.1
CLIP_LIMIT = 0.02
IMG = 6
COL = SIDE * IMG
ROWS = SIDE * COL
PAIR = 2 * COL
FORE = 432
REAR = 288
WF = 256
WB = 256
BF = jnp.bfloat16
F32 = jnp.float32
VMEM_LIMIT = 60 * 1024 * 1024
SHIFTED = COL + 40
TAPS = KERNEL * KERNEL
WIDE = 1024
STEM_LINES = PATCH * C1 // 128
ONE_LINES = 4 * C1 * C2 // 128
TWO_LINES = 4 * C2 * C3 // 128
KERN_LINES = LAYERS * TAPS * C3 // 128
HEAD_LINES = C3 * CLASSES // 128
FLAT_LINES = STEM_LINES + ONE_LINES + TWO_LINES + KERN_LINES + HEAD_LINES


def dot(a, b, da=1, db=0):
    return lax.dot_general(a, b, (((da,), (db,)), ((), ())), preferred_element_type=F32)


def fold8(values):
    rows, lanes = values.shape
    return jnp.sum(values.reshape(rows // 8, 8, lanes), axis=0)


def stats(values, count, mask):
    average = jnp.sum(values, axis=-1, keepdims=True) * (1.0 / count)
    centred = values - average
    if mask is not None:
        centred = centred * mask
    spread = jnp.sum(centred * centred, axis=-1, keepdims=True) * (1.0 / count)
    scale = lax.rsqrt(spread + NORM_EPSILON)
    return centred * scale, scale


def norm_back(delta, xhat, scale, gain, count, mask):
    scaled = delta * gain
    first = jnp.sum(scaled, axis=-1, keepdims=True) * (1.0 / count)
    second = jnp.sum(scaled * xhat, axis=-1, keepdims=True) * (1.0 / count)
    out = (scaled - first - xhat * second) * scale
    if mask is not None:
        out = out * mask
    return out


def sds(shape, dt=F32):
    return jax.ShapeDtypeStruct(shape, dt)


VM, AN, SM = pltpu.VMEM, pl.ANY, pltpu.SMEM


def call(kernel, ins, outs, scratch, flops=0, collective=None):
    params = pltpu.CompilerParams(vmem_limit_bytes=VMEM_LIMIT)
    if collective is not None:
        params = pltpu.CompilerParams(vmem_limit_bytes=VMEM_LIMIT, collective_id=collective, has_side_effects=True)
    return pl.pallas_call(
        kernel,
        in_specs=[pl.BlockSpec(memory_space=space) for _, space in ins],
        out_specs=[pl.BlockSpec(memory_space=space) for _, space in outs],
        out_shape=[shape for shape, _ in outs],
        scratch_shapes=scratch,
        cost_estimate=pl.CostEstimate(flops=flops, bytes_accessed=0, transcendentals=0),
        compiler_params=params,
    )(*[array for array, _ in ins])


def listed(space, *arrays):
    return [(array, space) for array in arrays]


def spread_shifted(cp_ref, lt, c, val):
    for ki in range(4):
        cp_ref[ki, lt, c, 18 - 2 * ki:90 - 2 * ki, :] = val


def zero_edges(cp_ref):
    head, tail = jnp.zeros((24, 128), F32), jnp.zeros((32, 128), F32)
    for ki in range(4):
        for lt in range(3):
            def body(c, _):
                cp_ref[ki, lt, c, 0:24, :] = head
                cp_ref[ki, lt, c, 80:112, :] = tail
                return 0
            lax.fori_loop(0, 12, body, 0)


def gate(h):
    phi_wide = 0.5 * (1.0 + lax.erf(h * 0.7071067811865476))
    dens = jnp.exp(h * h * -0.5) * 0.3989422804014327
    return h * phi_wide, phi_wide + h * dens


PARTS = 4


def weight_send(net, low, quarter, sems, base):
    size = C3 // 2 // PARTS
    k = net.z % PARTS
    part = pl.ds(pl.multiple_of(k * size, 16), size)
    rows = pl.ds(pl.multiple_of(net.y * (C3 // 2) + k * size, 16), size)
    across = remote(low.at[net.c, rows, :], quarter.at[part, :], sems, base, net.plane[0])
    along = [remote(quarter.at[part, :], quarter.at[part, :], sems, base + o, net.four[o - 1]) for o in range(1, PARTS)]

    def step1():
        across.wait()
        begin(along)

    return across.start, step1, lambda: end(along)


def weight_spread(net, quarter, far, sems, local_sem):
    c, y = net.c, net.y
    mine = far.at[c, pl.ds(pl.multiple_of(y * (C3 // 2), 16), C3 // 2), :]
    theirs = far.at[c, pl.ds(pl.multiple_of((1 - y) * (C3 // 2), 16), C3 // 2), :]
    own = pltpu.make_async_copy(quarter, mine, local_sem)
    first = [remote(quarter, mine, sems, 0, net.plane[1]), remote(quarter, mine, sems, 1, net.core)]
    second = remote(theirs, theirs, sems, 2, net.core)

    def step0():
        own.start()
        begin(first)

    def step1():
        first[0].wait()
        second.start()

    def step2():
        own.wait()
        first[1].wait()
        second.wait()

    return step0, step1, step2


def block_kernel(planes, *refs):
    res_ref, kern_ref, vec_ref, bin_ref, keep_ref, own_any, other_any = refs[:7]
    spread, sent = planes
    planes = max(planes)
    refs = refs[7:]
    if spread:
        quarter_ref, refs = refs[0], refs[1:]
    if sent:
        low_ref, refs = refs[0], refs[1:]
    new_ref, depth_out, normed_out, act_out, dg_out, out_out = refs[:6]
    refs = refs[6:]
    if spread:
        far_out, refs = refs[0], refs[1:]
    if sent:
        quarter_out, refs = refs[0], refs[1:]
    cp_ref, wb_ref, own_ref, other_ref, depth_ref, normed_ref, act_ref, dg_ref, out_ref, in_sem, out_sem = refs[:11]
    loads = [pltpu.make_async_copy(own_any, own_ref, in_sem.at[0]), pltpu.make_async_copy(other_any, other_ref, in_sem.at[1])]
    begin(loads)
    nothing = lambda: None
    spread0 = spread1 = spread2 = send1 = send2 = nothing
    if planes:
        net = Net(planes)
        peers = [net.core] + net.plane[:2] + net.four
        if not sent:
            peers = [net.core, net.plane[1]]
        for peer in peers:
            net.signal(peer)
        pl.semaphore_wait(pltpu.get_barrier_semaphore(), len(peers))
        spread0, spread1, spread2 = weight_spread(net, quarter_ref, far_out, refs[11], in_sem.at[2])
        spread0()
        if sent:
            send0, send1, send2 = weight_send(net, low_ref, quarter_out, refs[11], 3)
            send0()
    zero_edges(cp_ref)

    def prep_rows(c, _):
        rows = pl.ds(pl.multiple_of(c * COL, 8), COL)
        for lt in range(3):
            val = res_ref[rows, lt * 128:(lt + 1) * 128].astype(BF).astype(F32)
            spread_shifted(cp_ref, lt, c, val)
        return 0
    lax.fori_loop(0, SIDE, prep_rows, 0)
    for lt in range(3):
        for t in range(TAPS):
            wb_ref[lt, t] = jnp.broadcast_to(kern_ref[3 * t + lt:3 * t + lt + 1, :], (8, 128))
    for lt in range(3):
        lanes = slice(lt * 128, (lt + 1) * 128)
        bias = jnp.broadcast_to(vec_ref[0:1, lanes], (8, 128))

        def conv(v, _, lt=lt, lanes=lanes, bias=bias):
            acc = [bias] * SIDE
            for i in range(KERNEL):
                k = (6 * i) % 8
                row = pl.ds(pl.multiple_of(6 * i - k + v * 8, 8), 8)
                xs = [cp_ref[k // 2, lt, c, row, :] for c in range(SIDE)]
                for j in range(KERNEL):
                    w = wb_ref[lt, i * KERNEL + j]
                    for c in range(SIDE):
                        cc = c + j - 3
                        if 0 <= cc < SIDE:
                            acc[c] = acc[c] + w * xs[cc]
            for c in range(SIDE):
                depth_ref[pl.ds(pl.multiple_of(c * COL + v * 8, 8), 8), lanes] = acc[c]
            return 0
        lax.fori_loop(0, COL // 8, conv, 0)
    writes = [pltpu.make_async_copy(depth_ref, depth_out, out_sem.at[0])]
    writes[0].start()
    gain, shift = vec_ref[1:2, :], vec_ref[2:3, :]
    for r in range(ROWS // FORE):
        rows = slice(r * FORE, (r + 1) * FORE)
        xhat, _s = stats(depth_ref[rows, :], C3, None)
        normed_ref[rows, :] = (xhat * gain + shift).astype(BF)
    writes.append(pltpu.make_async_copy(normed_ref, normed_out, out_sem.at[1]))
    writes[1].start()
    bias_out, scale = vec_ref[3:4, :], vec_ref[4:5, :]
    keep_scale = keep_ref[...] * scale
    end(loads)
    for m in range(ROWS // FORE):
        rows, at_rows = slice(m * FORE, (m + 1) * FORE), pl.ds(m * FORE, FORE)
        low = normed_ref[rows, :]
        for n in range(HID // WF):
            lanes = slice(n * WF, (n + 1) * WF)
            half = own_ref if n * WF < HID // 2 else other_ref
            at = n * WF % (HID // 2)
            h = dot(low, half[0, :, at:at + WF]) + bin_ref[:, lanes]
            act, dg = gate(h)
            act_ref[rows, lanes] = act.astype(BF)
            dg_ref[rows, lanes] = dg.astype(BF)
            if n == HID // WF // 2 - 1 or n == HID // WF - 1:
                side = pl.ds(0 if n < HID // WF - 1 else HID // 2, HID // 2)
                for ref, out in ((act_ref, act_out), (dg_ref, dg_out)):
                    writes.append(pltpu.make_async_copy(ref.at[at_rows, side], out.at[at_rows, side], out_sem.at[len(writes)]))
                    writes[-1].start()
        if m == 0:
            spread1()
            send1()
        o = (dot(act_ref[rows, :HID // 2], own_ref[1], 1, 1) + dot(act_ref[rows, HID // 2:], other_ref[1], 1, 1)
             + bias_out)
        out_ref[rows, :] = o
        writes.append(pltpu.make_async_copy(out_ref.at[at_rows, :], out_out.at[at_rows, :], out_sem.at[len(writes)]))
        writes[-1].start()
        new_ref[rows, :] = res_ref[rows, :] + jnp.concatenate([keep_scale] * (FORE // COL), axis=0) * o
    end(writes)
    spread2()
    send2()


def block(planes, res, kern, vec, bin_, keep, own, other, quarter=None, low=None):
    half = (2, C3, HID // 2)
    kept = [sds((ROWS, C3)), sds((ROWS, C3), BF), sds((ROWS, HID), BF), sds((ROWS, HID), BF), sds((ROWS, C3))]
    outs = listed(VM, sds((ROWS, C3))) + listed(AN, *kept)
    ins = listed(VM, res, kern, vec, bin_, keep) + listed(AN, own, other)
    scratch = [pltpu.VMEM((4, 3, SIDE, SHIFTED, 128), F32), pltpu.VMEM((3, TAPS, 8, 128), F32),
               pltpu.VMEM(half, BF), pltpu.VMEM(half, BF)]
    scratch += [pltpu.VMEM(k.shape, k.dtype) for k in kept]
    scratch += [pltpu.SemaphoreType.DMA((3,)), pltpu.SemaphoreType.DMA((2 + 5 * ROWS // FORE,))]
    collective = None
    if quarter is not None:
        ins = ins + listed(AN, quarter)
        outs = outs + listed(AN, sds(half, BF))
        scratch.append(pltpu.SemaphoreType.DMA((2, 3 + PARTS)))
        collective = 7
    if low is not None:
        ins = ins + listed(AN, low)
        outs = outs + listed(AN, sds((C3 // 2, HID // 2), BF))
        collective = 8
    part = (planes if quarter is not None else 0, planes if low is not None else 0)
    return call(functools.partial(block_kernel, part), ins, outs, scratch, 4_000_000_000, collective)


def head_flatten(wide_ref, line_ref):
    lane = lax.broadcasted_iota(jnp.int32, (C3 // 16, 128), 1)

    def tile(k, t, shift):
        value = wide_ref[t, pl.ds(k, C3 // 16, stride=16), :]
        return pltpu.roll(value, shift % 128, 1) if shift % 128 else value

    for f in range(CLASSES // 8):
        k, col = f * 128 // CLASSES, f * 128 % CLASSES
        t, s = col // 128, col % 128
        take = min(128, CLASSES - col)
        value = tile(k, t, 128 - s)
        if s and t < 7:
            value = jnp.where(lane < 128 - s, value, tile(k, t + 1, 128 - s))
        if take < 128:
            value = jnp.where(lane < take, value, tile(k + 1, 0, take))
        line_ref[pl.ds(f, C3 // 16, stride=CLASSES // 8), :] = value


def head_kernel(res_ref, vec_ref, head_ref, bias_ref, label_ref, valid_ref,
                dr_ref, dhead_ref, dbias_ref, dvec_ref, loss_ref, sum_ref, wide_ref, line_ref):
    def add(c, total):
        return total + res_ref[pl.ds(pl.multiple_of(c * COL, 8), COL), :]
    total = lax.fori_loop(1, SIDE, add, res_ref[0:COL, :])
    sum_ref[...] = total
    pooled = sum_ref[0:IMG, :]
    for r in range(1, SIDE):
        pooled = pooled + sum_ref[r * IMG:(r + 1) * IMG, :]
    pooled = jnp.concatenate([pooled * (1.0 / (SIDE * SIDE)), jnp.zeros((2, C3), F32)], axis=0)
    gain, shift = vec_ref[0:1, :], vec_ref[1:2, :]
    xhat, scale = stats(pooled, C3, None)
    final = (xhat * gain + shift).astype(BF)
    real = lax.broadcasted_iota(jnp.int32, (8, WIDE), 1) < CLASSES
    logits = jnp.where(real, dot(final, head_ref[...]) + bias_ref[...], -1e30)
    top = jnp.max(logits, axis=-1, keepdims=True)
    shifted = logits - top
    expd = jnp.exp(shifted)
    total = jnp.sum(expd, axis=-1, keepdims=True)
    log_chance = jnp.where(real, shifted - jnp.log(total), 0.0)
    spot = lax.broadcasted_iota(jnp.int32, (8, 1), 0)
    first_image = lax.axis_index("mp") * IMG
    label, valid = jnp.zeros((8, 1), jnp.int32), jnp.zeros((8, 1), jnp.int32)
    for n in range(IMG):
        label = jnp.where(spot == n, label_ref[first_image + n], label)
        valid = jnp.where(spot == n, valid_ref[first_image + n], valid)
    valid = valid.astype(F32)
    onehot = (label == lax.broadcasted_iota(jnp.int32, (8, WIDE), 1)).astype(F32)
    per_image = (-(1.0 - SMOOTH) * jnp.sum(log_chance * onehot, axis=-1, keepdims=True)
                 - (SMOOTH / CLASSES) * jnp.sum(log_chance, axis=-1, keepdims=True))
    lane = lax.broadcasted_iota(jnp.int32, (1, 128), 1)
    loss_ref[...] = jnp.where(lane == 0, jnp.sum(per_image * valid, axis=0, keepdims=True),
                              jnp.where(lane == 1, jnp.sum(valid, axis=0, keepdims=True), 0.0))
    delta = jnp.where(real, (jnp.exp(log_chance) - (1.0 - SMOOTH) * onehot - SMOOTH / CLASSES) * valid, 0.0)
    dbias_ref[...] = jnp.sum(delta, axis=0, keepdims=True)
    high = delta.astype(BF)
    rest = (delta - high.astype(F32)).astype(BF)
    for t in range(8):
        lanes = slice(t * 128, (t + 1) * 128)
        wide_ref[t] = dot(final, high[:, lanes], 0, 0) + dot(final, rest[:, lanes], 0, 0)
    head_flatten(wide_ref, line_ref)
    line_ref[HEAD_LINES:, :] = jnp.zeros((line_ref.shape[0] - HEAD_LINES, 128), F32)
    dhead_ref[...] = line_ref[...].astype(BF)
    dfinal = dot(high, head_ref[...], 1, 1) + dot(rest, head_ref[...], 1, 1)
    dvec_ref[0:1, :] = jnp.sum(dfinal * xhat, axis=0, keepdims=True)
    dvec_ref[1:2, :] = jnp.sum(dfinal, axis=0, keepdims=True)
    dpooled = norm_back(dfinal, xhat, scale, gain, C3, None) * (1.0 / (SIDE * SIDE))
    for r in range(SIDE):
        sum_ref[r * IMG:(r + 1) * IMG, :] = dpooled[0:IMG, :]

    def put(c, _):
        dr_ref[pl.ds(pl.multiple_of(c * COL, 8), COL), :] = sum_ref[...]
        return 0
    lax.fori_loop(0, SIDE, put, 0)


def head(res, vec, head_low, bias, labels, valid, lines):
    return call(
        head_kernel,
        listed(VM, res, vec, head_low, bias) + listed(SM, labels, valid),
        listed(VM, sds((ROWS, C3)), sds((lines, 128), BF), sds((1, WIDE)), sds((2, C3)), sds((1, 128))),
        [pltpu.VMEM((COL, C3), F32), pltpu.VMEM((8, C3, 128), F32), pltpu.VMEM((lines, 128), F32)],
        20_000_000,
    )


def ceil_to(value, step):
    return -(-value // step) * step


class Net:
    def __init__(self, planes):
        self.planes = planes
        self.d = lax.axis_index("dp")
        self.m = lax.axis_index("mp")
        self.c = self.d % 2
        self.y = self.d // 2 % 2
        self.z = self.d // 4
        self.core = (self.d + 1 - 2 * self.c, self.m)
        flip = self.d + 2 - 4 * self.y
        self.plane = [(self.d, 1 - self.m), (flip, self.m), (flip, 1 - self.m)]
        self.all_plane = []
        for k in range(1, 8):
            mm = 1 - self.m if k & 4 else self.m
            yy = 1 - self.y if k & 2 else self.y
            cc = 1 - self.c if k & 1 else self.c
            self.all_plane.append(((mm, yy, cc), (4 * self.z + 2 * yy + cc, mm)))
        group = self.z // 4 * 4
        self.four = [(4 * (group + (self.z % 4 + o) % 4) + 2 * self.y + self.c, self.m) for o in range(1, 4)]
        self.column = [(4 * ((self.z + o) % planes) + 2 * self.y + self.c, self.m) for o in range(1, planes)]

    def signal(self, peer):
        pl.semaphore_signal(pltpu.get_barrier_semaphore(), inc=1, device_id=peer, device_id_type=pl.DeviceIdType.MESH)

    def greet(self):
        peers = [self.core] + self.plane + self.column
        for peer in peers:
            self.signal(peer)
        pl.semaphore_wait(pltpu.get_barrier_semaphore(), len(peers))


def remote(src, dst, sems, number, peer):
    return pltpu.make_async_remote_copy(
        src_ref=src, dst_ref=dst, send_sem=sems.at[0, number], recv_sem=sems.at[1, number],
        device_id=peer, device_id_type=pl.DeviceIdType.MESH)


def begin(copies):
    for copy in copies:
        copy.start()


def end(copies):
    for copy in copies:
        copy.wait()


CHUNKS = 2


def layer_scratch(planes, rows, width):
    part = width // CHUNKS
    return [
        pltpu.VMEM((CHUNKS, 2, planes, 2, rows, part), BF),
        pltpu.VMEM((CHUNKS, 2, 2, planes, rows, part), BF),
        pltpu.VMEM((CHUNKS, 3, planes, rows, part), BF),
        pltpu.VMEM((2, planes, 2, rows, width), BF),
        pltpu.SemaphoreType.DMA((2, 5 * CHUNKS)),
        pltpu.SemaphoreType.DMA((2,)),
    ]


def layer_steps(net, own, other, out, r1, s1, r2, held, sems, held_sem):
    c, y = net.c, net.y
    part = own.shape[4] // CHUNKS
    first, second = [], []
    for k in range(CHUNKS):
        lanes = pl.ds(k * part, part)
        first.append([remote(own.at[:, :, 1 - c, :, lanes], r1.at[k, 0], sems, 5 * k, net.core),
                      remote(other.at[:, :, 1 - c, :, lanes], r1.at[k, 1], sems, 5 * k + 1, net.core)])
        second.append([remote(s1.at[k, 1, y], r2.at[k, 0], sems, 5 * k + 2, net.plane[0]),
                       remote(s1.at[k, 0, 1 - y], r2.at[k, 1], sems, 5 * k + 3, net.plane[1]),
                       remote(s1.at[k, 1, 1 - y], r2.at[k, 2], sems, 5 * k + 4, net.plane[2])])

    loads = [pltpu.make_async_copy(own.at[:, :, c], held.at[0], held_sem.at[0]),
             pltpu.make_async_copy(other.at[:, :, c], held.at[1], held_sem.at[1])]

    def step0():
        begin(first[0])
        begin(loads)

    def step1(k):
        end(first[k])
        if k + 1 < CHUNKS:
            begin(first[k + 1])
        if k == 0:
            end(loads)
        lanes = slice(k * part, (k + 1) * part)

        def add(n, _):
            for yy in range(2):
                s1[k, 0, yy, n] = (held[0, n, yy, :, lanes].astype(F32) + r1[k, 0, n, yy].astype(F32)).astype(BF)
                s1[k, 1, yy, n] = (held[1, n, yy, :, lanes].astype(F32) + r1[k, 1, n, yy].astype(F32)).astype(BF)
            return 0
        lax.fori_loop(0, net.planes, add, 0)
        begin(second[k])

    def step2(k):
        end(second[k])
        lanes = slice(k * part, (k + 1) * part)

        def add(n, _):
            total = s1[k, 0, y, n].astype(F32)
            for j in range(3):
                total = total + r2[k, j, n].astype(F32)
            out[n, :, lanes] = total.astype(BF)
            return 0
        lax.fori_loop(0, net.planes, add, 0)

    return step0, step1, step2


def column_scratch(planes, rows, width):
    return [pltpu.VMEM((planes - 1, rows, width), BF), pltpu.SemaphoreType.DMA((2, planes))]


def column_steps(net, held, out, r3, sems):
    copies = [remote(held.at[(net.z + o) % net.planes], r3.at[o - 1], sems, o - 1, net.column[o - 1])
              for o in range(1, net.planes)]

    def step1():
        end(copies)

        def add(k, total):
            return total + r3[k].astype(F32)
        out[...] = lax.fori_loop(0, net.planes - 1, add, held[net.z].astype(F32)).astype(BF)

    return (lambda: begin(copies)), step1


def flat_scratch(planes, rows, dtype):
    return [
        pltpu.VMEM((2, 2, planes, rows, 128), dtype),
        pltpu.VMEM((2, 2, planes, rows, 128), dtype),
        pltpu.VMEM((3, planes, rows, 128), dtype),
        pltpu.VMEM((planes, rows, 128), dtype),
        pltpu.VMEM((planes - 1, rows, 128), dtype),
        pltpu.SemaphoreType.DMA((2, 3 + planes)),
    ]


def spread_scratch(planes):
    return [pltpu.SemaphoreType.DMA((2, 3 + planes))]


def flat_sum_steps(net, grad, shard, r1, s1, r2, s2, r3, sems):
    c, y, z, m = net.c, net.y, net.z, net.m
    planes = net.planes
    dtype = shard.dtype
    first = [remote(grad.at[:, :, 1 - c], r1, sems, 0, net.core)]
    second = [remote(s1.at[1 - m, y], r2.at[0], sems, 1, net.plane[0]),
              remote(s1.at[m, 1 - y], r2.at[1], sems, 2, net.plane[1]),
              remote(s1.at[1 - m, 1 - y], r2.at[2], sems, 3, net.plane[2])]
    third = [remote(s2.at[(z + o) % planes], r3.at[o - 1], sems, 3 + o, net.column[o - 1]) for o in range(1, planes)]

    def step1():
        end(first)
        for mm in range(2):
            for yy in range(2):
                s1[mm, yy] = (grad[mm, yy, c].astype(F32) + r1[mm, yy].astype(F32)).astype(dtype)
        begin(second)

    def step2():
        end(second)
        total = s1[m, y].astype(F32)
        for n in range(3):
            total = total + r2[n].astype(F32)
        s2[...] = total.astype(dtype)
        begin(third)

    def step3():
        end(third)

        def add(k, total):
            return total + r3[k].astype(F32)
        shard[...] = lax.fori_loop(0, planes - 1, add, s2[z].astype(F32)).astype(dtype)

    return [lambda: begin(first), step1, step2, step3]


def spread_steps(net, shard, out, sems):
    c, y, z, m = net.c, net.y, net.z, net.m
    planes = net.planes
    first = [remote(out.at[m, y, c, z], out.at[m, y, c, z], sems, o - 1, net.column[o - 1]) for o in range(1, planes)]
    second = [remote(out.at[m, y, c], out.at[m, y, c], sems, planes - 1 + k, net.plane[k]) for k in range(3)]
    third = [remote(out.at[:, :, c], out.at[:, :, c], sems, planes + 2, net.core)]

    def step0():
        out[m, y, c, z] = shard[...]
        begin(first)

    def step1():
        end(first)
        begin(second)

    def step2():
        end(second)
        begin(third)

    return [step0, step1, step2, lambda: end(third)]


def tail_scratch(planes, rows, dtype):
    return [
        pltpu.VMEM((7, planes, rows, 128), dtype),
        pltpu.VMEM((planes, rows, 128), dtype),
        pltpu.VMEM((planes - 1, rows, 128), dtype),
        pltpu.SemaphoreType.DMA((2, 12 + 2 * planes)),
    ]


def tail_steps(net, grad, out, r1, s1, r2, sems):
    c, y, z, m = net.c, net.y, net.z, net.m
    planes = net.planes
    first = [remote(grad.at[mm, yy, cc], r1.at[n], sems, n, net.all_plane[n][1])
             for n, ((mm, yy, cc), _) in enumerate(net.all_plane)]
    second = [remote(s1.at[(z + o) % planes], r2.at[o - 1], sems, 6 + o, net.column[o - 1]) for o in range(1, planes)]
    third = [remote(out.at[m, y, c, z], out.at[m, y, c, z], sems, 5 + planes + o, net.column[o - 1])
             for o in range(1, planes)]
    fourth = [remote(out.at[m, y, c], out.at[m, y, c], sems, 5 + 2 * planes + n, net.all_plane[n][1]) for n in range(7)]

    def step1():
        end(first)
        total = grad[m, y, c]
        for n in range(7):
            total = total + r1[n]
        s1[...] = total
        begin(second)

    def step2():
        end(second)

        def add(k, total):
            return total + r2[k]
        out[m, y, c, z] = lax.fori_loop(0, planes - 1, add, s1[z])
        begin(third)

    def step3():
        end(third)
        begin(fourth)

    return [lambda: begin(first), step1, step2, step3, lambda: end(fourth)]


def block_back_body(hooks, dr_ref, keep_ref, vec_ref, kern_ref, act_any, dg_any, out_any, normed_any, depth_any, res_any,
                    own_any, other_any,
                    new_ref, down_any, dother_any, dkern_ref, dvec_ref, dbin_ref,
                    cp_ref, wb_ref, dout_ref, dhid_ref, kacc_ref, act_ref, dg_ref, out_ref, normed_ref, depth_ref, res_ref,
                    own_ref, other_ref, down_ref, dother_ref, in_sem):
    pairs = ((own_any, own_ref), (other_any, other_ref), (dg_any, dg_ref), (depth_any, depth_ref), (act_any, act_ref),
             (normed_any, normed_ref), (out_any, out_ref), (res_any, res_ref))
    load = [pltpu.make_async_copy(a, b, in_sem.at[n]) for n, (a, b) in enumerate(pairs)]
    begin(load[:3])
    hooks = iter(hooks)

    def tick():
        for hook in next(hooks):
            hook()
    tick()
    zero_edges(cp_ref)
    for lt in range(3):
        for t in range(TAPS):
            wb_ref[lt, t] = jnp.broadcast_to(kern_ref[3 * t + lt:3 * t + lt + 1, :], (8, 128))
    kacc_ref[...] = jnp.zeros_like(kacc_ref)
    gain, scale = vec_ref[1:2, :], vec_ref[4:5, :]

    def pre(m, a_bias):
        rows = pl.ds(pl.multiple_of(m * PAIR, 16), PAIR)
        keep = jnp.concatenate([keep_ref[...], keep_ref[...]], axis=0)
        dk = dr_ref[rows, :] * keep
        low = (dk * scale).astype(BF)
        dout_ref[rows, :] = low
        return a_bias + fold8(low.astype(F32))
    zero = jnp.zeros((8, C3), F32)
    a_bias = lax.fori_loop(0, ROWS // PAIR, pre, zero)
    dvec_ref[3:4, :] = jnp.sum(a_bias, axis=0, keepdims=True)
    dbin_ref[...] = jnp.zeros_like(dbin_ref)
    end(load[:3])
    begin(load[3:])

    def mm(m, carry):
        a_gain, a_shift, a_depth = carry
        rows = slice(m * REAR, (m + 1) * REAR)
        low = dout_ref[rows, :]
        for n in range(HID // WB):
            lanes = slice(n * WB, (n + 1) * WB)
            half = own_ref if n * WB < HID // 2 else other_ref
            at = n * WB % (HID // 2)
            d = dot(low, half[1, :, at:at + WB]) * dg_ref[rows, lanes].astype(F32)
            dlow = d.astype(BF)
            dhid_ref[rows, lanes] = dlow
            dbin_ref[:, lanes] += fold8(dlow.astype(F32))
        d = dot(dhid_ref[rows, :HID // 2], own_ref[0], 1, 1) + dot(dhid_ref[rows, HID // 2:], other_ref[0], 1, 1)
        if m == 0:
            load[3].wait()
        xhat, rs = stats(depth_ref[rows, :], C3, None)
        a_gain = a_gain + fold8(d * xhat)
        a_shift = a_shift + fold8(d)
        dd = norm_back(d, xhat, rs, gain, C3, None)
        a_depth = a_depth + fold8(dd)
        for n in range(REAR // COL):
            for lt in range(3):
                spread_shifted(cp_ref, lt, m * (REAR // COL) + n, dd[n * COL:(n + 1) * COL, lt * 128:(lt + 1) * 128])
        return a_gain, a_shift, a_depth
    sums = (zero, zero, zero)
    for n in range(ROWS // REAR):
        sums = mm(n, sums)
        tick()
    end(load[4:])

    def scale_rows(m, total):
        rows = pl.ds(pl.multiple_of(m * PAIR, 16), PAIR)
        keep = jnp.concatenate([keep_ref[...], keep_ref[...]], axis=0)
        return total + fold8(dr_ref[rows, :] * keep * out_ref[rows, :])
    a_scale = lax.fori_loop(0, ROWS // PAIR, scale_rows, zero)
    dvec_ref[4:5, :] = jnp.sum(a_scale, axis=0, keepdims=True)
    a_gain, a_shift, a_depth = sums
    dvec_ref[0:1, :] = jnp.sum(a_depth, axis=0, keepdims=True)
    dvec_ref[1:2, :] = jnp.sum(a_gain, axis=0, keepdims=True)
    dvec_ref[2:3, :] = jnp.sum(a_shift, axis=0, keepdims=True)
    dvec_ref[5:8, :] = jnp.zeros((3, C3), F32)
    writes = []
    for n in range(HID // 256):
        lanes = slice(n * 256, (n + 1) * 256)
        half = down_ref if n < 3 else dother_ref
        part = slice((n % 3) * 256, (n % 3 + 1) * 256)
        half[1, :, part] = dot(dout_ref[...], act_ref[:, lanes], 0, 0).astype(BF)
        half[0, :, part] = dot(normed_ref[...], dhid_ref[:, lanes], 0, 0).astype(BF)
        if n % 3 == 2:
            out = down_any if n == 2 else dother_any
            writes.append(pltpu.make_async_copy(half, out, in_sem.at[8 + n // 3]))
            writes[-1].start()
            tick()
    for lt in range(3):
        lanes = slice(lt * 128, (lt + 1) * 128)

        def conv(v, _, lt=lt, lanes=lanes):
            spots = [pl.ds(pl.multiple_of(c * COL + v * 8, 8), 8) for c in range(SIDE)]
            acc = [dr_ref[s, lanes] for s in spots]
            sent = [res_ref[s, lanes].astype(BF).astype(F32) for s in spots]
            for i in range(KERNEL):
                flip = 6 - i
                k = (6 * flip) % 8
                row = pl.ds(pl.multiple_of(6 * flip - k + v * 8, 8), 8)
                xs = [cp_ref[k // 2, lt, c, row, :] for c in range(SIDE)]
                for j in range(KERNEL):
                    t = i * KERNEL + j
                    w = wb_ref[lt, t]
                    tap = None
                    for c in range(SIDE):
                        cc = c - (j - 3)
                        if 0 <= cc < SIDE:
                            acc[c] = acc[c] + w * xs[cc]
                            term = sent[c] * xs[cc]
                            tap = term if tap is None else tap + term
                    kacc_ref[lt, t] += tap
            for c in range(SIDE):
                new_ref[spots[c], lanes] = acc[c]
            return 0
        lax.fori_loop(0, COL // 8, conv, 0)
        tick()
    for lt in range(3):
        for t in range(TAPS):
            dkern_ref[3 * t + lt:3 * t + lt + 1, :] = jnp.sum(kacc_ref[lt, t], axis=0, keepdims=True)
    end(writes)


HOOKS = 9
BODY_INS, BODY_OUTS, BODY_SCRATCH = 12, 6, 16


def back_parts():
    outs = (listed(VM, sds((ROWS, C3))) + listed(AN, sds((2, C3, HID // 2), BF), sds((2, C3, HID // 2), BF))
            + listed(VM, sds((3 * TAPS, 128)), sds((8, C3)), sds((8, HID))))
    wide, half = (ROWS, HID), (2, C3, HID // 2)
    scratch = [pltpu.VMEM((4, 3, SIDE, SHIFTED, 128), F32), pltpu.VMEM((3, TAPS, 8, 128), F32),
               pltpu.VMEM((ROWS, C3), BF), pltpu.VMEM(wide, BF), pltpu.VMEM((3, TAPS, 8, 128), F32),
               pltpu.VMEM(wide, BF), pltpu.VMEM(wide, BF), pltpu.VMEM((ROWS, C3), F32), pltpu.VMEM((ROWS, C3), BF),
               pltpu.VMEM((ROWS, C3), F32), pltpu.VMEM((ROWS, C3), F32), pltpu.VMEM(half, BF), pltpu.VMEM(half, BF),
               pltpu.VMEM(half, BF), pltpu.VMEM(half, BF), pltpu.SemaphoreType.DMA((10,))]
    return outs, scratch


def take(refs, count):
    return refs[:count], refs[count:]


def block_back_kernel(planes, kind, *refs):
    net = Net(planes)
    args, refs = take(refs, BODY_INS)
    more_in, refs = take(refs, (1, 3, 3)[kind])
    outs, refs = take(refs, BODY_OUTS)
    more_out, refs = take(refs, (1, 2, 2)[kind])
    scratch, refs = take(refs, BODY_SCRATCH)
    hooks = [[] for _ in range(HOOKS)]
    if kind == 0:
        steps = flat_sum_steps(net, more_in[0], more_out[0], *refs)
        hooks[0], hooks[2], hooks[4], hooks[6] = [net.greet, steps[0]], [steps[1]], [steps[2]], [steps[3]]
    else:
        step0, step1, step2 = layer_steps(net, more_in[0], more_in[1], more_out[0], *refs[:6])
        hooks[0] = [net.greet, step0]
        hooks[1] = [lambda: step1(0)]
        hooks[2] = [lambda: step1(1)]
        hooks[5] = [lambda: step2(0)]
        hooks[7] = [lambda: step2(1)]
        if kind == 1:
            steps = spread_steps(net, more_in[2], more_out[1], *refs[6:])
            hooks[0] = [net.greet, steps[0], step0]
            hooks[1] = [steps[1], lambda: step1(0)]
            hooks[5] = [steps[2]]
            hooks[6] = [lambda: step2(0)]
            hooks[7] = []
            hooks[8] = [lambda: step2(1), steps[3]]
        else:
            col0, col1 = column_steps(net, more_in[2], more_out[1], *refs[6:])
            hooks[0].append(col0)
            hooks[4].append(col1)
    block_back_body(hooks, *args, *outs, *scratch)


def block_back(planes, kind, args, *more):
    outs, scratch = back_parts()
    ins = listed(VM, *args[:4]) + listed(AN, *args[4:])
    if kind == 0:
        grad, = more
        rows = grad.shape[4]
        ins += listed(VM, grad)
        outs += listed(VM, sds((rows, 128), BF))
        scratch += flat_scratch(planes, rows, BF)
    else:
        own, other, held = more
        rows, width = own.shape[3:]
        ins += listed(AN, own, other) + listed(VM, held)
        outs += listed(VM, sds((planes, rows, width), BF))
        scratch += layer_scratch(planes, rows, width)
        if kind == 1:
            outs += listed(VM, sds((2, 2, 2, planes) + held.shape, BF))
            scratch += spread_scratch(planes)
        else:
            outs += listed(VM, sds((rows, width), BF))
            scratch += column_scratch(planes, rows, width)
    return call(functools.partial(block_back_kernel, planes, kind), ins, outs, scratch, 8_000_000_000, (1, 2, 5)[kind])


def back_kernel(planes, dr_ref, xp_any, n1_any, s2_any, n2_any, wbig_ref, d1_ref, d2_ref, vs_ref, v2_ref, dk0_ref, dk1_ref,
                dk2_ref, own_ref, other_ref, held_ref,
                tail_ref, dvs_ref, dv2_ref, dv3_ref, two_ref, piece0_ref, piece1_ref, one_ref,
                mid_ref, line1_ref, grad1_ref, shard1_ref,
                xp_ref, n1_ref, s2_ref, n2_ref, in_sem,
                sum_ref, shard_ref, st_ref, dn1_ref, dlow_ref, base_ref, aw_ref, dd1_ref, line_ref, grad_ref, *scratch):
    load_n2 = pltpu.make_async_copy(n2_any, n2_ref, in_sem.at[18])
    load_n2.start()
    loads = [[pltpu.make_async_copy(a.at[g], b.at[g], in_sem.at[3 * g + n])
              for n, (a, b) in enumerate(((xp_any, xp_ref), (n1_any, n1_ref), (s2_any, s2_ref)))] for g in range(6)]
    begin(loads[0][1:])
    net = Net(planes)
    net.greet()
    layer0, layer1, layer2 = layer_steps(net, own_ref, other_ref, sum_ref, *scratch[:6])
    high0, high1 = column_steps(net, held_ref, piece1_ref, *scratch[6:8])
    low0, low1 = column_steps(net, sum_ref, piece0_ref, *scratch[8:10])
    high0()
    layer0()
    mask1 = (lax.broadcasted_iota(jnp.int32, (1, 128), 1) < C1).astype(F32)
    mask2 = (lax.broadcasted_iota(jnp.int32, (1, 256), 1) < C2).astype(F32)
    bias_stem, gain_stem, shift_stem = vs_ref[0:1, :], vs_ref[1:2, :], vs_ref[2:3, :]
    gain_one = vs_ref[3:4, :]
    gain_two = v2_ref[1:2, :]
    z1, z2, z3 = jnp.zeros((8, 128), F32), jnp.zeros((8, 256), F32), jnp.zeros((8, C3), F32)
    dd1_ref[...] = jnp.zeros_like(dd1_ref)
    aw_ref[...] = jnp.zeros_like(aw_ref)

    base_ref[...] = dr_ref[...].astype(BF)
    shard = grad_ref.shape[4]
    load_n2.wait()
    for g in range(1, 6):
        begin(loads[g][1:])
    for g in range(6):
        loads[g][0].start()
    for or2 in range(2):
        total = dot(n2_ref[or2], base_ref[...], 0, 0)
        for oc2 in range(2):
            for lt in range(3):
                line_ref[pl.ds(3 * (or2 * 384 + oc2 * 192) + lt, 192, stride=3), :] = (
                    total[oc2 * 256:oc2 * 256 + 192, lt * 128:(lt + 1) * 128])
    for l in range(LAYERS):
        line_ref[TWO_LINES + l * 3 * TAPS:TWO_LINES + (l + 1) * 3 * TAPS, :] = (dk0_ref, dk1_ref, dk2_ref)[l][...]
    line_ref[TWO_LINES + KERN_LINES:, :] = jnp.zeros((8 * planes * shard - TWO_LINES - KERN_LINES, 128), F32)
    for mm in range(2):
        for yy in range(2):
            for cc in range(2):
                for k in range(planes):
                    at = (((mm * 2 + yy) * 2 + cc) * planes + k) * shard
                    grad_ref[mm, yy, cc, k] = line_ref[at:at + shard, :].astype(BF)
    flat = flat_sum_steps(net, grad_ref, shard_ref, *scratch[10:16])
    flat += spread_steps(net, shard_ref, two_ref, *scratch[16:17])
    layer1(0)

    def upper(g, carry):
        rows = pl.ds(g * 144, 144)
        base = base_ref[rows, :]
        a3 = carry[0] + fold8(base.astype(F32))
        a_bias2, a_gain2, a_shift2 = carry[1:4]
        dn2 = [dot(base, d2_ref[or2], 1, 1) for or2 in range(2)]
        loads[g][1].wait()
        loads[g][2].wait()
        d = jnp.concatenate(
            [dn2[or2][q // 2 * 72:(q // 2 + 1) * 72, q % 2 * 256:(q % 2 + 1) * 256] for q in range(4) for or2 in range(2)], axis=0)
        xhat, rs = stats(s2_ref[g].reshape(4 * 144, 256), C2, mask2)
        a_gain2 = a_gain2 + fold8(d * xhat)
        a_shift2 = a_shift2 + fold8(d)
        mids = norm_back(d, xhat, rs, gain_two, C2, mask2).astype(BF)
        a_bias2 = a_bias2 + fold8(mids.astype(F32))
        mid_ref[g] = mids
        for q in range(4):
            lanes = slice(q * 256, (q + 1) * 256)
            for or1 in range(2):
                dd1_ref[or1] += dot(n1_ref[g, or1 * 144:(or1 + 1) * 144, lanes], mids[q * 144:(q + 1) * 144], 0, 0)
        return a3, a_bias2, a_gain2, a_shift2

    def lower(g, carry, hooks):
        loads[g][0].wait()
        for q in range(4):
            for or1 in range(2):
                part = slice(or1 * 144, (or1 + 1) * 144)
                o = dot(mid_ref[g, q * 144:(q + 1) * 144, :], d1_ref[or1], 1, 1)
                dn1_ref[2 * q, part, :] = o[:, :128]
                dn1_ref[2 * q + 1, part, :] = o[:, 128:]
        for q in range(4):
            o = dot(xp_ref[g], wbig_ref[:, q * 256:(q + 1) * 256])
            st_ref[2 * q] = o[:, :128]
            st_ref[2 * q + 1] = o[:, 128:]

        for hook in hooks:
            hook()
        b0, g0, s0, g1, s1 = carry
        v = st_ref[...].reshape(8 * 288, 128) + bias_stem
        xa, ra = stats(v, C1, mask1)
        y = xa * gain_stem + shift_stem
        xb, rb = stats(y, C1, mask1)
        d = dn1_ref[...].reshape(8 * 288, 128)
        g1 = g1 + fold8(d * xb)
        s1 = s1 + fold8(d)
        dy = norm_back(d, xb, rb, gain_one, C1, mask1)
        g0 = g0 + fold8(dy * xa)
        s0 = s0 + fold8(dy)
        dv = norm_back(dy, xa, ra, gain_stem, C1, mask1).astype(BF)
        b0 = b0 + fold8(dv.astype(F32))
        for j in range(8):
            dlow_ref[:, j * 128:(j + 1) * 128] = dv[j * 288:(j + 1) * 288]
        sums = (b0, g0, s0, g1, s1)
        aw_ref[...] += dot(xp_ref[g], dlow_ref[...], 0, 0)
        return sums

    sums = (z3, z2, z2, z2)
    between = [[], [lambda: layer1(1), flat[0]], [high1], [flat[1]], [], [lambda: layer2(0)]]
    for g in range(6):
        sums = upper(g, sums)
        for hook in between[g]:
            hook()
    lane = lax.broadcasted_iota(jnp.int32, (48, 128), 1)
    for or1 in range(2):
        for oc1 in range(2):
            left, right = st_ref.at[1], st_ref.at[2]
            left[0:96, :] = dd1_ref[or1, oc1 * 128:oc1 * 128 + 96, 0:128]
            right[0:96, :] = dd1_ref[or1, oc1 * 128:oc1 * 128 + 96, 128:256]
            e0, o0 = left[pl.ds(0, 48, stride=2), :], left[pl.ds(1, 48, stride=2), :]
            e1, o1 = right[pl.ds(0, 48, stride=2), :], right[pl.ds(1, 48, stride=2), :]
            at = (or1 * 192 + oc1 * 96) * 3 // 2
            line1_ref[pl.ds(at, 48, stride=3), :] = e0
            line1_ref[pl.ds(at + 1, 48, stride=3), :] = jnp.where(lane < 64, e1, pltpu.roll(o0, 64, 1))
            line1_ref[pl.ds(at + 2, 48, stride=3), :] = jnp.where(lane < 64, pltpu.roll(o0, 64, 1), pltpu.roll(o1, 64, 1))
    size = grad1_ref.shape[4]
    line1_ref[ONE_LINES:, :] = jnp.zeros((8 * planes * size - ONE_LINES, 128), F32)
    for mm in range(2):
        for yy in range(2):
            for cc in range(2):
                for k in range(planes):
                    at = (((mm * 2 + yy) * 2 + cc) * planes + k) * size
                    grad1_ref[mm, yy, cc, k] = line1_ref[at:at + size, :].astype(BF)
    first = flat_sum_steps(net, grad1_ref, shard1_ref, *scratch[17:23])
    first += spread_steps(net, shard1_ref, one_ref, *scratch[23:])
    first[0]()
    inner = [[], [lambda: layer2(1), flat[2]], [flat[3], flat[4], first[3], first[4]], [flat[5], first[5], low0], [], [low1]]
    outer = [[first[1]], [first[2]], [], [], [flat[6], first[6]], [flat[7], first[7]]]
    low_sums = (z1, z1, z1, z1, z1)
    for g in range(6):
        low_sums = lower(g, low_sums, inner[g])
        for hook in outer[g]:
            hook()
    done = sums + low_sums
    total = aw_ref[0:48, 0:128]
    for j in range(1, 8):
        total = total + aw_ref[j * 48:(j + 1) * 48, j * 128:(j + 1) * 128]
    dv3_ref[...] = jnp.sum(done[0], axis=0, keepdims=True)
    for n in range(3):
        dv2_ref[n:n + 1, :] = jnp.sum(done[1 + n], axis=0, keepdims=True)
    for n in range(5):
        dvs_ref[n:n + 1, :] = jnp.sum(done[4 + n], axis=0, keepdims=True)
    base = st_ref.at[0]
    base[0:48, :] = total
    lane = lax.broadcasted_iota(jnp.int32, (12, 128), 1)
    a0, a1, a2, a3 = [base[pl.ds(n, 12, stride=4), :] for n in range(4)]
    tail_ref[pl.ds(0, 12, stride=3), :] = jnp.where(lane < 96, a0, pltpu.roll(a1, 96, 1))
    tail_ref[pl.ds(1, 12, stride=3), :] = jnp.where(lane < 64, pltpu.roll(a1, 96, 1), pltpu.roll(a2, 64, 1))
    tail_ref[pl.ds(2, 12, stride=3), :] = jnp.where(lane < 32, pltpu.roll(a2, 64, 1), pltpu.roll(a3, 32, 1))


def back(planes, dr, kept, weights, dkern, own, other, held):
    shard = ceil_to(TWO_LINES + KERN_LINES, 8 * planes * 16) // (8 * planes)
    rows, width = own.shape[3:]
    shard1 = ceil_to(ONE_LINES, 8 * planes * 16) // (8 * planes)
    shape1 = (2, 2, 2, planes, shard1, 128)
    shape = (2, 2, 2, planes, shard, 128)
    return call(
        functools.partial(back_kernel, planes),
        listed(VM, dr) + listed(AN, *kept) + listed(VM, *weights, *dkern) + listed(AN, own, other) + listed(VM, held),
        listed(VM, sds((STEM_LINES, 128)), sds((5, 128)), sds((3, 256)), sds((1, C3)), sds(shape, BF),
               sds((rows, width), BF), sds((rows, width), BF), sds(shape1, BF)),
        [pltpu.VMEM((6, 576, 256), BF), pltpu.VMEM((8 * planes * shard1, 128), F32), pltpu.VMEM(shape1, BF),
         pltpu.VMEM((shard1, 128), BF)]
        + [pltpu.VMEM(k.shape, k.dtype) for k in kept] + [pltpu.SemaphoreType.DMA((19,))]
        + [pltpu.VMEM((planes, rows, width), BF), pltpu.VMEM((shard, 128), BF),
           pltpu.VMEM((8, 288, 128), F32), pltpu.VMEM((8, 288, 128), F32), pltpu.VMEM((288, 1024), BF),
           pltpu.VMEM((ROWS, C3), BF), pltpu.VMEM((384, 1024), F32), pltpu.VMEM((2, 256, 256), F32),
           pltpu.VMEM((8 * planes * shard, 128), F32), pltpu.VMEM(shape, BF)]
        + layer_scratch(planes, rows, width) + column_scratch(planes, rows, width) + column_scratch(planes, rows, width)
        + flat_scratch(planes, shard, BF) + spread_scratch(planes) + flat_scratch(planes, shard1, BF) + spread_scratch(planes),
        8_000_000_000, 3,
    )


VECTOR_WIDTHS = (C1, C1, C2, LAYERS * C3, LAYERS * C3, C3, C1, C1, C1, C2, C2, C3, LAYERS * C3, LAYERS * C3, LAYERS * HID,
                 LAYERS * C3, C3, CLASSES)
VECTOR_NAMES = ("gain_stem", "gain_one", "gain_two", "gain_block", "layer_scale", "gain_final", "bias_stem", "shift_stem",
                "shift_one", "bias_one", "shift_two", "bias_two", "bias_depth", "shift_block", "bias_inner", "bias_outer",
                "shift_final", "bias_head")
VECTOR = sum(VECTOR_WIDTHS)
VECTOR_LINES = ceil_to(VECTOR, 1024) // 128


def vector_plan():
    plan, offset, row = {}, 0, 0
    for name, width in zip(VECTOR_NAMES, VECTOR_WIDTHS):
        plan[name] = (offset, width, row)
        offset, row = offset + width, row + ceil_to(width, 128) // 128
    return plan, row


VECTOR_PLAN, PADDED_LINES = vector_plan()
TAIL_LINES = STEM_LINES + PADDED_LINES + 1


def open_kernel(planes, flat_ref, vector_ref, master_ref, mask_ref, pix_ref, perm_ref,
                xp_out, n1_out, s2_out, n2_out, far_out, low0_out, quarter1_out,
                res_ref, wbig_ref, d1_ref, d2_ref, head_ref, vs_ref, v2_ref, v3_ref, hv_ref, hb_ref, *refs):
    kern_ref, vec_ref, bin_ref, keep_ref = [refs[LAYERS * n:LAYERS * (n + 1)] for n in range(4)]
    low_ref = (None,) + refs[4 * LAYERS:4 * LAYERS + 2]
    (wide_ref, pad_ref, master, master_sem, low0_ref, x_ref, xp_ref, n1_ref, s2_ref, n2_ref, st_ref, n2s_ref, pix_sem,
     out_sem, w_sem, quarter_ref) = refs[4 * LAYERS + 2:]
    net = Net(planes)
    m = net.m
    peers = [net.core] + net.plane[:2] + net.four
    for peer in peers:
        net.signal(peer)
    loads = [pltpu.make_async_copy(master_ref.at[l], master.at[l], master_sem.at[l]) for l in range(LAYERS)]
    loads[0].start()
    near = pl.ds(pl.multiple_of(m * PAIR, 16), PAIR)
    far = pl.ds(pl.multiple_of((1 - m) * PAIR, 16), PAIR)
    kept = pltpu.make_async_copy(pix_ref.at[near, :], x_ref.at[near, :], out_sem.at[24])
    kept.start()
    pl.semaphore_wait(pltpu.get_barrier_semaphore(), len(peers))
    moves = []
    for g in range(6):
        lanes = pl.ds(g * 384, 384)
        moves.append(remote(pix_ref.at[far, lanes], x_ref.at[near, lanes], pix_sem, g, net.plane[0]))
    moves[0].start()
    loads[0].wait()
    begin(loads[1:])
    low0_ref[...] = master[0].astype(BF)
    send0 = weight_send(net, low0_ref, quarter_ref, w_sem, 3)
    send1 = weight_send(net, low_ref[1], quarter1_out, w_sem, 3 + PARTS)
    send0[0]()
    moves[1].start()
    spread0, spread1, spread2 = weight_spread(net, quarter_ref, far_out, w_sem, out_sem.at[26])
    keep_low = pltpu.make_async_copy(low0_ref, low0_out, out_sem.at[25])
    keep_low.start()
    for name in VECTOR_NAMES:
        offset, width, row = VECTOR_PLAN[name]
        lines = ceil_to(width, 128) // 128
        at, s = offset // 128, offset % 128
        lane = lax.broadcasted_iota(jnp.int32, (lines, 128), 1)
        value = vector_ref[at:at + lines, :]
        if s:
            value = jnp.where(lane < 128 - s, pltpu.roll(value, 128 - s, 1),
                              pltpu.roll(vector_ref[at + 1:at + 1 + lines, :], 128 - s, 1))
        if width % 128:
            spot = lax.broadcasted_iota(jnp.int32, (lines, 128), 0) * 128 + lane
            value = jnp.where(spot < width, value, 0.0)
        pad_ref[row:row + lines, :] = value

    def place(ref, at, name, start, lines):
        row = VECTOR_PLAN[name][2] + start
        for n in range(lines):
            ref[at + (slice(n * 128, (n + 1) * 128),)] = pad_ref[row + n:row + n + 1, :]
    one = lambda n: (slice(n, n + 1),)
    for n, name in enumerate(("bias_stem", "gain_stem", "shift_stem", "gain_one", "shift_one")):
        place(vs_ref, one(n), name, 0, 1)
    for n, name in enumerate(("bias_one", "gain_two", "shift_two")):
        place(v2_ref, one(n), name, 0, 2)
    place(v3_ref, one(0), "bias_two", 0, 3)
    for l in range(LAYERS):
        for n, name in enumerate(("bias_depth", "gain_block", "shift_block", "bias_outer", "layer_scale")):
            place(vec_ref[l], one(n), name, 3 * l, 3)
        for n in range(12):
            part = (n // 6 + m) % 2
            row = VECTOR_PLAN["bias_inner"][2] + 12 * l + part * 6 + n % 6
            bin_ref[l][:, n * 128:(n + 1) * 128] = pad_ref[pl.ds(row, 1), :]
    place(hv_ref, one(0), "gain_final", 0, 3)
    place(hv_ref, one(1), "shift_final", 0, 3)
    place(hb_ref, one(0), "bias_head", 0, 8)
    lane = lax.broadcasted_iota(jnp.int32, (12, 128), 1)
    f0, f1, f2 = [flat_ref[pl.ds(n, 12, stride=3), :] for n in range(3)]
    parts = (f0, jnp.where(lane < 32, pltpu.roll(f0, 32, 1), pltpu.roll(f1, 32, 1)),
             jnp.where(lane < 64, pltpu.roll(f1, 64, 1), pltpu.roll(f2, 64, 1)), pltpu.roll(f2, 96, 1))
    for n in range(4):
        wide_ref[0, pl.ds(n, 12, stride=4), :] = jnp.where(lane < C1, parts[n], 0.0)
    stem = wide_ref[0, 0:48, :].astype(BF)
    wbig_ref[...] = jnp.zeros_like(wbig_ref)
    for j in range(8):
        wbig_ref[j * 48:(j + 1) * 48, j * 128:(j + 1) * 128] = stem
    lane = lax.broadcasted_iota(jnp.int32, (192, 128), 1)
    f0, f1, f2 = [flat_ref[pl.ds(STEM_LINES + n, 192, stride=3), :] for n in range(3)]
    f1 = pltpu.roll(f1, 64, 1)
    f2 = pltpu.roll(f2, 64, 1)
    wide_ref[0, pl.ds(0, 192, stride=2), :] = f0
    wide_ref[1, pl.ds(0, 192, stride=2), :] = jnp.where(lane < 64, pltpu.roll(f1, 64, 1), 0.0)
    wide_ref[0, pl.ds(1, 192, stride=2), :] = jnp.where(lane < 64, f1, f2)
    wide_ref[1, pl.ds(1, 192, stride=2), :] = jnp.where(lane < 64, f2, 0.0)
    d1_ref[...] = jnp.zeros_like(d1_ref)
    d2_ref[...] = jnp.zeros_like(d2_ref)
    for or1 in range(2):
        for oc1 in range(2):
            at = or1 * 192 + oc1 * 96
            for t in range(2):
                d1_ref[or1, oc1 * 128:oc1 * 128 + 96, t * 128:(t + 1) * 128] = wide_ref[t, at:at + 96, :].astype(BF)
    base = STEM_LINES + ONE_LINES
    for lt in range(3):
        for or2 in range(2):
            for oc2 in range(2):
                at = base + (or2 * 384 + oc2 * 192) * 3 + lt
                d2_ref[or2, oc2 * 256:oc2 * 256 + 192, lt * 128:(lt + 1) * 128] = flat_ref[pl.ds(at, 192, stride=3), :].astype(BF)
    mask1 = (lax.broadcasted_iota(jnp.int32, (1, 128), 1) < C1).astype(F32)
    mask2 = (lax.broadcasted_iota(jnp.int32, (1, 256), 1) < C2).astype(F32)
    bias_stem, gain_stem, shift_stem = vs_ref[0:1, :], vs_ref[1:2, :], vs_ref[2:3, :]
    gain_one, shift_one = vs_ref[3:4, :], vs_ref[4:5, :]
    bias_one, gain_two, shift_two = v2_ref[0:1, :], v2_ref[1:2, :], v2_ref[2:3, :]
    kern_base = STEM_LINES + ONE_LINES + TWO_LINES

    def more_low():
        for l in range(1, LAYERS):
            loads[l].wait()
            low_ref[l][...] = master[l].astype(BF)

    def more_small():
        spot = lax.broadcasted_iota(jnp.int32, (COL, 128), 0) % IMG
        for l in range(LAYERS):
            value = jnp.zeros((COL, 128), jnp.int32)
            for n in range(IMG):
                value = jnp.where(spot == n, mask_ref[l, m * IMG + n], value)
            value = value.astype(F32)
            for lt in range(3):
                keep_ref[l][:, lt * 128:(lt + 1) * 128] = value
        for l in range(LAYERS):
            kern_ref[l][...] = flat_ref[kern_base + l * 3 * TAPS:kern_base + (l + 1) * 3 * TAPS, :]

    def more_head():
        base = kern_base + KERN_LINES
        count = C3 // 16
        lane = lax.broadcasted_iota(jnp.int32, (count, 128), 1)
        for k in range(16):
            for t in range(8):
                start = k * CLASSES + t * 128
                f, s = start // 128, start % 128
                need = min(128, CLASSES - t * 128)
                value = flat_ref[pl.ds(base + f, count, stride=CLASSES // 8), :]
                if s:
                    value = pltpu.roll(value, 128 - s, 1)
                    if need > 128 - s:
                        after = flat_ref[pl.ds(base + f + 1, count, stride=CLASSES // 8), :]
                        value = jnp.where(lane < 128 - s, value, pltpu.roll(after, 128 - s, 1))
                if need < 128:
                    value = jnp.where(lane < need, value, 0.0)
                wide_ref[t, pl.ds(k, count, stride=16), :] = value
        for t in range(8):
            head_ref[:, t * 128:(t + 1) * 128] = wide_ref[t].astype(BF)

    def spread0_first():
        send0[2]()
        spread0()

    def spread_last():
        send1[2]()
        spread2()
    send0[1]()
    ahead = [moves[2:4], [], moves[4:6], [], [], []]
    extras = [[more_low], [more_head, spread0_first, send1[0]], [], [more_small, spread1, send1[1]], [], [spread_last]]
    kept.wait()
    writes = []
    for g in range(6):
        moves[g].wait()
        begin(ahead[g])
        x2 = dot(perm_ref[...], x_ref[:, g * 384:(g + 1) * 384]).astype(BF)
        xp_ref[g] = x2
        for q in range(4):
            o = dot(x2, wbig_ref[:, q * 256:(q + 1) * 256])
            st_ref[2 * q] = o[:, :128]
            st_ref[2 * q + 1] = o[:, 128:]
        v = st_ref[...].reshape(8 * 288, 128) + bias_stem
        xhat, _s = stats(v, C1, mask1)
        y = xhat * gain_stem + shift_stem
        xhat, _s = stats(y, C1, mask1)
        low = (xhat * gain_one + shift_one).astype(BF).reshape(8, 288, 128)
        for j in range(8):
            n1_ref[g, :, j * 128:(j + 1) * 128] = low[j]
        for q in range(4):
            lanes = slice(q * 256, (q + 1) * 256)
            s2_ref[g, q] = dot(n1_ref[g, 0:144, lanes], d1_ref[0]) + dot(n1_ref[g, 144:288, lanes], d1_ref[1]) + bias_one
        for ref, out, at in ((xp_ref, xp_out, 0), (n1_ref, n1_out, 6), (s2_ref, s2_out, 12)):
            writes.append(pltpu.make_async_copy(ref.at[g], out.at[g], out_sem.at[at + g]))
            writes[-1].start()
        xhat, _s = stats(s2_ref[g].reshape(4 * 144, 256), C2, mask2)
        n2 = xhat * gain_two + shift_two
        for q in range(4):
            c2, oc2 = q // 2, q % 2
            for or2 in range(2):
                at = q * 144 + or2 * 72
                n2s_ref[or2, c2 * 72:(c2 + 1) * 72, oc2 * 256:(oc2 + 1) * 256] = n2[at:at + 72]
        rows = slice(g * 144, (g + 1) * 144)
        low0, low1 = n2s_ref[0].astype(BF), n2s_ref[1].astype(BF)
        n2_ref[0, rows, :] = low0
        n2_ref[1, rows, :] = low1
        writes.append(pltpu.make_async_copy(n2_ref.at[:, pl.ds(g * 144, 144), :], n2_out.at[:, pl.ds(g * 144, 144), :],
                                            out_sem.at[18 + g]))
        writes[-1].start()
        res_ref[rows, :] = dot(low0, d2_ref[0]) + dot(low1, d2_ref[1]) + v3_ref[0:1, :]
        for extra in extras[g]:
            extra()
    end(writes)
    keep_low.wait()


def opening(planes, flat, vector, master, keep_mask, pix, perm):
    kept = [(6, 288, 384), (6, 288, 1024), (6, 4, 144, 256), (2, ROWS, 512)]
    types = [BF, BF, F32, BF]
    half = sds((2, C3, HID // 2), BF)
    each = lambda shape: [sds(shape)] * LAYERS
    outs = ([sds((ROWS, C3)), sds((384, 1024), BF), sds((2, 256, 256), BF), sds((2, 512, C3), BF), sds((C3, WIDE), BF),
             sds((8, 128)), sds((8, 256)), sds((8, C3)), sds((2, C3)), sds((1, WIDE))]
            + each((3 * TAPS, 128)) + each((8, C3)) + each((1, HID)) + each((COL, C3)) + [half, half])
    return call(
        functools.partial(open_kernel, planes),
        listed(VM, flat, vector) + listed(AN, master) + listed(SM, keep_mask) + listed(AN, pix) + listed(VM, perm),
        listed(AN, *[sds(a, b) for a, b in zip(kept, types)], half, half, sds((C3 // 2, HID // 2), BF)) + listed(VM, *outs),
        [pltpu.VMEM((8, C3, 128), F32), pltpu.VMEM((ceil_to(PADDED_LINES, 8), 128), F32),
         pltpu.VMEM((LAYERS, 2, C3, HID // 2), F32), pltpu.SemaphoreType.DMA((LAYERS,)), pltpu.VMEM((2, C3, HID // 2), BF),
         pltpu.VMEM((4 * COL, 4 * SIDE * PATCH), BF)]
        + [pltpu.VMEM(a, b) for a, b in zip(kept, types)]
        + [pltpu.VMEM((8, 288, 128), F32), pltpu.VMEM((2, 144, 512), F32), pltpu.SemaphoreType.DMA((2, 6)),
           pltpu.SemaphoreType.DMA((27,)), pltpu.SemaphoreType.DMA((2, 3 + 2 * PARTS)), pltpu.VMEM((C3 // 2, HID // 2), BF)],
        4_000_000_000, 6,
    )


def finish_kernel(planes, p0_ref, p1_ref, p2_ref, tail_ref, dvs_ref, dv2_ref, dv3_ref, dvec0_ref, dvec1_ref, dvec2_ref,
                  dbin0_ref, dbin1_ref, dbin2_ref, dfinal_ref, dbias_ref, loss_ref, head_ref, two_ref, one_ref,
                  own_ref, flat_ref, vector_ref, info_ref,
                  grad_ref, full_ref, line_ref, arrived_ref, move_sem, local_sem, *scratch):
    net = Net(planes)
    m, d = net.m, net.d
    dp = 4 * planes
    pieces_ref, dvec_ref, dbin_ref = (p0_ref, p1_ref, p2_ref), (dvec0_ref, dvec1_ref, dvec2_ref), (dbin0_ref, dbin1_ref, dbin2_ref)
    shard = grad_ref.shape[4]
    targets = [((l * dp + d) // 3, (l * dp + d) % 3) for l in range(LAYERS)]
    sources = [(3 * d + s) % dp for s in range(LAYERS)]
    for s in range(LAYERS):
        @pl.when(sources[s] != d)
        def _(s=s):
            net.signal((sources[s], m))
    peers = [peer for _, peer in net.all_plane] + net.column
    for peer in peers:
        net.signal(peer)
    awaited = len(peers)
    for l in range(LAYERS):
        awaited = awaited + jnp.where(targets[l][0] != d, 1, 0)
    pl.semaphore_wait(pltpu.get_barrier_semaphore(), awaited)

    def move(l):
        owner, slot = targets[l]
        return pltpu.make_async_remote_copy(
            src_ref=pieces_ref[l], dst_ref=arrived_ref.at[slot], send_sem=move_sem.at[0, l],
            recv_sem=move_sem.at[1, slot], device_id=(owner, m), device_id_type=pl.DeviceIdType.MESH)

    def keep(l):
        return pltpu.make_async_copy(pieces_ref[l], arrived_ref.at[targets[l][1]], local_sem.at[l])

    for l in range(LAYERS):
        @pl.when(targets[l][0] != d)
        def _(l=l):
            move(l).start()

        @pl.when(targets[l][0] == d)
        def _(l=l):
            keep(l).start()
    squares = jnp.zeros((8, 128), F32)
    for l in range(LAYERS):
        piece = pieces_ref[l][...].astype(F32)
        line = jnp.sum(piece * piece, axis=0, keepdims=True)
        for n in range(6):
            squares = squares + jnp.concatenate([line[:, n * 128:(n + 1) * 128], jnp.zeros((7, 128), F32)], axis=0)
    square = jnp.sum(squares, axis=(0, 1), keepdims=True)
    lead = STEM_LINES
    line_ref[0:lead, :] = tail_ref[...]
    line_ref[lead:, :] = jnp.zeros((8 * planes * shard - lead, 128), F32)

    def place(name, start, value):
        row = lead + VECTOR_PLAN[name][2] + start
        for n in range(value.shape[1] // 128):
            line_ref[row + n:row + n + 1, :] = value[:, n * 128:(n + 1) * 128]
    for n, name in enumerate(("bias_stem", "gain_stem", "shift_stem", "gain_one", "shift_one")):
        place(name, 0, dvs_ref[n:n + 1, :])
    for n, name in enumerate(("bias_one", "gain_two", "shift_two")):
        place(name, 0, dv2_ref[n:n + 1, :])
    place("bias_two", 0, dv3_ref[...])
    for l in range(LAYERS):
        for n, name in enumerate(("bias_depth", "gain_block", "shift_block", "bias_outer", "layer_scale")):
            place(name, 3 * l, dvec_ref[l][n:n + 1, :])
        sums = jnp.sum(dbin_ref[l][...], axis=0, keepdims=True)
        for n in range(12):
            part = (n // 6 + m) % 2
            row = lead + VECTOR_PLAN["bias_inner"][2] + 12 * l + part * 6 + n % 6
            line_ref[pl.ds(row, 1), :] = sums[:, n * 128:(n + 1) * 128]
    place("gain_final", 0, dfinal_ref[0:1, :])
    place("shift_final", 0, dfinal_ref[1:2, :])
    place("bias_head", 0, dbias_ref[...])
    lane = lax.broadcasted_iota(jnp.int32, (1, 128), 1)
    info = jnp.where(lane == 2, square, loss_ref[...])
    line_ref[lead + PADDED_LINES:lead + PADDED_LINES + 1, :] = info

    def each_shard(move_one):
        for mm in range(2):
            for yy in range(2):
                for cc in range(2):
                    for k in range(planes):
                        move_one((mm, yy, cc, k), ((((mm * 2 + yy) * 2 + cc) * planes) + k))

    def pack(where, n):
        grad_ref[where] = line_ref[n * shard:(n + 1) * shard, :]
    each_shard(pack)
    steps = tail_steps(net, grad_ref, full_ref, *scratch)
    steps[0]()

    def unpack_big(ref, base, lines):
        size = ref.shape[4]
        sums = [jnp.zeros((8, 128), F32)]

        def inner(where, n):
            at = n * size
            if at < lines:
                rows = min(size, lines - at)
                value = ref[where].astype(F32)
                flat_ref[base + at:base + at + rows, :] = value[0:rows]
                sums[0] = sums[0] + fold8(value * value)
        each_shard(inner)
        return jnp.sum(sums[0], axis=0, keepdims=True)
    total = unpack_big(two_ref, STEM_LINES + ONE_LINES, TWO_LINES + KERN_LINES)
    steps[1]()
    total = total + unpack_big(head_ref, STEM_LINES + ONE_LINES + TWO_LINES + KERN_LINES, HEAD_LINES)
    steps[2]()
    total = total + unpack_big(one_ref, STEM_LINES, ONE_LINES)
    for step in steps[3:]:
        step()

    def unpack(where, n):
        line_ref[n * shard:(n + 1) * shard, :] = full_ref[where]
    each_shard(unpack)
    value = line_ref[0:lead, :]
    flat_ref[0:lead, :] = value
    total = total + jnp.sum(value * value, axis=0, keepdims=True)
    value = line_ref[lead:lead + PADDED_LINES, :]
    total = total + jnp.sum(value * value, axis=0, keepdims=True)
    info = line_ref[lead + PADDED_LINES:lead + PADDED_LINES + 1, :]
    pick = lambda n: jnp.sum(jnp.where(lane == n, info, 0.0), axis=1, keepdims=True)
    count = jnp.maximum(pick(1), 1.0)
    norm = jnp.sqrt(jnp.sum(total, axis=1, keepdims=True) + pick(2)) / count
    factor = CLIP_LIMIT / jnp.maximum(norm, CLIP_LIMIT) / count
    info_ref[...] = jnp.where(lane == 0, pick(0), jnp.where(lane == 1, count, jnp.where(lane == 2, norm, factor)))
    vector_ref[...] = jnp.zeros_like(vector_ref)
    for name in VECTOR_NAMES:
        offset, width, row = VECTOR_PLAN[name]
        lines = ceil_to(width, 128) // 128
        at, s = offset // 128, offset % 128
        lane8 = lax.broadcasted_iota(jnp.int32, (lines, 128), 1)
        value = line_ref[lead + row:lead + row + lines, :]
        if s:
            value = pltpu.roll(value, s, 1)
            vector_ref[at:at + lines, :] += jnp.where(lane8 < s, 0.0, value)
            vector_ref[at + 1:at + 1 + lines, :] += jnp.where(lane8 < s, value, 0.0)
        else:
            vector_ref[at:at + lines, :] += value
    for l in range(LAYERS):
        @pl.when(targets[l][0] != d)
        def _(l=l):
            move(l).wait_send()

        @pl.when(targets[l][0] == d)
        def _(l=l):
            keep(l).wait()
    for s in range(LAYERS):
        @pl.when(sources[s] != d)
        def _(s=s):
            pltpu.make_async_remote_copy(
                src_ref=pieces_ref[s], dst_ref=arrived_ref.at[s], send_sem=move_sem.at[0, s],
                recv_sem=move_sem.at[1, s], device_id=(sources[s], m), device_id_type=pl.DeviceIdType.MESH).wait_recv()
    own_ref[...] = arrived_ref[...]


def finish(planes, pieces, tail, dvs, dv2, dv3, dvec, dbin, dfinal, dbias, loss, head_sum, two_sum, one_sum):
    shard = ceil_to(TAIL_LINES, 8 * planes * 8) // (8 * planes)
    shape = (2, 2, 2, planes, shard, 128)
    held = (LAYERS,) + pieces[0].shape
    return call(
        functools.partial(finish_kernel, planes),
        listed(VM, *pieces, tail, dvs, dv2, dv3, *dvec, *dbin, dfinal, dbias, loss, head_sum, two_sum, one_sum),
        listed(VM, sds(held, BF), sds((FLAT_LINES, 128)), sds((VECTOR_LINES, 128)), sds((1, 128))),
        [pltpu.VMEM(shape, F32), pltpu.VMEM(shape, F32),
         pltpu.VMEM((8 * planes * shard, 128), F32),
         pltpu.VMEM(held, BF), pltpu.SemaphoreType.DMA((2, LAYERS)), pltpu.SemaphoreType.DMA((LAYERS,))]
        + tail_scratch(planes, shard, F32),
        0, 4,
    )


LEARN_RATE = 0.05
VECTOR_RATE = 0.15
WEIGHT_DECAY = 0.05
BETA_ONE = 0.9
BETA_TWO = 0.999
ADAM_EPSILON = 1e-08


def vector_lengths():
    return list(VECTOR_WIDTHS)


def flat_lengths():
    return [PATCH * C1, 4 * C1 * C2, 4 * C2 * C3, LAYERS * TAPS * C3, C3 * CLASSES]


def adam_update(weight, moment_one, moment_two, gradient, step_float, rate):
    first_new = BETA_ONE * moment_one + (1.0 - BETA_ONE) * gradient
    second_new = BETA_TWO * moment_two + (1.0 - BETA_TWO) * gradient * gradient
    first_hat = first_new / (1.0 - BETA_ONE**step_float)
    second_hat = second_new / (1.0 - BETA_TWO**step_float)
    weight_new = weight - rate * (first_hat / (jnp.sqrt(second_hat) + ADAM_EPSILON) + WEIGHT_DECAY * weight)
    return (weight_new, first_new, second_new, weight_new.astype(BF))


def row_source():
    target = np.arange(4 * COL)
    img = target % IMG
    r = target // IMG % SIDE
    or2 = target // COL % 2
    or1 = target // (2 * COL)
    row = 4 * r + 2 * or2 + or1
    return (row // (2 * SIDE)) * (2 * COL) + img * (2 * SIDE) + row % (2 * SIDE)


def per_device(pixels, labels, valid_flags, keep_mask, step_count, pointwise_weight, pointwise_first, pointwise_second,
               flat_weight, flat_first, flat_second, vector_weight, vector_first, vector_second):
    dp = lax.axis_size("dp")
    planes = dp // 4
    vectors = jnp.pad(vector_weight, (0, VECTOR_LINES * 128 - VECTOR)).reshape(VECTOR_LINES, 128)
    perm = jnp.asarray(row_source()[:, None] == np.arange(4 * COL)[None], BF)
    pix = pixels.reshape(4 * COL, 4 * SIDE * PATCH)
    ready = opening(planes, flat_weight.reshape(FLAT_LINES, 128), vectors, pointwise_weight, keep_mask, pix, perm)
    xp, n1, s2, n2, far, low0, quarter, res, wbig, d1, d2, head_low, vs, v2, v3, hv, hb = ready[:17]
    kern, vec, bins, keep = [ready[17 + LAYERS * n:17 + LAYERS * (n + 1)] for n in range(4)]
    low = [low0] + list(ready[17 + 4 * LAYERS:])
    kept = []
    for l in range(LAYERS):
        more = (quarter, low[2]) if l == 0 else (quarter,) if l == 1 else ()
        new, depth, normed, act, dg, out, *arrived = block(planes, res, kern[l], vec[l], bins[l], keep[l], low[l], far, *more)
        kept.append((keep[l], vec[l], kern[l], act, dg, out, normed, depth, res, low[l], far))
        res = new
        if l == 0:
            far, quarter = arrived
        elif l == 1:
            far, = arrived
    shard = ceil_to(HEAD_LINES, 8 * planes * 16) // (8 * planes)
    dr, dhead, dbias, dfinal, loss = head(res, hv, head_low, hb, labels, valid_flags, 8 * planes * shard)
    blocked = lambda a: a.reshape(planes, 2, 2, 2 * C3 // dp, HID // 2)
    dkern, dvec, dbin = [None] * LAYERS, [None] * LAYERS, [None] * LAYERS
    dr, own, other, dkern[2], dvec[2], dbin[2], head_shard = block_back(
        planes, 0, (dr,) + kept[2], dhead.reshape(2, 2, 2, planes, shard, 128))
    dr, own_new, other_new, dkern[1], dvec[1], dbin[1], held, head_sum = block_back(
        planes, 1, (dr,) + kept[1], blocked(own), blocked(other), head_shard)
    dr, own, other, dkern[0], dvec[0], dbin[0], held, piece2 = block_back(
        planes, 2, (dr,) + kept[0], blocked(own_new), blocked(other_new), held)
    tail, dvs, dv2, dv3, two_sum, piece0, piece1, one_sum = back(
        planes, dr, (xp, n1, s2, n2), (wbig, d1, d2, vs, v2), dkern, blocked(own), blocked(other), held)
    pointwise_own, flat_sum, vector_sum, info = finish(
        planes, (piece0, piece1, piece2), tail, dvs, dv2, dv3, dvec, dbin, dfinal, dbias, loss, head_sum, two_sum,
        one_sum)
    loss_total, valid_total, gradient_norm, factor = info[0, 0], info[0, 1], info[0, 2], info[0, 3]
    pointwise_own = pointwise_own.reshape(pointwise_first.shape).astype(F32)
    flat_sum = flat_sum.reshape(-1)
    vector_sum = vector_sum.reshape(-1)[:VECTOR]
    step_float = step_count.astype(F32)
    rows_owned = pointwise_first.shape[0]
    master_rows = pointwise_weight.reshape(2 * LAYERS * C3, HID // 2)
    master_own = lax.dynamic_slice_in_dim(master_rows, lax.axis_index("dp") * rows_owned, rows_owned, 0)
    pointwise_out = adam_update(master_own, pointwise_first, pointwise_second, factor * pointwise_own, step_float, LEARN_RATE)
    flat_out = adam_update(flat_weight, flat_first, flat_second, factor * flat_sum, step_float, LEARN_RATE)
    vector_out = adam_update(vector_weight, vector_first, vector_second, factor * vector_sum, step_float, VECTOR_RATE)
    return (loss_total, valid_total, gradient_norm, *pointwise_out, *flat_out, *vector_out)


def solution(mesh):
    placed = (P("dp", "mp", None), P("dp"), P("dp"), P(None, "dp"), P(), P(None, None, None, "mp"), P("dp", "mp"),
              P("dp", "mp"), P(), P(), P(), P(), P(), P())
    return jax.shard_map(
        per_device,
        mesh=mesh,
        in_specs=placed,
        out_specs=(P(), P(), P()) + (P("dp", "mp"),) * 4 + (P(),) * 8,
        check_vma=False,
    )
```

```python
import functools
import jax
import numpy as np
from jax.sharding import PartitionSpec as P
import jax.numpy as jnp
from jax import lax
from jax.experimental import pallas as pl
from jax.experimental.pallas import tpu as pltpu

C1 = 96
C2 = 192
C3 = 384
HID = 1536
CLASSES = 1000
PATCH = 48
KERNEL = 7
LAYERS = 3
SIDE = 12
NORM_EPSILON = 1e-06
SMOOTH = 0.1
CLIP_LIMIT = 0.02
IMG = 6
COL = SIDE * IMG
ROWS = SIDE * COL
PAIR = 2 * COL
FORE = 432
REAR = 288
WF = 256
WB = 256
BF = jnp.bfloat16
F32 = jnp.float32
VMEM_LIMIT = 60 * 1024 * 1024
SHIFTED = COL + 40
TAPS = KERNEL * KERNEL
WIDE = 1024
STEM_LINES = PATCH * C1 // 128
ONE_LINES = 4 * C1 * C2 // 128
TWO_LINES = 4 * C2 * C3 // 128
KERN_LINES = LAYERS * TAPS * C3 // 128
HEAD_LINES = C3 * CLASSES // 128
FLAT_LINES = STEM_LINES + ONE_LINES + TWO_LINES + KERN_LINES + HEAD_LINES


def dot(a, b, da=1, db=0):
    return lax.dot_general(a, b, (((da,), (db,)), ((), ())), preferred_element_type=F32)


def fold8(values):
    rows, lanes = values.shape
    return jnp.sum(values.reshape(rows // 8, 8, lanes), axis=0)


def stats(values, count, mask):
    average = jnp.sum(values, axis=-1, keepdims=True) * (1.0 / count)
    centred = values - average
    if mask is not None:
        centred = centred * mask
    spread = jnp.sum(centred * centred, axis=-1, keepdims=True) * (1.0 / count)
    scale = lax.rsqrt(spread + NORM_EPSILON)
    return centred * scale, scale


def norm_back(delta, xhat, scale, gain, count, mask):
    scaled = delta * gain
    first = jnp.sum(scaled, axis=-1, keepdims=True) * (1.0 / count)
    second = jnp.sum(scaled * xhat, axis=-1, keepdims=True) * (1.0 / count)
    out = (scaled - first - xhat * second) * scale
    if mask is not None:
        out = out * mask
    return out


def sds(shape, dt=F32):
    return jax.ShapeDtypeStruct(shape, dt)


VM, AN, SM = pltpu.VMEM, pl.ANY, pltpu.SMEM


def call(kernel, ins, outs, scratch, flops=0, collective=None):
    params = pltpu.CompilerParams(vmem_limit_bytes=VMEM_LIMIT)
    if collective is not None:
        params = pltpu.CompilerParams(vmem_limit_bytes=VMEM_LIMIT, collective_id=collective, has_side_effects=True)
    return pl.pallas_call(
        kernel,
        in_specs=[pl.BlockSpec(memory_space=space) for _, space in ins],
        out_specs=[pl.BlockSpec(memory_space=space) for _, space in outs],
        out_shape=[shape for shape, _ in outs],
        scratch_shapes=scratch,
        cost_estimate=pl.CostEstimate(flops=flops, bytes_accessed=0, transcendentals=0),
        compiler_params=params,
    )(*[array for array, _ in ins])


def listed(space, *arrays):
    return [(array, space) for array in arrays]


def spread_shifted(cp_ref, lt, c, val):
    for ki in range(4):
        cp_ref[ki, lt, c, 18 - 2 * ki:90 - 2 * ki, :] = val


def zero_edges(cp_ref):
    head, tail = jnp.zeros((24, 128), F32), jnp.zeros((32, 128), F32)
    for ki in range(4):
        for lt in range(3):
            def body(c, _):
                cp_ref[ki, lt, c, 0:24, :] = head
                cp_ref[ki, lt, c, 80:112, :] = tail
                return 0
            lax.fori_loop(0, 12, body, 0)


def gate(h):
    phi_wide = 0.5 * (1.0 + lax.erf(h * 0.7071067811865476))
    dens = jnp.exp(h * h * -0.5) * 0.3989422804014327
    return h * phi_wide, phi_wide + h * dens


PARTS = 4


def weight_send(net, low, quarter, sems, base):
    size = C3 // 2 // PARTS
    k = net.z % PARTS
    part = pl.ds(pl.multiple_of(k * size, 16), size)
    rows = pl.ds(pl.multiple_of(net.y * (C3 // 2) + k * size, 16), size)
    across = remote(low.at[net.c, rows, :], quarter.at[part, :], sems, base, net.plane[0])
    along = [remote(quarter.at[part, :], quarter.at[part, :], sems, base + o, net.four[o - 1]) for o in range(1, PARTS)]

    def step1():
        across.wait()
        begin(along)

    return across.start, step1, lambda: end(along)


def weight_spread(net, quarter, far, sems, local_sem):
    c, y = net.c, net.y
    mine = far.at[c, pl.ds(pl.multiple_of(y * (C3 // 2), 16), C3 // 2), :]
    theirs = far.at[c, pl.ds(pl.multiple_of((1 - y) * (C3 // 2), 16), C3 // 2), :]
    own = pltpu.make_async_copy(quarter, mine, local_sem)
    first = [remote(quarter, mine, sems, 0, net.plane[1]), remote(quarter, mine, sems, 1, net.core)]
    second = remote(theirs, theirs, sems, 2, net.core)

    def step0():
        own.start()
        begin(first)

    def step1():
        first[0].wait()
        second.start()

    def step2():
        own.wait()
        first[1].wait()
        second.wait()

    return step0, step1, step2


def block_kernel(planes, *refs):
    res_ref, kern_ref, vec_ref, bin_ref, keep_ref, own_any, other_any = refs[:7]
    spread, sent = planes
    planes = max(planes)
    refs = refs[7:]
    if spread:
        quarter_ref, refs = refs[0], refs[1:]
    if sent:
        low_ref, refs = refs[0], refs[1:]
    new_ref, depth_out, normed_out, act_out, dg_out, out_out = refs[:6]
    refs = refs[6:]
    if spread:
        far_out, refs = refs[0], refs[1:]
    if sent:
        quarter_out, refs = refs[0], refs[1:]
    cp_ref, wb_ref, own_ref, other_ref, depth_ref, normed_ref, act_ref, dg_ref, out_ref, in_sem, out_sem = refs[:11]
    loads = [pltpu.make_async_copy(own_any, own_ref, in_sem.at[0]), pltpu.make_async_copy(other_any, other_ref, in_sem.at[1])]
    begin(loads)
    nothing = lambda: None
    spread0 = spread1 = spread2 = send1 = send2 = nothing
    if planes:
        net = Net(planes)
        peers = [net.core] + net.plane[:2] + net.four
        if not sent:
            peers = [net.core, net.plane[1]]
        for peer in peers:
            net.signal(peer)
        pl.semaphore_wait(pltpu.get_barrier_semaphore(), len(peers))
        spread0, spread1, spread2 = weight_spread(net, quarter_ref, far_out, refs[11], in_sem.at[2])
        spread0()
        if sent:
            send0, send1, send2 = weight_send(net, low_ref, quarter_out, refs[11], 3)
            send0()
    zero_edges(cp_ref)

    def prep_rows(c, _):
        rows = pl.ds(pl.multiple_of(c * COL, 8), COL)
        for lt in range(3):
            val = res_ref[rows, lt * 128:(lt + 1) * 128].astype(BF).astype(F32)
            spread_shifted(cp_ref, lt, c, val)
        return 0
    lax.fori_loop(0, SIDE, prep_rows, 0)
    for lt in range(3):
        for t in range(TAPS):
            wb_ref[lt, t] = jnp.broadcast_to(kern_ref[3 * t + lt:3 * t + lt + 1, :], (8, 128))
    for lt in range(3):
        lanes = slice(lt * 128, (lt + 1) * 128)
        bias = jnp.broadcast_to(vec_ref[0:1, lanes], (8, 128))

        def conv(v, _, lt=lt, lanes=lanes, bias=bias):
            acc = [bias] * SIDE
            for i in range(KERNEL):
                k = (6 * i) % 8
                row = pl.ds(pl.multiple_of(6 * i - k + v * 8, 8), 8)
                xs = [cp_ref[k // 2, lt, c, row, :] for c in range(SIDE)]
                for j in range(KERNEL):
                    w = wb_ref[lt, i * KERNEL + j]
                    for c in range(SIDE):
                        cc = c + j - 3
                        if 0 <= cc < SIDE:
                            acc[c] = acc[c] + w * xs[cc]
            for c in range(SIDE):
                depth_ref[pl.ds(pl.multiple_of(c * COL + v * 8, 8), 8), lanes] = acc[c]
            return 0
        lax.fori_loop(0, COL // 8, conv, 0)
        if lt == 0:
            send1()
    writes = [pltpu.make_async_copy(depth_ref, depth_out, out_sem.at[0])]
    writes[0].start()
    gain, shift = vec_ref[1:2, :], vec_ref[2:3, :]
    for r in range(ROWS // FORE):
        rows = slice(r * FORE, (r + 1) * FORE)
        xhat, _s = stats(depth_ref[rows, :], C3, None)
        normed_ref[rows, :] = (xhat * gain + shift).astype(BF)
    writes.append(pltpu.make_async_copy(normed_ref, normed_out, out_sem.at[1]))
    writes[1].start()
    bias_out, scale = vec_ref[3:4, :], vec_ref[4:5, :]
    keep_scale = keep_ref[...] * scale
    end(loads)
    for m in range(ROWS // FORE):
        rows, at_rows = slice(m * FORE, (m + 1) * FORE), pl.ds(m * FORE, FORE)
        low = normed_ref[rows, :]
        for n in range(HID // WF):
            lanes = slice(n * WF, (n + 1) * WF)
            half = own_ref if n * WF < HID // 2 else other_ref
            at = n * WF % (HID // 2)
            h = dot(low, half[0, :, at:at + WF]) + bin_ref[:, lanes]
            act, dg = gate(h)
            act_ref[rows, lanes] = act.astype(BF)
            dg_ref[rows, lanes] = dg.astype(BF)
            if n == HID // WF // 2 - 1 or n == HID // WF - 1:
                side = pl.ds(0 if n < HID // WF - 1 else HID // 2, HID // 2)
                for ref, out in ((act_ref, act_out), (dg_ref, dg_out)):
                    writes.append(pltpu.make_async_copy(ref.at[at_rows, side], out.at[at_rows, side], out_sem.at[len(writes)]))
                    writes[-1].start()
        if m == 0:
            spread1()
        o = (dot(act_ref[rows, :HID // 2], own_ref[1], 1, 1) + dot(act_ref[rows, HID // 2:], other_ref[1], 1, 1)
             + bias_out)
        out_ref[rows, :] = o
        writes.append(pltpu.make_async_copy(out_ref.at[at_rows, :], out_out.at[at_rows, :], out_sem.at[len(writes)]))
        writes[-1].start()
        new_ref[rows, :] = res_ref[rows, :] + jnp.concatenate([keep_scale] * (FORE // COL), axis=0) * o
    end(writes)
    spread2()
    send2()


def block(planes, res, kern, vec, bin_, keep, own, other, quarter=None, low=None):
    half = (2, C3, HID // 2)
    kept = [sds((ROWS, C3)), sds((ROWS, C3), BF), sds((ROWS, HID), BF), sds((ROWS, HID), BF), sds((ROWS, C3))]
    outs = listed(VM, sds((ROWS, C3))) + listed(AN, *kept)
    ins = listed(VM, res, kern, vec, bin_, keep) + listed(AN, own, other)
    scratch = [pltpu.VMEM((4, 3, SIDE, SHIFTED, 128), F32), pltpu.VMEM((3, TAPS, 8, 128), F32),
               pltpu.VMEM(half, BF), pltpu.VMEM(half, BF)]
    scratch += [pltpu.VMEM(k.shape, k.dtype) for k in kept]
    scratch += [pltpu.SemaphoreType.DMA((3,)), pltpu.SemaphoreType.DMA((2 + 5 * ROWS // FORE,))]
    collective = None
    if quarter is not None:
        ins = ins + listed(AN, quarter)
        outs = outs + listed(AN, sds(half, BF))
        scratch.append(pltpu.SemaphoreType.DMA((2, 3 + PARTS)))
        collective = 7
    if low is not None:
        ins = ins + listed(AN, low)
        outs = outs + listed(AN, sds((C3 // 2, HID // 2), BF))
        collective = 8
    part = (planes if quarter is not None else 0, planes if low is not None else 0)
    return call(functools.partial(block_kernel, part), ins, outs, scratch, 4_000_000_000, collective)


def head_flatten(wide_ref, line_ref):
    lane = lax.broadcasted_iota(jnp.int32, (C3 // 16, 128), 1)

    def tile(k, t, shift):
        value = wide_ref[t, pl.ds(k, C3 // 16, stride=16), :]
        return pltpu.roll(value, shift % 128, 1) if shift % 128 else value

    for f in range(CLASSES // 8):
        k, col = f * 128 // CLASSES, f * 128 % CLASSES
        t, s = col // 128, col % 128
        take = min(128, CLASSES - col)
        value = tile(k, t, 128 - s)
        if s and t < 7:
            value = jnp.where(lane < 128 - s, value, tile(k, t + 1, 128 - s))
        if take < 128:
            value = jnp.where(lane < take, value, tile(k + 1, 0, take))
        line_ref[pl.ds(f, C3 // 16, stride=CLASSES // 8), :] = value


def head_kernel(res_ref, vec_ref, head_ref, bias_ref, label_ref, valid_ref,
                dr_ref, dhead_ref, dbias_ref, dvec_ref, loss_ref, sum_ref, wide_ref, line_ref):
    def add(c, total):
        return total + res_ref[pl.ds(pl.multiple_of(c * COL, 8), COL), :]
    total = lax.fori_loop(1, SIDE, add, res_ref[0:COL, :])
    sum_ref[...] = total
    pooled = sum_ref[0:IMG, :]
    for r in range(1, SIDE):
        pooled = pooled + sum_ref[r * IMG:(r + 1) * IMG, :]
    pooled = jnp.concatenate([pooled * (1.0 / (SIDE * SIDE)), jnp.zeros((2, C3), F32)], axis=0)
    gain, shift = vec_ref[0:1, :], vec_ref[1:2, :]
    xhat, scale = stats(pooled, C3, None)
    final = (xhat * gain + shift).astype(BF)
    real = lax.broadcasted_iota(jnp.int32, (8, WIDE), 1) < CLASSES
    logits = jnp.where(real, dot(final, head_ref[...]) + bias_ref[...], -1e30)
    top = jnp.max(logits, axis=-1, keepdims=True)
    shifted = logits - top
    expd = jnp.exp(shifted)
    total = jnp.sum(expd, axis=-1, keepdims=True)
    log_chance = jnp.where(real, shifted - jnp.log(total), 0.0)
    spot = lax.broadcasted_iota(jnp.int32, (8, 1), 0)
    first_image = lax.axis_index("mp") * IMG
    label, valid = jnp.zeros((8, 1), jnp.int32), jnp.zeros((8, 1), jnp.int32)
    for n in range(IMG):
        label = jnp.where(spot == n, label_ref[first_image + n], label)
        valid = jnp.where(spot == n, valid_ref[first_image + n], valid)
    valid = valid.astype(F32)
    onehot = (label == lax.broadcasted_iota(jnp.int32, (8, WIDE), 1)).astype(F32)
    per_image = (-(1.0 - SMOOTH) * jnp.sum(log_chance * onehot, axis=-1, keepdims=True)
                 - (SMOOTH / CLASSES) * jnp.sum(log_chance, axis=-1, keepdims=True))
    lane = lax.broadcasted_iota(jnp.int32, (1, 128), 1)
    loss_ref[...] = jnp.where(lane == 0, jnp.sum(per_image * valid, axis=0, keepdims=True),
                              jnp.where(lane == 1, jnp.sum(valid, axis=0, keepdims=True), 0.0))
    delta = jnp.where(real, (jnp.exp(log_chance) - (1.0 - SMOOTH) * onehot - SMOOTH / CLASSES) * valid, 0.0)
    dbias_ref[...] = jnp.sum(delta, axis=0, keepdims=True)
    high = delta.astype(BF)
    rest = (delta - high.astype(F32)).astype(BF)
    for t in range(8):
        lanes = slice(t * 128, (t + 1) * 128)
        wide_ref[t] = dot(final, high[:, lanes], 0, 0) + dot(final, rest[:, lanes], 0, 0)
    head_flatten(wide_ref, line_ref)
    line_ref[HEAD_LINES:, :] = jnp.zeros((line_ref.shape[0] - HEAD_LINES, 128), F32)
    dhead_ref[...] = line_ref[...].astype(BF)
    dfinal = dot(high, head_ref[...], 1, 1) + dot(rest, head_ref[...], 1, 1)
    dvec_ref[0:1, :] = jnp.sum(dfinal * xhat, axis=0, keepdims=True)
    dvec_ref[1:2, :] = jnp.sum(dfinal, axis=0, keepdims=True)
    dpooled = norm_back(dfinal, xhat, scale, gain, C3, None) * (1.0 / (SIDE * SIDE))
    for r in range(SIDE):
        sum_ref[r * IMG:(r + 1) * IMG, :] = dpooled[0:IMG, :]

    def put(c, _):
        dr_ref[pl.ds(pl.multiple_of(c * COL, 8), COL), :] = sum_ref[...]
        return 0
    lax.fori_loop(0, SIDE, put, 0)


def head(res, vec, head_low, bias, labels, valid, lines):
    return call(
        head_kernel,
        listed(VM, res, vec, head_low, bias) + listed(SM, labels, valid),
        listed(VM, sds((ROWS, C3)), sds((lines, 128), BF), sds((1, WIDE)), sds((2, C3)), sds((1, 128))),
        [pltpu.VMEM((COL, C3), F32), pltpu.VMEM((8, C3, 128), F32), pltpu.VMEM((lines, 128), F32)],
        20_000_000,
    )


def ceil_to(value, step):
    return -(-value // step) * step


class Net:
    def __init__(self, planes):
        self.planes = planes
        self.d = lax.axis_index("dp")
        self.m = lax.axis_index("mp")
        self.c = self.d % 2
        self.y = self.d // 2 % 2
        self.z = self.d // 4
        self.core = (self.d + 1 - 2 * self.c, self.m)
        flip = self.d + 2 - 4 * self.y
        self.plane = [(self.d, 1 - self.m), (flip, self.m), (flip, 1 - self.m)]
        self.all_plane = []
        for k in range(1, 8):
            mm = 1 - self.m if k & 4 else self.m
            yy = 1 - self.y if k & 2 else self.y
            cc = 1 - self.c if k & 1 else self.c
            self.all_plane.append(((mm, yy, cc), (4 * self.z + 2 * yy + cc, mm)))
        group = self.z // 4 * 4
        self.four = [(4 * (group + (self.z % 4 + o) % 4) + 2 * self.y + self.c, self.m) for o in range(1, 4)]
        self.column = [(4 * ((self.z + o) % planes) + 2 * self.y + self.c, self.m) for o in range(1, planes)]

    def signal(self, peer):
        pl.semaphore_signal(pltpu.get_barrier_semaphore(), inc=1, device_id=peer, device_id_type=pl.DeviceIdType.MESH)

    def greet(self, whole=False):
        peers = ([peer for _, peer in self.all_plane] if whole else [self.core] + self.plane) + self.column
        for peer in peers:
            self.signal(peer)
        pl.semaphore_wait(pltpu.get_barrier_semaphore(), len(peers))


def remote(src, dst, sems, number, peer):
    return pltpu.make_async_remote_copy(
        src_ref=src, dst_ref=dst, send_sem=sems.at[0, number], recv_sem=sems.at[1, number],
        device_id=peer, device_id_type=pl.DeviceIdType.MESH)


def begin(copies):
    for copy in copies:
        copy.start()


def end(copies):
    for copy in copies:
        copy.wait()


CHUNKS = 2


def layer_scratch(planes, rows, width):
    part = width // CHUNKS
    return [
        pltpu.VMEM((CHUNKS, 2, planes, 2, rows, part), BF),
        pltpu.VMEM((CHUNKS, 2, 2, planes, rows, part), BF),
        pltpu.VMEM((CHUNKS, 3, planes, rows, part), BF),
        pltpu.VMEM((2, planes, 2, rows, width), BF),
        pltpu.SemaphoreType.DMA((2, 5 * CHUNKS)),
        pltpu.SemaphoreType.DMA((2,)),
    ]


def layer_steps(net, own, other, out, r1, s1, r2, held, sems, held_sem):
    c, y = net.c, net.y
    part = own.shape[4] // CHUNKS
    first, second = [], []
    for k in range(CHUNKS):
        lanes = pl.ds(k * part, part)
        first.append([remote(own.at[:, :, 1 - c, :, lanes], r1.at[k, 0], sems, 5 * k, net.core),
                      remote(other.at[:, :, 1 - c, :, lanes], r1.at[k, 1], sems, 5 * k + 1, net.core)])
        second.append([remote(s1.at[k, 1, y], r2.at[k, 0], sems, 5 * k + 2, net.plane[0]),
                       remote(s1.at[k, 0, 1 - y], r2.at[k, 1], sems, 5 * k + 3, net.plane[1]),
                       remote(s1.at[k, 1, 1 - y], r2.at[k, 2], sems, 5 * k + 4, net.plane[2])])

    loads = [pltpu.make_async_copy(own.at[:, :, c], held.at[0], held_sem.at[0]),
             pltpu.make_async_copy(other.at[:, :, c], held.at[1], held_sem.at[1])]

    def step0():
        begin(first[0])
        begin(loads)

    def step1(k):
        end(first[k])
        if k + 1 < CHUNKS:
            begin(first[k + 1])
        if k == 0:
            end(loads)
        lanes = slice(k * part, (k + 1) * part)

        def add(n, _):
            for yy in range(2):
                s1[k, 0, yy, n] = (held[0, n, yy, :, lanes].astype(F32) + r1[k, 0, n, yy].astype(F32)).astype(BF)
                s1[k, 1, yy, n] = (held[1, n, yy, :, lanes].astype(F32) + r1[k, 1, n, yy].astype(F32)).astype(BF)
            return 0
        lax.fori_loop(0, net.planes, add, 0)
        begin(second[k])

    def step2(k):
        end(second[k])
        lanes = slice(k * part, (k + 1) * part)

        def add(n, _):
            total = s1[k, 0, y, n].astype(F32)
            for j in range(3):
                total = total + r2[k, j, n].astype(F32)
            out[n, :, lanes] = total.astype(BF)
            return 0
        lax.fori_loop(0, net.planes, add, 0)

    return step0, step1, step2


def column_scratch(planes, rows, width):
    return [pltpu.VMEM((planes - 1, rows, width), BF), pltpu.SemaphoreType.DMA((2, planes))]


def column_steps(net, held, out, r3, sems):
    copies = [remote(held.at[(net.z + o) % net.planes], r3.at[o - 1], sems, o - 1, net.column[o - 1])
              for o in range(1, net.planes)]

    def step1():
        end(copies)

        def add(k, total):
            return total + r3[k].astype(F32)
        out[...] = lax.fori_loop(0, net.planes - 1, add, held[net.z].astype(F32)).astype(BF)

    return (lambda: begin(copies)), step1


def flat_scratch(planes, rows, dtype):
    return [
        pltpu.VMEM((2, 2, planes, rows, 128), dtype),
        pltpu.VMEM((2, 2, planes, rows, 128), dtype),
        pltpu.VMEM((3, planes, rows, 128), dtype),
        pltpu.VMEM((planes, rows, 128), dtype),
        pltpu.VMEM((planes - 1, rows, 128), dtype),
        pltpu.SemaphoreType.DMA((2, 3 + planes)),
    ]


def spread_scratch(planes):
    return [pltpu.SemaphoreType.DMA((2, 3 + planes))]


def flat_sum_steps(net, grad, shard, r1, s1, r2, s2, r3, sems):
    c, y, z, m = net.c, net.y, net.z, net.m
    planes = net.planes
    dtype = shard.dtype
    first = [remote(grad.at[:, :, 1 - c], r1, sems, 0, net.core)]
    second = [remote(s1.at[1 - m, y], r2.at[0], sems, 1, net.plane[0]),
              remote(s1.at[m, 1 - y], r2.at[1], sems, 2, net.plane[1]),
              remote(s1.at[1 - m, 1 - y], r2.at[2], sems, 3, net.plane[2])]
    third = [remote(s2.at[(z + o) % planes], r3.at[o - 1], sems, 3 + o, net.column[o - 1]) for o in range(1, planes)]

    def step1():
        end(first)
        for mm in range(2):
            for yy in range(2):
                s1[mm, yy] = (grad[mm, yy, c].astype(F32) + r1[mm, yy].astype(F32)).astype(dtype)
        begin(second)

    def step2():
        end(second)
        total = s1[m, y].astype(F32)
        for n in range(3):
            total = total + r2[n].astype(F32)
        s2[...] = total.astype(dtype)
        begin(third)

    def step3():
        end(third)

        def add(k, total):
            return total + r3[k].astype(F32)
        shard[...] = lax.fori_loop(0, planes - 1, add, s2[z].astype(F32)).astype(dtype)

    return [lambda: begin(first), step1, step2, step3]


def spread_steps(net, shard, out, sems):
    c, y, z, m = net.c, net.y, net.z, net.m
    planes = net.planes
    first = [remote(out.at[m, y, c, z], out.at[m, y, c, z], sems, o - 1, net.column[o - 1]) for o in range(1, planes)]
    second = [remote(out.at[m, y, c], out.at[m, y, c], sems, planes - 1 + k, net.plane[k]) for k in range(3)]
    third = [remote(out.at[:, :, c], out.at[:, :, c], sems, planes + 2, net.core)]

    def step0():
        out[m, y, c, z] = shard[...]
        begin(first)

    def step1():
        end(first)
        begin(second)

    def step2():
        end(second)
        begin(third)

    return [step0, step1, step2, lambda: end(third)]


def tail_scratch(planes, rows, dtype):
    return [
        pltpu.VMEM((7, planes, rows, 128), dtype),
        pltpu.VMEM((planes, rows, 128), dtype),
        pltpu.VMEM((planes - 1, rows, 128), dtype),
        pltpu.SemaphoreType.DMA((2, 12 + 2 * planes)),
    ]


def tail_steps(net, grad, out, r1, s1, r2, sems):
    c, y, z, m = net.c, net.y, net.z, net.m
    planes = net.planes
    dtype = out.dtype
    first = [remote(grad.at[mm, yy, cc], r1.at[n], sems, n, net.all_plane[n][1])
             for n, ((mm, yy, cc), _) in enumerate(net.all_plane)]
    second = [remote(s1.at[(z + o) % planes], r2.at[o - 1], sems, 6 + o, net.column[o - 1]) for o in range(1, planes)]
    third = [remote(out.at[m, y, c, z], out.at[m, y, c, z], sems, 5 + planes + o, net.column[o - 1])
             for o in range(1, planes)]
    fourth = [remote(out.at[m, y, c], out.at[m, y, c], sems, 5 + 2 * planes + n, net.all_plane[n][1]) for n in range(7)]

    def step1():
        end(first)
        total = grad[m, y, c].astype(F32)
        for n in range(7):
            total = total + r1[n].astype(F32)
        s1[...] = total.astype(dtype)
        begin(second)

    def step2():
        end(second)

        def add(k, total):
            return total + r2[k].astype(F32)
        out[m, y, c, z] = lax.fori_loop(0, planes - 1, add, s1[z].astype(F32)).astype(dtype)
        begin(third)

    def step3():
        end(third)
        begin(fourth)

    return [lambda: begin(first), step1, step2, step3, lambda: end(fourth)]


def block_back_body(hooks, dr_ref, keep_ref, vec_ref, kern_ref, act_any, dg_any, out_any, normed_any, depth_any, res_any,
                    own_any, other_any,
                    new_ref, down_any, dother_any, dkern_ref, dvec_ref, dbin_ref,
                    cp_ref, wb_ref, dout_ref, dhid_ref, kacc_ref, act_ref, dg_ref, out_ref, normed_ref, depth_ref, res_ref,
                    own_ref, other_ref, down_ref, dother_ref, in_sem):
    pairs = ((own_any, own_ref), (other_any, other_ref), (dg_any, dg_ref), (depth_any, depth_ref), (act_any, act_ref),
             (normed_any, normed_ref), (out_any, out_ref), (res_any, res_ref))
    load = [pltpu.make_async_copy(a, b, in_sem.at[n]) for n, (a, b) in enumerate(pairs)]
    begin(load[:3])
    hooks = iter(hooks)

    def tick():
        for hook in next(hooks):
            hook()
    tick()
    zero_edges(cp_ref)
    for lt in range(3):
        for t in range(TAPS):
            wb_ref[lt, t] = jnp.broadcast_to(kern_ref[3 * t + lt:3 * t + lt + 1, :], (8, 128))
    kacc_ref[...] = jnp.zeros_like(kacc_ref)
    gain, scale = vec_ref[1:2, :], vec_ref[4:5, :]

    def pre(m, a_bias):
        rows = pl.ds(pl.multiple_of(m * PAIR, 16), PAIR)
        keep = jnp.concatenate([keep_ref[...], keep_ref[...]], axis=0)
        dk = dr_ref[rows, :] * keep
        low = (dk * scale).astype(BF)
        dout_ref[rows, :] = low
        return a_bias + fold8(low.astype(F32))
    zero = jnp.zeros((8, C3), F32)
    a_bias = lax.fori_loop(0, ROWS // PAIR, pre, zero)
    dvec_ref[3:4, :] = jnp.sum(a_bias, axis=0, keepdims=True)
    dbin_ref[...] = jnp.zeros_like(dbin_ref)
    end(load[:3])
    begin(load[3:])

    def mm(m, carry):
        a_gain, a_shift, a_depth = carry
        rows = slice(m * REAR, (m + 1) * REAR)
        low = dout_ref[rows, :]
        for n in range(HID // WB):
            lanes = slice(n * WB, (n + 1) * WB)
            half = own_ref if n * WB < HID // 2 else other_ref
            at = n * WB % (HID // 2)
            d = dot(low, half[1, :, at:at + WB]) * dg_ref[rows, lanes].astype(F32)
            dlow = d.astype(BF)
            dhid_ref[rows, lanes] = dlow
            dbin_ref[:, lanes] += fold8(dlow.astype(F32))
        d = dot(dhid_ref[rows, :HID // 2], own_ref[0], 1, 1) + dot(dhid_ref[rows, HID // 2:], other_ref[0], 1, 1)
        if m == 0:
            load[3].wait()
        xhat, rs = stats(depth_ref[rows, :], C3, None)
        a_gain = a_gain + fold8(d * xhat)
        a_shift = a_shift + fold8(d)
        dd = norm_back(d, xhat, rs, gain, C3, None)
        a_depth = a_depth + fold8(dd)
        for n in range(REAR // COL):
            for lt in range(3):
                spread_shifted(cp_ref, lt, m * (REAR // COL) + n, dd[n * COL:(n + 1) * COL, lt * 128:(lt + 1) * 128])
        return a_gain, a_shift, a_depth
    sums = (zero, zero, zero)
    for n in range(ROWS // REAR):
        sums = mm(n, sums)
        tick()
    end(load[4:])

    def scale_rows(m, total):
        rows = pl.ds(pl.multiple_of(m * PAIR, 16), PAIR)
        keep = jnp.concatenate([keep_ref[...], keep_ref[...]], axis=0)
        return total + fold8(dr_ref[rows, :] * keep * out_ref[rows, :])
    a_scale = lax.fori_loop(0, ROWS // PAIR, scale_rows, zero)
    dvec_ref[4:5, :] = jnp.sum(a_scale, axis=0, keepdims=True)
    a_gain, a_shift, a_depth = sums
    dvec_ref[0:1, :] = jnp.sum(a_depth, axis=0, keepdims=True)
    dvec_ref[1:2, :] = jnp.sum(a_gain, axis=0, keepdims=True)
    dvec_ref[2:3, :] = jnp.sum(a_shift, axis=0, keepdims=True)
    dvec_ref[5:8, :] = jnp.zeros((3, C3), F32)
    writes = []
    for n in range(HID // 256):
        lanes = slice(n * 256, (n + 1) * 256)
        half = down_ref if n < 3 else dother_ref
        part = slice((n % 3) * 256, (n % 3 + 1) * 256)
        half[1, :, part] = dot(dout_ref[...], act_ref[:, lanes], 0, 0).astype(BF)
        half[0, :, part] = dot(normed_ref[...], dhid_ref[:, lanes], 0, 0).astype(BF)
        if n % 3 == 2:
            out = down_any if n == 2 else dother_any
            writes.append(pltpu.make_async_copy(half, out, in_sem.at[8 + n // 3]))
            writes[-1].start()
            tick()
    for lt in range(3):
        lanes = slice(lt * 128, (lt + 1) * 128)

        def conv(v, _, lt=lt, lanes=lanes):
            spots = [pl.ds(pl.multiple_of(c * COL + v * 8, 8), 8) for c in range(SIDE)]
            acc = [dr_ref[s, lanes] for s in spots]
            sent = [res_ref[s, lanes].astype(BF).astype(F32) for s in spots]
            for i in range(KERNEL):
                flip = 6 - i
                k = (6 * flip) % 8
                row = pl.ds(pl.multiple_of(6 * flip - k + v * 8, 8), 8)
                xs = [cp_ref[k // 2, lt, c, row, :] for c in range(SIDE)]
                for j in range(KERNEL):
                    t = i * KERNEL + j
                    w = wb_ref[lt, t]
                    tap = None
                    for c in range(SIDE):
                        cc = c - (j - 3)
                        if 0 <= cc < SIDE:
                            acc[c] = acc[c] + w * xs[cc]
                            term = sent[c] * xs[cc]
                            tap = term if tap is None else tap + term
                    kacc_ref[lt, t] += tap
            for c in range(SIDE):
                new_ref[spots[c], lanes] = acc[c]
            return 0
        lax.fori_loop(0, COL // 8, conv, 0)
        tick()
    for lt in range(3):
        for t in range(TAPS):
            dkern_ref[3 * t + lt:3 * t + lt + 1, :] = jnp.sum(kacc_ref[lt, t], axis=0, keepdims=True)
    end(writes)


HOOKS = 9
BODY_INS, BODY_OUTS, BODY_SCRATCH = 12, 6, 16


def back_parts():
    outs = (listed(VM, sds((ROWS, C3))) + listed(AN, sds((2, C3, HID // 2), BF), sds((2, C3, HID // 2), BF))
            + listed(VM, sds((3 * TAPS, 128)), sds((8, C3)), sds((8, HID))))
    wide, half = (ROWS, HID), (2, C3, HID // 2)
    scratch = [pltpu.VMEM((4, 3, SIDE, SHIFTED, 128), F32), pltpu.VMEM((3, TAPS, 8, 128), F32),
               pltpu.VMEM((ROWS, C3), BF), pltpu.VMEM(wide, BF), pltpu.VMEM((3, TAPS, 8, 128), F32),
               pltpu.VMEM(wide, BF), pltpu.VMEM(wide, BF), pltpu.VMEM((ROWS, C3), F32), pltpu.VMEM((ROWS, C3), BF),
               pltpu.VMEM((ROWS, C3), F32), pltpu.VMEM((ROWS, C3), F32), pltpu.VMEM(half, BF), pltpu.VMEM(half, BF),
               pltpu.VMEM(half, BF), pltpu.VMEM(half, BF), pltpu.SemaphoreType.DMA((10,))]
    return outs, scratch


def take(refs, count):
    return refs[:count], refs[count:]


def block_back_kernel(planes, kind, *refs):
    net = Net(planes)
    args, refs = take(refs, BODY_INS)
    more_in, refs = take(refs, (1, 3, 3)[kind])
    outs, refs = take(refs, BODY_OUTS)
    more_out, refs = take(refs, (1, 2, 2)[kind])
    scratch, refs = take(refs, BODY_SCRATCH)
    hooks = [[] for _ in range(HOOKS)]
    if kind == 0:
        steps = flat_sum_steps(net, more_in[0], more_out[0], *refs)
        hooks[0], hooks[2], hooks[5], hooks[8] = [net.greet, steps[0]], [steps[1]], [steps[2]], [steps[3]]
    else:
        step0, step1, step2 = layer_steps(net, more_in[0], more_in[1], more_out[0], *refs[:6])
        hooks[0] = [net.greet, step0]
        hooks[1] = [lambda: step1(0)]
        hooks[2] = [lambda: step1(1)]
        hooks[8] = [lambda: step2(0), lambda: step2(1)]
        if kind == 1:
            steps = spread_steps(net, more_in[2], more_out[1], *refs[6:])
            hooks[0] = [net.greet, steps[0], step0]
            hooks[1] = [steps[1], lambda: step1(0)]
            hooks[5] = [steps[2]]
            hooks[8] = [lambda: step2(0), lambda: step2(1), steps[3]]
        else:
            col0, col1 = column_steps(net, more_in[2], more_out[1], *refs[6:])
            hooks[0].append(col0)
            hooks[4].append(col1)
    block_back_body(hooks, *args, *outs, *scratch)


def block_back(planes, kind, args, *more):
    outs, scratch = back_parts()
    ins = listed(VM, *args[:4]) + listed(AN, *args[4:])
    if kind == 0:
        grad, = more
        rows = grad.shape[4]
        ins += listed(VM, grad)
        outs += listed(VM, sds((rows, 128), BF))
        scratch += flat_scratch(planes, rows, BF)
    else:
        own, other, held = more
        rows, width = own.shape[3:]
        ins += listed(AN, own, other) + listed(VM, held)
        outs += listed(VM, sds((planes, rows, width), BF))
        scratch += layer_scratch(planes, rows, width)
        if kind == 1:
            outs += listed(VM, sds((2, 2, 2, planes) + held.shape, BF))
            scratch += spread_scratch(planes)
        else:
            outs += listed(VM, sds((rows, width), BF))
            scratch += column_scratch(planes, rows, width)
    return call(functools.partial(block_back_kernel, planes, kind), ins, outs, scratch, 8_000_000_000, (1, 2, 5)[kind])


def back_kernel(planes, dr_ref, xp_any, n1_any, s2_any, n2_any, wbig_ref, d1_ref, d2_ref, vs_ref, v2_ref, dk0_ref, dk1_ref,
                dk2_ref, own_ref, other_ref, held_ref,
                tail_ref, dvs_ref, dv2_ref, dv3_ref, two_ref, piece0_ref, piece1_ref, one_ref,
                mid_ref, line1_ref, grad1_ref,
                xp_ref, n1_ref, s2_ref, n2_ref, in_sem,
                sum_ref, shard_ref, st_ref, dn1_ref, dlow_ref, base_ref, aw_ref, dd1_ref, line_ref, grad_ref, *scratch):
    load_n2 = pltpu.make_async_copy(n2_any, n2_ref, in_sem.at[18])
    load_n2.start()
    loads = [[pltpu.make_async_copy(a.at[g], b.at[g], in_sem.at[3 * g + n])
              for n, (a, b) in enumerate(((xp_any, xp_ref), (n1_any, n1_ref), (s2_any, s2_ref)))] for g in range(6)]
    begin(loads[0][1:])
    net = Net(planes)
    net.greet(True)
    layer0, layer1, layer2 = layer_steps(net, own_ref, other_ref, sum_ref, *scratch[:6])
    high0, high1 = column_steps(net, held_ref, piece1_ref, *scratch[6:8])
    low0, low1 = column_steps(net, sum_ref, piece0_ref, *scratch[8:10])
    high0()
    layer0()
    mask1 = (lax.broadcasted_iota(jnp.int32, (1, 128), 1) < C1).astype(F32)
    mask2 = (lax.broadcasted_iota(jnp.int32, (1, 256), 1) < C2).astype(F32)
    bias_stem, gain_stem, shift_stem = vs_ref[0:1, :], vs_ref[1:2, :], vs_ref[2:3, :]
    gain_one = vs_ref[3:4, :]
    gain_two = v2_ref[1:2, :]
    z1, z2, z3 = jnp.zeros((8, 128), F32), jnp.zeros((8, 256), F32), jnp.zeros((8, C3), F32)
    dd1_ref[...] = jnp.zeros_like(dd1_ref)
    aw_ref[...] = jnp.zeros_like(aw_ref)

    base_ref[...] = dr_ref[...].astype(BF)
    shard = grad_ref.shape[4]
    load_n2.wait()
    for g in range(1, 6):
        begin(loads[g][1:])
    for g in range(6):
        loads[g][0].start()
    for or2 in range(2):
        total = dot(n2_ref[or2], base_ref[...], 0, 0)
        for oc2 in range(2):
            for lt in range(3):
                line_ref[pl.ds(3 * (or2 * 384 + oc2 * 192) + lt, 192, stride=3), :] = (
                    total[oc2 * 256:oc2 * 256 + 192, lt * 128:(lt + 1) * 128])
    for l in range(LAYERS):
        line_ref[TWO_LINES + l * 3 * TAPS:TWO_LINES + (l + 1) * 3 * TAPS, :] = (dk0_ref, dk1_ref, dk2_ref)[l][...]
    line_ref[TWO_LINES + KERN_LINES:, :] = jnp.zeros((8 * planes * shard - TWO_LINES - KERN_LINES, 128), F32)
    for mm in range(2):
        for yy in range(2):
            for cc in range(2):
                for k in range(planes):
                    at = (((mm * 2 + yy) * 2 + cc) * planes + k) * shard
                    grad_ref[mm, yy, cc, k] = line_ref[at:at + shard, :].astype(BF)
    flat = flat_sum_steps(net, grad_ref, shard_ref, *scratch[10:16])
    flat += spread_steps(net, shard_ref, two_ref, *scratch[16:17])
    flat[0]()
    layer1(0)

    def upper(g, carry):
        rows = pl.ds(g * 144, 144)
        base = base_ref[rows, :]
        a3 = carry[0] + fold8(base.astype(F32))
        a_bias2, a_gain2, a_shift2 = carry[1:4]
        dn2 = [dot(base, d2_ref[or2], 1, 1) for or2 in range(2)]
        loads[g][1].wait()
        loads[g][2].wait()
        d = jnp.concatenate(
            [dn2[or2][q // 2 * 72:(q // 2 + 1) * 72, q % 2 * 256:(q % 2 + 1) * 256] for q in range(4) for or2 in range(2)], axis=0)
        xhat, rs = stats(s2_ref[g].reshape(4 * 144, 256), C2, mask2)
        a_gain2 = a_gain2 + fold8(d * xhat)
        a_shift2 = a_shift2 + fold8(d)
        mids = norm_back(d, xhat, rs, gain_two, C2, mask2).astype(BF)
        a_bias2 = a_bias2 + fold8(mids.astype(F32))
        mid_ref[g] = mids
        for q in range(4):
            lanes = slice(q * 256, (q + 1) * 256)
            for or1 in range(2):
                dd1_ref[or1] += dot(n1_ref[g, or1 * 144:(or1 + 1) * 144, lanes], mids[q * 144:(q + 1) * 144], 0, 0)
        return a3, a_bias2, a_gain2, a_shift2

    def lower(g, carry, hooks):
        loads[g][0].wait()
        for q in range(4):
            for or1 in range(2):
                part = slice(or1 * 144, (or1 + 1) * 144)
                o = dot(mid_ref[g, q * 144:(q + 1) * 144, :], d1_ref[or1], 1, 1)
                dn1_ref[2 * q, part, :] = o[:, :128]
                dn1_ref[2 * q + 1, part, :] = o[:, 128:]
        for q in range(4):
            o = dot(xp_ref[g], wbig_ref[:, q * 256:(q + 1) * 256])
            st_ref[2 * q] = o[:, :128]
            st_ref[2 * q + 1] = o[:, 128:]

        for hook in hooks:
            hook()
        b0, g0, s0, g1, s1 = carry
        v = st_ref[...].reshape(8 * 288, 128) + bias_stem
        xa, ra = stats(v, C1, mask1)
        y = xa * gain_stem + shift_stem
        xb, rb = stats(y, C1, mask1)
        d = dn1_ref[...].reshape(8 * 288, 128)
        g1 = g1 + fold8(d * xb)
        s1 = s1 + fold8(d)
        dy = norm_back(d, xb, rb, gain_one, C1, mask1)
        g0 = g0 + fold8(dy * xa)
        s0 = s0 + fold8(dy)
        dv = norm_back(dy, xa, ra, gain_stem, C1, mask1).astype(BF)
        b0 = b0 + fold8(dv.astype(F32))
        for j in range(8):
            dlow_ref[:, j * 128:(j + 1) * 128] = dv[j * 288:(j + 1) * 288]
        sums = (b0, g0, s0, g1, s1)
        aw_ref[...] += dot(xp_ref[g], dlow_ref[...], 0, 0)
        return sums

    sums = (z3, z2, z2, z2)
    between = [[high1], [flat[1]], [lambda: layer1(1)], [], [], [lambda: layer2(0), flat[2]]]
    for g in range(6):
        sums = upper(g, sums)
        for hook in between[g]:
            hook()
    lane = lax.broadcasted_iota(jnp.int32, (48, 128), 1)
    for or1 in range(2):
        for oc1 in range(2):
            left, right = st_ref.at[1], st_ref.at[2]
            left[0:96, :] = dd1_ref[or1, oc1 * 128:oc1 * 128 + 96, 0:128]
            right[0:96, :] = dd1_ref[or1, oc1 * 128:oc1 * 128 + 96, 128:256]
            e0, o0 = left[pl.ds(0, 48, stride=2), :], left[pl.ds(1, 48, stride=2), :]
            e1, o1 = right[pl.ds(0, 48, stride=2), :], right[pl.ds(1, 48, stride=2), :]
            at = (or1 * 192 + oc1 * 96) * 3 // 2
            line1_ref[pl.ds(at, 48, stride=3), :] = e0
            line1_ref[pl.ds(at + 1, 48, stride=3), :] = jnp.where(lane < 64, e1, pltpu.roll(o0, 64, 1))
            line1_ref[pl.ds(at + 2, 48, stride=3), :] = jnp.where(lane < 64, pltpu.roll(o0, 64, 1), pltpu.roll(o1, 64, 1))
    size = grad1_ref.shape[4]
    line1_ref[ONE_LINES:, :] = jnp.zeros((8 * planes * size - ONE_LINES, 128), F32)
    for mm in range(2):
        for yy in range(2):
            for cc in range(2):
                for k in range(planes):
                    at = (((mm * 2 + yy) * 2 + cc) * planes + k) * size
                    grad1_ref[mm, yy, cc, k] = line1_ref[at:at + size, :].astype(BF)
    first = tail_steps(net, grad1_ref, one_ref, *scratch[17:])
    first[0]()
    inner = [[], [flat[3], flat[4]], [lambda: layer2(1), first[2], flat[5]], [first[3]], [flat[6]], [flat[7], first[4]]]
    outer = [[first[1]], [], [low0], [], [], [low1]]
    low_sums = (z1, z1, z1, z1, z1)
    for g in range(6):
        low_sums = lower(g, low_sums, inner[g])
        for hook in outer[g]:
            hook()
    done = sums + low_sums
    total = aw_ref[0:48, 0:128]
    for j in range(1, 8):
        total = total + aw_ref[j * 48:(j + 1) * 48, j * 128:(j + 1) * 128]
    dv3_ref[...] = jnp.sum(done[0], axis=0, keepdims=True)
    for n in range(3):
        dv2_ref[n:n + 1, :] = jnp.sum(done[1 + n], axis=0, keepdims=True)
    for n in range(5):
        dvs_ref[n:n + 1, :] = jnp.sum(done[4 + n], axis=0, keepdims=True)
    base = st_ref.at[0]
    base[0:48, :] = total
    lane = lax.broadcasted_iota(jnp.int32, (12, 128), 1)
    a0, a1, a2, a3 = [base[pl.ds(n, 12, stride=4), :] for n in range(4)]
    tail_ref[pl.ds(0, 12, stride=3), :] = jnp.where(lane < 96, a0, pltpu.roll(a1, 96, 1))
    tail_ref[pl.ds(1, 12, stride=3), :] = jnp.where(lane < 64, pltpu.roll(a1, 96, 1), pltpu.roll(a2, 64, 1))
    tail_ref[pl.ds(2, 12, stride=3), :] = jnp.where(lane < 32, pltpu.roll(a2, 64, 1), pltpu.roll(a3, 32, 1))


def back(planes, dr, kept, weights, dkern, own, other, held):
    shard = ceil_to(TWO_LINES + KERN_LINES, 8 * planes * 16) // (8 * planes)
    rows, width = own.shape[3:]
    shard1 = ceil_to(ONE_LINES, 8 * planes * 16) // (8 * planes)
    shape1 = (2, 2, 2, planes, shard1, 128)
    shape = (2, 2, 2, planes, shard, 128)
    return call(
        functools.partial(back_kernel, planes),
        listed(VM, dr) + listed(AN, *kept) + listed(VM, *weights, *dkern) + listed(AN, own, other) + listed(VM, held),
        listed(VM, sds((STEM_LINES, 128)), sds((5, 128)), sds((3, 256)), sds((1, C3)), sds(shape, BF),
               sds((rows, width), BF), sds((rows, width), BF), sds(shape1, BF)),
        [pltpu.VMEM((6, 576, 256), BF), pltpu.VMEM((8 * planes * shard1, 128), F32), pltpu.VMEM(shape1, BF)]
        + [pltpu.VMEM(k.shape, k.dtype) for k in kept] + [pltpu.SemaphoreType.DMA((19,))]
        + [pltpu.VMEM((planes, rows, width), BF), pltpu.VMEM((shard, 128), BF),
           pltpu.VMEM((8, 288, 128), F32), pltpu.VMEM((8, 288, 128), F32), pltpu.VMEM((288, 1024), BF),
           pltpu.VMEM((ROWS, C3), BF), pltpu.VMEM((384, 1024), F32), pltpu.VMEM((2, 256, 256), F32),
           pltpu.VMEM((8 * planes * shard, 128), F32), pltpu.VMEM(shape, BF)]
        + layer_scratch(planes, rows, width) + column_scratch(planes, rows, width) + column_scratch(planes, rows, width)
        + flat_scratch(planes, shard, BF) + spread_scratch(planes) + tail_scratch(planes, shard1, BF),
        8_000_000_000, 3,
    )


VECTOR_WIDTHS = (C1, C1, C2, LAYERS * C3, LAYERS * C3, C3, C1, C1, C1, C2, C2, C3, LAYERS * C3, LAYERS * C3, LAYERS * HID,
                 LAYERS * C3, C3, CLASSES)
VECTOR_NAMES = ("gain_stem", "gain_one", "gain_two", "gain_block", "layer_scale", "gain_final", "bias_stem", "shift_stem",
                "shift_one", "bias_one", "shift_two", "bias_two", "bias_depth", "shift_block", "bias_inner", "bias_outer",
                "shift_final", "bias_head")
VECTOR = sum(VECTOR_WIDTHS)
VECTOR_LINES = ceil_to(VECTOR, 1024) // 128


def vector_plan():
    plan, offset, row = {}, 0, 0
    for name, width in zip(VECTOR_NAMES, VECTOR_WIDTHS):
        plan[name] = (offset, width, row)
        offset, row = offset + width, row + ceil_to(width, 128) // 128
    return plan, row


VECTOR_PLAN, PADDED_LINES = vector_plan()
TAIL_LINES = STEM_LINES + PADDED_LINES + 1


def open_kernel(planes, flat_ref, vector_ref, master_ref, mask_ref, pix_ref, perm_ref,
                xp_out, n1_out, s2_out, n2_out, far_out, low0_out, quarter1_out,
                res_ref, wbig_ref, d1_ref, d2_ref, head_ref, vs_ref, v2_ref, v3_ref, hv_ref, hb_ref, *refs):
    kern_ref, vec_ref, bin_ref, keep_ref = [refs[LAYERS * n:LAYERS * (n + 1)] for n in range(4)]
    low_ref = (None,) + refs[4 * LAYERS:4 * LAYERS + 2]
    (wide_ref, pad_ref, master, master_sem, low0_ref, x_ref, xp_ref, n1_ref, s2_ref, n2_ref, st_ref, n2s_ref, pix_sem,
     out_sem, w_sem, quarter_ref) = refs[4 * LAYERS + 2:]
    net = Net(planes)
    m = net.m
    peers = [net.core] + net.plane[:2] + net.four
    for peer in peers:
        net.signal(peer)
    loads = [pltpu.make_async_copy(master_ref.at[l], master.at[l], master_sem.at[l]) for l in range(LAYERS)]
    loads[0].start()
    near = pl.ds(pl.multiple_of(m * PAIR, 16), PAIR)
    far = pl.ds(pl.multiple_of((1 - m) * PAIR, 16), PAIR)
    kept = pltpu.make_async_copy(pix_ref.at[near, :], x_ref.at[near, :], out_sem.at[24])
    kept.start()
    pl.semaphore_wait(pltpu.get_barrier_semaphore(), len(peers))
    moves = []
    for g in range(6):
        lanes = pl.ds(g * 384, 384)
        moves.append(remote(pix_ref.at[far, lanes], x_ref.at[near, lanes], pix_sem, g, net.plane[0]))
    moves[0].start()
    loads[0].wait()
    begin(loads[1:])
    low0_ref[...] = master[0].astype(BF)
    send0 = weight_send(net, low0_ref, quarter_ref, w_sem, 3)
    send1 = weight_send(net, low_ref[1], quarter1_out, w_sem, 3 + PARTS)
    send0[0]()
    moves[1].start()
    spread0, spread1, spread2 = weight_spread(net, quarter_ref, far_out, w_sem, out_sem.at[26])
    keep_low = pltpu.make_async_copy(low0_ref, low0_out, out_sem.at[25])
    keep_low.start()
    for name in VECTOR_NAMES:
        offset, width, row = VECTOR_PLAN[name]
        lines = ceil_to(width, 128) // 128
        at, s = offset // 128, offset % 128
        lane = lax.broadcasted_iota(jnp.int32, (lines, 128), 1)
        value = vector_ref[at:at + lines, :]
        if s:
            value = jnp.where(lane < 128 - s, pltpu.roll(value, 128 - s, 1),
                              pltpu.roll(vector_ref[at + 1:at + 1 + lines, :], 128 - s, 1))
        if width % 128:
            spot = lax.broadcasted_iota(jnp.int32, (lines, 128), 0) * 128 + lane
            value = jnp.where(spot < width, value, 0.0)
        pad_ref[row:row + lines, :] = value

    def place(ref, at, name, start, lines):
        row = VECTOR_PLAN[name][2] + start
        for n in range(lines):
            ref[at + (slice(n * 128, (n + 1) * 128),)] = pad_ref[row + n:row + n + 1, :]
    one = lambda n: (slice(n, n + 1),)
    for n, name in enumerate(("bias_stem", "gain_stem", "shift_stem", "gain_one", "shift_one")):
        place(vs_ref, one(n), name, 0, 1)
    for n, name in enumerate(("bias_one", "gain_two", "shift_two")):
        place(v2_ref, one(n), name, 0, 2)
    place(v3_ref, one(0), "bias_two", 0, 3)
    for l in range(LAYERS):
        for n, name in enumerate(("bias_depth", "gain_block", "shift_block", "bias_outer", "layer_scale")):
            place(vec_ref[l], one(n), name, 3 * l, 3)
        for n in range(12):
            part = (n // 6 + m) % 2
            row = VECTOR_PLAN["bias_inner"][2] + 12 * l + part * 6 + n % 6
            bin_ref[l][:, n * 128:(n + 1) * 128] = pad_ref[pl.ds(row, 1), :]
    place(hv_ref, one(0), "gain_final", 0, 3)
    place(hv_ref, one(1), "shift_final", 0, 3)
    place(hb_ref, one(0), "bias_head", 0, 8)
    lane = lax.broadcasted_iota(jnp.int32, (12, 128), 1)
    f0, f1, f2 = [flat_ref[pl.ds(n, 12, stride=3), :] for n in range(3)]
    parts = (f0, jnp.where(lane < 32, pltpu.roll(f0, 32, 1), pltpu.roll(f1, 32, 1)),
             jnp.where(lane < 64, pltpu.roll(f1, 64, 1), pltpu.roll(f2, 64, 1)), pltpu.roll(f2, 96, 1))
    for n in range(4):
        wide_ref[0, pl.ds(n, 12, stride=4), :] = jnp.where(lane < C1, parts[n], 0.0)
    stem = wide_ref[0, 0:48, :].astype(BF)
    wbig_ref[...] = jnp.zeros_like(wbig_ref)
    for j in range(8):
        wbig_ref[j * 48:(j + 1) * 48, j * 128:(j + 1) * 128] = stem
    lane = lax.broadcasted_iota(jnp.int32, (192, 128), 1)
    f0, f1, f2 = [flat_ref[pl.ds(STEM_LINES + n, 192, stride=3), :] for n in range(3)]
    f1 = pltpu.roll(f1, 64, 1)
    f2 = pltpu.roll(f2, 64, 1)
    wide_ref[0, pl.ds(0, 192, stride=2), :] = f0
    wide_ref[1, pl.ds(0, 192, stride=2), :] = jnp.where(lane < 64, pltpu.roll(f1, 64, 1), 0.0)
    wide_ref[0, pl.ds(1, 192, stride=2), :] = jnp.where(lane < 64, f1, f2)
    wide_ref[1, pl.ds(1, 192, stride=2), :] = jnp.where(lane < 64, f2, 0.0)
    d1_ref[...] = jnp.zeros_like(d1_ref)
    d2_ref[...] = jnp.zeros_like(d2_ref)
    for or1 in range(2):
        for oc1 in range(2):
            at = or1 * 192 + oc1 * 96
            for t in range(2):
                d1_ref[or1, oc1 * 128:oc1 * 128 + 96, t * 128:(t + 1) * 128] = wide_ref[t, at:at + 96, :].astype(BF)
    base = STEM_LINES + ONE_LINES
    for lt in range(3):
        for or2 in range(2):
            for oc2 in range(2):
                at = base + (or2 * 384 + oc2 * 192) * 3 + lt
                d2_ref[or2, oc2 * 256:oc2 * 256 + 192, lt * 128:(lt + 1) * 128] = flat_ref[pl.ds(at, 192, stride=3), :].astype(BF)
    mask1 = (lax.broadcasted_iota(jnp.int32, (1, 128), 1) < C1).astype(F32)
    mask2 = (lax.broadcasted_iota(jnp.int32, (1, 256), 1) < C2).astype(F32)
    bias_stem, gain_stem, shift_stem = vs_ref[0:1, :], vs_ref[1:2, :], vs_ref[2:3, :]
    gain_one, shift_one = vs_ref[3:4, :], vs_ref[4:5, :]
    bias_one, gain_two, shift_two = v2_ref[0:1, :], v2_ref[1:2, :], v2_ref[2:3, :]
    kern_base = STEM_LINES + ONE_LINES + TWO_LINES

    def more_low():
        for l in range(1, LAYERS):
            loads[l].wait()
            low_ref[l][...] = master[l].astype(BF)

    def more_small():
        spot = lax.broadcasted_iota(jnp.int32, (COL, 128), 0) % IMG
        for l in range(LAYERS):
            value = jnp.zeros((COL, 128), jnp.int32)
            for n in range(IMG):
                value = jnp.where(spot == n, mask_ref[l, m * IMG + n], value)
            value = value.astype(F32)
            for lt in range(3):
                keep_ref[l][:, lt * 128:(lt + 1) * 128] = value
        for l in range(LAYERS):
            kern_ref[l][...] = flat_ref[kern_base + l * 3 * TAPS:kern_base + (l + 1) * 3 * TAPS, :]

    def more_head():
        base = kern_base + KERN_LINES
        count = C3 // 16
        lane = lax.broadcasted_iota(jnp.int32, (count, 128), 1)
        for k in range(16):
            for t in range(8):
                start = k * CLASSES + t * 128
                f, s = start // 128, start % 128
                need = min(128, CLASSES - t * 128)
                value = flat_ref[pl.ds(base + f, count, stride=CLASSES // 8), :]
                if s:
                    value = pltpu.roll(value, 128 - s, 1)
                    if need > 128 - s:
                        after = flat_ref[pl.ds(base + f + 1, count, stride=CLASSES // 8), :]
                        value = jnp.where(lane < 128 - s, value, pltpu.roll(after, 128 - s, 1))
                if need < 128:
                    value = jnp.where(lane < need, value, 0.0)
                wide_ref[t, pl.ds(k, count, stride=16), :] = value
        for t in range(8):
            head_ref[:, t * 128:(t + 1) * 128] = wide_ref[t].astype(BF)

    def spread0_first():
        send0[2]()
        spread0()

    def spread_last():
        send1[2]()
        spread2()
    send0[1]()
    ahead = [moves[2:4], [], moves[4:6], [], [], []]
    extras = [[more_low], [more_head, spread0_first, send1[0]], [], [more_small, spread1, send1[1]], [], [spread_last]]
    kept.wait()
    writes = []
    for g in range(6):
        moves[g].wait()
        begin(ahead[g])
        x2 = dot(perm_ref[...], x_ref[:, g * 384:(g + 1) * 384]).astype(BF)
        xp_ref[g] = x2
        for q in range(4):
            o = dot(x2, wbig_ref[:, q * 256:(q + 1) * 256])
            st_ref[2 * q] = o[:, :128]
            st_ref[2 * q + 1] = o[:, 128:]
        v = st_ref[...].reshape(8 * 288, 128) + bias_stem
        xhat, _s = stats(v, C1, mask1)
        y = xhat * gain_stem + shift_stem
        xhat, _s = stats(y, C1, mask1)
        low = (xhat * gain_one + shift_one).astype(BF).reshape(8, 288, 128)
        for j in range(8):
            n1_ref[g, :, j * 128:(j + 1) * 128] = low[j]
        for q in range(4):
            lanes = slice(q * 256, (q + 1) * 256)
            s2_ref[g, q] = dot(n1_ref[g, 0:144, lanes], d1_ref[0]) + dot(n1_ref[g, 144:288, lanes], d1_ref[1]) + bias_one
        for ref, out, at in ((xp_ref, xp_out, 0), (n1_ref, n1_out, 6), (s2_ref, s2_out, 12)):
            writes.append(pltpu.make_async_copy(ref.at[g], out.at[g], out_sem.at[at + g]))
            writes[-1].start()
        xhat, _s = stats(s2_ref[g].reshape(4 * 144, 256), C2, mask2)
        n2 = xhat * gain_two + shift_two
        for q in range(4):
            c2, oc2 = q // 2, q % 2
            for or2 in range(2):
                at = q * 144 + or2 * 72
                n2s_ref[or2, c2 * 72:(c2 + 1) * 72, oc2 * 256:(oc2 + 1) * 256] = n2[at:at + 72]
        rows = slice(g * 144, (g + 1) * 144)
        low0, low1 = n2s_ref[0].astype(BF), n2s_ref[1].astype(BF)
        n2_ref[0, rows, :] = low0
        n2_ref[1, rows, :] = low1
        writes.append(pltpu.make_async_copy(n2_ref.at[:, pl.ds(g * 144, 144), :], n2_out.at[:, pl.ds(g * 144, 144), :],
                                            out_sem.at[18 + g]))
        writes[-1].start()
        res_ref[rows, :] = dot(low0, d2_ref[0]) + dot(low1, d2_ref[1]) + v3_ref[0:1, :]
        for extra in extras[g]:
            extra()
    end(writes)
    keep_low.wait()


def opening(planes, flat, vector, master, keep_mask, pix, perm):
    kept = [(6, 288, 384), (6, 288, 1024), (6, 4, 144, 256), (2, ROWS, 512)]
    types = [BF, BF, F32, BF]
    half = sds((2, C3, HID // 2), BF)
    each = lambda shape: [sds(shape)] * LAYERS
    outs = ([sds((ROWS, C3)), sds((384, 1024), BF), sds((2, 256, 256), BF), sds((2, 512, C3), BF), sds((C3, WIDE), BF),
             sds((8, 128)), sds((8, 256)), sds((8, C3)), sds((2, C3)), sds((1, WIDE))]
            + each((3 * TAPS, 128)) + each((8, C3)) + each((1, HID)) + each((COL, C3)) + [half, half])
    return call(
        functools.partial(open_kernel, planes),
        listed(VM, flat, vector) + listed(AN, master) + listed(SM, keep_mask) + listed(AN, pix) + listed(VM, perm),
        listed(AN, *[sds(a, b) for a, b in zip(kept, types)], half, half, sds((C3 // 2, HID // 2), BF)) + listed(VM, *outs),
        [pltpu.VMEM((8, C3, 128), F32), pltpu.VMEM((ceil_to(PADDED_LINES, 8), 128), F32),
         pltpu.VMEM((LAYERS, 2, C3, HID // 2), F32), pltpu.SemaphoreType.DMA((LAYERS,)), pltpu.VMEM((2, C3, HID // 2), BF),
         pltpu.VMEM((4 * COL, 4 * SIDE * PATCH), BF)]
        + [pltpu.VMEM(a, b) for a, b in zip(kept, types)]
        + [pltpu.VMEM((8, 288, 128), F32), pltpu.VMEM((2, 144, 512), F32), pltpu.SemaphoreType.DMA((2, 6)),
           pltpu.SemaphoreType.DMA((27,)), pltpu.SemaphoreType.DMA((2, 3 + 2 * PARTS)), pltpu.VMEM((C3 // 2, HID // 2), BF)],
        4_000_000_000, 6,
    )


def finish_kernel(planes, p0_ref, p1_ref, p2_ref, tail_ref, dvs_ref, dv2_ref, dv3_ref, dvec0_ref, dvec1_ref, dvec2_ref,
                  dbin0_ref, dbin1_ref, dbin2_ref, dfinal_ref, dbias_ref, loss_ref, head_ref, two_ref, one_ref,
                  own_ref, flat_ref, vector_ref, info_ref,
                  grad_ref, full_ref, line_ref, arrived_ref, move_sem, local_sem, *scratch):
    net = Net(planes)
    m, d = net.m, net.d
    dp = 4 * planes
    pieces_ref, dvec_ref, dbin_ref = (p0_ref, p1_ref, p2_ref), (dvec0_ref, dvec1_ref, dvec2_ref), (dbin0_ref, dbin1_ref, dbin2_ref)
    shard = grad_ref.shape[4]
    targets = [((l * dp + d) // 3, (l * dp + d) % 3) for l in range(LAYERS)]
    sources = [(3 * d + s) % dp for s in range(LAYERS)]
    for s in range(LAYERS):
        @pl.when(sources[s] != d)
        def _(s=s):
            net.signal((sources[s], m))
    peers = [peer for _, peer in net.all_plane] + net.column
    for peer in peers:
        net.signal(peer)
    awaited = len(peers)
    for l in range(LAYERS):
        awaited = awaited + jnp.where(targets[l][0] != d, 1, 0)
    pl.semaphore_wait(pltpu.get_barrier_semaphore(), awaited)

    def move(l):
        owner, slot = targets[l]
        return pltpu.make_async_remote_copy(
            src_ref=pieces_ref[l], dst_ref=arrived_ref.at[slot], send_sem=move_sem.at[0, l],
            recv_sem=move_sem.at[1, slot], device_id=(owner, m), device_id_type=pl.DeviceIdType.MESH)

    def keep(l):
        return pltpu.make_async_copy(pieces_ref[l], arrived_ref.at[targets[l][1]], local_sem.at[l])

    for l in range(LAYERS):
        @pl.when(targets[l][0] != d)
        def _(l=l):
            move(l).start()

        @pl.when(targets[l][0] == d)
        def _(l=l):
            keep(l).start()
    squares = jnp.zeros((8, 128), F32)
    for l in range(LAYERS):
        piece = pieces_ref[l][...].astype(F32)
        line = jnp.sum(piece * piece, axis=0, keepdims=True)
        for n in range(6):
            squares = squares + jnp.concatenate([line[:, n * 128:(n + 1) * 128], jnp.zeros((7, 128), F32)], axis=0)
    square = jnp.sum(squares, axis=(0, 1), keepdims=True)
    lead = STEM_LINES
    line_ref[0:lead, :] = tail_ref[...]
    line_ref[lead:, :] = jnp.zeros((8 * planes * shard - lead, 128), F32)

    def place(name, start, value):
        row = lead + VECTOR_PLAN[name][2] + start
        for n in range(value.shape[1] // 128):
            line_ref[row + n:row + n + 1, :] = value[:, n * 128:(n + 1) * 128]
    for n, name in enumerate(("bias_stem", "gain_stem", "shift_stem", "gain_one", "shift_one")):
        place(name, 0, dvs_ref[n:n + 1, :])
    for n, name in enumerate(("bias_one", "gain_two", "shift_two")):
        place(name, 0, dv2_ref[n:n + 1, :])
    place("bias_two", 0, dv3_ref[...])
    for l in range(LAYERS):
        for n, name in enumerate(("bias_depth", "gain_block", "shift_block", "bias_outer", "layer_scale")):
            place(name, 3 * l, dvec_ref[l][n:n + 1, :])
        sums = jnp.sum(dbin_ref[l][...], axis=0, keepdims=True)
        for n in range(12):
            part = (n // 6 + m) % 2
            row = lead + VECTOR_PLAN["bias_inner"][2] + 12 * l + part * 6 + n % 6
            line_ref[pl.ds(row, 1), :] = sums[:, n * 128:(n + 1) * 128]
    place("gain_final", 0, dfinal_ref[0:1, :])
    place("shift_final", 0, dfinal_ref[1:2, :])
    place("bias_head", 0, dbias_ref[...])
    lane = lax.broadcasted_iota(jnp.int32, (1, 128), 1)
    info = jnp.where(lane == 2, square, loss_ref[...])
    line_ref[lead + PADDED_LINES:lead + PADDED_LINES + 1, :] = info

    def each_shard(move_one):
        for mm in range(2):
            for yy in range(2):
                for cc in range(2):
                    for k in range(planes):
                        move_one((mm, yy, cc, k), ((((mm * 2 + yy) * 2 + cc) * planes) + k))

    def pack(where, n):
        grad_ref[where] = line_ref[n * shard:(n + 1) * shard, :]
    each_shard(pack)
    steps = tail_steps(net, grad_ref, full_ref, *scratch)
    steps[0]()

    def unpack_big(ref, base, lines):
        size = ref.shape[4]
        sums = [jnp.zeros((8, 128), F32)]

        def inner(where, n):
            at = n * size
            if at < lines:
                rows = min(size, lines - at)
                value = ref[where].astype(F32)
                flat_ref[base + at:base + at + rows, :] = value[0:rows]
                sums[0] = sums[0] + fold8(value * value)
        each_shard(inner)
        return jnp.sum(sums[0], axis=0, keepdims=True)
    total = unpack_big(two_ref, STEM_LINES + ONE_LINES, TWO_LINES + KERN_LINES)
    steps[1]()
    total = total + unpack_big(head_ref, STEM_LINES + ONE_LINES + TWO_LINES + KERN_LINES, HEAD_LINES)
    steps[2]()
    total = total + unpack_big(one_ref, STEM_LINES, ONE_LINES)
    for step in steps[3:]:
        step()

    def unpack(where, n):
        line_ref[n * shard:(n + 1) * shard, :] = full_ref[where]
    each_shard(unpack)
    value = line_ref[0:lead, :]
    flat_ref[0:lead, :] = value
    total = total + jnp.sum(value * value, axis=0, keepdims=True)
    value = line_ref[lead:lead + PADDED_LINES, :]
    total = total + jnp.sum(value * value, axis=0, keepdims=True)
    info = line_ref[lead + PADDED_LINES:lead + PADDED_LINES + 1, :]
    pick = lambda n: jnp.sum(jnp.where(lane == n, info, 0.0), axis=1, keepdims=True)
    count = jnp.maximum(pick(1), 1.0)
    norm = jnp.sqrt(jnp.sum(total, axis=1, keepdims=True) + pick(2)) / count
    factor = CLIP_LIMIT / jnp.maximum(norm, CLIP_LIMIT) / count
    info_ref[...] = jnp.where(lane == 0, pick(0), jnp.where(lane == 1, count, jnp.where(lane == 2, norm, factor)))
    vector_ref[...] = jnp.zeros_like(vector_ref)
    for name in VECTOR_NAMES:
        offset, width, row = VECTOR_PLAN[name]
        lines = ceil_to(width, 128) // 128
        at, s = offset // 128, offset % 128
        lane8 = lax.broadcasted_iota(jnp.int32, (lines, 128), 1)
        value = line_ref[lead + row:lead + row + lines, :]
        if s:
            value = pltpu.roll(value, s, 1)
            vector_ref[at:at + lines, :] += jnp.where(lane8 < s, 0.0, value)
            vector_ref[at + 1:at + 1 + lines, :] += jnp.where(lane8 < s, value, 0.0)
        else:
            vector_ref[at:at + lines, :] += value
    for l in range(LAYERS):
        @pl.when(targets[l][0] != d)
        def _(l=l):
            move(l).wait_send()

        @pl.when(targets[l][0] == d)
        def _(l=l):
            keep(l).wait()
    for s in range(LAYERS):
        @pl.when(sources[s] != d)
        def _(s=s):
            pltpu.make_async_remote_copy(
                src_ref=pieces_ref[s], dst_ref=arrived_ref.at[s], send_sem=move_sem.at[0, s],
                recv_sem=move_sem.at[1, s], device_id=(sources[s], m), device_id_type=pl.DeviceIdType.MESH).wait_recv()
    own_ref[...] = arrived_ref[...]


def finish(planes, pieces, tail, dvs, dv2, dv3, dvec, dbin, dfinal, dbias, loss, head_sum, two_sum, one_sum):
    shard = ceil_to(TAIL_LINES, 8 * planes * 8) // (8 * planes)
    shape = (2, 2, 2, planes, shard, 128)
    held = (LAYERS,) + pieces[0].shape
    return call(
        functools.partial(finish_kernel, planes),
        listed(VM, *pieces, tail, dvs, dv2, dv3, *dvec, *dbin, dfinal, dbias, loss, head_sum, two_sum, one_sum),
        listed(VM, sds(held, BF), sds((FLAT_LINES, 128)), sds((VECTOR_LINES, 128)), sds((1, 128))),
        [pltpu.VMEM(shape, F32), pltpu.VMEM(shape, F32),
         pltpu.VMEM((8 * planes * shard, 128), F32),
         pltpu.VMEM(held, BF), pltpu.SemaphoreType.DMA((2, LAYERS)), pltpu.SemaphoreType.DMA((LAYERS,))]
        + tail_scratch(planes, shard, F32),
        0, 4,
    )


LEARN_RATE = 0.05
VECTOR_RATE = 0.15
WEIGHT_DECAY = 0.05
BETA_ONE = 0.9
BETA_TWO = 0.999
ADAM_EPSILON = 1e-08


def vector_lengths():
    return list(VECTOR_WIDTHS)


def flat_lengths():
    return [PATCH * C1, 4 * C1 * C2, 4 * C2 * C3, LAYERS * TAPS * C3, C3 * CLASSES]


def adam_update(weight, moment_one, moment_two, gradient, step_float, rate):
    first_new = BETA_ONE * moment_one + (1.0 - BETA_ONE) * gradient
    second_new = BETA_TWO * moment_two + (1.0 - BETA_TWO) * gradient * gradient
    first_hat = first_new / (1.0 - BETA_ONE**step_float)
    second_hat = second_new / (1.0 - BETA_TWO**step_float)
    weight_new = weight - rate * (first_hat / (jnp.sqrt(second_hat) + ADAM_EPSILON) + WEIGHT_DECAY * weight)
    return (weight_new, first_new, second_new, weight_new.astype(BF))


def row_source():
    target = np.arange(4 * COL)
    img = target % IMG
    r = target // IMG % SIDE
    or2 = target // COL % 2
    or1 = target // (2 * COL)
    row = 4 * r + 2 * or2 + or1
    return (row // (2 * SIDE)) * (2 * COL) + img * (2 * SIDE) + row % (2 * SIDE)


def per_device(pixels, labels, valid_flags, keep_mask, step_count, pointwise_weight, pointwise_first, pointwise_second,
               flat_weight, flat_first, flat_second, vector_weight, vector_first, vector_second):
    dp = lax.axis_size("dp")
    planes = dp // 4
    vectors = jnp.pad(vector_weight, (0, VECTOR_LINES * 128 - VECTOR)).reshape(VECTOR_LINES, 128)
    perm = jnp.asarray(row_source()[:, None] == np.arange(4 * COL)[None], BF)
    pix = pixels.reshape(4 * COL, 4 * SIDE * PATCH)
    ready = opening(planes, flat_weight.reshape(FLAT_LINES, 128), vectors, pointwise_weight, keep_mask, pix, perm)
    xp, n1, s2, n2, far, low0, quarter, res, wbig, d1, d2, head_low, vs, v2, v3, hv, hb = ready[:17]
    kern, vec, bins, keep = [ready[17 + LAYERS * n:17 + LAYERS * (n + 1)] for n in range(4)]
    low = [low0] + list(ready[17 + 4 * LAYERS:])
    kept = []
    for l in range(LAYERS):
        more = (quarter, low[2]) if l == 0 else (quarter,) if l == 1 else ()
        new, depth, normed, act, dg, out, *arrived = block(planes, res, kern[l], vec[l], bins[l], keep[l], low[l], far, *more)
        kept.append((keep[l], vec[l], kern[l], act, dg, out, normed, depth, res, low[l], far))
        res = new
        if l == 0:
            far, quarter = arrived
        elif l == 1:
            far, = arrived
    shard = ceil_to(HEAD_LINES, 8 * planes * 16) // (8 * planes)
    dr, dhead, dbias, dfinal, loss = head(res, hv, head_low, hb, labels, valid_flags, 8 * planes * shard)
    blocked = lambda a: a.reshape(planes, 2, 2, 2 * C3 // dp, HID // 2)
    dkern, dvec, dbin = [None] * LAYERS, [None] * LAYERS, [None] * LAYERS
    dr, own, other, dkern[2], dvec[2], dbin[2], head_shard = block_back(
        planes, 0, (dr,) + kept[2], dhead.reshape(2, 2, 2, planes, shard, 128))
    dr, own_new, other_new, dkern[1], dvec[1], dbin[1], held, head_sum = block_back(
        planes, 1, (dr,) + kept[1], blocked(own), blocked(other), head_shard)
    dr, own, other, dkern[0], dvec[0], dbin[0], held, piece2 = block_back(
        planes, 2, (dr,) + kept[0], blocked(own_new), blocked(other_new), held)
    tail, dvs, dv2, dv3, two_sum, piece0, piece1, one_sum = back(
        planes, dr, (xp, n1, s2, n2), (wbig, d1, d2, vs, v2), dkern, blocked(own), blocked(other), held)
    pointwise_own, flat_sum, vector_sum, info = finish(
        planes, (piece0, piece1, piece2), tail, dvs, dv2, dv3, dvec, dbin, dfinal, dbias, loss, head_sum, two_sum,
        one_sum)
    loss_total, valid_total, gradient_norm, factor = info[0, 0], info[0, 1], info[0, 2], info[0, 3]
    pointwise_own = pointwise_own.reshape(pointwise_first.shape).astype(F32)
    flat_sum = flat_sum.reshape(-1)
    vector_sum = vector_sum.reshape(-1)[:VECTOR]
    step_float = step_count.astype(F32)
    rows_owned = pointwise_first.shape[0]
    master_rows = pointwise_weight.reshape(2 * LAYERS * C3, HID // 2)
    master_own = lax.dynamic_slice_in_dim(master_rows, lax.axis_index("dp") * rows_owned, rows_owned, 0)
    pointwise_out = adam_update(master_own, pointwise_first, pointwise_second, factor * pointwise_own, step_float, LEARN_RATE)
    flat_out = adam_update(flat_weight, flat_first, flat_second, factor * flat_sum, step_float, LEARN_RATE)
    vector_out = adam_update(vector_weight, vector_first, vector_second, factor * vector_sum, step_float, VECTOR_RATE)
    return (loss_total, valid_total, gradient_norm, *pointwise_out, *flat_out, *vector_out)


def solution(mesh):
    placed = (P("dp", "mp", None), P("dp"), P("dp"), P(None, "dp"), P(), P(None, None, None, "mp"), P("dp", "mp"),
              P("dp", "mp"), P(), P(), P(), P(), P(), P())
    return jax.shard_map(
        per_device,
        mesh=mesh,
        in_specs=placed,
        out_specs=(P(), P(), P()) + (P("dp", "mp"),) * 4 + (P(),) * 8,
        check_vma=False,
    )
```

```python
import functools
import jax
import numpy as np
from jax.sharding import PartitionSpec as P
import jax.numpy as jnp
from jax import lax
from jax.experimental import pallas as pl
from jax.experimental.pallas import tpu as pltpu

C1 = 96
C2 = 192
C3 = 384
HID = 1536
CLASSES = 1000
PATCH = 48
KERNEL = 7
LAYERS = 3
SIDE = 12
NORM_EPSILON = 1e-06
SMOOTH = 0.1
CLIP_LIMIT = 0.02
IMG = 6
COL = SIDE * IMG
ROWS = SIDE * COL
PAIR = 2 * COL
FORE = 432
REAR = 288
WF = 256
WB = 256
BF = jnp.bfloat16
F32 = jnp.float32
VMEM_LIMIT = 60 * 1024 * 1024
SHIFTED = COL + 40
TAPS = KERNEL * KERNEL
WIDE = 1024
STEM_LINES = PATCH * C1 // 128
ONE_LINES = 4 * C1 * C2 // 128
TWO_LINES = 4 * C2 * C3 // 128
KERN_LINES = LAYERS * TAPS * C3 // 128
HEAD_LINES = C3 * CLASSES // 128
FLAT_LINES = STEM_LINES + ONE_LINES + TWO_LINES + KERN_LINES + HEAD_LINES


def dot(a, b, da=1, db=0):
    return lax.dot_general(a, b, (((da,), (db,)), ((), ())), preferred_element_type=F32)


def fold8(values):
    rows, lanes = values.shape
    return jnp.sum(values.reshape(rows // 8, 8, lanes), axis=0)


def stats(values, count, mask):
    average = jnp.sum(values, axis=-1, keepdims=True) * (1.0 / count)
    centred = values - average
    if mask is not None:
        centred = centred * mask
    spread = jnp.sum(centred * centred, axis=-1, keepdims=True) * (1.0 / count)
    scale = lax.rsqrt(spread + NORM_EPSILON)
    return centred * scale, scale


def norm_back(delta, xhat, scale, gain, count, mask):
    scaled = delta * gain
    first = jnp.sum(scaled, axis=-1, keepdims=True) * (1.0 / count)
    second = jnp.sum(scaled * xhat, axis=-1, keepdims=True) * (1.0 / count)
    out = (scaled - first - xhat * second) * scale
    if mask is not None:
        out = out * mask
    return out


def sds(shape, dt=F32):
    return jax.ShapeDtypeStruct(shape, dt)


VM, AN, SM = pltpu.VMEM, pl.ANY, pltpu.SMEM


def call(kernel, ins, outs, scratch, flops=0, collective=None):
    params = pltpu.CompilerParams(vmem_limit_bytes=VMEM_LIMIT)
    if collective is not None:
        params = pltpu.CompilerParams(vmem_limit_bytes=VMEM_LIMIT, collective_id=collective, has_side_effects=True)
    return pl.pallas_call(
        kernel,
        in_specs=[pl.BlockSpec(memory_space=space) for _, space in ins],
        out_specs=[pl.BlockSpec(memory_space=space) for _, space in outs],
        out_shape=[shape for shape, _ in outs],
        scratch_shapes=scratch,
        cost_estimate=pl.CostEstimate(flops=flops, bytes_accessed=0, transcendentals=0),
        compiler_params=params,
    )(*[array for array, _ in ins])


def listed(space, *arrays):
    return [(array, space) for array in arrays]


def spread_shifted(cp_ref, lt, c, val):
    for ki in range(4):
        cp_ref[ki, lt, c, 18 - 2 * ki:90 - 2 * ki, :] = val


def zero_edges(cp_ref):
    head, tail = jnp.zeros((24, 128), F32), jnp.zeros((32, 128), F32)
    for ki in range(4):
        for lt in range(3):
            def body(c, _):
                cp_ref[ki, lt, c, 0:24, :] = head
                cp_ref[ki, lt, c, 80:112, :] = tail
                return 0
            lax.fori_loop(0, 12, body, 0)


def gate(h):
    phi_wide = 0.5 * (1.0 + lax.erf(h * 0.7071067811865476))
    dens = jnp.exp(h * h * -0.5) * 0.3989422804014327
    return h * phi_wide, phi_wide + h * dens


PARTS = 4


def weight_send(net, low, quarter, sems, base):
    size = C3 // 2 // PARTS
    k = net.z % PARTS
    part = pl.ds(pl.multiple_of(k * size, 16), size)
    rows = pl.ds(pl.multiple_of(net.y * (C3 // 2) + k * size, 16), size)
    across = remote(low.at[net.c, rows, :], quarter.at[part, :], sems, base, net.plane[0])
    along = [remote(quarter.at[part, :], quarter.at[part, :], sems, base + o, net.four[o - 1]) for o in range(1, PARTS)]

    def step1():
        across.wait()
        begin(along)

    return across.start, step1, lambda: end(along)


def weight_spread(net, quarter, far, sems, local_sem):
    c, y = net.c, net.y
    mine = far.at[c, pl.ds(pl.multiple_of(y * (C3 // 2), 16), C3 // 2), :]
    theirs = far.at[c, pl.ds(pl.multiple_of((1 - y) * (C3 // 2), 16), C3 // 2), :]
    own = pltpu.make_async_copy(quarter, mine, local_sem)
    first = [remote(quarter, mine, sems, 0, net.plane[1]), remote(quarter, mine, sems, 1, net.core)]
    second = remote(theirs, theirs, sems, 2, net.core)

    def step0():
        own.start()
        begin(first)

    def step1():
        first[0].wait()
        second.start()

    def step2():
        own.wait()
        first[1].wait()
        second.wait()

    return step0, step1, step2


def block_kernel(planes, *refs):
    res_ref, kern_ref, vec_ref, bin_ref, keep_ref, own_any, other_any = refs[:7]
    spread, sent = planes
    planes = max(planes)
    refs = refs[7:]
    if spread:
        quarter_ref, refs = refs[0], refs[1:]
    if sent:
        low_ref, refs = refs[0], refs[1:]
    new_ref, depth_out, normed_out, act_out, dg_out, out_out = refs[:6]
    refs = refs[6:]
    if spread:
        far_out, refs = refs[0], refs[1:]
    if sent:
        quarter_out, refs = refs[0], refs[1:]
    cp_ref, wb_ref, own_ref, other_ref, depth_ref, normed_ref, act_ref, dg_ref, out_ref, in_sem, out_sem = refs[:11]
    loads = [pltpu.make_async_copy(own_any, own_ref, in_sem.at[0]), pltpu.make_async_copy(other_any, other_ref, in_sem.at[1])]
    begin(loads)
    nothing = lambda: None
    spread0 = spread1 = spread2 = send1 = send2 = nothing
    if planes:
        net = Net(planes)
        peers = [net.core] + net.plane[:2] + net.four
        if not sent:
            peers = [net.core, net.plane[1]]
        for peer in peers:
            net.signal(peer)
        pl.semaphore_wait(pltpu.get_barrier_semaphore(), len(peers))
        spread0, spread1, spread2 = weight_spread(net, quarter_ref, far_out, refs[11], in_sem.at[2])
        spread0()
        if sent:
            send0, send1, send2 = weight_send(net, low_ref, quarter_out, refs[11], 3)
            send0()
    zero_edges(cp_ref)

    def prep_rows(c, _):
        rows = pl.ds(pl.multiple_of(c * COL, 8), COL)
        for lt in range(3):
            val = res_ref[rows, lt * 128:(lt + 1) * 128].astype(BF).astype(F32)
            spread_shifted(cp_ref, lt, c, val)
        return 0
    lax.fori_loop(0, SIDE, prep_rows, 0)
    for lt in range(3):
        for t in range(TAPS):
            wb_ref[lt, t] = jnp.broadcast_to(kern_ref[3 * t + lt:3 * t + lt + 1, :], (8, 128))
    for lt in range(3):
        lanes = slice(lt * 128, (lt + 1) * 128)
        bias = jnp.broadcast_to(vec_ref[0:1, lanes], (8, 128))

        def conv(v, _, lt=lt, lanes=lanes, bias=bias):
            acc = [bias] * SIDE
            for i in range(KERNEL):
                k = (6 * i) % 8
                row = pl.ds(pl.multiple_of(6 * i - k + v * 8, 8), 8)
                xs = [cp_ref[k // 2, lt, c, row, :] for c in range(SIDE)]
                for j in range(KERNEL):
                    w = wb_ref[lt, i * KERNEL + j]
                    for c in range(SIDE):
                        cc = c + j - 3
                        if 0 <= cc < SIDE:
                            acc[c] = acc[c] + w * xs[cc]
            for c in range(SIDE):
                depth_ref[pl.ds(pl.multiple_of(c * COL + v * 8, 8), 8), lanes] = acc[c]
            return 0
        lax.fori_loop(0, COL // 8, conv, 0)
        if lt == 0:
            send1()
    writes = [pltpu.make_async_copy(depth_ref, depth_out, out_sem.at[0])]
    writes[0].start()
    gain, shift = vec_ref[1:2, :], vec_ref[2:3, :]
    for r in range(ROWS // FORE):
        rows = slice(r * FORE, (r + 1) * FORE)
        xhat, _s = stats(depth_ref[rows, :], C3, None)
        normed_ref[rows, :] = (xhat * gain + shift).astype(BF)
    writes.append(pltpu.make_async_copy(normed_ref, normed_out, out_sem.at[1]))
    writes[1].start()
    bias_out, scale = vec_ref[3:4, :], vec_ref[4:5, :]
    keep_scale = keep_ref[...] * scale
    end(loads)
    for m in range(ROWS // FORE):
        rows, at_rows = slice(m * FORE, (m + 1) * FORE), pl.ds(m * FORE, FORE)
        low = normed_ref[rows, :]
        for n in range(HID // WF):
            lanes = slice(n * WF, (n + 1) * WF)
            half = own_ref if n * WF < HID // 2 else other_ref
            at = n * WF % (HID // 2)
            h = dot(low, half[0, :, at:at + WF]) + bin_ref[:, lanes]
            act, dg = gate(h)
            act_ref[rows, lanes] = act.astype(BF)
            dg_ref[rows, lanes] = dg.astype(BF)
            if n == HID // WF // 2 - 1 or n == HID // WF - 1:
                side = pl.ds(0 if n < HID // WF - 1 else HID // 2, HID // 2)
                for ref, out in ((act_ref, act_out), (dg_ref, dg_out)):
                    writes.append(pltpu.make_async_copy(ref.at[at_rows, side], out.at[at_rows, side], out_sem.at[len(writes)]))
                    writes[-1].start()
        if m == 0:
            spread1()
        o = (dot(act_ref[rows, :HID // 2], own_ref[1], 1, 1) + dot(act_ref[rows, HID // 2:], other_ref[1], 1, 1)
             + bias_out)
        out_ref[rows, :] = o
        writes.append(pltpu.make_async_copy(out_ref.at[at_rows, :], out_out.at[at_rows, :], out_sem.at[len(writes)]))
        writes[-1].start()
        new_ref[rows, :] = res_ref[rows, :] + jnp.concatenate([keep_scale] * (FORE // COL), axis=0) * o
    end(writes)
    spread2()
    send2()


def block(planes, res, kern, vec, bin_, keep, own, other, quarter=None, low=None):
    half = (2, C3, HID // 2)
    kept = [sds((ROWS, C3)), sds((ROWS, C3), BF), sds((ROWS, HID), BF), sds((ROWS, HID), BF), sds((ROWS, C3))]
    outs = listed(VM, sds((ROWS, C3))) + listed(AN, *kept)
    ins = listed(VM, res, kern, vec, bin_, keep) + listed(AN, own, other)
    scratch = [pltpu.VMEM((4, 3, SIDE, SHIFTED, 128), F32), pltpu.VMEM((3, TAPS, 8, 128), F32),
               pltpu.VMEM(half, BF), pltpu.VMEM(half, BF)]
    scratch += [pltpu.VMEM(k.shape, k.dtype) for k in kept]
    scratch += [pltpu.SemaphoreType.DMA((3,)), pltpu.SemaphoreType.DMA((2 + 5 * ROWS // FORE,))]
    collective = None
    if quarter is not None:
        ins = ins + listed(AN, quarter)
        outs = outs + listed(AN, sds(half, BF))
        scratch.append(pltpu.SemaphoreType.DMA((2, 3 + PARTS)))
        collective = 7
    if low is not None:
        ins = ins + listed(AN, low)
        outs = outs + listed(AN, sds((C3 // 2, HID // 2), BF))
        collective = 8
    part = (planes if quarter is not None else 0, planes if low is not None else 0)
    return call(functools.partial(block_kernel, part), ins, outs, scratch, 4_000_000_000, collective)


def head_flatten(wide_ref, line_ref):
    lane = lax.broadcasted_iota(jnp.int32, (C3 // 16, 128), 1)

    def tile(k, t, shift):
        value = wide_ref[t, pl.ds(k, C3 // 16, stride=16), :]
        return pltpu.roll(value, shift % 128, 1) if shift % 128 else value

    for f in range(CLASSES // 8):
        k, col = f * 128 // CLASSES, f * 128 % CLASSES
        t, s = col // 128, col % 128
        take = min(128, CLASSES - col)
        value = tile(k, t, 128 - s)
        if s and t < 7:
            value = jnp.where(lane < 128 - s, value, tile(k, t + 1, 128 - s))
        if take < 128:
            value = jnp.where(lane < take, value, tile(k + 1, 0, take))
        line_ref[pl.ds(f, C3 // 16, stride=CLASSES // 8), :] = value


def head_kernel(res_ref, vec_ref, head_ref, bias_ref, label_ref, valid_ref,
                dr_ref, dhead_ref, dbias_ref, dvec_ref, loss_ref, sum_ref, wide_ref, line_ref):
    def add(c, total):
        return total + res_ref[pl.ds(pl.multiple_of(c * COL, 8), COL), :]
    total = lax.fori_loop(1, SIDE, add, res_ref[0:COL, :])
    sum_ref[...] = total
    pooled = sum_ref[0:IMG, :]
    for r in range(1, SIDE):
        pooled = pooled + sum_ref[r * IMG:(r + 1) * IMG, :]
    pooled = jnp.concatenate([pooled * (1.0 / (SIDE * SIDE)), jnp.zeros((2, C3), F32)], axis=0)
    gain, shift = vec_ref[0:1, :], vec_ref[1:2, :]
    xhat, scale = stats(pooled, C3, None)
    final = (xhat * gain + shift).astype(BF)
    real = lax.broadcasted_iota(jnp.int32, (8, WIDE), 1) < CLASSES
    logits = jnp.where(real, dot(final, head_ref[...]) + bias_ref[...], -1e30)
    top = jnp.max(logits, axis=-1, keepdims=True)
    shifted = logits - top
    expd = jnp.exp(shifted)
    total = jnp.sum(expd, axis=-1, keepdims=True)
    log_chance = jnp.where(real, shifted - jnp.log(total), 0.0)
    spot = lax.broadcasted_iota(jnp.int32, (8, 1), 0)
    first_image = lax.axis_index("mp") * IMG
    label, valid = jnp.zeros((8, 1), jnp.int32), jnp.zeros((8, 1), jnp.int32)
    for n in range(IMG):
        label = jnp.where(spot == n, label_ref[first_image + n], label)
        valid = jnp.where(spot == n, valid_ref[first_image + n], valid)
    valid = valid.astype(F32)
    onehot = (label == lax.broadcasted_iota(jnp.int32, (8, WIDE), 1)).astype(F32)
    per_image = (-(1.0 - SMOOTH) * jnp.sum(log_chance * onehot, axis=-1, keepdims=True)
                 - (SMOOTH / CLASSES) * jnp.sum(log_chance, axis=-1, keepdims=True))
    lane = lax.broadcasted_iota(jnp.int32, (1, 128), 1)
    loss_ref[...] = jnp.where(lane == 0, jnp.sum(per_image * valid, axis=0, keepdims=True),
                              jnp.where(lane == 1, jnp.sum(valid, axis=0, keepdims=True), 0.0))
    delta = jnp.where(real, (jnp.exp(log_chance) - (1.0 - SMOOTH) * onehot - SMOOTH / CLASSES) * valid, 0.0)
    dbias_ref[...] = jnp.sum(delta, axis=0, keepdims=True)
    high = delta.astype(BF)
    rest = (delta - high.astype(F32)).astype(BF)
    for t in range(8):
        lanes = slice(t * 128, (t + 1) * 128)
        wide_ref[t] = dot(final, high[:, lanes], 0, 0) + dot(final, rest[:, lanes], 0, 0)
    head_flatten(wide_ref, line_ref)
    line_ref[HEAD_LINES:, :] = jnp.zeros((line_ref.shape[0] - HEAD_LINES, 128), F32)
    dhead_ref[...] = line_ref[...].astype(BF)
    dfinal = dot(high, head_ref[...], 1, 1) + dot(rest, head_ref[...], 1, 1)
    dvec_ref[0:1, :] = jnp.sum(dfinal * xhat, axis=0, keepdims=True)
    dvec_ref[1:2, :] = jnp.sum(dfinal, axis=0, keepdims=True)
    dpooled = norm_back(dfinal, xhat, scale, gain, C3, None) * (1.0 / (SIDE * SIDE))
    for r in range(SIDE):
        sum_ref[r * IMG:(r + 1) * IMG, :] = dpooled[0:IMG, :]

    def put(c, _):
        dr_ref[pl.ds(pl.multiple_of(c * COL, 8), COL), :] = sum_ref[...]
        return 0
    lax.fori_loop(0, SIDE, put, 0)


def head(res, vec, head_low, bias, labels, valid, lines):
    return call(
        head_kernel,
        listed(VM, res, vec, head_low, bias) + listed(SM, labels, valid),
        listed(VM, sds((ROWS, C3)), sds((lines, 128), BF), sds((1, WIDE)), sds((2, C3)), sds((1, 128))),
        [pltpu.VMEM((COL, C3), F32), pltpu.VMEM((8, C3, 128), F32), pltpu.VMEM((lines, 128), F32)],
        20_000_000,
    )


def ceil_to(value, step):
    return -(-value // step) * step


class Net:
    def __init__(self, planes):
        self.planes = planes
        self.d = lax.axis_index("dp")
        self.m = lax.axis_index("mp")
        self.c = self.d % 2
        self.y = self.d // 2 % 2
        self.z = self.d // 4
        self.core = (self.d + 1 - 2 * self.c, self.m)
        flip = self.d + 2 - 4 * self.y
        self.plane = [(self.d, 1 - self.m), (flip, self.m), (flip, 1 - self.m)]
        self.all_plane = []
        for k in range(1, 8):
            mm = 1 - self.m if k & 4 else self.m
            yy = 1 - self.y if k & 2 else self.y
            cc = 1 - self.c if k & 1 else self.c
            self.all_plane.append(((mm, yy, cc), (4 * self.z + 2 * yy + cc, mm)))
        group = self.z // 4 * 4
        self.four = [(4 * (group + (self.z % 4 + o) % 4) + 2 * self.y + self.c, self.m) for o in range(1, 4)]
        self.column = [(4 * ((self.z + o) % planes) + 2 * self.y + self.c, self.m) for o in range(1, planes)]

    def signal(self, peer):
        pl.semaphore_signal(pltpu.get_barrier_semaphore(), inc=1, device_id=peer, device_id_type=pl.DeviceIdType.MESH)

    def greet(self, whole=False):
        peers = ([peer for _, peer in self.all_plane] if whole else [self.core] + self.plane) + self.column
        for peer in peers:
            self.signal(peer)
        pl.semaphore_wait(pltpu.get_barrier_semaphore(), len(peers))


def remote(src, dst, sems, number, peer):
    return pltpu.make_async_remote_copy(
        src_ref=src, dst_ref=dst, send_sem=sems.at[0, number], recv_sem=sems.at[1, number],
        device_id=peer, device_id_type=pl.DeviceIdType.MESH)


def begin(copies):
    for copy in copies:
        copy.start()


def end(copies):
    for copy in copies:
        copy.wait()


CHUNKS = 2


def layer_scratch(planes, rows, width):
    part = width // CHUNKS
    return [
        pltpu.VMEM((CHUNKS, 2, planes, 2, rows, part), BF),
        pltpu.VMEM((CHUNKS, 2, 2, planes, rows, part), BF),
        pltpu.VMEM((CHUNKS, 3, planes, rows, part), BF),
        pltpu.VMEM((2, planes, 2, rows, width), BF),
        pltpu.SemaphoreType.DMA((2, 5 * CHUNKS)),
        pltpu.SemaphoreType.DMA((2,)),
    ]


def layer_steps(net, own, other, out, r1, s1, r2, held, sems, held_sem):
    c, y = net.c, net.y
    part = own.shape[4] // CHUNKS
    first, second = [], []
    for k in range(CHUNKS):
        lanes = pl.ds(k * part, part)
        first.append([remote(own.at[:, :, 1 - c, :, lanes], r1.at[k, 0], sems, 5 * k, net.core),
                      remote(other.at[:, :, 1 - c, :, lanes], r1.at[k, 1], sems, 5 * k + 1, net.core)])
        second.append([remote(s1.at[k, 1, y], r2.at[k, 0], sems, 5 * k + 2, net.plane[0]),
                       remote(s1.at[k, 0, 1 - y], r2.at[k, 1], sems, 5 * k + 3, net.plane[1]),
                       remote(s1.at[k, 1, 1 - y], r2.at[k, 2], sems, 5 * k + 4, net.plane[2])])

    loads = [pltpu.make_async_copy(own.at[:, :, c], held.at[0], held_sem.at[0]),
             pltpu.make_async_copy(other.at[:, :, c], held.at[1], held_sem.at[1])]

    def step0():
        begin(first[0])
        begin(loads)

    def step1(k):
        end(first[k])
        if k + 1 < CHUNKS:
            begin(first[k + 1])
        if k == 0:
            end(loads)
        lanes = slice(k * part, (k + 1) * part)

        def add(n, _):
            for yy in range(2):
                s1[k, 0, yy, n] = (held[0, n, yy, :, lanes].astype(F32) + r1[k, 0, n, yy].astype(F32)).astype(BF)
                s1[k, 1, yy, n] = (held[1, n, yy, :, lanes].astype(F32) + r1[k, 1, n, yy].astype(F32)).astype(BF)
            return 0
        lax.fori_loop(0, net.planes, add, 0)
        begin(second[k])

    def step2(k):
        end(second[k])
        lanes = slice(k * part, (k + 1) * part)

        def add(n, _):
            total = s1[k, 0, y, n].astype(F32)
            for j in range(3):
                total = total + r2[k, j, n].astype(F32)
            out[n, :, lanes] = total.astype(BF)
            return 0
        lax.fori_loop(0, net.planes, add, 0)

    return step0, step1, step2


def column_scratch(planes, rows, width):
    return [pltpu.VMEM((planes - 1, rows, width), BF), pltpu.SemaphoreType.DMA((2, planes))]


def column_steps(net, held, out, r3, sems):
    copies = [remote(held.at[(net.z + o) % net.planes], r3.at[o - 1], sems, o - 1, net.column[o - 1])
              for o in range(1, net.planes)]

    def step1():
        end(copies)

        def add(k, total):
            return total + r3[k].astype(F32)
        out[...] = lax.fori_loop(0, net.planes - 1, add, held[net.z].astype(F32)).astype(BF)

    return (lambda: begin(copies)), step1


def flat_scratch(planes, rows, dtype):
    return [
        pltpu.VMEM((2, 2, planes, rows, 128), dtype),
        pltpu.VMEM((2, 2, planes, rows, 128), dtype),
        pltpu.VMEM((3, planes, rows, 128), dtype),
        pltpu.VMEM((planes, rows, 128), dtype),
        pltpu.VMEM((planes - 1, rows, 128), dtype),
        pltpu.SemaphoreType.DMA((2, 3 + planes)),
    ]


def spread_scratch(planes):
    return [pltpu.SemaphoreType.DMA((2, 3 + planes))]


def flat_sum_steps(net, grad, shard, r1, s1, r2, s2, r3, sems):
    c, y, z, m = net.c, net.y, net.z, net.m
    planes = net.planes
    dtype = shard.dtype
    first = [remote(grad.at[:, :, 1 - c], r1, sems, 0, net.core)]
    second = [remote(s1.at[1 - m, y], r2.at[0], sems, 1, net.plane[0]),
              remote(s1.at[m, 1 - y], r2.at[1], sems, 2, net.plane[1]),
              remote(s1.at[1 - m, 1 - y], r2.at[2], sems, 3, net.plane[2])]
    third = [remote(s2.at[(z + o) % planes], r3.at[o - 1], sems, 3 + o, net.column[o - 1]) for o in range(1, planes)]

    def step1():
        end(first)
        for mm in range(2):
            for yy in range(2):
                s1[mm, yy] = (grad[mm, yy, c].astype(F32) + r1[mm, yy].astype(F32)).astype(dtype)
        begin(second)

    def step2():
        end(second)
        total = s1[m, y].astype(F32)
        for n in range(3):
            total = total + r2[n].astype(F32)
        s2[...] = total.astype(dtype)
        begin(third)

    def step3():
        end(third)

        def add(k, total):
            return total + r3[k].astype(F32)
        shard[...] = lax.fori_loop(0, planes - 1, add, s2[z].astype(F32)).astype(dtype)

    return [lambda: begin(first), step1, step2, step3]


def spread_steps(net, shard, out, sems):
    c, y, z, m = net.c, net.y, net.z, net.m
    planes = net.planes
    first = [remote(out.at[m, y, c, z], out.at[m, y, c, z], sems, o - 1, net.column[o - 1]) for o in range(1, planes)]
    second = [remote(out.at[m, y, c], out.at[m, y, c], sems, planes - 1 + k, net.plane[k]) for k in range(3)]
    third = [remote(out.at[:, :, c], out.at[:, :, c], sems, planes + 2, net.core)]

    def step0():
        out[m, y, c, z] = shard[...]
        begin(first)

    def step1():
        end(first)
        begin(second)

    def step2():
        end(second)
        begin(third)

    return [step0, step1, step2, lambda: end(third)]


def tail_scratch(planes, rows, dtype):
    return [
        pltpu.VMEM((7, planes, rows, 128), dtype),
        pltpu.VMEM((planes, rows, 128), dtype),
        pltpu.VMEM((planes - 1, rows, 128), dtype),
        pltpu.SemaphoreType.DMA((2, 12 + 2 * planes)),
    ]


def tail_steps(net, grad, out, r1, s1, r2, sems):
    c, y, z, m = net.c, net.y, net.z, net.m
    planes = net.planes
    dtype = out.dtype
    first = [remote(grad.at[mm, yy, cc], r1.at[n], sems, n, net.all_plane[n][1])
             for n, ((mm, yy, cc), _) in enumerate(net.all_plane)]
    second = [remote(s1.at[(z + o) % planes], r2.at[o - 1], sems, 6 + o, net.column[o - 1]) for o in range(1, planes)]
    third = [remote(out.at[m, y, c, z], out.at[m, y, c, z], sems, 5 + planes + o, net.column[o - 1])
             for o in range(1, planes)]
    fourth = [remote(out.at[m, y, c], out.at[m, y, c], sems, 5 + 2 * planes + n, net.all_plane[n][1]) for n in range(7)]

    def step1():
        end(first)
        total = grad[m, y, c].astype(F32)
        for n in range(7):
            total = total + r1[n].astype(F32)
        s1[...] = total.astype(dtype)
        begin(second)

    def step2():
        end(second)

        def add(k, total):
            return total + r2[k].astype(F32)
        out[m, y, c, z] = lax.fori_loop(0, planes - 1, add, s1[z].astype(F32)).astype(dtype)
        begin(third)

    def step3():
        end(third)
        begin(fourth)

    return [lambda: begin(first), step1, step2, step3, lambda: end(fourth)]


def block_back_body(hooks, dr_ref, keep_ref, vec_ref, kern_ref, act_any, dg_any, out_any, normed_any, depth_any, res_any,
                    own_any, other_any,
                    new_ref, down_any, dother_any, dkern_ref, dvec_ref, dbin_ref,
                    cp_ref, wb_ref, dout_ref, dhid_ref, kacc_ref, act_ref, dg_ref, out_ref, normed_ref, depth_ref, res_ref,
                    own_ref, other_ref, down_ref, dother_ref, in_sem):
    pairs = ((own_any, own_ref), (other_any, other_ref), (dg_any, dg_ref), (depth_any, depth_ref), (act_any, act_ref),
             (normed_any, normed_ref), (out_any, out_ref), (res_any, res_ref))
    load = [pltpu.make_async_copy(a, b, in_sem.at[n]) for n, (a, b) in enumerate(pairs)]
    begin(load[:3])
    hooks = iter(hooks)

    def tick():
        for hook in next(hooks):
            hook()
    tick()
    zero_edges(cp_ref)
    for lt in range(3):
        for t in range(TAPS):
            wb_ref[lt, t] = jnp.broadcast_to(kern_ref[3 * t + lt:3 * t + lt + 1, :], (8, 128))
    kacc_ref[...] = jnp.zeros_like(kacc_ref)
    gain, scale = vec_ref[1:2, :], vec_ref[4:5, :]

    def pre(m, a_bias):
        rows = pl.ds(pl.multiple_of(m * PAIR, 16), PAIR)
        keep = jnp.concatenate([keep_ref[...], keep_ref[...]], axis=0)
        dk = dr_ref[rows, :] * keep
        low = (dk * scale).astype(BF)
        dout_ref[rows, :] = low
        return a_bias + fold8(low.astype(F32))
    zero = jnp.zeros((8, C3), F32)
    a_bias = lax.fori_loop(0, ROWS // PAIR, pre, zero)
    dvec_ref[3:4, :] = jnp.sum(a_bias, axis=0, keepdims=True)
    dbin_ref[...] = jnp.zeros_like(dbin_ref)
    end(load[:3])
    begin(load[3:])

    def mm(m, carry):
        a_gain, a_shift, a_depth = carry
        rows = slice(m * REAR, (m + 1) * REAR)
        low = dout_ref[rows, :]
        for n in range(HID // WB):
            lanes = slice(n * WB, (n + 1) * WB)
            half = own_ref if n * WB < HID // 2 else other_ref
            at = n * WB % (HID // 2)
            d = dot(low, half[1, :, at:at + WB]) * dg_ref[rows, lanes].astype(F32)
            dlow = d.astype(BF)
            dhid_ref[rows, lanes] = dlow
            dbin_ref[:, lanes] += fold8(dlow.astype(F32))
        d = dot(dhid_ref[rows, :HID // 2], own_ref[0], 1, 1) + dot(dhid_ref[rows, HID // 2:], other_ref[0], 1, 1)
        if m == 0:
            load[3].wait()
        xhat, rs = stats(depth_ref[rows, :], C3, None)
        a_gain = a_gain + fold8(d * xhat)
        a_shift = a_shift + fold8(d)
        dd = norm_back(d, xhat, rs, gain, C3, None)
        a_depth = a_depth + fold8(dd)
        for n in range(REAR // COL):
            for lt in range(3):
                spread_shifted(cp_ref, lt, m * (REAR // COL) + n, dd[n * COL:(n + 1) * COL, lt * 128:(lt + 1) * 128])
        return a_gain, a_shift, a_depth
    sums = (zero, zero, zero)
    for n in range(ROWS // REAR):
        sums = mm(n, sums)
        tick()
    end(load[4:])

    def scale_rows(m, total):
        rows = pl.ds(pl.multiple_of(m * PAIR, 16), PAIR)
        keep = jnp.concatenate([keep_ref[...], keep_ref[...]], axis=0)
        return total + fold8(dr_ref[rows, :] * keep * out_ref[rows, :])
    a_scale = lax.fori_loop(0, ROWS // PAIR, scale_rows, zero)
    dvec_ref[4:5, :] = jnp.sum(a_scale, axis=0, keepdims=True)
    a_gain, a_shift, a_depth = sums
    dvec_ref[0:1, :] = jnp.sum(a_depth, axis=0, keepdims=True)
    dvec_ref[1:2, :] = jnp.sum(a_gain, axis=0, keepdims=True)
    dvec_ref[2:3, :] = jnp.sum(a_shift, axis=0, keepdims=True)
    dvec_ref[5:8, :] = jnp.zeros((3, C3), F32)
    writes = []
    for n in range(HID // 256):
        lanes = slice(n * 256, (n + 1) * 256)
        half = down_ref if n < 3 else dother_ref
        part = slice((n % 3) * 256, (n % 3 + 1) * 256)
        half[1, :, part] = dot(dout_ref[...], act_ref[:, lanes], 0, 0).astype(BF)
        half[0, :, part] = dot(normed_ref[...], dhid_ref[:, lanes], 0, 0).astype(BF)
        if n % 3 == 2:
            out = down_any if n == 2 else dother_any
            writes.append(pltpu.make_async_copy(half, out, in_sem.at[8 + n // 3]))
            writes[-1].start()
            tick()
    for lt in range(3):
        lanes = slice(lt * 128, (lt + 1) * 128)

        def conv(v, _, lt=lt, lanes=lanes):
            spots = [pl.ds(pl.multiple_of(c * COL + v * 8, 8), 8) for c in range(SIDE)]
            acc = [dr_ref[s, lanes] for s in spots]
            sent = [res_ref[s, lanes].astype(BF).astype(F32) for s in spots]
            for i in range(KERNEL):
                flip = 6 - i
                k = (6 * flip) % 8
                row = pl.ds(pl.multiple_of(6 * flip - k + v * 8, 8), 8)
                xs = [cp_ref[k // 2, lt, c, row, :] for c in range(SIDE)]
                for j in range(KERNEL):
                    t = i * KERNEL + j
                    w = wb_ref[lt, t]
                    tap = None
                    for c in range(SIDE):
                        cc = c - (j - 3)
                        if 0 <= cc < SIDE:
                            acc[c] = acc[c] + w * xs[cc]
                            term = sent[c] * xs[cc]
                            tap = term if tap is None else tap + term
                    kacc_ref[lt, t] += tap
            for c in range(SIDE):
                new_ref[spots[c], lanes] = acc[c]
            return 0
        lax.fori_loop(0, COL // 8, conv, 0)
        tick()
    for lt in range(3):
        for t in range(TAPS):
            dkern_ref[3 * t + lt:3 * t + lt + 1, :] = jnp.sum(kacc_ref[lt, t], axis=0, keepdims=True)
    end(writes)


HOOKS = 9
BODY_INS, BODY_OUTS, BODY_SCRATCH = 12, 6, 16


def back_parts():
    outs = (listed(VM, sds((ROWS, C3))) + listed(AN, sds((2, C3, HID // 2), BF), sds((2, C3, HID // 2), BF))
            + listed(VM, sds((3 * TAPS, 128)), sds((8, C3)), sds((8, HID))))
    wide, half = (ROWS, HID), (2, C3, HID // 2)
    scratch = [pltpu.VMEM((4, 3, SIDE, SHIFTED, 128), F32), pltpu.VMEM((3, TAPS, 8, 128), F32),
               pltpu.VMEM((ROWS, C3), BF), pltpu.VMEM(wide, BF), pltpu.VMEM((3, TAPS, 8, 128), F32),
               pltpu.VMEM(wide, BF), pltpu.VMEM(wide, BF), pltpu.VMEM((ROWS, C3), F32), pltpu.VMEM((ROWS, C3), BF),
               pltpu.VMEM((ROWS, C3), F32), pltpu.VMEM((ROWS, C3), F32), pltpu.VMEM(half, BF), pltpu.VMEM(half, BF),
               pltpu.VMEM(half, BF), pltpu.VMEM(half, BF), pltpu.SemaphoreType.DMA((10,))]
    return outs, scratch


def take(refs, count):
    return refs[:count], refs[count:]


def block_back_kernel(planes, kind, *refs):
    net = Net(planes)
    args, refs = take(refs, BODY_INS)
    more_in, refs = take(refs, (1, 3, 3)[kind])
    outs, refs = take(refs, BODY_OUTS)
    more_out, refs = take(refs, (1, 2, 2)[kind])
    scratch, refs = take(refs, BODY_SCRATCH)
    hooks = [[] for _ in range(HOOKS)]
    if kind == 0:
        steps = flat_sum_steps(net, more_in[0], more_out[0], *refs)
        hooks[0], hooks[2], hooks[5], hooks[8] = [net.greet, steps[0]], [steps[1]], [steps[2]], [steps[3]]
    else:
        step0, step1, step2 = layer_steps(net, more_in[0], more_in[1], more_out[0], *refs[:6])
        hooks[0] = [net.greet, step0]
        hooks[1] = [lambda: step1(0)]
        hooks[2] = [lambda: step1(1)]
        hooks[8] = [lambda: step2(0), lambda: step2(1)]
        if kind == 1:
            steps = spread_steps(net, more_in[2], more_out[1], *refs[6:])
            hooks[0] = [net.greet, steps[0], step0]
            hooks[1] = [steps[1], lambda: step1(0)]
            hooks[7] = [steps[2]]
            hooks[8] = [lambda: step2(0), lambda: step2(1), steps[3]]
        else:
            col0, col1 = column_steps(net, more_in[2], more_out[1], *refs[6:])
            hooks[0].append(col0)
            hooks[4].append(col1)
    block_back_body(hooks, *args, *outs, *scratch)


def block_back(planes, kind, args, *more):
    outs, scratch = back_parts()
    ins = listed(VM, *args[:4]) + listed(AN, *args[4:])
    if kind == 0:
        grad, = more
        rows = grad.shape[4]
        ins += listed(VM, grad)
        outs += listed(VM, sds((rows, 128), BF))
        scratch += flat_scratch(planes, rows, BF)
    else:
        own, other, held = more
        rows, width = own.shape[3:]
        ins += listed(AN, own, other) + listed(VM, held)
        outs += listed(VM, sds((planes, rows, width), BF))
        scratch += layer_scratch(planes, rows, width)
        if kind == 1:
            outs += listed(VM, sds((2, 2, 2, planes) + held.shape, BF))
            scratch += spread_scratch(planes)
        else:
            outs += listed(VM, sds((rows, width), BF))
            scratch += column_scratch(planes, rows, width)
    return call(functools.partial(block_back_kernel, planes, kind), ins, outs, scratch, 8_000_000_000, (1, 2, 5)[kind])


def back_kernel(planes, dr_ref, xp_any, n1_any, s2_any, n2_any, wbig_ref, d1_ref, d2_ref, vs_ref, v2_ref, dk0_ref, dk1_ref,
                dk2_ref, own_ref, other_ref, held_ref,
                tail_ref, dvs_ref, dv2_ref, dv3_ref, two_ref, piece0_ref, piece1_ref, one_ref,
                mid_ref, line1_ref, grad1_ref,
                xp_ref, n1_ref, s2_ref, n2_ref, in_sem,
                sum_ref, shard_ref, st_ref, dn1_ref, dlow_ref, base_ref, aw_ref, dd1_ref, line_ref, grad_ref, *scratch):
    load_n2 = pltpu.make_async_copy(n2_any, n2_ref, in_sem.at[18])
    load_n2.start()
    loads = [[pltpu.make_async_copy(a.at[g], b.at[g], in_sem.at[3 * g + n])
              for n, (a, b) in enumerate(((xp_any, xp_ref), (n1_any, n1_ref), (s2_any, s2_ref)))] for g in range(6)]
    begin(loads[0][1:])
    net = Net(planes)
    net.greet(True)
    layer0, layer1, layer2 = layer_steps(net, own_ref, other_ref, sum_ref, *scratch[:6])
    high0, high1 = column_steps(net, held_ref, piece1_ref, *scratch[6:8])
    low0, low1 = column_steps(net, sum_ref, piece0_ref, *scratch[8:10])
    high0()
    layer0()
    mask1 = (lax.broadcasted_iota(jnp.int32, (1, 128), 1) < C1).astype(F32)
    mask2 = (lax.broadcasted_iota(jnp.int32, (1, 256), 1) < C2).astype(F32)
    bias_stem, gain_stem, shift_stem = vs_ref[0:1, :], vs_ref[1:2, :], vs_ref[2:3, :]
    gain_one = vs_ref[3:4, :]
    gain_two = v2_ref[1:2, :]
    z1, z2, z3 = jnp.zeros((8, 128), F32), jnp.zeros((8, 256), F32), jnp.zeros((8, C3), F32)
    dd1_ref[...] = jnp.zeros_like(dd1_ref)
    aw_ref[...] = jnp.zeros_like(aw_ref)

    base_ref[...] = dr_ref[...].astype(BF)
    shard = grad_ref.shape[4]
    load_n2.wait()
    for g in range(1, 6):
        begin(loads[g][1:])
    for g in range(6):
        loads[g][0].start()
    for or2 in range(2):
        total = dot(n2_ref[or2], base_ref[...], 0, 0)
        for oc2 in range(2):
            for lt in range(3):
                line_ref[pl.ds(3 * (or2 * 384 + oc2 * 192) + lt, 192, stride=3), :] = (
                    total[oc2 * 256:oc2 * 256 + 192, lt * 128:(lt + 1) * 128])
    for l in range(LAYERS):
        line_ref[TWO_LINES + l * 3 * TAPS:TWO_LINES + (l + 1) * 3 * TAPS, :] = (dk0_ref, dk1_ref, dk2_ref)[l][...]
    line_ref[TWO_LINES + KERN_LINES:, :] = jnp.zeros((8 * planes * shard - TWO_LINES - KERN_LINES, 128), F32)
    for mm in range(2):
        for yy in range(2):
            for cc in range(2):
                for k in range(planes):
                    at = (((mm * 2 + yy) * 2 + cc) * planes + k) * shard
                    grad_ref[mm, yy, cc, k] = line_ref[at:at + shard, :].astype(BF)
    flat = flat_sum_steps(net, grad_ref, shard_ref, *scratch[10:16])
    flat += spread_steps(net, shard_ref, two_ref, *scratch[16:17])
    flat[0]()
    layer1(0)

    def upper(g, carry):
        rows = pl.ds(g * 144, 144)
        base = base_ref[rows, :]
        a3 = carry[0] + fold8(base.astype(F32))
        a_bias2, a_gain2, a_shift2 = carry[1:4]
        dn2 = [dot(base, d2_ref[or2], 1, 1) for or2 in range(2)]
        loads[g][1].wait()
        loads[g][2].wait()
        d = jnp.concatenate(
            [dn2[or2][q // 2 * 72:(q // 2 + 1) * 72, q % 2 * 256:(q % 2 + 1) * 256] for q in range(4) for or2 in range(2)], axis=0)
        xhat, rs = stats(s2_ref[g].reshape(4 * 144, 256), C2, mask2)
        a_gain2 = a_gain2 + fold8(d * xhat)
        a_shift2 = a_shift2 + fold8(d)
        mids = norm_back(d, xhat, rs, gain_two, C2, mask2).astype(BF)
        a_bias2 = a_bias2 + fold8(mids.astype(F32))
        mid_ref[g] = mids
        for q in range(4):
            lanes = slice(q * 256, (q + 1) * 256)
            for or1 in range(2):
                dd1_ref[or1] += dot(n1_ref[g, or1 * 144:(or1 + 1) * 144, lanes], mids[q * 144:(q + 1) * 144], 0, 0)
        return a3, a_bias2, a_gain2, a_shift2

    def lower(g, carry, hooks):
        loads[g][0].wait()
        for q in range(4):
            for or1 in range(2):
                part = slice(or1 * 144, (or1 + 1) * 144)
                o = dot(mid_ref[g, q * 144:(q + 1) * 144, :], d1_ref[or1], 1, 1)
                dn1_ref[2 * q, part, :] = o[:, :128]
                dn1_ref[2 * q + 1, part, :] = o[:, 128:]
        for q in range(4):
            o = dot(xp_ref[g], wbig_ref[:, q * 256:(q + 1) * 256])
            st_ref[2 * q] = o[:, :128]
            st_ref[2 * q + 1] = o[:, 128:]

        for hook in hooks:
            hook()
        b0, g0, s0, g1, s1 = carry
        v = st_ref[...].reshape(8 * 288, 128) + bias_stem
        xa, ra = stats(v, C1, mask1)
        y = xa * gain_stem + shift_stem
        xb, rb = stats(y, C1, mask1)
        d = dn1_ref[...].reshape(8 * 288, 128)
        g1 = g1 + fold8(d * xb)
        s1 = s1 + fold8(d)
        dy = norm_back(d, xb, rb, gain_one, C1, mask1)
        g0 = g0 + fold8(dy * xa)
        s0 = s0 + fold8(dy)
        dv = norm_back(dy, xa, ra, gain_stem, C1, mask1).astype(BF)
        b0 = b0 + fold8(dv.astype(F32))
        for j in range(8):
            dlow_ref[:, j * 128:(j + 1) * 128] = dv[j * 288:(j + 1) * 288]
        sums = (b0, g0, s0, g1, s1)
        aw_ref[...] += dot(xp_ref[g], dlow_ref[...], 0, 0)
        return sums

    sums = (z3, z2, z2, z2)
    between = [[high1], [flat[1]], [lambda: layer1(1)], [], [], [lambda: layer2(0), flat[2]]]
    for g in range(6):
        sums = upper(g, sums)
        for hook in between[g]:
            hook()
    lane = lax.broadcasted_iota(jnp.int32, (48, 128), 1)
    for or1 in range(2):
        for oc1 in range(2):
            left, right = st_ref.at[1], st_ref.at[2]
            left[0:96, :] = dd1_ref[or1, oc1 * 128:oc1 * 128 + 96, 0:128]
            right[0:96, :] = dd1_ref[or1, oc1 * 128:oc1 * 128 + 96, 128:256]
            e0, o0 = left[pl.ds(0, 48, stride=2), :], left[pl.ds(1, 48, stride=2), :]
            e1, o1 = right[pl.ds(0, 48, stride=2), :], right[pl.ds(1, 48, stride=2), :]
            at = (or1 * 192 + oc1 * 96) * 3 // 2
            line1_ref[pl.ds(at, 48, stride=3), :] = e0
            line1_ref[pl.ds(at + 1, 48, stride=3), :] = jnp.where(lane < 64, e1, pltpu.roll(o0, 64, 1))
            line1_ref[pl.ds(at + 2, 48, stride=3), :] = jnp.where(lane < 64, pltpu.roll(o0, 64, 1), pltpu.roll(o1, 64, 1))
    size = grad1_ref.shape[4]
    line1_ref[ONE_LINES:, :] = jnp.zeros((8 * planes * size - ONE_LINES, 128), F32)
    for mm in range(2):
        for yy in range(2):
            for cc in range(2):
                for k in range(planes):
                    at = (((mm * 2 + yy) * 2 + cc) * planes + k) * size
                    grad1_ref[mm, yy, cc, k] = line1_ref[at:at + size, :].astype(BF)
    first = tail_steps(net, grad1_ref, one_ref, *scratch[17:])
    first[0]()
    inner = [[], [flat[3], flat[4]], [lambda: layer2(1), first[2], flat[5]], [first[3]], [flat[6]], [flat[7], first[4]]]
    outer = [[first[1]], [], [low0], [], [], [low1]]
    low_sums = (z1, z1, z1, z1, z1)
    for g in range(6):
        low_sums = lower(g, low_sums, inner[g])
        for hook in outer[g]:
            hook()
    done = sums + low_sums
    total = aw_ref[0:48, 0:128]
    for j in range(1, 8):
        total = total + aw_ref[j * 48:(j + 1) * 48, j * 128:(j + 1) * 128]
    dv3_ref[...] = jnp.sum(done[0], axis=0, keepdims=True)
    for n in range(3):
        dv2_ref[n:n + 1, :] = jnp.sum(done[1 + n], axis=0, keepdims=True)
    for n in range(5):
        dvs_ref[n:n + 1, :] = jnp.sum(done[4 + n], axis=0, keepdims=True)
    base = st_ref.at[0]
    base[0:48, :] = total
    lane = lax.broadcasted_iota(jnp.int32, (12, 128), 1)
    a0, a1, a2, a3 = [base[pl.ds(n, 12, stride=4), :] for n in range(4)]
    tail_ref[pl.ds(0, 12, stride=3), :] = jnp.where(lane < 96, a0, pltpu.roll(a1, 96, 1))
    tail_ref[pl.ds(1, 12, stride=3), :] = jnp.where(lane < 64, pltpu.roll(a1, 96, 1), pltpu.roll(a2, 64, 1))
    tail_ref[pl.ds(2, 12, stride=3), :] = jnp.where(lane < 32, pltpu.roll(a2, 64, 1), pltpu.roll(a3, 32, 1))


def back(planes, dr, kept, weights, dkern, own, other, held):
    shard = ceil_to(TWO_LINES + KERN_LINES, 8 * planes * 16) // (8 * planes)
    rows, width = own.shape[3:]
    shard1 = ceil_to(ONE_LINES, 8 * planes * 16) // (8 * planes)
    shape1 = (2, 2, 2, planes, shard1, 128)
    shape = (2, 2, 2, planes, shard, 128)
    return call(
        functools.partial(back_kernel, planes),
        listed(VM, dr) + listed(AN, *kept) + listed(VM, *weights, *dkern) + listed(AN, own, other) + listed(VM, held),
        listed(VM, sds((STEM_LINES, 128)), sds((5, 128)), sds((3, 256)), sds((1, C3)), sds(shape, BF),
               sds((rows, width), BF), sds((rows, width), BF), sds(shape1, BF)),
        [pltpu.VMEM((6, 576, 256), BF), pltpu.VMEM((8 * planes * shard1, 128), F32), pltpu.VMEM(shape1, BF)]
        + [pltpu.VMEM(k.shape, k.dtype) for k in kept] + [pltpu.SemaphoreType.DMA((19,))]
        + [pltpu.VMEM((planes, rows, width), BF), pltpu.VMEM((shard, 128), BF),
           pltpu.VMEM((8, 288, 128), F32), pltpu.VMEM((8, 288, 128), F32), pltpu.VMEM((288, 1024), BF),
           pltpu.VMEM((ROWS, C3), BF), pltpu.VMEM((384, 1024), F32), pltpu.VMEM((2, 256, 256), F32),
           pltpu.VMEM((8 * planes * shard, 128), F32), pltpu.VMEM(shape, BF)]
        + layer_scratch(planes, rows, width) + column_scratch(planes, rows, width) + column_scratch(planes, rows, width)
        + flat_scratch(planes, shard, BF) + spread_scratch(planes) + tail_scratch(planes, shard1, BF),
        8_000_000_000, 3,
    )


VECTOR_WIDTHS = (C1, C1, C2, LAYERS * C3, LAYERS * C3, C3, C1, C1, C1, C2, C2, C3, LAYERS * C3, LAYERS * C3, LAYERS * HID,
                 LAYERS * C3, C3, CLASSES)
VECTOR_NAMES = ("gain_stem", "gain_one", "gain_two", "gain_block", "layer_scale", "gain_final", "bias_stem", "shift_stem",
                "shift_one", "bias_one", "shift_two", "bias_two", "bias_depth", "shift_block", "bias_inner", "bias_outer",
                "shift_final", "bias_head")
VECTOR = sum(VECTOR_WIDTHS)
VECTOR_LINES = ceil_to(VECTOR, 1024) // 128


def vector_plan():
    plan, offset, row = {}, 0, 0
    for name, width in zip(VECTOR_NAMES, VECTOR_WIDTHS):
        plan[name] = (offset, width, row)
        offset, row = offset + width, row + ceil_to(width, 128) // 128
    return plan, row


VECTOR_PLAN, PADDED_LINES = vector_plan()
TAIL_LINES = STEM_LINES + PADDED_LINES + 1


def open_kernel(planes, flat_ref, vector_ref, master_ref, mask_ref, pix_ref, perm_ref,
                xp_out, n1_out, s2_out, n2_out, far_out, low0_out, quarter1_out,
                res_ref, wbig_ref, d1_ref, d2_ref, head_ref, vs_ref, v2_ref, v3_ref, hv_ref, hb_ref, *refs):
    kern_ref, vec_ref, bin_ref, keep_ref = [refs[LAYERS * n:LAYERS * (n + 1)] for n in range(4)]
    low_ref = (None,) + refs[4 * LAYERS:4 * LAYERS + 2]
    (wide_ref, pad_ref, master, master_sem, low0_ref, x_ref, xp_ref, n1_ref, s2_ref, n2_ref, st_ref, n2s_ref, pix_sem,
     out_sem, w_sem, quarter_ref) = refs[4 * LAYERS + 2:]
    net = Net(planes)
    m = net.m
    peers = [net.core] + net.plane[:2] + net.four
    for peer in peers:
        net.signal(peer)
    loads = [pltpu.make_async_copy(master_ref.at[l], master.at[l], master_sem.at[l]) for l in range(LAYERS)]
    loads[0].start()
    near = pl.ds(pl.multiple_of(m * PAIR, 16), PAIR)
    far = pl.ds(pl.multiple_of((1 - m) * PAIR, 16), PAIR)
    kept = pltpu.make_async_copy(pix_ref.at[near, :], x_ref.at[near, :], out_sem.at[24])
    kept.start()
    pl.semaphore_wait(pltpu.get_barrier_semaphore(), len(peers))
    moves = []
    for g in range(6):
        lanes = pl.ds(g * 384, 384)
        moves.append(remote(pix_ref.at[far, lanes], x_ref.at[near, lanes], pix_sem, g, net.plane[0]))
    moves[0].start()
    loads[0].wait()
    begin(loads[1:])
    low0_ref[...] = master[0].astype(BF)
    send0 = weight_send(net, low0_ref, quarter_ref, w_sem, 3)
    send1 = weight_send(net, low_ref[1], quarter1_out, w_sem, 3 + PARTS)
    send0[0]()
    moves[1].start()
    spread0, spread1, spread2 = weight_spread(net, quarter_ref, far_out, w_sem, out_sem.at[26])
    keep_low = pltpu.make_async_copy(low0_ref, low0_out, out_sem.at[25])
    keep_low.start()
    for name in VECTOR_NAMES:
        offset, width, row = VECTOR_PLAN[name]
        lines = ceil_to(width, 128) // 128
        at, s = offset // 128, offset % 128
        lane = lax.broadcasted_iota(jnp.int32, (lines, 128), 1)
        value = vector_ref[at:at + lines, :]
        if s:
            value = jnp.where(lane < 128 - s, pltpu.roll(value, 128 - s, 1),
                              pltpu.roll(vector_ref[at + 1:at + 1 + lines, :], 128 - s, 1))
        if width % 128:
            spot = lax.broadcasted_iota(jnp.int32, (lines, 128), 0) * 128 + lane
            value = jnp.where(spot < width, value, 0.0)
        pad_ref[row:row + lines, :] = value

    def place(ref, at, name, start, lines):
        row = VECTOR_PLAN[name][2] + start
        for n in range(lines):
            ref[at + (slice(n * 128, (n + 1) * 128),)] = pad_ref[row + n:row + n + 1, :]
    one = lambda n: (slice(n, n + 1),)
    for n, name in enumerate(("bias_stem", "gain_stem", "shift_stem", "gain_one", "shift_one")):
        place(vs_ref, one(n), name, 0, 1)
    for n, name in enumerate(("bias_one", "gain_two", "shift_two")):
        place(v2_ref, one(n), name, 0, 2)
    place(v3_ref, one(0), "bias_two", 0, 3)
    for l in range(LAYERS):
        for n, name in enumerate(("bias_depth", "gain_block", "shift_block", "bias_outer", "layer_scale")):
            place(vec_ref[l], one(n), name, 3 * l, 3)
        for n in range(12):
            part = (n // 6 + m) % 2
            row = VECTOR_PLAN["bias_inner"][2] + 12 * l + part * 6 + n % 6
            bin_ref[l][:, n * 128:(n + 1) * 128] = pad_ref[pl.ds(row, 1), :]
    place(hv_ref, one(0), "gain_final", 0, 3)
    place(hv_ref, one(1), "shift_final", 0, 3)
    place(hb_ref, one(0), "bias_head", 0, 8)
    lane = lax.broadcasted_iota(jnp.int32, (12, 128), 1)
    f0, f1, f2 = [flat_ref[pl.ds(n, 12, stride=3), :] for n in range(3)]
    parts = (f0, jnp.where(lane < 32, pltpu.roll(f0, 32, 1), pltpu.roll(f1, 32, 1)),
             jnp.where(lane < 64, pltpu.roll(f1, 64, 1), pltpu.roll(f2, 64, 1)), pltpu.roll(f2, 96, 1))
    for n in range(4):
        wide_ref[0, pl.ds(n, 12, stride=4), :] = jnp.where(lane < C1, parts[n], 0.0)
    stem = wide_ref[0, 0:48, :].astype(BF)
    wbig_ref[...] = jnp.zeros_like(wbig_ref)
    for j in range(8):
        wbig_ref[j * 48:(j + 1) * 48, j * 128:(j + 1) * 128] = stem
    lane = lax.broadcasted_iota(jnp.int32, (192, 128), 1)
    f0, f1, f2 = [flat_ref[pl.ds(STEM_LINES + n, 192, stride=3), :] for n in range(3)]
    f1 = pltpu.roll(f1, 64, 1)
    f2 = pltpu.roll(f2, 64, 1)
    wide_ref[0, pl.ds(0, 192, stride=2), :] = f0
    wide_ref[1, pl.ds(0, 192, stride=2), :] = jnp.where(lane < 64, pltpu.roll(f1, 64, 1), 0.0)
    wide_ref[0, pl.ds(1, 192, stride=2), :] = jnp.where(lane < 64, f1, f2)
    wide_ref[1, pl.ds(1, 192, stride=2), :] = jnp.where(lane < 64, f2, 0.0)
    d1_ref[...] = jnp.zeros_like(d1_ref)
    d2_ref[...] = jnp.zeros_like(d2_ref)
    for or1 in range(2):
        for oc1 in range(2):
            at = or1 * 192 + oc1 * 96
            for t in range(2):
                d1_ref[or1, oc1 * 128:oc1 * 128 + 96, t * 128:(t + 1) * 128] = wide_ref[t, at:at + 96, :].astype(BF)
    base = STEM_LINES + ONE_LINES
    for lt in range(3):
        for or2 in range(2):
            for oc2 in range(2):
                at = base + (or2 * 384 + oc2 * 192) * 3 + lt
                d2_ref[or2, oc2 * 256:oc2 * 256 + 192, lt * 128:(lt + 1) * 128] = flat_ref[pl.ds(at, 192, stride=3), :].astype(BF)
    mask1 = (lax.broadcasted_iota(jnp.int32, (1, 128), 1) < C1).astype(F32)
    mask2 = (lax.broadcasted_iota(jnp.int32, (1, 256), 1) < C2).astype(F32)
    bias_stem, gain_stem, shift_stem = vs_ref[0:1, :], vs_ref[1:2, :], vs_ref[2:3, :]
    gain_one, shift_one = vs_ref[3:4, :], vs_ref[4:5, :]
    bias_one, gain_two, shift_two = v2_ref[0:1, :], v2_ref[1:2, :], v2_ref[2:3, :]
    kern_base = STEM_LINES + ONE_LINES + TWO_LINES

    def more_low():
        for l in range(1, LAYERS):
            loads[l].wait()
            low_ref[l][...] = master[l].astype(BF)

    def more_small():
        spot = lax.broadcasted_iota(jnp.int32, (COL, 128), 0) % IMG
        for l in range(LAYERS):
            value = jnp.zeros((COL, 128), jnp.int32)
            for n in range(IMG):
                value = jnp.where(spot == n, mask_ref[l, m * IMG + n], value)
            value = value.astype(F32)
            for lt in range(3):
                keep_ref[l][:, lt * 128:(lt + 1) * 128] = value
        for l in range(LAYERS):
            kern_ref[l][...] = flat_ref[kern_base + l * 3 * TAPS:kern_base + (l + 1) * 3 * TAPS, :]

    def more_head():
        base = kern_base + KERN_LINES
        count = C3 // 16
        lane = lax.broadcasted_iota(jnp.int32, (count, 128), 1)
        for k in range(16):
            for t in range(8):
                start = k * CLASSES + t * 128
                f, s = start // 128, start % 128
                need = min(128, CLASSES - t * 128)
                value = flat_ref[pl.ds(base + f, count, stride=CLASSES // 8), :]
                if s:
                    value = pltpu.roll(value, 128 - s, 1)
                    if need > 128 - s:
                        after = flat_ref[pl.ds(base + f + 1, count, stride=CLASSES // 8), :]
                        value = jnp.where(lane < 128 - s, value, pltpu.roll(after, 128 - s, 1))
                if need < 128:
                    value = jnp.where(lane < need, value, 0.0)
                wide_ref[t, pl.ds(k, count, stride=16), :] = value
        for t in range(8):
            head_ref[:, t * 128:(t + 1) * 128] = wide_ref[t].astype(BF)

    def spread0_first():
        send0[2]()
        spread0()

    def spread_last():
        send1[2]()
        spread2()
    send0[1]()
    ahead = [moves[2:4], [], moves[4:6], [], [], []]
    extras = [[more_low], [more_head, spread0_first, send1[0]], [], [more_small, spread1, send1[1]], [], [spread_last]]
    kept.wait()
    writes = []
    for g in range(6):
        moves[g].wait()
        begin(ahead[g])
        x2 = dot(perm_ref[...], x_ref[:, g * 384:(g + 1) * 384]).astype(BF)
        xp_ref[g] = x2
        for q in range(4):
            o = dot(x2, wbig_ref[:, q * 256:(q + 1) * 256])
            st_ref[2 * q] = o[:, :128]
            st_ref[2 * q + 1] = o[:, 128:]
        v = st_ref[...].reshape(8 * 288, 128) + bias_stem
        xhat, _s = stats(v, C1, mask1)
        y = xhat * gain_stem + shift_stem
        xhat, _s = stats(y, C1, mask1)
        low = (xhat * gain_one + shift_one).astype(BF).reshape(8, 288, 128)
        for j in range(8):
            n1_ref[g, :, j * 128:(j + 1) * 128] = low[j]
        for q in range(4):
            lanes = slice(q * 256, (q + 1) * 256)
            s2_ref[g, q] = dot(n1_ref[g, 0:144, lanes], d1_ref[0]) + dot(n1_ref[g, 144:288, lanes], d1_ref[1]) + bias_one
        for ref, out, at in ((xp_ref, xp_out, 0), (n1_ref, n1_out, 6), (s2_ref, s2_out, 12)):
            writes.append(pltpu.make_async_copy(ref.at[g], out.at[g], out_sem.at[at + g]))
            writes[-1].start()
        xhat, _s = stats(s2_ref[g].reshape(4 * 144, 256), C2, mask2)
        n2 = xhat * gain_two + shift_two
        for q in range(4):
            c2, oc2 = q // 2, q % 2
            for or2 in range(2):
                at = q * 144 + or2 * 72
                n2s_ref[or2, c2 * 72:(c2 + 1) * 72, oc2 * 256:(oc2 + 1) * 256] = n2[at:at + 72]
        rows = slice(g * 144, (g + 1) * 144)
        low0, low1 = n2s_ref[0].astype(BF), n2s_ref[1].astype(BF)
        n2_ref[0, rows, :] = low0
        n2_ref[1, rows, :] = low1
        writes.append(pltpu.make_async_copy(n2_ref.at[:, pl.ds(g * 144, 144), :], n2_out.at[:, pl.ds(g * 144, 144), :],
                                            out_sem.at[18 + g]))
        writes[-1].start()
        res_ref[rows, :] = dot(low0, d2_ref[0]) + dot(low1, d2_ref[1]) + v3_ref[0:1, :]
        for extra in extras[g]:
            extra()
    end(writes)
    keep_low.wait()


def opening(planes, flat, vector, master, keep_mask, pix, perm):
    kept = [(6, 288, 384), (6, 288, 1024), (6, 4, 144, 256), (2, ROWS, 512)]
    types = [BF, BF, F32, BF]
    half = sds((2, C3, HID // 2), BF)
    each = lambda shape: [sds(shape)] * LAYERS
    outs = ([sds((ROWS, C3)), sds((384, 1024), BF), sds((2, 256, 256), BF), sds((2, 512, C3), BF), sds((C3, WIDE), BF),
             sds((8, 128)), sds((8, 256)), sds((8, C3)), sds((2, C3)), sds((1, WIDE))]
            + each((3 * TAPS, 128)) + each((8, C3)) + each((1, HID)) + each((COL, C3)) + [half, half])
    return call(
        functools.partial(open_kernel, planes),
        listed(VM, flat, vector) + listed(AN, master) + listed(SM, keep_mask) + listed(AN, pix) + listed(VM, perm),
        listed(AN, *[sds(a, b) for a, b in zip(kept, types)], half, half, sds((C3 // 2, HID // 2), BF)) + listed(VM, *outs),
        [pltpu.VMEM((8, C3, 128), F32), pltpu.VMEM((ceil_to(PADDED_LINES, 8), 128), F32),
         pltpu.VMEM((LAYERS, 2, C3, HID // 2), F32), pltpu.SemaphoreType.DMA((LAYERS,)), pltpu.VMEM((2, C3, HID // 2), BF),
         pltpu.VMEM((4 * COL, 4 * SIDE * PATCH), BF)]
        + [pltpu.VMEM(a, b) for a, b in zip(kept, types)]
        + [pltpu.VMEM((8, 288, 128), F32), pltpu.VMEM((2, 144, 512), F32), pltpu.SemaphoreType.DMA((2, 6)),
           pltpu.SemaphoreType.DMA((27,)), pltpu.SemaphoreType.DMA((2, 3 + 2 * PARTS)), pltpu.VMEM((C3 // 2, HID // 2), BF)],
        4_000_000_000, 6,
    )


def finish_kernel(planes, p0_ref, p1_ref, p2_ref, tail_ref, dvs_ref, dv2_ref, dv3_ref, dvec0_ref, dvec1_ref, dvec2_ref,
                  dbin0_ref, dbin1_ref, dbin2_ref, dfinal_ref, dbias_ref, loss_ref, head_ref, two_ref, one_ref,
                  own_ref, flat_ref, vector_ref, info_ref,
                  grad_ref, full_ref, line_ref, arrived_ref, move_sem, local_sem, *scratch):
    net = Net(planes)
    m, d = net.m, net.d
    dp = 4 * planes
    pieces_ref, dvec_ref, dbin_ref = (p0_ref, p1_ref, p2_ref), (dvec0_ref, dvec1_ref, dvec2_ref), (dbin0_ref, dbin1_ref, dbin2_ref)
    shard = grad_ref.shape[4]
    targets = [((l * dp + d) // 3, (l * dp + d) % 3) for l in range(LAYERS)]
    sources = [(3 * d + s) % dp for s in range(LAYERS)]
    for s in range(LAYERS):
        @pl.when(sources[s] != d)
        def _(s=s):
            net.signal((sources[s], m))
    peers = [peer for _, peer in net.all_plane] + net.column
    for peer in peers:
        net.signal(peer)
    awaited = len(peers)
    for l in range(LAYERS):
        awaited = awaited + jnp.where(targets[l][0] != d, 1, 0)
    pl.semaphore_wait(pltpu.get_barrier_semaphore(), awaited)

    def move(l):
        owner, slot = targets[l]
        return pltpu.make_async_remote_copy(
            src_ref=pieces_ref[l], dst_ref=arrived_ref.at[slot], send_sem=move_sem.at[0, l],
            recv_sem=move_sem.at[1, slot], device_id=(owner, m), device_id_type=pl.DeviceIdType.MESH)

    def keep(l):
        return pltpu.make_async_copy(pieces_ref[l], arrived_ref.at[targets[l][1]], local_sem.at[l])

    for l in range(LAYERS):
        @pl.when(targets[l][0] != d)
        def _(l=l):
            move(l).start()

        @pl.when(targets[l][0] == d)
        def _(l=l):
            keep(l).start()
    squares = jnp.zeros((8, 128), F32)
    for l in range(LAYERS):
        piece = pieces_ref[l][...].astype(F32)
        line = jnp.sum(piece * piece, axis=0, keepdims=True)
        for n in range(6):
            squares = squares + jnp.concatenate([line[:, n * 128:(n + 1) * 128], jnp.zeros((7, 128), F32)], axis=0)
    square = jnp.sum(squares, axis=(0, 1), keepdims=True)
    lead = STEM_LINES
    line_ref[0:lead, :] = tail_ref[...]
    line_ref[lead:, :] = jnp.zeros((8 * planes * shard - lead, 128), F32)

    def place(name, start, value):
        row = lead + VECTOR_PLAN[name][2] + start
        for n in range(value.shape[1] // 128):
            line_ref[row + n:row + n + 1, :] = value[:, n * 128:(n + 1) * 128]
    for n, name in enumerate(("bias_stem", "gain_stem", "shift_stem", "gain_one", "shift_one")):
        place(name, 0, dvs_ref[n:n + 1, :])
    for n, name in enumerate(("bias_one", "gain_two", "shift_two")):
        place(name, 0, dv2_ref[n:n + 1, :])
    place("bias_two", 0, dv3_ref[...])
    for l in range(LAYERS):
        for n, name in enumerate(("bias_depth", "gain_block", "shift_block", "bias_outer", "layer_scale")):
            place(name, 3 * l, dvec_ref[l][n:n + 1, :])
        sums = jnp.sum(dbin_ref[l][...], axis=0, keepdims=True)
        for n in range(12):
            part = (n // 6 + m) % 2
            row = lead + VECTOR_PLAN["bias_inner"][2] + 12 * l + part * 6 + n % 6
            line_ref[pl.ds(row, 1), :] = sums[:, n * 128:(n + 1) * 128]
    place("gain_final", 0, dfinal_ref[0:1, :])
    place("shift_final", 0, dfinal_ref[1:2, :])
    place("bias_head", 0, dbias_ref[...])
    lane = lax.broadcasted_iota(jnp.int32, (1, 128), 1)
    info = jnp.where(lane == 2, square, loss_ref[...])
    line_ref[lead + PADDED_LINES:lead + PADDED_LINES + 1, :] = info

    def each_shard(move_one):
        for mm in range(2):
            for yy in range(2):
                for cc in range(2):
                    for k in range(planes):
                        move_one((mm, yy, cc, k), ((((mm * 2 + yy) * 2 + cc) * planes) + k))

    def pack(where, n):
        grad_ref[where] = line_ref[n * shard:(n + 1) * shard, :]
    each_shard(pack)
    steps = tail_steps(net, grad_ref, full_ref, *scratch)
    steps[0]()

    def unpack_big(ref, base, lines):
        size = ref.shape[4]
        sums = [jnp.zeros((8, 128), F32)]

        def inner(where, n):
            at = n * size
            if at < lines:
                rows = min(size, lines - at)
                value = ref[where].astype(F32)
                flat_ref[base + at:base + at + rows, :] = value[0:rows]
                sums[0] = sums[0] + fold8(value * value)
        each_shard(inner)
        return jnp.sum(sums[0], axis=0, keepdims=True)
    total = unpack_big(two_ref, STEM_LINES + ONE_LINES, TWO_LINES + KERN_LINES)
    steps[1]()
    total = total + unpack_big(head_ref, STEM_LINES + ONE_LINES + TWO_LINES + KERN_LINES, HEAD_LINES)
    steps[2]()
    total = total + unpack_big(one_ref, STEM_LINES, ONE_LINES)
    for step in steps[3:]:
        step()

    def unpack(where, n):
        line_ref[n * shard:(n + 1) * shard, :] = full_ref[where]
    each_shard(unpack)
    value = line_ref[0:lead, :]
    flat_ref[0:lead, :] = value
    total = total + jnp.sum(value * value, axis=0, keepdims=True)
    value = line_ref[lead:lead + PADDED_LINES, :]
    total = total + jnp.sum(value * value, axis=0, keepdims=True)
    info = line_ref[lead + PADDED_LINES:lead + PADDED_LINES + 1, :]
    pick = lambda n: jnp.sum(jnp.where(lane == n, info, 0.0), axis=1, keepdims=True)
    count = jnp.maximum(pick(1), 1.0)
    norm = jnp.sqrt(jnp.sum(total, axis=1, keepdims=True) + pick(2)) / count
    factor = CLIP_LIMIT / jnp.maximum(norm, CLIP_LIMIT) / count
    info_ref[...] = jnp.where(lane == 0, pick(0), jnp.where(lane == 1, count, jnp.where(lane == 2, norm, factor)))
    vector_ref[...] = jnp.zeros_like(vector_ref)
    for name in VECTOR_NAMES:
        offset, width, row = VECTOR_PLAN[name]
        lines = ceil_to(width, 128) // 128
        at, s = offset // 128, offset % 128
        lane8 = lax.broadcasted_iota(jnp.int32, (lines, 128), 1)
        value = line_ref[lead + row:lead + row + lines, :]
        if s:
            value = pltpu.roll(value, s, 1)
            vector_ref[at:at + lines, :] += jnp.where(lane8 < s, 0.0, value)
            vector_ref[at + 1:at + 1 + lines, :] += jnp.where(lane8 < s, value, 0.0)
        else:
            vector_ref[at:at + lines, :] += value
    for l in range(LAYERS):
        @pl.when(targets[l][0] != d)
        def _(l=l):
            move(l).wait_send()

        @pl.when(targets[l][0] == d)
        def _(l=l):
            keep(l).wait()
    for s in range(LAYERS):
        @pl.when(sources[s] != d)
        def _(s=s):
            pltpu.make_async_remote_copy(
                src_ref=pieces_ref[s], dst_ref=arrived_ref.at[s], send_sem=move_sem.at[0, s],
                recv_sem=move_sem.at[1, s], device_id=(sources[s], m), device_id_type=pl.DeviceIdType.MESH).wait_recv()
    own_ref[...] = arrived_ref[...]


def finish(planes, pieces, tail, dvs, dv2, dv3, dvec, dbin, dfinal, dbias, loss, head_sum, two_sum, one_sum):
    shard = ceil_to(TAIL_LINES, 8 * planes * 8) // (8 * planes)
    shape = (2, 2, 2, planes, shard, 128)
    held = (LAYERS,) + pieces[0].shape
    return call(
        functools.partial(finish_kernel, planes),
        listed(VM, *pieces, tail, dvs, dv2, dv3, *dvec, *dbin, dfinal, dbias, loss, head_sum, two_sum, one_sum),
        listed(VM, sds(held, BF), sds((FLAT_LINES, 128)), sds((VECTOR_LINES, 128)), sds((1, 128))),
        [pltpu.VMEM(shape, F32), pltpu.VMEM(shape, F32),
         pltpu.VMEM((8 * planes * shard, 128), F32),
         pltpu.VMEM(held, BF), pltpu.SemaphoreType.DMA((2, LAYERS)), pltpu.SemaphoreType.DMA((LAYERS,))]
        + tail_scratch(planes, shard, F32),
        0, 4,
    )


LEARN_RATE = 0.05
VECTOR_RATE = 0.15
WEIGHT_DECAY = 0.05
BETA_ONE = 0.9
BETA_TWO = 0.999
ADAM_EPSILON = 1e-08


def vector_lengths():
    return list(VECTOR_WIDTHS)


def flat_lengths():
    return [PATCH * C1, 4 * C1 * C2, 4 * C2 * C3, LAYERS * TAPS * C3, C3 * CLASSES]


def adam_update(weight, moment_one, moment_two, gradient, step_float, rate):
    first_new = BETA_ONE * moment_one + (1.0 - BETA_ONE) * gradient
    second_new = BETA_TWO * moment_two + (1.0 - BETA_TWO) * gradient * gradient
    first_hat = first_new / (1.0 - BETA_ONE**step_float)
    second_hat = second_new / (1.0 - BETA_TWO**step_float)
    weight_new = weight - rate * (first_hat / (jnp.sqrt(second_hat) + ADAM_EPSILON) + WEIGHT_DECAY * weight)
    return (weight_new, first_new, second_new, weight_new.astype(BF))


def row_source():
    target = np.arange(4 * COL)
    img = target % IMG
    r = target // IMG % SIDE
    or2 = target // COL % 2
    or1 = target // (2 * COL)
    row = 4 * r + 2 * or2 + or1
    return (row // (2 * SIDE)) * (2 * COL) + img * (2 * SIDE) + row % (2 * SIDE)


def per_device(pixels, labels, valid_flags, keep_mask, step_count, pointwise_weight, pointwise_first, pointwise_second,
               flat_weight, flat_first, flat_second, vector_weight, vector_first, vector_second):
    dp = lax.axis_size("dp")
    planes = dp // 4
    vectors = jnp.pad(vector_weight, (0, VECTOR_LINES * 128 - VECTOR)).reshape(VECTOR_LINES, 128)
    perm = jnp.asarray(row_source()[:, None] == np.arange(4 * COL)[None], BF)
    pix = pixels.reshape(4 * COL, 4 * SIDE * PATCH)
    ready = opening(planes, flat_weight.reshape(FLAT_LINES, 128), vectors, pointwise_weight, keep_mask, pix, perm)
    xp, n1, s2, n2, far, low0, quarter, res, wbig, d1, d2, head_low, vs, v2, v3, hv, hb = ready[:17]
    kern, vec, bins, keep = [ready[17 + LAYERS * n:17 + LAYERS * (n + 1)] for n in range(4)]
    low = [low0] + list(ready[17 + 4 * LAYERS:])
    kept = []
    for l in range(LAYERS):
        more = (quarter, low[2]) if l == 0 else (quarter,) if l == 1 else ()
        new, depth, normed, act, dg, out, *arrived = block(planes, res, kern[l], vec[l], bins[l], keep[l], low[l], far, *more)
        kept.append((keep[l], vec[l], kern[l], act, dg, out, normed, depth, res, low[l], far))
        res = new
        if l == 0:
            far, quarter = arrived
        elif l == 1:
            far, = arrived
    shard = ceil_to(HEAD_LINES, 8 * planes * 16) // (8 * planes)
    dr, dhead, dbias, dfinal, loss = head(res, hv, head_low, hb, labels, valid_flags, 8 * planes * shard)
    blocked = lambda a: a.reshape(planes, 2, 2, 2 * C3 // dp, HID // 2)
    dkern, dvec, dbin = [None] * LAYERS, [None] * LAYERS, [None] * LAYERS
    dr, own, other, dkern[2], dvec[2], dbin[2], head_shard = block_back(
        planes, 0, (dr,) + kept[2], dhead.reshape(2, 2, 2, planes, shard, 128))
    dr, own_new, other_new, dkern[1], dvec[1], dbin[1], held, head_sum = block_back(
        planes, 1, (dr,) + kept[1], blocked(own), blocked(other), head_shard)
    dr, own, other, dkern[0], dvec[0], dbin[0], held, piece2 = block_back(
        planes, 2, (dr,) + kept[0], blocked(own_new), blocked(other_new), held)
    tail, dvs, dv2, dv3, two_sum, piece0, piece1, one_sum = back(
        planes, dr, (xp, n1, s2, n2), (wbig, d1, d2, vs, v2), dkern, blocked(own), blocked(other), held)
    pointwise_own, flat_sum, vector_sum, info = finish(
        planes, (piece0, piece1, piece2), tail, dvs, dv2, dv3, dvec, dbin, dfinal, dbias, loss, head_sum, two_sum,
        one_sum)
    loss_total, valid_total, gradient_norm, factor = info[0, 0], info[0, 1], info[0, 2], info[0, 3]
    pointwise_own = pointwise_own.reshape(pointwise_first.shape).astype(F32)
    flat_sum = flat_sum.reshape(-1)
    vector_sum = vector_sum.reshape(-1)[:VECTOR]
    step_float = step_count.astype(F32)
    rows_owned = pointwise_first.shape[0]
    master_rows = pointwise_weight.reshape(2 * LAYERS * C3, HID // 2)
    master_own = lax.dynamic_slice_in_dim(master_rows, lax.axis_index("dp") * rows_owned, rows_owned, 0)
    pointwise_out = adam_update(master_own, pointwise_first, pointwise_second, factor * pointwise_own, step_float, LEARN_RATE)
    flat_out = adam_update(flat_weight, flat_first, flat_second, factor * flat_sum, step_float, LEARN_RATE)
    vector_out = adam_update(vector_weight, vector_first, vector_second, factor * vector_sum, step_float, VECTOR_RATE)
    return (loss_total, valid_total, gradient_norm, *pointwise_out, *flat_out, *vector_out)


def solution(mesh):
    placed = (P("dp", "mp", None), P("dp"), P("dp"), P(None, "dp"), P(), P(None, None, None, "mp"), P("dp", "mp"),
              P("dp", "mp"), P(), P(), P(), P(), P(), P())
    return jax.shard_map(
        per_device,
        mesh=mesh,
        in_specs=placed,
        out_specs=(P(), P(), P()) + (P("dp", "mp"),) * 4 + (P(),) * 8,
        check_vma=False,
    )
```
